32 devices in a mesh: dp: 16 (over z, x, core), fsdp: 2 (over y).
Axes of the slice: x: 2, y: 2, z: 4, core: 2. Of those that a mesh axis runs over, the one named last changes fastest.
Arguments:
- tokens: bfloat16 [32, 512, 768], P(('dp', 'fsdp')), may hold values from -6 to 6
- context: bfloat16 [32, 1024, 768], P(('dp', 'fsdp')), may hold values from -6 to 6
- past_coeffs: bfloat16 [32, 512, 768], P(('dp', 'fsdp')), may hold values from -6 to 6
- doc_lengths: int32 [32, 4], P(('dp', 'fsdp')), may hold values from 1 to 256, 512 in all within a row
- carried: int32 [32], P(('dp', 'fsdp')), may hold values 0 or 1
- histogram: int32 [32, 64], P(('dp', 'fsdp')), may hold values from 1 to 128, 512 in all within a row
- cotangent: bfloat16 [32, 512, 768], P(('dp', 'fsdp')), may hold values from -6 to 6
- attn_gain: bfloat16 [768], P(('dp', 'fsdp')), may hold values from 0.5 to 1.5
- attn_shift: bfloat16 [768], P(('dp', 'fsdp')), may hold values from -2 to 2
- project_in: bfloat16 [768, 2304], P('dp', 'fsdp'), may hold values from -0.21875 to 0.21875
- query_bias: bfloat16 [768], P(('dp', 'fsdp')), may hold values from -2 to 2
- value_bias: bfloat16 [768], P(('dp', 'fsdp')), may hold values from -2 to 2
- project_out: bfloat16 [768, 768], P('dp', 'fsdp'), may hold values from -0.625 to 0.625
- out_bias: bfloat16 [768], P(('dp', 'fsdp')), may hold values from -2 to 2
- memory_keys: bfloat16 [768, 768], P('dp', 'fsdp'), may hold values from -0.21875 to 0.21875
- memory_values: bfloat16 [768, 768], P('dp', 'fsdp'), may hold values from -0.4375 to 0.4375
- centre_weight: bfloat16 [512, 12], P(('dp', 'fsdp')), may hold values from -0.25 to 0.25
- spread_weight: bfloat16 [512, 12], P(('dp', 'fsdp')), may hold values from -0.25 to 0.25
- mlp_gain: bfloat16 [768], P(('dp', 'fsdp')), may hold values from 0.5 to 1.5
- mlp_shift: bfloat16 [768], P(('dp', 'fsdp')), may hold values from -2 to 2
- up_weight: bfloat16 [768, 3072], P('dp', 'fsdp'), may hold values from -0.21875 to 0.21875
- up_bias: bfloat16 [3072], P(('dp', 'fsdp')), may hold values from -2 to 2
- down_weight: bfloat16 [3072, 768], P('dp', 'fsdp'), may hold values from -0.109375 to 0.109375
- down_bias: bfloat16 [768], P(('dp', 'fsdp')), may hold values from -2 to 2
Outputs:
- output: bfloat16 [32, 512, 768], P(('dp', 'fsdp'))
- grad_tokens: float32 [32, 512, 768], P(('dp', 'fsdp'))
- grad_attn_gain: float32 [768], P(('dp', 'fsdp'))
- grad_attn_shift: float32 [768], P(('dp', 'fsdp'))
- grad_project_in: float32 [768, 2304], P('dp', 'fsdp')
- grad_query_bias: float32 [768], P(('dp', 'fsdp'))
- grad_value_bias: float32 [768], P(('dp', 'fsdp'))
- grad_project_out: float32 [768, 768], P('dp', 'fsdp')
- grad_out_bias: float32 [768], P(('dp', 'fsdp'))
- grad_memory_keys: float32 [768, 768], P('dp', 'fsdp')
- grad_memory_values: float32 [768, 768], P('dp', 'fsdp')
- grad_centre_weight: float32 [512, 12], P(('dp', 'fsdp'))
- grad_spread_weight: float32 [512, 12], P(('dp', 'fsdp'))
- grad_mlp_gain: float32 [768], P(('dp', 'fsdp'))
- grad_mlp_shift: float32 [768], P(('dp', 'fsdp'))
- grad_up_weight: float32 [768, 3072], P('dp', 'fsdp')
- grad_up_bias: float32 [3072], P(('dp', 'fsdp'))
- grad_down_weight: float32 [3072, 768], P('dp', 'fsdp')
- grad_down_bias: float32 [768], P(('dp', 'fsdp'))
- locations: float32 [32, 512], P(('dp', 'fsdp'))
The draws below stay inside these ranges and needn't reach their ends.
Inputs may be any that keep to these rules, and one draw needn't show every extreme that they name: `doc_lengths`: the 4 document lengths of a segment, in order, sum to 512. `histogram`: A segment's 64 bin counts sum to 512.
All inputs are finite; a program needn't handle non-finite values. No bound on the sum of `carried` on one device may be relied on, other than what follows from the above.
Results may differ from the reference program's by a relative error of at most 0.025.
Values may be sent and summed in bfloat16 or wider, within the bound.
No kernel may reach another device: no remote copies, remote signals or barrier semaphores. Data moves between devices by JAX's collectives and lax.ppermute only.
A program may use at most 192 MiB of HBM per device.

```python
import math
import jax
import jax.numpy as jnp
import numpy as np
from jax import lax

D = 768
H = 12
FF = 3072
DH = 64
N = 512
SEG = 512
CTX = 1024
M = 512
NBINS = 64
DOCS = 4
SEGMENTS = 32


def with_ends(drawn, key, smallest, largest):
    shape = drawn.shape
    index_at = [jax.random.randint(jax.random.fold_in(key, axis), (), 0, shape[axis]) for axis in range(len(shape))]
    drawn = drawn.at[tuple(index_at)].set(smallest)
    longest = shape.index(max(shape))
    index_at[longest] = (index_at[longest] + 1) % shape[longest]
    return drawn.at[tuple(index_at)].set(largest)


def level_of(own_key, shape, cuts, least, high):
    gain, own = 1.0, jax.random.fold_in(own_key, 6)
    for position, parts in cuts:
        steps = jnp.exp(jax.random.uniform(jax.random.fold_in(own, position), (parts,), jnp.float32, least / len(cuts), high / len(cuts)))
        gain = gain * jnp.repeat(steps, shape[position] // parts).reshape([-1 if axis == position else 1 for axis in range(len(shape))])
    return gain


def length_profile(number_of, total, reach, slope):
    portions = [(1 << 20) // math.isqrt(standing ** slope) + 1 for standing in range(2, number_of + 1)]
    rest, counts = total - reach - (number_of - 1), [1] * (number_of - 1)
    while rest > 0:
        candidates = [i for i in range(number_of - 1) if counts[i] < reach]
        pool, left = sum([portions[i] for i in candidates]), rest
        for i in candidates:
            addition = min(reach - counts[i], max(1, left * portions[i] // pool), rest)
            counts[i] = counts[i] + addition
            rest = rest - addition
    return np.array([reach] + counts)


def uneven_parts(key, amount, total, limit, lean):
    if amount == 2:
        one = jax.random.randint(key, (), max(1, total - limit), min(limit, total - 1) + 1)
        return jnp.stack([one, total - one])
    sizes = jnp.asarray(length_profile(amount, total, limit, lean), jnp.int32)
    twos = (amount - 1) // 2
    source_of, receiver = sizes[1:1 + 2 * twos:2], sizes[2:2 + 2 * twos:2]
    room = jnp.minimum(source_of - 1, limit - receiver)
    shifted = jax.random.randint(jax.random.fold_in(key, 1), (twos,), 0, 1 << 20) % (room + 1)
    sizes = sizes.at[1:1 + 2 * twos:2].set(source_of - shifted).at[2:2 + 2 * twos:2].set(receiver + shifted)
    return sizes[jax.random.permutation(jax.random.fold_in(key, 2), amount)]


def scatter_about(stream_key, extent, scale, limit, split=(), kind=jnp.bfloat16):
    loudness = level_of(stream_key, extent, split, -0.22, 0.18) if split else 1.0
    array = jax.random.normal(stream_key, extent, jnp.float32) * scale * loudness
    return jnp.minimum(jnp.maximum(array, -limit), limit).astype(kind)


def setup_inputs(seed: int = 0) -> dict:
    key_list = jax.random.split(jax.random.key(seed), 25)
    return {
        "tokens": scatter_about(key_list[0], (SEGMENTS, SEG, D), 1.0, 6.0, ((0, 32),)),
        "context": scatter_about(key_list[1], (SEGMENTS, CTX, D), 1.0, 6.0, ((0, 32),)),
        "past_coeffs": scatter_about(key_list[2], (SEGMENTS, N, D), 0.4, 6.0, ((0, 32),)),
        "doc_lengths": jax.vmap(lambda own: uneven_parts(own, DOCS, SEG, SEG // 2, 1))(jax.random.split(key_list[3], SEGMENTS)).reshape((SEGMENTS, DOCS)).astype(jnp.int32),
        "carried": with_ends((jax.random.randint(key_list[4], (SEGMENTS,), 0, 4) < 3).astype(jnp.int32), jax.random.fold_in(key_list[4], 1), 0, 1),
        "histogram": jax.vmap(lambda own: uneven_parts(own, NBINS, M, M // 4, 2))(jax.random.split(key_list[5], SEGMENTS)).reshape((SEGMENTS, NBINS)).astype(jnp.int32),
        "cotangent": scatter_about(key_list[6], (SEGMENTS, SEG, D), 1.0, 6.0, ((0, 32),)),
        "attn_gain": jnp.clip(1.0 + 0.1 * jax.random.normal(key_list[7], (D,), jnp.float32), 0.5, 1.5).astype(jnp.bfloat16),
        "attn_shift": scatter_about(key_list[8], (D,), 0.3, 2.0, ((0, 32),)),
        "project_in": scatter_about(key_list[9], (D, 3 * D), D ** -0.5, 0.21875, ((0, 16), (1, 2))),
        "query_bias": scatter_about(key_list[10], (D,), 0.3, 2.0, ((0, 32),)),
        "value_bias": scatter_about(key_list[11], (D,), 0.3, 2.0, ((0, 32),)),
        "project_out": scatter_about(key_list[12], (D, D), (D // 8) ** -0.5, 0.625, ((0, 16), (1, 2))),
        "out_bias": scatter_about(key_list[13], (D,), 0.3, 2.0, ((0, 32),)),
        "memory_keys": scatter_about(key_list[14], (D, D), D ** -0.5, 0.21875, ((0, 16), (1, 2))),
        "memory_values": scatter_about(key_list[15], (D, D), (D // 4) ** -0.5, 0.4375, ((0, 16), (1, 2))),
        "centre_weight": scatter_about(key_list[16], (N, H), N ** -0.5, 0.25, ((0, 32),)),
        "spread_weight": scatter_about(key_list[17], (N, H), N ** -0.5, 0.25, ((0, 32),)),
        "mlp_gain": jnp.clip(1.0 + 0.1 * jax.random.normal(key_list[18], (D,), jnp.float32), 0.5, 1.5).astype(jnp.bfloat16),
        "mlp_shift": scatter_about(key_list[19], (D,), 0.3, 2.0, ((0, 32),)),
        "up_weight": scatter_about(key_list[20], (D, FF), D ** -0.5, 0.21875, ((0, 16), (1, 2))),
        "up_bias": scatter_about(key_list[21], (FF,), 0.3, 2.0, ((0, 32),)),
        "down_weight": scatter_about(key_list[22], (FF, D), FF ** -0.5, 0.109375, ((0, 16), (1, 2))),
        "down_bias": scatter_about(key_list[23], (D,), 0.3, 2.0, ((0, 32),)),
    }


precise = lax.Precision.HIGHEST
memory_tau = 0.75
ridge_weight = 1.0
norm_epsilon = 1e-05
spread_scale = 0.25
masked_fill = -1e+30

@jax.custom_vjp
def low(v):
    return lax.optimization_barrier(v.astype(jnp.bfloat16)).astype(jnp.float32)

@jax.custom_vjp
def low_back(v):
    return v

def low_keep(v):
    return (low(v), None)

def low_pass(kept, grad):
    return (grad,)

def back_keep(v):
    return (v, None)

def back_low(kept, grad):
    return (low(grad),)
low.defvjp(low_keep, low_pass)
low_back.defvjp(back_keep, back_low)

def matmul_high(left_side, right_factor):
    return jnp.dot(left_side, right_factor, precision=precise)

def layer_norm(values, norm_gain, norm_shift):
    row_mean = lax.optimization_barrier(jnp.mean(values, axis=-1, keepdims=True))
    centred = values - row_mean
    variance = lax.optimization_barrier(jnp.mean(centred * centred, axis=-1, keepdims=True))
    return centred * lax.rsqrt(variance + norm_epsilon) * norm_gain + norm_shift

def gelu_tanh(values):
    return jax.nn.gelu(values, approximate=True)

def basis_table(points):
    centres = (jnp.arange(N, dtype=jnp.float32) + 0.5) / N
    distance = points[:, None] - centres[None, :]
    return jnp.exp(-0.5 * distance * distance * (N * N))

def sample_points(histogram):
    bin_ends = jnp.cumsum(histogram)
    bin_starts = bin_ends - histogram
    sample_slots = jnp.arange(M, dtype=jnp.int32)
    inside = ((sample_slots[:, None] >= bin_starts[None, :]) & (sample_slots[:, None] < bin_ends[None, :])).astype(jnp.int32)
    bin_first = lax.optimization_barrier(jnp.sum(inside * bin_starts[None, :], axis=1))
    bin_count = lax.optimization_barrier(jnp.sum(inside * histogram[None, :], axis=1))
    bin_number = lax.optimization_barrier(jnp.sum(inside * jnp.arange(NBINS, dtype=jnp.int32)[None, :], axis=1))
    offset = (sample_slots - bin_first).astype(jnp.float32) + 0.5
    return (bin_number.astype(jnp.float32) + offset / bin_count.astype(jnp.float32)) / NBINS

def memory_coeffs(context_rows, past_rows, points):
    past_values = matmul_high(basis_table(points), past_rows.astype(jnp.float32))
    recent = memory_tau + (1.0 - memory_tau) * (jnp.arange(CTX, dtype=jnp.float32) + 0.5) / CTX
    positions = jnp.concatenate([memory_tau * points, recent])
    design = basis_table(positions)
    gram_matrix = matmul_high(design.T, design) + ridge_weight * jnp.eye(N, dtype=jnp.float32)
    stacked = jnp.concatenate([past_values, context_rows.astype(jnp.float32)], axis=0)
    right_side = matmul_high(design.T, stacked)
    factor = jnp.linalg.cholesky(gram_matrix)
    return jax.scipy.linalg.cho_solve((factor, True), right_side)

def read_local(memory_scores, centre_weight, spread_weight):
    centres = (jnp.arange(N, dtype=jnp.float32) + 0.5) / N
    centre = jax.nn.sigmoid(jnp.einsum('shn,nh->sh', memory_scores, centre_weight, precision=precise))
    spread = spread_scale * jax.nn.softplus(jnp.einsum('shn,nh->sh', memory_scores, spread_weight, precision=precise))
    variance = 1.0 / (N * N) + spread * spread
    distance = centre[..., None] - centres
    return lax.rsqrt(variance)[..., None] / N * jnp.exp(-0.5 * distance * distance / variance[..., None])

def doc_masks(lengths, carry_flag):
    doc_ends = jnp.cumsum(lengths)
    places = jnp.arange(SEG, dtype=jnp.int32)
    document = lax.optimization_barrier(jnp.sum((places[:, None] >= doc_ends[None, :]).astype(jnp.int32), axis=1))
    allowed = (places[:, None] >= places[None, :]) & (document[:, None] == document[None, :])
    reading = (document == 0).astype(jnp.int32) * carry_flag
    return (allowed, reading.astype(jnp.float32))

def segment_forward(params, tokens_seg, coeff_low, allowed, reading):
    attn_gain, attn_shift, project_in, query_bias, value_bias, project_out, out_bias, memory_keys, memory_values, centre_weight, spread_weight, mlp_gain, mlp_shift, up_weight, up_bias, down_weight, down_bias = params
    model_width = H * DH
    score_scale = DH ** (-0.5)
    normed = low(layer_norm(tokens_seg, attn_gain, attn_shift))
    in_bias = jnp.concatenate([query_bias, jnp.zeros_like(query_bias), value_bias])
    projected = low(low_back(matmul_high(normed, project_in) + in_bias))
    queries = projected[:, :model_width].reshape(SEG, H, DH)
    key_rows = projected[:, model_width:2 * model_width].reshape(SEG, H, DH)
    values = projected[:, 2 * model_width:].reshape(SEG, H, DH)
    raw_scores = low_back(jnp.einsum('shd,thd->hst', queries, key_rows, precision=precise) * score_scale)
    scores = jnp.where(allowed[None], raw_scores, masked_fill)
    attn_probs = low(jax.nn.softmax(scores, axis=-1))
    short_term = jnp.einsum('hst,thd->shd', attn_probs, values, precision=precise)
    memory_key_rows = low(low_back(matmul_high(coeff_low, memory_keys))).reshape(N, H, DH)
    memory_value_rows = low(low_back(matmul_high(coeff_low, memory_values))).reshape(N, H, DH)
    memory_scores = low_back(jnp.einsum('shd,nhd->shn', queries, memory_key_rows, precision=precise) * score_scale)
    density = low(read_local(memory_scores, centre_weight, spread_weight))
    recall = jnp.einsum('shn,nhd->shd', density, memory_value_rows, precision=precise)
    head_outputs = low(low_back(short_term + recall * reading[:, None, None])).reshape(SEG, model_width)
    middle = tokens_seg + low_back(matmul_high(head_outputs, project_out) + out_bias)
    normed_mlp = low(layer_norm(middle, mlp_gain, mlp_shift))
    hidden = low_back(matmul_high(normed_mlp, up_weight) + up_bias)
    active = low(gelu_tanh(hidden))
    return middle + matmul_high(active, down_weight) + down_bias

def reference(tokens, context, past_coeffs, doc_lengths, carried, histogram, cotangent, attn_gain, attn_shift, project_in, query_bias, value_bias, project_out, out_bias, memory_keys, memory_values, centre_weight, spread_weight, mlp_gain, mlp_shift, up_weight, up_bias, down_weight, down_bias):
    points = jax.vmap(sample_points)(histogram)
    coeffs = lax.map(lambda segment_item: memory_coeffs(segment_item[0], segment_item[1], segment_item[2]), (context, past_coeffs, points))
    coeff_low = lax.optimization_barrier(coeffs.astype(jnp.bfloat16)).astype(jnp.float32)
    params = jax.tree.map(lambda weight_piece: weight_piece.astype(jnp.float32), (attn_gain, attn_shift, project_in, query_bias, value_bias, project_out, out_bias, memory_keys, memory_values, centre_weight, spread_weight, mlp_gain, mlp_shift, up_weight, up_bias, down_weight, down_bias))

    def whole_layer(params_float, tokens_float):

        def run_segment(segment_item):
            tokens_seg, coeff_seg, lengths_seg, carry_seg = segment_item
            allowed, reading = doc_masks(lengths_seg, carry_seg)
            return segment_forward(params_float, tokens_seg, coeff_seg, allowed, reading)
        return lax.map(jax.checkpoint(run_segment), (tokens_float, coeff_low, doc_lengths, carried))
    outputs, pullback = jax.vjp(whole_layer, params, tokens.astype(jnp.float32))
    grad_params, grad_tokens = pullback(cotangent.astype(jnp.float32))
    return (outputs.astype(jnp.bfloat16), grad_tokens, grad_params[0], grad_params[1], grad_params[2], grad_params[3], grad_params[4], grad_params[5], grad_params[6], grad_params[7], grad_params[8], grad_params[9], grad_params[10], grad_params[11], grad_params[12], grad_params[13], grad_params[14], grad_params[15], grad_params[16], points)
```

```python
import functools

import jax
import jax.numpy as jnp
from jax import lax
from jax.experimental import pallas as pl
from jax.experimental.pallas import tpu as pltpu
from jax.sharding import PartitionSpec as P

H = 12
DH = 64
N = 512
CTX = 1024
M = 512
NBINS = 64


precise = lax.Precision.HIGHEST
memory_tau = 0.75
ridge_weight = 1.0
norm_epsilon = 1e-05
spread_scale = 0.25
masked_fill = -1e30


def layer_norm(values, norm_gain, norm_shift):
    row_mean = jnp.mean(values, axis=-1, keepdims=True)
    centred = values - row_mean
    variance = jnp.mean(centred * centred, axis=-1, keepdims=True)
    return centred * lax.rsqrt(variance + norm_epsilon) * norm_gain + norm_shift


def gelu_tanh(values):
    return jax.nn.gelu(values, approximate=True)


def basis_table(points):
    centres = (jnp.arange(N, dtype=jnp.float32) + 0.5) / N
    distance = points[:, None] - centres[None, :]
    return jnp.exp(-0.5 * distance * distance * (N * N))


def sample_points(histogram):
    bin_ends = jnp.cumsum(histogram)
    bin_starts = bin_ends - histogram
    sample_slots = jnp.arange(M, dtype=jnp.int32)
    inside = (
        (sample_slots[:, None] >= bin_starts[None, :]) & (sample_slots[:, None] < bin_ends[None, :])
    ).astype(jnp.int32)
    bin_first = jnp.sum(inside * bin_starts[None, :], axis=1)
    bin_count = jnp.sum(inside * histogram[None, :], axis=1)
    bin_number = jnp.sum(inside * jnp.arange(NBINS, dtype=jnp.int32)[None, :], axis=1)
    offset = (sample_slots - bin_first).astype(jnp.float32) + 0.5
    return (bin_number.astype(jnp.float32) + offset / bin_count.astype(jnp.float32)) / NBINS


def memory_coeffs(context_rows, past_rows, points):
    past_values = jnp.dot(basis_table(points), past_rows.astype(jnp.float32), precision=precise)
    recent = memory_tau + (1.0 - memory_tau) * (jnp.arange(CTX, dtype=jnp.float32) + 0.5) / CTX
    positions = jnp.concatenate([memory_tau * points, recent])
    design = basis_table(positions)
    gram_matrix = jnp.dot(design.T, design, precision=precise) + ridge_weight * jnp.eye(
        N, dtype=jnp.float32
    )
    stacked = jnp.concatenate([past_values, context_rows.astype(jnp.float32)], axis=0)
    right_side = jnp.dot(design.T, stacked, precision=precise)
    factor = jnp.linalg.cholesky(gram_matrix)
    return jax.scipy.linalg.cho_solve((factor, True), right_side)


def read_local(memory_scores, centre_weight, spread_weight):
    centres = (jnp.arange(N, dtype=jnp.float32) + 0.5) / N
    centre = jax.nn.sigmoid(
        jnp.einsum("shn,nh->sh", memory_scores, centre_weight, precision=precise)
    )
    spread = spread_scale * jax.nn.softplus(
        jnp.einsum("shn,nh->sh", memory_scores, spread_weight, precision=precise)
    )
    variance = 1.0 / (N * N) + spread * spread
    distance = centre[..., None] - centres
    return (
        lax.rsqrt(variance)[..., None]
        / N
        * jnp.exp(-0.5 * distance * distance / variance[..., None])
    )


def doc_masks(lengths, carry_flag, seg_rows):
    doc_ends = jnp.cumsum(lengths)
    places = jnp.arange(seg_rows, dtype=jnp.int32)
    document = jnp.sum((places[:, None] >= doc_ends[None, :]).astype(jnp.int32), axis=1)
    allowed = (places[:, None] >= places[None, :]) & (document[:, None] == document[None, :])
    reading = (document == 0).astype(jnp.int32) * carry_flag
    return (allowed, reading.astype(jnp.float32))


BOTH = ("dp", "fsdp")
SMALL_COLUMNS = 128


def hypercube(mesh_sizes):
    return mesh_sizes == (16, 2)


def place_of():
    dp = lax.axis_index("dp")
    return dp // 4, (dp // 2) % 2, dp % 2, lax.axis_index("fsdp")


def hop(value, z=0, x=0, core=0, f=0):
    pairs = []
    for dp in range(16):
        for side in range(2):
            other = (((dp // 4) ^ z) * 4) + ((((dp // 2) % 2) ^ x) * 2) + ((dp % 2) ^ core)
            pairs.append((dp * 2 + side, other * 2 + (side ^ f)))
    return lax.ppermute(value, BOTH, pairs)


def gather_hops(block, x_first):
    quad = jnp.stack([block] + [hop(block, z=k) for k in (1, 2, 3)])
    first, second = (dict(x=1), dict(f=1)) if x_first else (dict(f=1), dict(x=1))
    near = hop(quad, **first)
    mine = [quad, near, hop(quad, **second), hop(near, **second)]
    return mine + [hop(part, core=1) for part in mine]


def block_offsets(x_first):
    for array in range(8):
        core, first, second = array // 4, array % 2, (array // 2) % 2
        x, f = (first, second) if x_first else (second, first)
        for z in range(4):
            yield array, z, z, x, core, f


def join_blocks(place, proj_parts, mem_parts, late_parts):
    rows, proj_columns = proj_parts[0].shape[1:]
    square = late_parts.shape[-1] // 9
    width = 16 * rows

    def kernel(place_ref, *refs):
        proj_refs, mem_refs, late_ref = refs[:8], refs[8:16], refs[16]
        proj, keys, values, small, out, up, down, sem = refs[17:]
        copies = []

        def move(source, target):
            copy = pltpu.make_async_copy(source, target, sem)
            copy.start()
            copies.append(copy)

        for x_first, parts in ((True, proj_refs), (False, mem_refs)):
            for array, index, z, x, core, f in block_offsets(x_first):
                dp = (place_ref[0] ^ z) * 4 + (place_ref[1] ^ x) * 2 + (place_ref[2] ^ core)
                side = place_ref[3] ^ f
                at = pl.ds(pl.multiple_of(dp * rows, 16), rows)
                source = parts[array].at[index]
                if x_first:
                    move(source, proj.at[at, pl.ds(pl.multiple_of(side * proj_columns, 128), proj_columns)])
                else:
                    across = pl.ds(pl.multiple_of(side * square, 128), square)
                    move(source.at[:, pl.ds(0, square)], keys.at[at, across])
                    move(source.at[:, pl.ds(square, square)], values.at[at, across])
                    move(source.at[:, pl.ds(2 * square, SMALL_COLUMNS)], small.at[dp * 2 + side])
        for dp in range(16):
            for side in range(2):
                source = late_ref.at[dp * 2 + side]
                at = pl.ds(dp * rows, rows)
                move(source.at[:, pl.ds(0, square)], out.at[at, pl.ds(side * square, square)])
                move(source.at[:, pl.ds(square, 4 * square)], up.at[at, pl.ds(side * 4 * square, 4 * square)])
                for q in range(4):
                    move(
                        source.at[:, pl.ds((5 + q) * square, square)],
                        down.at[pl.ds(dp * 4 * rows + q * rows, rows), pl.ds(side * square, square)],
                    )
        for copy in copies:
            copy.wait()

    shapes = [
        (width, 2 * proj_columns),
        (width, width),
        (width, width),
        (32, rows, SMALL_COLUMNS),
        (width, width),
        (width, 4 * width),
        (4 * width, width),
    ]
    return pl.pallas_call(
        kernel,
        out_shape=[jax.ShapeDtypeStruct(shape, jnp.bfloat16) for shape in shapes],
        in_specs=[pl.BlockSpec(memory_space=pltpu.SMEM)] + [pl.BlockSpec(memory_space=pl.ANY)] * 17,
        out_specs=[pl.BlockSpec(memory_space=pl.ANY)] * 7,
        scratch_shapes=[pltpu.SemaphoreType.DMA],
        cost_estimate=pl.CostEstimate(flops=0, bytes_accessed=33_000_000, transcendentals=0),
    )(place, *proj_parts, *mem_parts, late_parts)


def collect_hops(shards):
    rows, square = shards[5].shape
    vectors = [shards[k] for k in VECTORS]
    small = jnp.concatenate([v.reshape(-1) for v in vectors + [shards[k] for k in TABLES]])
    small = jnp.pad(small, (0, rows * SMALL_COLUMNS - small.shape[0])).reshape(rows, SMALL_COLUMNS)
    late = jnp.concatenate(
        [shards[5], shards[13]] + [shards[15][q * rows : (q + 1) * rows] for q in range(4)], axis=1
    )
    late_parts = lax.all_gather(late, BOTH, axis=0)
    mem_parts = gather_hops(jnp.concatenate([shards[7], shards[8], small], axis=1), False)
    proj_parts = gather_hops(shards[2], True)
    place = jnp.stack(place_of()).astype(jnp.int32)
    proj, keys, values, small, out, up, down = join_blocks(place, proj_parts, mem_parts, late_parts)
    small = small.reshape(32, rows * SMALL_COLUMNS)
    found = {2: proj, 5: out, 7: keys, 8: values, 13: up, 15: down}
    at = 0
    for k in VECTORS + TABLES:
        size = shards[k].size
        found[k] = small[:, at : at + size].reshape((-1,) + shards[k].shape[1:])
        at += size
    return tuple(found[k] for k in range(17))


VECTORS = [0, 1, 3, 4, 6, 11, 12, 16, 14]
TABLES = [9, 10]
COLUMN_SPLIT = (2, 5, 7, 8, 13, 15)


def collect(shards, mesh_sizes):
    if hypercube(mesh_sizes):
        return collect_hops(shards)

    def whole(k, shard):
        near = lax.all_gather(shard, "fsdp", axis=1 if k in COLUMN_SPLIT else 0, tiled=True)
        return lax.all_gather(near, "dp", axis=0, tiled=True)

    return tuple(whole(k, shard) for k, shard in enumerate(shards))


def scatter_hops(total, x_first):
    z, x, core, f = place_of()
    rows, columns = total.shape
    value = total.reshape(4, 2, 2, rows // 16, columns)

    def pick(array, axis, index):
        return lax.dynamic_index_in_dim(array, index, axis, keepdims=False)

    def pick_columns(array, index):
        return lax.dynamic_slice_in_dim(array, index * (columns // 2), columns // 2, array.ndim - 1)

    def plus(a, b):
        return (a.astype(jnp.float32) + b.astype(jnp.float32)).astype(jnp.bfloat16)

    kept, got = pick(value, 2, core), hop(pick(value, 2, 1 - core), core=1)

    def by_x(kept, got):
        sent = plus(pick(kept, 1, 1 - x), pick(got, 1, 1 - x))
        return plus(pick(kept, 1, x), pick(got, 1, x)), hop(sent, x=1)

    def by_f(kept, got):
        sent = plus(pick_columns(kept, 1 - f), pick_columns(got, 1 - f))
        return plus(pick_columns(kept, f), pick_columns(got, f)), hop(sent, f=1)

    for step in (by_x, by_f) if x_first else (by_f, by_x):
        kept, got = step(kept, got)
    result = pick(kept, 0, z).astype(jnp.float32) + pick(got, 0, z).astype(jnp.float32)
    for k in (1, 2, 3):
        result = result + hop(plus(pick(kept, 0, z ^ k), pick(got, 0, z ^ k)), z=k).astype(jnp.float32)
    return result


def spread_hops(grads, shards):
    bf = jnp.bfloat16
    rows, square = shards[5].shape
    summed = {13: scatter_hops(grads[13].astype(bf), True), 15: scatter_hops(grads[15].astype(bf), False)}
    halves = [grads[k].astype(bf).reshape(-1, 2, square) for k in (5, 7, 8)]
    middle = scatter_hops(jnp.concatenate(halves, axis=2).reshape(-1, 6 * square), False)
    for n, k in enumerate((5, 7, 8)):
        summed[k] = middle[:, n * square : (n + 1) * square]
    small = jnp.concatenate([grads[k].astype(bf).reshape(32, -1) for k in VECTORS + TABLES], axis=1)
    small = jnp.pad(small, ((0, 0), (0, rows * SMALL_COLUMNS - small.shape[1])))
    small = small.reshape(16, 2, rows, SMALL_COLUMNS).transpose(0, 2, 1, 3).reshape(-1, 2, SMALL_COLUMNS)
    proj = grads[2].astype(bf).reshape(small.shape[0], 2, -1)
    last = jnp.concatenate([proj, small], axis=2)
    last = scatter_hops(last.reshape(last.shape[0], -1), True)
    summed[2] = last[:, : proj.shape[2]]
    small, at = last[:, proj.shape[2] :].reshape(-1), 0
    for k in VECTORS + TABLES:
        summed[k] = small[at : at + shards[k].size].reshape(shards[k].shape)
        at += shards[k].size
    return tuple(summed[k] for k in range(17))


def spread(grads, shards, mesh_sizes):
    if hypercube(mesh_sizes):
        return spread_hops(grads, shards)

    def part(k, grad):
        near = lax.psum_scatter(grad.astype(jnp.bfloat16), "dp", scatter_dimension=0, tiled=True)
        axis = 1 if k in COLUMN_SPLIT else 0
        return lax.psum_scatter(near, "fsdp", scatter_dimension=axis, tiled=True).astype(jnp.float32)

    return tuple(part(k, grad) for k, grad in enumerate(grads))


def short_scores(queries, key_rows, allowed):
    raw_scores = jnp.einsum(
        "shd,thd->hst", queries, key_rows, preferred_element_type=jnp.float32
    ) * DH ** (-0.5)
    return jnp.where(allowed[None], raw_scores, masked_fill)


def forward_segment(tokens_seg, coeff_low, allowed, reading, weights):
    (
        attn_gain,
        attn_shift,
        project_in,
        query_bias,
        value_bias,
        project_out,
        out_bias,
        memory_keys,
        memory_values,
        centre_weight,
        spread_weight,
        mlp_gain,
        mlp_shift,
        up_weight,
        up_bias,
        down_weight,
        down_bias,
    ) = weights
    seg_rows = tokens_seg.shape[0]
    model_width = H * DH
    score_scale = DH ** (-0.5)
    inputs = tokens_seg.astype(jnp.float32)
    normed = layer_norm(
        inputs, attn_gain.astype(jnp.float32), attn_shift.astype(jnp.float32)
    ).astype(jnp.bfloat16)
    in_bias = jnp.concatenate([query_bias, jnp.zeros_like(query_bias), value_bias]).astype(
        jnp.float32
    )
    projected = (jnp.dot(normed, project_in, preferred_element_type=jnp.float32) + in_bias).astype(
        jnp.bfloat16
    )
    queries = projected[:, :model_width].reshape(seg_rows, H, DH)
    key_rows = projected[:, model_width : 2 * model_width].reshape(seg_rows, H, DH)
    values = projected[:, 2 * model_width :].reshape(seg_rows, H, DH)
    scores = short_scores(queries, key_rows, allowed)
    log_total = jax.nn.logsumexp(scores, axis=-1, keepdims=True)
    probs_low = jnp.exp(scores - log_total).astype(jnp.bfloat16)
    short_term = jnp.einsum("hst,thd->shd", probs_low, values, preferred_element_type=jnp.float32)
    basis_rows = coeff_low.shape[0]
    memory_key_rows = (
        jnp.dot(coeff_low, memory_keys, preferred_element_type=jnp.float32)
        .astype(jnp.bfloat16)
        .reshape(basis_rows, H, DH)
    )
    memory_value_rows = (
        jnp.dot(coeff_low, memory_values, preferred_element_type=jnp.float32)
        .astype(jnp.bfloat16)
        .reshape(basis_rows, H, DH)
    )
    memory_scores = (
        jnp.einsum("shd,nhd->shn", queries, memory_key_rows, preferred_element_type=jnp.float32)
        * score_scale
    )
    density = read_local(
        memory_scores, centre_weight.astype(jnp.float32), spread_weight.astype(jnp.float32)
    ).astype(jnp.bfloat16)
    recall = jnp.einsum(
        "shn,nhd->shd", density, memory_value_rows, preferred_element_type=jnp.float32
    )
    head_outputs = (
        (short_term + recall * reading[:, None, None])
        .astype(jnp.bfloat16)
        .reshape(seg_rows, model_width)
    )
    middle = (
        inputs
        + jnp.dot(head_outputs, project_out, preferred_element_type=jnp.float32)
        + out_bias.astype(jnp.float32)
    )
    normed_mlp = layer_norm(
        middle, mlp_gain.astype(jnp.float32), mlp_shift.astype(jnp.float32)
    ).astype(jnp.bfloat16)
    hidden = jnp.dot(normed_mlp, up_weight, preferred_element_type=jnp.float32) + up_bias.astype(
        jnp.float32
    )
    active = gelu_tanh(hidden).astype(jnp.bfloat16)
    result = (
        middle
        + jnp.dot(active, down_weight, preferred_element_type=jnp.float32)
        + down_bias.astype(jnp.float32)
    )
    kept_state = (
        inputs,
        normed,
        projected,
        log_total,
        memory_key_rows,
        memory_value_rows,
        memory_scores,
        density,
        head_outputs,
        middle,
        normed_mlp,
        hidden,
        active,
    )
    return (result, kept_state)


def backward_segment(cot_values, coeff_low, allowed, reading, kept_state, weights):
    (
        attn_gain,
        attn_shift,
        project_in,
        query_bias,
        value_bias,
        project_out,
        out_bias,
        memory_keys,
        memory_values,
        centre_weight,
        spread_weight,
        mlp_gain,
        mlp_shift,
        up_weight,
        up_bias,
        down_weight,
        down_bias,
    ) = weights
    (
        inputs,
        normed,
        projected,
        log_total,
        memory_key_rows,
        memory_value_rows,
        memory_scores,
        density,
        head_outputs,
        middle,
        normed_mlp,
        hidden,
        active,
    ) = kept_state
    seg_rows = cot_values.shape[0]
    basis_rows = coeff_low.shape[0]
    model_width = H * DH
    score_scale = DH ** (-0.5)
    queries = projected[:, :model_width].reshape(seg_rows, H, DH)
    key_rows = projected[:, model_width : 2 * model_width].reshape(seg_rows, H, DH)
    values = projected[:, 2 * model_width :].reshape(seg_rows, H, DH)
    cot_float = cot_values.astype(jnp.float32)
    grad_down_bias = jnp.sum(cot_float, axis=0)
    grad_down_weight = jnp.einsum(
        "sf,sd->fd", active, cot_values, preferred_element_type=jnp.float32
    )
    grad_active = jnp.einsum(
        "sd,fd->sf", cot_values, down_weight, preferred_element_type=jnp.float32
    )
    gelu_back = jax.vjp(gelu_tanh, hidden)[1]
    grad_hidden = gelu_back(grad_active)[0].astype(jnp.bfloat16)
    grad_up_bias = jnp.sum(grad_hidden.astype(jnp.float32), axis=0)
    grad_up_weight = jnp.einsum(
        "sd,sf->df", normed_mlp, grad_hidden, preferred_element_type=jnp.float32
    )
    grad_normed_mlp = jnp.einsum(
        "sf,df->sd", grad_hidden, up_weight, preferred_element_type=jnp.float32
    )
    mlp_back = jax.vjp(
        layer_norm, middle, mlp_gain.astype(jnp.float32), mlp_shift.astype(jnp.float32)
    )[1]
    grad_middle_part, grad_mlp_gain, grad_mlp_shift = mlp_back(grad_normed_mlp)
    grad_middle = cot_float + grad_middle_part
    grad_attended = grad_middle.astype(jnp.bfloat16)
    grad_out_bias = jnp.sum(grad_attended.astype(jnp.float32), axis=0)
    grad_project_out = jnp.einsum(
        "se,sd->ed", head_outputs, grad_attended, preferred_element_type=jnp.float32
    )
    grad_heads = jnp.einsum(
        "sd,ed->se", grad_attended, project_out, preferred_element_type=jnp.float32
    )
    grad_heads = grad_heads.astype(jnp.bfloat16).reshape(seg_rows, H, DH)
    scores = short_scores(queries, key_rows, allowed)
    attn_probs = jnp.exp(scores - log_total)
    grad_probs = jnp.einsum("shd,thd->hst", grad_heads, values, preferred_element_type=jnp.float32)
    grad_values = jnp.einsum(
        "hst,shd->thd",
        attn_probs.astype(jnp.bfloat16),
        grad_heads,
        preferred_element_type=jnp.float32,
    )
    row_terms = jnp.sum(attn_probs * grad_probs, axis=-1, keepdims=True)
    grad_scores = (attn_probs * (grad_probs - row_terms)).astype(jnp.bfloat16)
    grad_queries = (
        jnp.einsum("hst,thd->shd", grad_scores, key_rows, preferred_element_type=jnp.float32)
        * score_scale
    )
    grad_keys = (
        jnp.einsum("hst,shd->thd", grad_scores, queries, preferred_element_type=jnp.float32)
        * score_scale
    )
    grad_recall = (grad_heads.astype(jnp.float32) * reading[:, None, None]).astype(jnp.bfloat16)
    grad_density = jnp.einsum(
        "shd,nhd->shn", grad_recall, memory_value_rows, preferred_element_type=jnp.float32
    )
    grad_mem_values = jnp.einsum(
        "shn,shd->nhd", density, grad_recall, preferred_element_type=jnp.float32
    )
    grad_mem_values = grad_mem_values.astype(jnp.bfloat16).reshape(basis_rows, model_width)
    read_back = jax.vjp(
        read_local,
        memory_scores,
        centre_weight.astype(jnp.float32),
        spread_weight.astype(jnp.float32),
    )[1]
    grad_mscores, grad_centre_weight, grad_spread_weight = read_back(grad_density)
    grad_mscores = grad_mscores.astype(jnp.bfloat16)
    grad_queries = (
        grad_queries
        + jnp.einsum(
            "shn,nhd->shd", grad_mscores, memory_key_rows, preferred_element_type=jnp.float32
        )
        * score_scale
    )
    grad_mem_keys = (
        jnp.einsum("shn,shd->nhd", grad_mscores, queries, preferred_element_type=jnp.float32)
        * score_scale
    )
    grad_mem_keys = grad_mem_keys.astype(jnp.bfloat16).reshape(basis_rows, model_width)
    grad_memory_keys = jnp.einsum(
        "nd,ne->de", coeff_low, grad_mem_keys, preferred_element_type=jnp.float32
    )
    grad_memory_values = jnp.einsum(
        "nd,ne->de", coeff_low, grad_mem_values, preferred_element_type=jnp.float32
    )
    grad_projected = jnp.concatenate(
        [
            grad_queries.reshape(seg_rows, model_width),
            grad_keys.reshape(seg_rows, model_width),
            grad_values.reshape(seg_rows, model_width),
        ],
        axis=1,
    ).astype(jnp.bfloat16)
    grad_columns = jnp.sum(grad_projected.astype(jnp.float32), axis=0)
    grad_query_bias = grad_columns[:model_width]
    grad_value_bias = grad_columns[2 * model_width :]
    grad_project_in = jnp.einsum(
        "sd,se->de", normed, grad_projected, preferred_element_type=jnp.float32
    )
    grad_normed = jnp.einsum(
        "se,de->sd", grad_projected, project_in, preferred_element_type=jnp.float32
    )
    attn_back = jax.vjp(
        layer_norm, inputs, attn_gain.astype(jnp.float32), attn_shift.astype(jnp.float32)
    )[1]
    grad_inputs_part, grad_attn_gain, grad_attn_shift = attn_back(grad_normed)
    grad_inputs = grad_middle + grad_inputs_part
    grads = (
        grad_attn_gain,
        grad_attn_shift,
        grad_project_in,
        grad_query_bias,
        grad_value_bias,
        grad_project_out,
        grad_out_bias,
        grad_memory_keys,
        grad_memory_values,
        grad_centre_weight,
        grad_spread_weight,
        grad_mlp_gain,
        grad_mlp_shift,
        grad_up_weight,
        grad_up_bias,
        grad_down_weight,
        grad_down_bias,
    )
    return (grad_inputs, grads)


def local(
    mesh_sizes,
    tokens,
    context,
    past_coeffs,
    doc_lengths,
    carried,
    histogram,
    cotangent,
    attn_gain,
    attn_shift,
    project_in,
    query_bias,
    value_bias,
    project_out,
    out_bias,
    memory_keys,
    memory_values,
    centre_weight,
    spread_weight,
    mlp_gain,
    mlp_shift,
    up_weight,
    up_bias,
    down_weight,
    down_bias,
):
    shards = (
        attn_gain,
        attn_shift,
        project_in,
        query_bias,
        value_bias,
        project_out,
        out_bias,
        memory_keys,
        memory_values,
        centre_weight,
        spread_weight,
        mlp_gain,
        mlp_shift,
        up_weight,
        up_bias,
        down_weight,
        down_bias,
    )
    weights = collect(shards, mesh_sizes)
    points = jax.vmap(sample_points)(histogram)
    seg_rows = tokens.shape[1]
    segment_index = 0
    coeff_low = memory_coeffs(
        context[segment_index], past_coeffs[segment_index], points[segment_index]
    ).astype(jnp.bfloat16)
    allowed, reading = doc_masks(doc_lengths[segment_index], carried[segment_index], seg_rows)
    result, kept_state = forward_segment(
        tokens[segment_index], coeff_low, allowed, reading, weights
    )
    results = [result.astype(jnp.bfloat16)]
    states = [kept_state]
    settings = [(coeff_low, allowed, reading)]
    segment_index = 0
    coeff_low, allowed, reading = settings[segment_index]
    grad_inputs, grads = backward_segment(
        cotangent[segment_index], coeff_low, allowed, reading, states[segment_index], weights
    )
    input_grads = [grad_inputs]
    (
        grad_attn_gain,
        grad_attn_shift,
        grad_project_in,
        grad_query_bias,
        grad_value_bias,
        grad_project_out,
        grad_out_bias,
        grad_memory_keys,
        grad_memory_values,
        grad_centre_weight,
        grad_spread_weight,
        grad_mlp_gain,
        grad_mlp_shift,
        grad_up_weight,
        grad_up_bias,
        grad_down_weight,
        grad_down_bias,
    ) = spread(grads, shards, mesh_sizes)
    return (
        jnp.stack(results),
        jnp.stack(input_grads),
        grad_attn_gain,
        grad_attn_shift,
        grad_project_in,
        grad_query_bias,
        grad_value_bias,
        grad_project_out,
        grad_out_bias,
        grad_memory_keys,
        grad_memory_values,
        grad_centre_weight,
        grad_spread_weight,
        grad_mlp_gain,
        grad_mlp_shift,
        grad_up_weight,
        grad_up_bias,
        grad_down_weight,
        grad_down_bias,
        points,
    )


def solution(mesh):
    in_specs = (
        P(("dp", "fsdp"), None, None),
        P(("dp", "fsdp"), None, None),
        P(("dp", "fsdp"), None, None),
        P(("dp", "fsdp"), None),
        P(("dp", "fsdp")),
        P(("dp", "fsdp"), None),
        P(("dp", "fsdp"), None, None),
        P(("dp", "fsdp")),
        P(("dp", "fsdp")),
        P("dp", "fsdp"),
        P(("dp", "fsdp")),
        P(("dp", "fsdp")),
        P("dp", "fsdp"),
        P(("dp", "fsdp")),
        P("dp", "fsdp"),
        P("dp", "fsdp"),
        P(("dp", "fsdp"), None),
        P(("dp", "fsdp"), None),
        P(("dp", "fsdp")),
        P(("dp", "fsdp")),
        P("dp", "fsdp"),
        P(("dp", "fsdp")),
        P("dp", "fsdp"),
        P(("dp", "fsdp")),
    )
    out_specs = (
        P(("dp", "fsdp"), None, None),
        P(("dp", "fsdp"), None, None),
        P(("dp", "fsdp")),
        P(("dp", "fsdp")),
        P("dp", "fsdp"),
        P(("dp", "fsdp")),
        P(("dp", "fsdp")),
        P("dp", "fsdp"),
        P(("dp", "fsdp")),
        P("dp", "fsdp"),
        P("dp", "fsdp"),
        P(("dp", "fsdp"), None),
        P(("dp", "fsdp"), None),
        P(("dp", "fsdp")),
        P(("dp", "fsdp")),
        P("dp", "fsdp"),
        P(("dp", "fsdp")),
        P("dp", "fsdp"),
        P(("dp", "fsdp")),
        P(("dp", "fsdp"), None),
    )
    sizes = (mesh.shape["dp"], mesh.shape["fsdp"])
    return jax.shard_map(functools.partial(local, sizes), mesh=mesh, in_specs=in_specs, out_specs=out_specs, check_vma=False)
```

```python
import functools

import jax
import jax.numpy as jnp
from jax import lax
from jax.experimental import pallas as pl
from jax.experimental.pallas import tpu as pltpu
from jax.sharding import PartitionSpec as P

H = 12
DH = 64
D = H * DH
N = 512
CTX = 1024
M = 512
NBINS = 64
FF = 4 * D
PAIRS = H // 2
PART = 128
TILE = 768

memory_tau = 0.75
ridge_weight = 1.0
norm_epsilon = 1e-05
spread_scale = 0.25
masked_fill = -1e30
score_scale = DH ** (-0.5)

F32, BF16 = jnp.float32, jnp.bfloat16
VMEM_LIMIT = 56 * 1024 * 1024
BOTH = ("dp", "fsdp")
HBM = pl.BlockSpec(memory_space=pl.ANY)
SMEM = pl.BlockSpec(memory_space=pltpu.SMEM)
VMEM = pl.BlockSpec(memory_space=pltpu.VMEM)


def shape_of(shape, dtype=BF16):
    return jax.ShapeDtypeStruct(shape, dtype)


def call(kernel, out_shape, in_specs, out_specs, scratch=(), flops=0, grid=None, moved=0):
    extra = {} if grid is None else {"grid": grid}
    return pl.pallas_call(
        kernel,
        out_shape=out_shape,
        in_specs=in_specs,
        out_specs=out_specs,
        scratch_shapes=list(scratch),
        compiler_params=pltpu.CompilerParams(vmem_limit_bytes=VMEM_LIMIT),
        cost_estimate=pl.CostEstimate(flops=flops, bytes_accessed=moved, transcendentals=0),
        **extra,
    )


def nn(a, b):
    return lax.dot_general(a, b, (((1,), (0,)), ((), ())), preferred_element_type=F32)


def nt(a, b):
    return lax.dot_general(a, b, (((1,), (1,)), ((), ())), preferred_element_type=F32)


def tn(a, b):
    return lax.dot_general(a, b, (((0,), (0,)), ((), ())), preferred_element_type=F32)


def split(value):
    high = value.astype(BF16)
    return high, (value - high.astype(F32)).astype(BF16)


def both_split(product, a, b):
    a_high, a_low = split(a)
    b_high, b_low = split(b)
    return product(a_high, b_high) + (product(a_high, b_low) + product(a_low, b_high))


def one_split(product, a, b):
    a_high, a_low = split(a)
    return product(a_high, b) + product(a_low, b)


def iota(shape, axis):
    return lax.broadcasted_iota(jnp.int32, shape, axis)


def gaussian(points, centres):
    distance = points - centres
    return jnp.exp(-0.5 * distance * distance * (N * N))


def normalise(values, gain, shift):
    mean = jnp.mean(values, axis=-1, keepdims=True)
    centred = values - mean
    variance = jnp.mean(centred * centred, axis=-1, keepdims=True)
    inverse = lax.rsqrt(variance + norm_epsilon)
    return centred * inverse * gain + shift


def normalise_back(values, gain, grad):
    mean = jnp.mean(values, axis=-1, keepdims=True)
    centred = values - mean
    variance = jnp.mean(centred * centred, axis=-1, keepdims=True)
    inverse = lax.rsqrt(variance + norm_epsilon)
    standard = centred * inverse
    scaled = grad * gain
    first = jnp.mean(scaled, axis=-1, keepdims=True)
    second = jnp.mean(scaled * standard, axis=-1, keepdims=True)
    back = inverse * (scaled - first - standard * second)
    return back, jnp.sum(grad * standard, axis=0, keepdims=True), jnp.sum(grad, axis=0, keepdims=True)


def system_kernel(hist_ref, past_ref, context_ref, points_ref, gram_ref, right_ref):
    hist = hist_ref[...]
    counts = jnp.broadcast_to(hist, (NBINS, NBINS))
    row, column = iota((NBINS, NBINS), 0), iota((NBINS, NBINS), 1)

    def down(keep):
        return jnp.sum(jnp.where(keep, counts, 0), axis=1, keepdims=True)

    ends, starts, count = down(column <= row), down(column < row), down(column == row)
    slot = iota((NBINS, M), 1)
    inside = (slot >= starts) & (slot < ends)

    def across(values):
        return jnp.sum(jnp.where(inside, values, 0), axis=0, keepdims=True)

    first, amount, number = across(starts), across(count), across(iota((NBINS, M), 0))
    offset = (iota((1, M), 1) - first).astype(F32) + 0.5
    points = (number.astype(F32) + offset / amount.astype(F32)) / NBINS
    points_ref[...] = points
    upright = jnp.sum(
        jnp.where(iota((M, M), 0) == iota((M, M), 1), points, 0.0), axis=1, keepdims=True
    )
    centre_row = (iota((1, N), 1).astype(F32) + 0.5) / N
    centre_column = (iota((N, 1), 0).astype(F32) + 0.5) / N
    past_values = one_split(nn, gaussian(upright, centre_row), past_ref[0])
    recent = memory_tau + (1.0 - memory_tau) * (iota((1, CTX), 1).astype(F32) + 0.5) / CTX
    old = gaussian(memory_tau * points, centre_column)
    new = gaussian(recent, centre_column)
    right_ref[...] = both_split(nn, old, past_values) + one_split(nn, new, context_ref[0])
    eye = (iota((N, N), 0) == iota((N, N), 1)).astype(F32) * ridge_weight
    gram_ref[...] = both_split(nt, old, old) + both_split(nt, new, new) + eye


def memory_system(histogram, past, context):
    return call(
        system_kernel,
        [shape_of((1, M), F32), shape_of((N, N), F32), shape_of((N, D), F32)],
        [VMEM] * 3,
        [VMEM] * 3,
        flops=8_000_000_000,
    )(histogram, past, context)


def inverse_of(block):
    size = block.shape[0]
    row, column = iota((size, 1), 0), iota((1, size), 1)
    eye = (iota((size, size), 0) == iota((size, size), 1)).astype(F32)
    work = block - 2.0 * eye
    for k in range(size):
        line = work[k : k + 1, :]
        pivot = line[:, k : k + 1] + 2.0
        left = work[:, k : k + 1] + (row == k).astype(F32)
        right = (line + (column == k).astype(F32)) * (1.0 / pivot)
        work = work - left * right
    return -work


def eliminate_kernel(gram_ref, right_ref, link_ref, known_ref, *rest):
    inverse = inverse_of(gram_ref[:PART, :PART])
    top = right_ref[:PART, :]
    known_ref[...] = both_split(nn, inverse, top)
    if rest:
        next_gram_ref, next_right_ref = rest
        beside = gram_ref[:PART, PART:]
        link = both_split(nn, inverse, beside)
        link_ref[...] = link
        next_gram_ref[...] = gram_ref[PART:, PART:] - both_split(tn, beside, link)
        next_right_ref[...] = right_ref[PART:, :] - both_split(tn, link, top)
    else:
        link_ref[...] = jnp.zeros(link_ref.shape, F32)


def substitute_kernel(*refs):
    links, known, out = refs[:3], refs[3:7], refs[7]
    found = known[3][...]
    out[pl.ds(3 * PART, PART), :] = found.astype(BF16)
    for k in (2, 1, 0):
        part = known[k][...] - both_split(nn, links[k][...], found)
        out[pl.ds(k * PART, PART), :] = part.astype(BF16)
        found = jnp.concatenate([part, found], axis=0)


def solve(gram, right):
    links, known, size = [], [], N
    while size:
        left = size - PART
        shapes = [shape_of((PART, max(left, PART)), F32), shape_of((PART, D), F32)]
        if left:
            shapes += [shape_of((left, left), F32), shape_of((left, D), F32)]
        found = call(
            eliminate_kernel, shapes, [VMEM] * 2, [VMEM] * len(shapes), flops=10_000_000_000
        )(gram, right)
        links.append(found[0])
        known.append(found[1])
        if left:
            gram, right = found[2:]
        size = left
    return call(substitute_kernel, shape_of((N, D)), [VMEM] * 7, VMEM, flops=2_000_000_000)(*links[:3], *known)


def block_offsets(x_first):
    for array in range(8):
        core, first, second = array // 4, array % 2, (array // 2) % 2
        x, f = (first, second) if x_first else (second, first)
        for z in range(4):
            yield array, z, z, x, core, f


def position(place_ref, z, x, core, f):
    dp = (place_ref[0] ^ z) * 4 + (place_ref[1] ^ x) * 2 + (place_ref[2] ^ core)
    return dp, place_ref[3] ^ f


def aligned(index, size):
    return pl.ds(pl.multiple_of(index * size, size), size)


def start(source, target, sem):
    copy = pltpu.make_async_copy(source, target, sem)
    copy.start()
    return copy


def wait_all(copies):
    for copy in copies:
        copy.wait()


class Hops:
    def __init__(self, parts, x_first, first, columns):
        self.parts, self.x_first, self.first, self.columns = parts, x_first, first, columns

    def fetch(self, refs, place_ref, whole, sem):
        copies, rows = [], self.parts[0].shape[1]
        for array, index, z, x, core, f in block_offsets(self.x_first):
            dp, side = position(place_ref, z, x, core, f)
            source = refs[array].at[index, :, pl.ds(self.first, self.columns)]
            target = whole.at[aligned(dp, rows), aligned(side, self.columns)]
            copies.append(start(source, target, sem))
        return copies


class Late:
    def __init__(self, parts, first, columns, groups=1):
        self.parts, self.first, self.columns, self.groups = parts, first, columns, groups

    def fetch(self, refs, place_ref, whole, sem):
        copies, rows = [], self.parts[0].shape[1]
        for device in range(32):
            dp, side = device // 2, device % 2
            for q in range(self.groups):
                source = refs[0].at[device, :, pl.ds(self.first + q * self.columns, self.columns)]
                target = whole.at[
                    pl.ds((dp * self.groups + q) * rows, rows), pl.ds(side * self.columns, self.columns)
                ]
                copies.append(start(source, target, sem))
        return copies


class Whole:
    def __init__(self, array):
        self.parts = [array]

    def fetch(self, refs, place_ref, whole, sem):
        return [start(refs[0], whole, sem)]


class Blocks:
    def __init__(self, x_first, rows, columns):
        self.x_first, self.rows, self.columns = x_first, rows, columns
        self.shapes = [shape_of((2, 2, 4, rows, columns))] * 2

    def put(self, staged, refs, place_ref, sem, rows=None, columns=None, first=0, dps=range(16), sides=(0, 1)):
        rows, columns = rows or self.rows, columns or self.columns
        z0, x0, core0, f0 = (place_ref[n] for n in range(4))

        def send(core_here):
            for n, dp in enumerate(dps):
                z, x, core = dp // 4, (dp // 2) % 2, dp % 2
                target = refs[0] if core == core_here else refs[1]
                for m, side in enumerate(sides):
                    bits = (x ^ x0, side ^ f0) if self.x_first else (side ^ f0, x ^ x0)
                    source = staged.at[pl.ds(n * rows, rows), pl.ds(m * columns, columns)]
                    start(source, target.at[bits[0], bits[1], z ^ z0, :, pl.ds(first, columns)], sem)

        pl.when(core0 == 0)(lambda: send(0))
        pl.when(core0 == 1)(lambda: send(1))

    def wait(self, staged, refs, sem, rows=None, columns=None, first=0, dps=range(16), sides=(0, 1)):
        rows, columns = rows or self.rows, columns or self.columns
        for n in range(len(dps)):
            for m in range(len(sides)):
                source = staged.at[pl.ds(n * rows, rows), pl.ds(m * columns, columns)]
                pltpu.make_async_copy(source, refs[0].at[0, 0, 0, :, pl.ds(first, columns)], sem).wait()

    def put_devices(self, staged, refs, place_ref, sem, first):
        for side in (0, 1):
            self._put_side(staged, refs, place_ref, sem, first, side)

    def _put_side(self, staged, refs, place_ref, sem, first, side):
        z0, x0, core0, f0 = (place_ref[n] for n in range(4))

        def send(core_here):
            for dp in range(16):
                z, x, core = dp // 4, (dp // 2) % 2, dp % 2
                target = refs[0] if core == core_here else refs[1]
                bits = (x ^ x0, side ^ f0) if self.x_first else (side ^ f0, x ^ x0)
                source = staged.at[pl.ds((dp * 2 + side) * self.rows, self.rows), :]
                start(source, target.at[bits[0], bits[1], z ^ z0, :, pl.ds(first, staged.shape[1])], sem)

        pl.when(core0 == 0)(lambda: send(0))
        pl.when(core0 == 1)(lambda: send(1))

    def wait_devices(self, staged, refs, sem, first):
        for n in range(32):
            source = staged.at[pl.ds(n * self.rows, self.rows), :]
            pltpu.make_async_copy(source, refs[0].at[0, 0, 0, :, pl.ds(first, staged.shape[1])], sem).wait()


def spread_table(width, lanes):
    return (iota((PART, lanes), 0) == iota((PART, lanes), 1) % width).astype(BF16)


def vectors_kernel(place_ref, *refs):
    parts, (vec_ref, up_ref, table_ref, held, sem) = refs[:8], refs[8:]
    copies = []
    for array, index, z, x, core, f in block_offsets(False):
        dp, side = position(place_ref, z, x, core, f)
        first = parts[array].shape[2] - PART
        copies.append(start(parts[array].at[index, :, pl.ds(first, PART)], held.at[dp * 2 + side], sem))
    wait_all(copies)
    table_ref[...] = held[:, 16:32, :].reshape(512, PART)
    rows = held[:, :16, :].reshape(512, PART)
    device = iota((512, D), 0) // 16
    spread = nn(rows, spread_table(24, D))
    spread = jnp.where(iota((512, D), 1) // 24 == device, spread, 0.0)
    vec_ref[...] = jnp.sum(spread.reshape(32, 16, D), axis=0)
    wide = nn(rows, spread_table(96, D))
    wide = jnp.where(iota((512, D), 1) // 96 == device % 8, wide, 0.0)
    for t in range(4):
        group = wide[t * 128 : (t + 1) * 128, :].reshape(8, 16, D)
        up_ref[:, t * D : (t + 1) * D] = jnp.sum(group, axis=0)[8:16, :]


def gathered_vectors(place, mem_parts):
    return call(
        vectors_kernel,
        [shape_of((16, D), F32), shape_of((8, FF), F32), shape_of((N, PART))],
        [SMEM] + [HBM] * 8,
        [VMEM] * 3,
        [pltpu.VMEM((32, 48, PART), BF16), pltpu.SemaphoreType.DMA],
        flops=1_500_000_000,
    )(place, *mem_parts)


def pack_vectors(vectors, up_grad, tables):
    device, kind = iota((512, D), 0) // 16, iota((512, D), 0) % 16
    tiled = jnp.broadcast_to(vectors[None], (32, 16, D)).reshape(512, D)
    tiled = jnp.where((iota((512, D), 1) // 24 == device) & (kind < 8), tiled, 0.0).astype(BF16)
    ups = [jnp.broadcast_to(up_grad[0:1, t * D : (t + 1) * D], (128, D)) for t in range(4)]
    ups = jnp.concatenate(ups, axis=0)
    ups = jnp.where((iota((512, D), 1) // 96 == device % 8) & (kind == 8), ups, 0.0).astype(BF16)
    rows = nt(tiled, spread_table(24, D)) + nt(ups, spread_table(96, D))
    rows = rows.astype(BF16).reshape(32, 16, PART)
    table_rows = tables.astype(BF16).reshape(32, 16, PART)
    return jnp.concatenate([rows, table_rows, jnp.zeros((32, 16, PART), BF16)], axis=1)


def head_mask(rows, lanes, heads):
    return iota((rows, lanes), 1) // DH == heads


def front_call(place, tokens, vectors, coeff, tables, proj, keys, values):
    weights = (proj, keys, values)
    counts = [len(w.parts) for w in weights]

    def kernel(place_ref, tokens_ref, vec_ref, coeff_ref, table_ref, *refs):
        sources, at = [], 0
        for count in counts:
            sources.append(refs[at : at + count])
            at += count
        normed_ref, projected_ref, mem_values_ref, reads_ref, proj_ref, keys_ref, values_ref, sems = refs[at:]
        held = (proj_ref, keys_ref, values_ref)
        copies = [w.fetch(s, place_ref, h, sems.at[n]) for n, (w, s, h) in enumerate(zip(weights, sources, held))]
        normed = normalise(tokens_ref[0].astype(F32), vec_ref[0:1, :], vec_ref[1:2, :]).astype(BF16)
        normed_ref[...] = normed
        summary = tn(table_ref[...], coeff_ref[...])[:32, :]
        wait_all(copies[1])
        reads = one_split(nn, summary, keys_ref[...])
        head = iota((32, D), 1) // DH
        kind = iota((32, D), 0)
        centre = jnp.sum(jnp.where(kind == head, reads, 0.0), axis=0, keepdims=True)
        spread = jnp.sum(jnp.where(kind == head + H, reads, 0.0), axis=0, keepdims=True)
        row = iota((8, D), 0)
        reads_ref[...] = jnp.where(row == 0, centre, jnp.where(row == 1, spread, 0.0))
        wait_all(copies[2])
        mem_values_ref[...] = nn(coeff_ref[...], values_ref[...]).astype(BF16)
        wait_all(copies[0])

        def block(n, bias):
            at = pl.ds(n * D, D)
            projected_ref[:, at] = (nn(normed_ref[...], proj_ref[:, at]) + bias).astype(BF16)

        block(0, vec_ref[2:3, :])
        block(1, 0.0)
        block(2, vec_ref[3:4, :])

    return call(
        kernel,
        [shape_of((512, D)), shape_of((512, 3 * D)), shape_of((N, D)), shape_of((8, D), F32)],
        [SMEM] + [VMEM] * 4 + [HBM] * sum(counts),
        [VMEM] * 4,
        [
            pltpu.VMEM((D, 3 * D), BF16),
            pltpu.VMEM((D, D), BF16),
            pltpu.VMEM((D, D), BF16),
            pltpu.SemaphoreType.DMA((3,)),
        ],
        flops=5_000_000_000,
    )(place, tokens, vectors, coeff, tables, *proj.parts, *keys.parts, *values.parts)


READ = 256


def document_rows(length_ref):
    place = iota((1, 512), 1)
    first = jnp.zeros((1, 512), jnp.int32)
    end = jnp.int32(0)
    for n in range(length_ref.shape[1] - 1):
        end = end + length_ref[0, n]
        first = jnp.where(place >= end, end, first)
    return first


def mask_bias(length_ref, bias_ref):
    first = document_rows(length_ref)
    key, query = iota((512, 512), 0), iota((512, 512), 1)
    bias_ref[...] = jnp.where((key <= query) & (key >= first), 0.0, masked_fill)


def reading_row(length_ref, carried_ref):
    inside = iota((1, READ), 1) < length_ref[0, 0]
    return jnp.where(inside, carried_ref[0].astype(F32), 0.0)


def read_parameters(scaled, reads):
    lane_head = iota((1, PART), 1) // DH
    rows = [jnp.where(lane_head == h, reads[kind : kind + 1, :], 0.0) for kind in (0, 1) for h in (0, 1)]
    rows = jnp.concatenate(rows + [jnp.zeros((4, PART), F32)], axis=0)
    high, low = split(rows)
    lowest = (rows - high.astype(F32) - low.astype(F32)).astype(BF16)
    logits = nt(high, scaled) + (nt(low, scaled) + nt(lowest, scaled))
    found = []
    for h in (0, 1):
        centre = 1.0 / (1.0 + jnp.exp(-logits[h : h + 1, :]))
        raw = logits[2 + h : 3 + h, :]
        spread = spread_scale * (jnp.maximum(raw, 0.0) + jnp.log1p(jnp.exp(-jnp.abs(raw))))
        variance = 1.0 / (N * N) + spread * spread
        found.append((centre, spread, variance, raw))
    return rows, found


def basis_column():
    return (iota((N, 1), 0).astype(F32) + 0.5) / N


def density_of(centre, variance):
    distance = centre - basis_column()
    return lax.rsqrt(variance) / N * jnp.exp(distance * distance * (-0.5 / variance)), distance


def head_lanes(value, h):
    return jnp.where(iota((1, PART), 1) // DH == h, value, jnp.zeros_like(value))


def attend_kernel(length_ref, carried_ref, q_ref, k_ref, v_ref, mem_ref, reads_ref, out_ref, lse_ref, bias_ref):
    pl.when(pl.program_id(0) == 0)(lambda: mask_bias(length_ref, bias_ref))
    scaled = q_ref[...] * jnp.asarray(score_scale, BF16)
    outs, totals = [], []
    for h in (0, 1):
        halves, lse = [], []
        for first in (0, 256):
            keys = first + 256
            scores = nt(k_ref[:keys, :], head_lanes(scaled[first : first + 256, :], h))
            scores = scores + bias_ref[:keys, first : first + 256]
            top = jnp.max(scores, axis=0, keepdims=True)
            weights = jnp.exp(scores - top)
            total = jnp.sum(weights, axis=0, keepdims=True)
            probs = (weights * (1.0 / total)).astype(BF16)
            halves.append(tn(v_ref[:keys, :], probs)[h * DH : (h + 1) * DH, :])
            lse.append(top + jnp.log(total))
        outs.append(halves)
        totals.append(jnp.concatenate(lse, axis=1))
    lse_ref[...] = jnp.concatenate(totals + [jnp.zeros((6, 512), F32)], axis=0)
    _, found = read_parameters(scaled[:READ, :], reads_ref[...])
    reading = reading_row(length_ref, carried_ref)
    for h in (0, 1):
        centre, _, variance, _ = found[h]
        density, _ = density_of(centre, variance)
        recall = tn(mem_ref[...], density.astype(BF16))[h * DH : (h + 1) * DH, :]
        outs[h][0] = outs[h][0] + recall * reading
    for n in (0, 1):
        block = jnp.concatenate([outs[0][n], outs[1][n]], axis=0)
        out_ref[n * 256 : (n + 1) * 256, :] = jnp.transpose(block).astype(BF16)


def pair_block(shift=0):
    return pl.BlockSpec((512, PART), lambda i: (0, i + shift))


def attend_call(lengths, carried, projected, mem_values, reads):
    return call(
        attend_kernel,
        [shape_of((512, D)), shape_of((PAIRS * 8, 512), F32)],
        [SMEM, SMEM, pair_block(), pair_block(PAIRS), pair_block(2 * PAIRS), pair_block(), pl.BlockSpec((8, PART), lambda i: (0, i))],
        [pair_block(), pl.BlockSpec((8, 512), lambda i: (i, 0))],
        [pltpu.VMEM((512, 512), F32)],
        flops=12_000_000_000,
        grid=(PAIRS,),
    )(lengths, carried, projected, projected, projected, mem_values, reads)


def attend_back_kernel(
    length_ref, carried_ref, q_ref, k_ref, v_ref, mem_ref, reads_ref, lse_ref, heads_ref,
    gq_ref, gk_ref, gv_ref, gmem_ref, sums_ref, bias_ref,
):
    pl.when(pl.program_id(0) == 0)(lambda: mask_bias(length_ref, bias_ref))
    scaled = q_ref[...] * jnp.asarray(score_scale, BF16)
    keys, values, grad = k_ref[...], v_ref[...], heads_ref[...]
    lane_head = iota((1, PART), 1) // DH
    grad_queries, grad_keys, grad_values = [], [], []
    for h in (0, 1):
        parts = []
        gk, gv = [], []
        for first in (0, 256):
            last = first + 256
            own, own_grad = head_lanes(scaled[first:last, :], h), head_lanes(grad[first:last, :], h)
            scores = nt(keys[:last, :], own) + bias_ref[:last, first:last]
            probs = jnp.exp(scores - lse_ref[h : h + 1, first:last])
            grad_probs = nt(values[:last, :], own_grad)
            row_terms = jnp.sum(probs * grad_probs, axis=0, keepdims=True)
            grad_scores = (probs * (grad_probs - row_terms)).astype(BF16)
            gv.append(nn(probs.astype(BF16), grad[first:last, :]))
            gk.append(nn(grad_scores, scaled[first:last, :]))
            parts.append(tn(keys[:last, :], grad_scores)[h * DH : (h + 1) * DH, :])
        grad_queries.append(parts)
        grad_keys.append((gk[0] + gk[1][:256, :], gk[1][256:, :]))
        grad_values.append((gv[0] + gv[1][:256, :], gv[1][256:, :]))
    for n in (0, 1):
        at = slice(n * 256, (n + 1) * 256)
        gk_ref[at, :] = jnp.where(lane_head == 0, grad_keys[0][n], grad_keys[1][n]).astype(BF16)
        gv_ref[at, :] = jnp.where(lane_head == 0, grad_values[0][n], grad_values[1][n]).astype(BF16)

    rows, found = read_parameters(scaled[:READ, :], reads_ref[...])
    reading = reading_row(length_ref, carried_ref)
    centre_grads, spread_grads, grad_mems = [], [], []
    for h in (0, 1):
        centre, spread, variance, raw = found[h]
        density, distance = density_of(centre, variance)
        own_grad = head_lanes(grad[:READ, :], h)
        grad_density = nt(mem_ref[...], own_grad) * reading
        grad_mems.append(nn((density * reading).astype(BF16), own_grad))
        weight = grad_density * density
        moment0 = jnp.sum(weight, axis=0, keepdims=True)
        weight = weight * distance
        moment1 = jnp.sum(weight, axis=0, keepdims=True)
        moment2 = jnp.sum(weight * distance, axis=0, keepdims=True)
        inverse = 1.0 / variance
        grad_variance = 0.5 * inverse * (moment2 * inverse - moment0)
        centre_grads.append(-moment1 * inverse * centre * (1.0 - centre))
        spread_grads.append(grad_variance * 2.0 * spread * spread_scale / (1.0 + jnp.exp(-raw)))
    gmem_ref[...] = (grad_mems[0] + grad_mems[1]).astype(BF16)
    logit_grads = jnp.concatenate(centre_grads + spread_grads + [jnp.zeros((4, READ), F32)], axis=0)
    sums = one_split(nn, logit_grads, scaled[:READ, :])
    centre_sum = jnp.where(lane_head == 0, sums[0:1, :], sums[1:2, :])
    spread_sum = jnp.where(lane_head == 0, sums[2:3, :], sums[3:4, :])
    sums_ref[...] = jnp.concatenate([centre_sum, spread_sum, jnp.zeros((6, PART), F32)], axis=0)
    from_memory = both_split(tn, rows, logit_grads)
    for n in (0, 1):
        block = jnp.concatenate([grad_queries[0][n], grad_queries[1][n]], axis=0)
        if n == 0:
            block = block + from_memory
        gq_ref[n * 256 : (n + 1) * 256, :] = (jnp.transpose(block) * score_scale).astype(BF16)


def attend_back_call(lengths, carried, projected, mem_values, reads, lse, grad_heads):
    few = pl.BlockSpec((8, PART), lambda i: (0, i))
    return call(
        attend_back_kernel,
        [shape_of((512, D))] * 3 + [shape_of((N, D)), shape_of((8, D), F32)],
        [SMEM, SMEM, pair_block(), pair_block(PAIRS), pair_block(2 * PAIRS), pair_block(), few,
         pl.BlockSpec((8, 512), lambda i: (i, 0)), pair_block()],
        [pair_block()] * 4 + [few],
        [pltpu.VMEM((512, 512), F32)],
        flops=25_000_000_000,
        grid=(PAIRS,),
    )(lengths, carried, projected, projected, projected, mem_values, reads, lse, grad_heads)


GELU_SCALE = 0.7978845608028654
GELU_CUBE = 0.044715


def column_tiles(step_columns):
    return pl.BlockSpec((512, step_columns), lambda t: (0, t))


def fixed(shape):
    return pl.BlockSpec(shape, lambda t: (0,) * len(shape))


def weight_refs(weights, refs):
    found, at = [], 0
    for weight in weights:
        found.append(refs[at : at + len(weight.parts)])
        at += len(weight.parts)
    return found, refs[at:]


def mlp_call(place, tokens, heads, cotangent, vectors, up_bias, out, up, down, target):
    weights = (out, up, down)
    steps = FF // TILE

    def kernel(place_ref, tokens_ref, heads_ref, cot_ref, vec_ref, bias_ref, *refs):
        sources, refs = weight_refs(weights, refs)
        result_ref, middle_ref, normed_ref, slope_ref = refs[:4]
        grad_refs, (out_ref, up_ref, down_ref, total_ref, staged_ref, sems) = refs[4 : 4 + len(target.shapes)], refs[4 + len(target.shapes) :]
        held = (out_ref, up_ref, down_ref)
        step = pl.program_id(0)

        @pl.when(step == 0)
        def _():
            copies = [w.fetch(s, place_ref, h, sems.at[n]) for n, (w, s, h) in enumerate(zip(weights, sources, held))]
            wait_all(copies[0])
            middle = tokens_ref[0].astype(F32) + nn(heads_ref[...], out_ref[...]) + vec_ref[4:5, :]
            middle_ref[...] = middle
            normed_ref[...] = normalise(middle, vec_ref[5:6, :], vec_ref[6:7, :]).astype(BF16)
            total_ref[...] = middle + vec_ref[7:8, :]
            wait_all(copies[1])
            wait_all(copies[2])

        at = aligned(step, TILE)
        hidden = nn(normed_ref[...], up_ref[:, at]) + bias_ref[0:1, :]
        square = hidden * hidden
        bent = jnp.tanh(GELU_SCALE * hidden * (1.0 + GELU_CUBE * square))
        half = 0.5 + 0.5 * bent
        active = (hidden * half).astype(BF16)
        slope_ref[...] = half + 0.5 * hidden * (1.0 - bent * bent) * (GELU_SCALE + 3.0 * GELU_SCALE * GELU_CUBE * square)
        total_ref[...] += nn(active, down_ref[at, :])
        grad = tn(active, cot_ref[0]).astype(BF16)
        for n in range(steps):
            pl.when(step == n)(lambda n=n: target.tile_put(n, grad, staged_ref, grad_refs, place_ref, sems))

        @pl.when(step == steps - 1)
        def _():
            result_ref[0] = total_ref[...].astype(BF16)
            target.tile_wait(staged_ref, grad_refs, sems)

    found = call(
        kernel,
        [shape_of((1, 512, D)), shape_of((512, D), F32), shape_of((512, D)), shape_of((512, FF), F32)] + target.shapes,
        [SMEM, fixed((1, 512, D)), fixed((512, D)), fixed((1, 512, D)), fixed((16, D)), pl.BlockSpec((8, TILE), lambda t: (0, t))]
        + [HBM] * sum(len(w.parts) for w in weights),
        [fixed((1, 512, D)), fixed((512, D)), fixed((512, D)), column_tiles(TILE)] + [HBM] * len(target.shapes),
        [
            pltpu.VMEM((D, D), BF16),
            pltpu.VMEM((D, FF), BF16),
            pltpu.VMEM((FF, D), BF16),
            pltpu.VMEM((512, D), F32),
            pltpu.VMEM((FF, D), BF16),
            pltpu.SemaphoreType.DMA((4,)),
        ],
        flops=15_000_000_000,
        grid=(steps,),
    )(place, tokens, heads, cotangent, vectors, up_bias, *out.parts, *up.parts, *down.parts)
    return found[:4], found[4:]


class DownTarget:
    def __init__(self, blocks):
        self.blocks = blocks
        self.shapes = blocks.shapes if blocks else [shape_of((FF, D))]

    def tile_put(self, n, grad, staged, refs, place_ref, sems):
        rows = pl.ds(n * TILE, TILE)
        staged[rows, :] = grad
        if self.blocks:
            self.blocks.put(staged.at[rows, :], refs, place_ref, sems.at[3], dps=range(4 * n, 4 * n + 4))

    def tile_wait(self, staged, refs, sems):
        if self.blocks:
            self.blocks.wait(staged, refs, sems.at[3])
        else:
            start(staged, refs[0], sems.at[3]).wait()


class UpTarget:
    def __init__(self, blocks):
        self.blocks = blocks
        self.shapes = blocks.shapes if blocks else [shape_of((D, FF))]

    def tile_put(self, n, grad, staged, refs, place_ref, sems):
        staged[:, n * TILE : (n + 1) * TILE] = grad
        if self.blocks:
            self.blocks.put(
                staged.at[:, pl.ds(n * TILE, TILE)], refs, place_ref, sems.at[3],
                columns=TILE, first=(n % 2) * TILE, sides=(n // 2,),
            )

    def tile_wait(self, staged, refs, sems):
        if self.blocks:
            self.blocks.wait(staged, refs, sems.at[3])
        else:
            start(staged, refs[0], sems.at[3]).wait()


def mlp_back_call(place, cotangent, slope, normed, up, down, target):
    weights = (up, down)
    steps = FF // TILE

    def kernel(place_ref, cot_ref, slope_ref, normed_ref, *refs):
        sources, refs = weight_refs(weights, refs)
        total_ref, bias_ref = refs[:2]
        grad_refs, (up_ref, down_ref, staged_ref, sems) = refs[2 : 2 + len(target.shapes)], refs[2 + len(target.shapes) :]
        step = pl.program_id(0)

        @pl.when(step == 0)
        def _():
            copies = [w.fetch(s, place_ref, h, sems.at[n]) for n, (w, s, h) in enumerate(zip(weights, sources, (up_ref, down_ref)))]
            wait_all(copies[1])
            wait_all(copies[0])
            total_ref[...] = jnp.zeros((512, D), F32)

        at = aligned(step, TILE)
        grad_hidden = (nt(cot_ref[0], down_ref[at, :]) * slope_ref[...]).astype(BF16)
        bias_ref[...] = jnp.broadcast_to(jnp.sum(grad_hidden.astype(F32), axis=0, keepdims=True), (8, TILE))
        total_ref[...] += nt(grad_hidden, up_ref[:, at])
        grad = tn(normed_ref[...], grad_hidden).astype(BF16)
        for n in range(steps):
            pl.when(step == n)(lambda n=n: target.tile_put(n, grad, staged_ref, grad_refs, place_ref, sems))
        pl.when(step == steps - 1)(lambda: target.tile_wait(staged_ref, grad_refs, sems))

    found = call(
        kernel,
        [shape_of((512, D), F32), shape_of((8, FF), F32)] + target.shapes,
        [SMEM, fixed((1, 512, D)), column_tiles(TILE), fixed((512, D))] + [HBM] * sum(len(w.parts) for w in weights),
        [fixed((512, D)), pl.BlockSpec((8, TILE), lambda t: (0, t))] + [HBM] * len(target.shapes),
        [
            pltpu.VMEM((D, FF), BF16),
            pltpu.VMEM((FF, D), BF16),
            pltpu.VMEM((D, FF), BF16),
            pltpu.SemaphoreType.DMA((4,)),
        ],
        flops=15_000_000_000,
        grid=(steps,),
    )(place, cotangent, slope, normed, *up.parts, *down.parts)
    return found[:2], found[2:]


def middle_back_call(place, cotangent, middle, grad_normed, vectors, heads, out):
    def kernel(place_ref, cot_ref, middle_ref, grad_ref, vec_ref, heads_ref, *refs):
        sources, refs = weight_refs((out,), refs)
        grad_middle_ref, grad_heads_ref, out_grad_ref, sums_ref, out_ref, sem = refs
        copies = out.fetch(sources[0], place_ref, out_ref, sem)
        cot = cot_ref[0].astype(F32)
        back, gain, shift = normalise_back(middle_ref[...], vec_ref[5:6, :], grad_ref[...])
        grad_middle = cot + back
        grad_middle_ref[...] = grad_middle
        attended = grad_middle.astype(BF16)
        bias = jnp.sum(attended.astype(F32), axis=0, keepdims=True)
        last = jnp.sum(cot, axis=0, keepdims=True)
        nothing = jnp.zeros((4, D), F32)
        sums_ref[...] = jnp.concatenate([nothing, bias, gain, shift, last, nothing, nothing], axis=0)
        wait_all(copies)
        grad_heads_ref[...] = nt(attended, out_ref[...]).astype(BF16)
        out_grad_ref[...] = tn(heads_ref[...], attended).astype(BF16)

    return call(
        kernel,
        [shape_of((512, D), F32), shape_of((512, D)), shape_of((D, D)), shape_of((16, D), F32)],
        [SMEM] + [VMEM] * 5 + [HBM] * len(out.parts),
        [VMEM] * 4,
        [pltpu.VMEM((D, D), BF16), pltpu.SemaphoreType.DMA],
        flops=4_000_000_000,
    )(place, cotangent, middle, grad_normed, vectors, heads, *out.parts)


def memory_back_call(place, coeff, grad_mem_values, tables, sums, out_grad, keys, blocks):
    shapes = blocks.shapes if blocks else [shape_of((D, D))] * 3

    def kernel(place_ref, coeff_ref, grad_values_ref, table_ref, sums_ref, out_grad_ref, *refs):
        sources, refs = weight_refs((keys,), refs)
        tables_ref = refs[0]
        grad_refs, (keys_ref, key_grad_ref, value_grad_ref, sems) = refs[1 : 1 + len(shapes)], refs[1 + len(shapes) :]
        copies = keys.fetch(sources[0], place_ref, keys_ref, sems.at[0])
        staged = (out_grad_ref, key_grad_ref, value_grad_ref)

        def put(n):
            if blocks:
                blocks.put(staged[n], grad_refs, place_ref, sems.at[1 + n], columns=D // 2, first=n * (D // 2))
            else:
                start(staged[n], grad_refs[n], sems.at[1 + n])

        put(0)
        value_grad_ref[...] = tn(coeff_ref[...], grad_values_ref[...]).astype(BF16)
        put(2)
        head, kind = iota((32, D), 1) // DH, iota((32, D), 0)
        by_head = jnp.where(kind == head, sums_ref[0:1, :], jnp.where(kind == head + H, sums_ref[1:2, :], 0.0))
        summary = tn(coeff_ref[...], table_ref[...])[:, :32]
        key_grad_ref[...] = both_split(nn, summary, by_head).astype(BF16)
        put(1)
        wait_all(copies)
        high, low = split(by_head)
        wide = jnp.concatenate([high, low, jnp.zeros((PART - 64, D), BF16)], axis=0)
        reads = nt(keys_ref[...], wide)
        high, low = split(reads)
        found = nn(coeff_ref[...], high) + nn(coeff_ref[...], low)
        lane = iota((N, PART), 1)
        found = found + jnp.concatenate([found[:, 32:64], jnp.zeros((N, PART - 32), F32)], axis=1)
        tables_ref[...] = jnp.where(lane < 2 * H, found, 0.0)
        for n in range(3):
            if blocks:
                blocks.wait(staged[n], grad_refs, sems.at[1 + n], columns=D // 2, first=n * (D // 2))
            else:
                pltpu.make_async_copy(staged[n], grad_refs[n], sems.at[1 + n]).wait()

    found = call(
        kernel,
        [shape_of((N, PART), F32)] + shapes,
        [SMEM] + [VMEM] * 5 + [HBM] * len(keys.parts),
        [VMEM] + [HBM] * len(shapes),
        [pltpu.VMEM((D, D), BF16)] * 3 + [pltpu.SemaphoreType.DMA((4,))],
        flops=3_000_000_000,
    )(place, coeff, grad_mem_values, tables, sums, out_grad, *keys.parts)
    return found[0], found[1:]


def input_back_call(place, tokens, vectors, normed, grads, grad_middle, sums, up_bias_grad, tables, proj, blocks):
    shapes = blocks.shapes if blocks else [shape_of((D, 3 * D)), shape_of((16, D), F32)]

    def kernel(place_ref, tokens_ref, vec_ref, normed_ref, gq_ref, gk_ref, gv_ref, middle_ref, sums_ref, up_ref, table_ref, *refs):
        sources, refs = weight_refs((proj,), refs)
        result_ref = refs[0]
        grad_refs, (proj_ref, staged_ref, small_ref, sems) = refs[1 : 1 + len(shapes)], refs[1 + len(shapes) :]
        copies = proj.fetch(sources[0], place_ref, proj_ref, sems.at[0])
        for n, grad_ref in enumerate((gq_ref, gk_ref, gv_ref)):
            staged_ref[:, n * D : (n + 1) * D] = tn(normed_ref[...], grad_ref[...]).astype(BF16)
        if blocks:
            blocks.put(staged_ref, grad_refs, place_ref, sems.at[1], columns=3 * D // 2)
        else:
            start(staged_ref, grad_refs[0], sems.at[1])
        wait_all(copies)
        grad_normed = nt(gq_ref[...], proj_ref[:, :D]) + nt(gk_ref[...], proj_ref[:, D : 2 * D]) + nt(gv_ref[...], proj_ref[:, 2 * D :])
        back, gain, shift = normalise_back(tokens_ref[0].astype(F32), vec_ref[0:1, :], grad_normed)
        result_ref[0] = middle_ref[...] + back
        query_bias = jnp.sum(gq_ref[...].astype(F32), axis=0, keepdims=True)
        value_bias = jnp.sum(gv_ref[...].astype(F32), axis=0, keepdims=True)
        vectors_grad = jnp.concatenate([gain, shift, query_bias, value_bias, sums_ref[4:16, :]], axis=0)
        if blocks:
            small_ref[...] = pack_vectors(vectors_grad, up_ref[...], table_ref[...]).reshape(32 * 48, PART)
            blocks.put_devices(small_ref, grad_refs, place_ref, sems.at[2], 3 * D // 2)
            blocks.wait(staged_ref, grad_refs, sems.at[1], columns=3 * D // 2)
            blocks.wait_devices(small_ref, grad_refs, sems.at[2], 3 * D // 2)
        else:
            small_ref[...] = jnp.zeros(small_ref.shape, BF16)
            grad_refs[1][...] = vectors_grad
            pltpu.make_async_copy(staged_ref, grad_refs[0], sems.at[1]).wait()

    found = call(
        kernel,
        [shape_of((1, 512, D), F32)] + shapes,
        [SMEM] + [VMEM] * 10 + [HBM] * len(proj.parts),
        [VMEM] + ([HBM] * 2 if blocks else [HBM, VMEM]),
        [
            pltpu.VMEM((D, 3 * D), BF16),
            pltpu.VMEM((D, 3 * D), BF16),
            pltpu.VMEM((32 * 48, PART), BF16),
            pltpu.SemaphoreType.DMA((3,)),
        ],
        flops=8_000_000_000,
    )(place, tokens, vectors, normed, *grads, grad_middle, sums, up_bias_grad, tables, *proj.parts)
    return found[0], found[1:]


def hop(value, z=0, x=0, core=0, f=0):
    pairs = []
    for dp in range(16):
        for side in range(2):
            other = (((dp // 4) ^ z) * 4) + ((((dp // 2) % 2) ^ x) * 2) + ((dp % 2) ^ core)
            pairs.append((dp * 2 + side, other * 2 + (side ^ f)))
    return lax.ppermute(value, BOTH, pairs)


def gather_hops(block, x_first):
    quad = jnp.stack([block] + [hop(block, z=k) for k in (1, 2, 3)])
    first, second = (dict(x=1), dict(f=1)) if x_first else (dict(f=1), dict(x=1))
    near = hop(quad, **first)
    mine = [quad, near, hop(quad, **second), hop(near, **second)]
    return mine + [hop(part, core=1) for part in mine]


def plus(a, b):
    return (a.astype(F32) + b.astype(F32)).astype(BF16)


def scatter_hops(keep, send, x_first):
    first, second = (dict(x=1), dict(f=1)) if x_first else (dict(f=1), dict(x=1))
    got = hop(send, core=1)
    sent, kept = plus(keep[1], got[1]), plus(keep[0], got[0])
    got = hop(sent, **first)
    sent, kept = plus(kept[1], got[1]), plus(kept[0], got[0])
    got = hop(sent, **second)
    parts = [hop(plus(kept[k], got[k]), z=k) for k in (1, 2, 3)]
    total = kept[0].astype(F32) + got[0].astype(F32)
    for part in parts:
        total = total + part.astype(F32)
    return total


COLUMN_SPLIT = (2, 5, 7, 8, 13, 15)
VECTORS = (0, 1, 3, 4, 6, 11, 12, 16)


def gather_whole(shards):
    def whole(k, shard):
        near = lax.all_gather(shard, "fsdp", axis=1 if k in COLUMN_SPLIT else 0, tiled=True)
        return lax.all_gather(near, "dp", axis=0, tiled=True)

    found = [whole(k, shard) for k, shard in enumerate(shards)]
    vectors = jnp.stack([found[k].astype(F32) for k in VECTORS] + [jnp.zeros((D,), F32)] * 8)
    up_bias = jnp.broadcast_to(found[14].astype(F32)[None], (8, FF))
    tables = jnp.pad(jnp.concatenate([found[9], found[10]], axis=1), ((0, 0), (0, PART - 2 * H)))
    weights = {k: Whole(found[k]) for k in COLUMN_SPLIT}
    return weights, vectors, up_bias, tables


def scatter_whole(totals):
    def part(k, total):
        near = lax.psum_scatter(total.astype(BF16), "dp", scatter_dimension=0, tiled=True)
        return lax.psum_scatter(near, "fsdp", scatter_dimension=1 if k in COLUMN_SPLIT else 0, tiled=True).astype(F32)

    return [part(k, total) for k, total in enumerate(totals)]


def small_block(shards, rows):
    vectors = jnp.stack([shards[k] for k in VECTORS])
    vectors = jnp.pad(vectors, ((0, 8), (0, PART - vectors.shape[1])))
    vectors = vectors.at[8, : shards[14].shape[0]].set(shards[14])
    tables = jnp.concatenate([shards[9], shards[10]], axis=1)
    tables = jnp.pad(tables, ((0, rows - 32), (0, PART - 2 * H)))
    return jnp.concatenate([vectors, tables], axis=0)


def local(
    mesh_sizes, tokens, context, past_coeffs, doc_lengths, carried, histogram, cotangent, *shards
):
    hops = mesh_sizes == (16, 2)
    dp = lax.axis_index("dp")
    place = jnp.stack([dp // 4, (dp // 2) % 2, dp % 2, lax.axis_index("fsdp")]).astype(jnp.int32)
    rows, half = shards[5].shape
    if hops:
        late = [shards[5], shards[13]] + [shards[15][q * rows : (q + 1) * rows] for q in range(4)]
        late = lax.all_gather(jnp.concatenate(late, axis=1), BOTH, axis=0)
        small = small_block(shards, rows)
        mem_parts = gather_hops(jnp.concatenate([shards[7], shards[8], small], axis=1), False)
        proj_parts = gather_hops(shards[2], True)
        vectors, up_bias, tables = gathered_vectors(place, mem_parts)
        weights = {
            2: Hops(proj_parts, True, 0, 3 * half),
            7: Hops(mem_parts, False, 0, half),
            8: Hops(mem_parts, False, half, half),
            5: Late([late], 0, half),
            13: Late([late], half, 4 * half),
            15: Late([late], 5 * half, half, 4),
        }
    else:
        weights, vectors, up_bias, tables = gather_whole(shards)
    points, gram, right = memory_system(histogram, past_coeffs, context)
    coeff = solve(gram, right)
    normed, projected, mem_values, reads = front_call(
        place, tokens, vectors, coeff, tables, weights[2], weights[7], weights[8]
    )
    heads, lse = attend_call(doc_lengths, carried, projected, mem_values, reads)
    down_blocks = Blocks(False, 4 * rows, half) if hops else None
    (result, middle, normed_mlp, slope), grad_down = mlp_call(
        place, tokens, heads, cotangent, vectors, up_bias, weights[5], weights[13], weights[15], DownTarget(down_blocks)
    )
    up_blocks = Blocks(True, rows, 4 * half) if hops else None
    (grad_normed_mlp, grad_up_bias), grad_up = mlp_back_call(
        place, cotangent, slope, normed_mlp, weights[13], weights[15], UpTarget(up_blocks)
    )
    grad_middle, grad_heads, grad_out, sums = middle_back_call(
        place, cotangent, middle, grad_normed_mlp, vectors, heads, weights[5]
    )
    grad_q, grad_k, grad_v, grad_mem, read_sums = attend_back_call(
        doc_lengths, carried, projected, mem_values, reads, lse, grad_heads
    )
    mem_blocks = Blocks(False, rows, 3 * half) if hops else None
    grad_tables, grad_mems = memory_back_call(
        place, coeff, grad_mem, tables, read_sums, grad_out, weights[7], mem_blocks
    )
    proj_blocks = Blocks(True, rows, 3 * half + PART) if hops else None
    grad_tokens, grad_proj = input_back_call(
        place, tokens, vectors, normed, (grad_q, grad_k, grad_v), grad_middle, sums, grad_up_bias, grad_tables,
        weights[2], proj_blocks,
    )
    if hops:
        summed = {15: scatter_hops(*grad_down, False), 13: scatter_hops(*grad_up, True)}
        mems = scatter_hops(*grad_mems, False)
        for n, k in enumerate((5, 7, 8)):
            summed[k] = mems[:, n * half : (n + 1) * half]
        last = scatter_hops(*grad_proj, True)
        summed[2] = last[:, : 3 * half]
        small = last[:, 3 * half :]
        for n, k in enumerate(VECTORS):
            summed[k] = small[n, : shards[k].shape[0]]
        summed[14] = small[8, : shards[14].shape[0]]
        summed[9], summed[10] = small[16:32, :H], small[16:32, H : 2 * H]
    else:
        totals = {13: grad_up[0], 15: grad_down[0], 2: grad_proj[0], 14: grad_up_bias[0]}
        totals[5], totals[7], totals[8] = grad_mems
        totals[9], totals[10] = grad_tables[:, :H], grad_tables[:, H : 2 * H]
        for n, k in enumerate(VECTORS):
            totals[k] = grad_proj[1][n]
        summed = scatter_whole([totals[k] for k in range(17)])
    return (result, grad_tokens, *(summed[k] for k in range(17)), points)


def solution(mesh):
    both, row, table = P(BOTH), P("dp", "fsdp"), P(BOTH, None)
    block = P(BOTH, None, None)
    weights = (
        both, both, row, both, both, row, both, row, row, table, table, both, both, row, both, row, both,
    )
    in_specs = (block, block, block, table, both, table, block) + weights
    out_specs = (block, block) + weights + (table,)
    sizes = (mesh.shape["dp"], mesh.shape["fsdp"])
    return jax.shard_map(
        functools.partial(local, sizes), mesh=mesh, in_specs=in_specs, out_specs=out_specs, check_vma=False
    )
```

```python
import functools

import jax
import jax.numpy as jnp
from jax import lax
from jax.experimental import pallas as pl
from jax.experimental.pallas import tpu as pltpu
from jax.sharding import PartitionSpec as P

H = 12
DH = 64
D = H * DH
N = 512
CTX = 1024
M = 512
NBINS = 64
FF = 4 * D
PAIRS = H // 2
PART = 128
TILE = 768

memory_tau = 0.75
ridge_weight = 1.0
norm_epsilon = 1e-05
spread_scale = 0.25
masked_fill = -1e30
score_scale = DH ** (-0.5)

F32, BF16 = jnp.float32, jnp.bfloat16
VMEM_LIMIT = 56 * 1024 * 1024
BOTH = ("dp", "fsdp")
HBM = pl.BlockSpec(memory_space=pl.ANY)
SMEM = pl.BlockSpec(memory_space=pltpu.SMEM)
VMEM = pl.BlockSpec(memory_space=pltpu.VMEM)


FLOPS = {
    "pack": 1, "system": 11, "eliminate": 14, "substitute": 4, "vectors": 3, "front": 9, "attend": 15, "mlp": 20,
    "mlp_back": 17, "middle_back": 6, "memory_read_back": 6, "memory_back": 7, "attend_back": 8, "project_back": 4,
    "input_back": 8,
}
FLOPS = {name: work * 1_000_000_000 for name, work in FLOPS.items()}


def shape_of(shape, dtype=BF16):
    return jax.ShapeDtypeStruct(shape, dtype)


def call(kernel, out_shape, in_specs, out_specs, scratch=(), flops=0, grid=None, after=()):
    extra = {} if grid is None else {"grid": grid}
    inputs, unread = len(in_specs), len(after)

    def body(*refs):
        kernel(*refs[:inputs], *refs[inputs + unread :])

    run = pl.pallas_call(
        body,
        out_shape=out_shape,
        in_specs=list(in_specs) + [HBM] * unread,
        out_specs=out_specs,
        scratch_shapes=list(scratch),
        compiler_params=pltpu.CompilerParams(vmem_limit_bytes=VMEM_LIMIT),
        cost_estimate=pl.CostEstimate(flops=flops, bytes_accessed=0, transcendentals=0),
        **extra,
    )
    return lambda *operands: run(*operands, *after)


def nn(a, b):
    return lax.dot_general(a, b, (((1,), (0,)), ((), ())), preferred_element_type=F32)


def nt(a, b):
    return lax.dot_general(a, b, (((1,), (1,)), ((), ())), preferred_element_type=F32)


def tn(a, b):
    return lax.dot_general(a, b, (((0,), (0,)), ((), ())), preferred_element_type=F32)


def split(value):
    high = value.astype(BF16)
    return high, (value - high.astype(F32)).astype(BF16)


def both_split(product, a, b):
    a_high, a_low = split(a)
    b_high, b_low = split(b)
    return product(a_high, b_high) + (product(a_high, b_low) + product(a_low, b_high))


def one_split(product, a, b):
    a_high, a_low = split(a)
    return product(a_high, b) + product(a_low, b)


def iota(shape, axis):
    return lax.broadcasted_iota(jnp.int32, shape, axis)


def gaussian(points, centres):
    distance = points - centres
    return jnp.exp(-0.5 * distance * distance * (N * N))


def normalise(values, gain, shift):
    mean = jnp.mean(values, axis=-1, keepdims=True)
    centred = values - mean
    variance = jnp.mean(centred * centred, axis=-1, keepdims=True)
    inverse = lax.rsqrt(variance + norm_epsilon)
    return centred * inverse * gain + shift


def normalise_back(values, gain, grad):
    mean = jnp.mean(values, axis=-1, keepdims=True)
    centred = values - mean
    variance = jnp.mean(centred * centred, axis=-1, keepdims=True)
    inverse = lax.rsqrt(variance + norm_epsilon)
    standard = centred * inverse
    scaled = grad * gain
    first = jnp.mean(scaled, axis=-1, keepdims=True)
    second = jnp.mean(scaled * standard, axis=-1, keepdims=True)
    back = inverse * (scaled - first - standard * second)
    return back, jnp.sum(grad * standard, axis=0, keepdims=True), jnp.sum(grad, axis=0, keepdims=True)


def system_kernel(hist_ref, past_ref, context_ref, points_ref, gram_ref, right_ref):
    hist = hist_ref[...]
    counts = jnp.broadcast_to(hist, (NBINS, NBINS))
    row, column = iota((NBINS, NBINS), 0), iota((NBINS, NBINS), 1)

    def down(keep):
        return jnp.sum(jnp.where(keep, counts, 0), axis=1, keepdims=True)

    ends, starts, count = down(column <= row), down(column < row), down(column == row)
    slot = iota((NBINS, M), 1)
    inside = (slot >= starts) & (slot < ends)

    def across(values):
        return jnp.sum(jnp.where(inside, values, 0), axis=0, keepdims=True)

    first, amount, number = across(starts), across(count), across(iota((NBINS, M), 0))
    offset = (iota((1, M), 1) - first).astype(F32) + 0.5
    points = (number.astype(F32) + offset / amount.astype(F32)) / NBINS
    points_ref[...] = points
    upright = jnp.sum(
        jnp.where(iota((M, M), 0) == iota((M, M), 1), points, 0.0), axis=1, keepdims=True
    )
    centre_row = (iota((1, N), 1).astype(F32) + 0.5) / N
    centre_column = (iota((N, 1), 0).astype(F32) + 0.5) / N
    past_values = one_split(nn, gaussian(upright, centre_row), past_ref[0])
    recent = memory_tau + (1.0 - memory_tau) * (iota((1, CTX), 1).astype(F32) + 0.5) / CTX
    old = gaussian(memory_tau * points, centre_column)
    new = gaussian(recent, centre_column)
    right_ref[...] = both_split(nn, old, past_values) + one_split(nn, new, context_ref[0])
    eye = (iota((N, N), 0) == iota((N, N), 1)).astype(F32) * ridge_weight
    gram_ref[...] = both_split(nt, old, old) + both_split(nt, new, new) + eye


def memory_system(histogram, past, context, after=()):
    return call(
        system_kernel,
        [shape_of((1, M), F32), shape_of((N, N), F32), shape_of((N, D), F32)],
        [VMEM] * 3,
        [VMEM] * 3,
        flops=FLOPS["system"],
        after=after,
    )(histogram, past, context)


def inverse_of(block):
    size = block.shape[0]
    row, column = iota((size, 1), 0), iota((1, size), 1)
    eye = (iota((size, size), 0) == iota((size, size), 1)).astype(F32)
    work = block - 2.0 * eye
    for k in range(size):
        line = work[k : k + 1, :]
        pivot = line[:, k : k + 1] + 2.0
        left = work[:, k : k + 1] + (row == k).astype(F32)
        right = (line + (column == k).astype(F32)) * (1.0 / pivot)
        work = work - left * right
    return -work


def eliminate_kernel(gram_ref, right_ref, link_ref, known_ref, *rest):
    inverse = inverse_of(gram_ref[:PART, :PART])
    top = right_ref[:PART, :]
    known_ref[...] = both_split(nn, inverse, top)
    if rest:
        next_gram_ref, next_right_ref = rest
        beside = gram_ref[:PART, PART:]
        link = both_split(nn, inverse, beside)
        link_ref[...] = link
        next_gram_ref[...] = gram_ref[PART:, PART:] - both_split(tn, beside, link)
        next_right_ref[...] = right_ref[PART:, :] - both_split(tn, link, top)
    else:
        link_ref[...] = jnp.zeros(link_ref.shape, F32)


def substitute_kernel(*refs):
    links, known, out = refs[:3], refs[3:7], refs[7]
    found = known[3][...]
    out[pl.ds(3 * PART, PART), :] = found.astype(BF16)
    for k in (2, 1, 0):
        part = known[k][...] - both_split(nn, links[k][...], found)
        out[pl.ds(k * PART, PART), :] = part.astype(BF16)
        found = jnp.concatenate([part, found], axis=0)


def eliminate(system, after=()):
    gram, right = system
    left = gram.shape[0] - PART
    shapes = [shape_of((PART, max(left, PART)), F32), shape_of((PART, D), F32)]
    if left:
        shapes += [shape_of((left, left), F32), shape_of((left, D), F32)]
    return call(
        eliminate_kernel, shapes, [VMEM] * 2, [VMEM] * len(shapes), flops=FLOPS["eliminate"], after=after
    )(gram, right)


def substitute(steps):
    links, known = [step[0] for step in steps[:-1]], [step[1] for step in steps]
    return call(substitute_kernel, shape_of((N, D)), [VMEM] * 7, VMEM, flops=FLOPS["substitute"])(*links, *known)


def block_offsets(x_first):
    for array in range(8):
        core, first, second = array // 4, array % 2, (array // 2) % 2
        x, f = (first, second) if x_first else (second, first)
        for z in range(4):
            yield array, z, z, x, core, f


def position(place_ref, z, x, core, f):
    dp = (place_ref[0] ^ z) * 4 + (place_ref[1] ^ x) * 2 + (place_ref[2] ^ core)
    return dp, place_ref[3] ^ f


def aligned(index, size):
    return pl.ds(pl.multiple_of(index * size, size), size)


def start(source, target, sem):
    copy = pltpu.make_async_copy(source, target, sem)
    copy.start()
    return copy


def wait_all(copies):
    for copy in copies:
        copy.wait()


class Hops:
    def __init__(self, parts, x_first, first, columns, groups=1):
        self.parts, self.x_first, self.first, self.columns = parts, x_first, first, columns
        self.groups = groups

    def fetch(self, refs, place_ref, whole, sem):
        copies, rows = [], self.parts[0].shape[1]
        for array, index, z, x, core, f in block_offsets(self.x_first):
            dp, side = position(place_ref, z, x, core, f)
            for q in range(self.groups):
                source = refs[array].at[index, :, pl.ds(self.first + q * self.columns, self.columns)]
                target = whole.at[aligned(dp * self.groups + q, rows), aligned(side, self.columns)]
                copies.append(start(source, target, sem))
        return copies


class Whole:
    def __init__(self, array):
        self.parts = [array]

    def fetch(self, refs, place_ref, whole, sem):
        return [start(refs[0], whole, sem)]


class Blocks:
    def __init__(self, x_first, rows, columns):
        self.x_first, self.rows, self.columns = x_first, rows, columns
        self.shapes = [shape_of((2, 2, 4, rows, columns))] * 2

    def _each(self, refs, place_ref, core_here, dps, sides):
        z0, x0, f0 = place_ref[0], place_ref[1], place_ref[3]
        for n, dp in enumerate(dps):
            z, x, core = dp // 4, (dp // 2) % 2, dp % 2
            target = refs[0] if core == core_here else refs[1]
            for m, side in enumerate(sides):
                bits = (x ^ x0, side ^ f0) if self.x_first else (side ^ f0, x ^ x0)
                yield n, m, target.at[bits[0], bits[1], z ^ z0]

    def put(self, staged, refs, place_ref, sem, pieces, dps=range(16), sides=(0, 1)):
        def send(core_here):
            for n, m, where in self._each(refs, place_ref, core_here, dps, sides):
                for steps, offsets, first, columns in pieces:
                    rows = pl.ds(n * steps[0] + offsets[0], self.rows)
                    across = pl.ds(m * steps[1] + offsets[1], columns)
                    start(staged.at[rows, across], where.at[:, pl.ds(first, columns)], sem)

        pl.when(place_ref[2] == 0)(lambda: send(0))
        pl.when(place_ref[2] == 1)(lambda: send(1))

    def wait(self, staged, refs, sem, pieces, dps=range(16), sides=(0, 1)):
        for _ in range(len(dps) * len(sides)):
            for _, _, first, columns in pieces:
                source = staged.at[pl.ds(0, self.rows), pl.ds(0, columns)]
                pltpu.make_async_copy(source, refs[0].at[0, 0, 0, :, pl.ds(first, columns)], sem).wait()


def spread_table(width, lanes):
    return (iota((PART, lanes), 0) == iota((PART, lanes), 1) % width).astype(BF16)


def vectors_kernel(place_ref, *refs):
    parts, (vec_ref, up_ref, table_ref, held, sem) = refs[:8], refs[8:]
    copies = []
    for array, index, z, x, core, f in block_offsets(False):
        dp, side = position(place_ref, z, x, core, f)
        first = parts[array].shape[2] - PART
        copies.append(start(parts[array].at[index, :, pl.ds(first, PART)], held.at[dp * 2 + side], sem))
    wait_all(copies)
    table_ref[...] = held[:, 16:32, :].reshape(512, PART)
    rows = held[:, :16, :].reshape(512, PART)
    device = iota((512, D), 0) // 16
    spread = nn(rows, spread_table(24, D))
    spread = jnp.where(iota((512, D), 1) // 24 == device, spread, 0.0)
    vec_ref[...] = jnp.sum(spread.reshape(32, 16, D), axis=0)
    wide = nn(rows, spread_table(96, D))
    wide = jnp.where(iota((512, D), 1) // 96 == device % 8, wide, 0.0)
    for t in range(4):
        group = wide[t * 128 : (t + 1) * 128, :].reshape(8, 16, D)
        up_ref[:, t * D : (t + 1) * D] = jnp.sum(group, axis=0)[8:16, :]


def gathered_vectors(place, mem_parts, after=()):
    return call(
        vectors_kernel,
        [shape_of((16, D), F32), shape_of((8, FF), F32), shape_of((N, PART))],
        [SMEM] + [HBM] * 8,
        [VMEM] * 3,
        [pltpu.VMEM((32, 48, PART), BF16), pltpu.SemaphoreType.DMA],
        flops=FLOPS["vectors"],
        after=after,
    )(place, *mem_parts)


def pack_vectors(vectors, up_grad, tables):
    device, kind = iota((512, D), 0) // 16, iota((512, D), 0) % 16
    tiled = jnp.broadcast_to(vectors[None], (32, 16, D)).reshape(512, D)
    tiled = jnp.where((iota((512, D), 1) // 24 == device) & (kind < 8), tiled, 0.0).astype(BF16)
    ups = [jnp.broadcast_to(up_grad[0:1, t * D : (t + 1) * D], (128, D)) for t in range(4)]
    ups = jnp.concatenate(ups, axis=0)
    ups = jnp.where((iota((512, D), 1) // 96 == device % 8) & (kind == 8), ups, 0.0).astype(BF16)
    rows = nt(tiled, spread_table(24, D)) + nt(ups, spread_table(96, D))
    rows = rows.astype(BF16).reshape(32, 16, PART)
    table_rows = tables.astype(BF16).reshape(32, 16, PART)
    return jnp.concatenate([rows, table_rows, jnp.zeros((32, 16, PART), BF16)], axis=1)


def head_mask(rows, lanes, heads):
    return iota((rows, lanes), 1) // DH == heads


def front_call(place, tokens, vectors, coeff, tables, proj, keys, values, after=()):
    weights = (proj, keys, values)
    counts = [len(w.parts) for w in weights]

    def kernel(place_ref, tokens_ref, vec_ref, coeff_ref, table_ref, *refs):
        sources, at = [], 0
        for count in counts:
            sources.append(refs[at : at + count])
            at += count
        normed_ref, projected_ref, mem_values_ref, reads_ref, proj_ref, keys_ref, values_ref, sems = refs[at:]
        held = (proj_ref, keys_ref, values_ref)
        copies = [w.fetch(s, place_ref, h, sems.at[n]) for n, (w, s, h) in enumerate(zip(weights, sources, held))]
        normed = normalise(tokens_ref[0].astype(F32), vec_ref[0:1, :], vec_ref[1:2, :]).astype(BF16)
        normed_ref[...] = normed
        summary = tn(table_ref[...], coeff_ref[...])[:32, :]
        wait_all(copies[1])
        reads = one_split(nn, summary, keys_ref[...])
        head = iota((32, D), 1) // DH
        kind = iota((32, D), 0)
        centre = jnp.sum(jnp.where(kind == head, reads, 0.0), axis=0, keepdims=True)
        spread = jnp.sum(jnp.where(kind == head + H, reads, 0.0), axis=0, keepdims=True)
        row = iota((8, D), 0)
        reads_ref[...] = jnp.where(row == 0, centre, jnp.where(row == 1, spread, 0.0))
        wait_all(copies[2])
        mem_values_ref[...] = nn(coeff_ref[...], values_ref[...]).astype(BF16)
        wait_all(copies[0])

        def block(n, bias):
            at = pl.ds(n * D, D)
            projected_ref[:, at] = (nn(normed_ref[...], proj_ref[:, at]) + bias).astype(BF16)

        block(0, vec_ref[2:3, :])
        block(1, 0.0)
        block(2, vec_ref[3:4, :])

    return call(
        kernel,
        [shape_of((512, D)), shape_of((512, 3 * D)), shape_of((N, D)), shape_of((8, D), F32)],
        [SMEM] + [VMEM] * 4 + [HBM] * sum(counts),
        [VMEM] * 4,
        [
            pltpu.VMEM((D, 3 * D), BF16),
            pltpu.VMEM((D, D), BF16),
            pltpu.VMEM((D, D), BF16),
            pltpu.SemaphoreType.DMA((3,)),
        ],
        flops=FLOPS["front"],
        after=after,
    )(place, tokens, vectors, coeff, tables, *proj.parts, *keys.parts, *values.parts)


READ = 256


def document_rows(length_ref):
    place = iota((1, 512), 1)
    first = jnp.zeros((1, 512), jnp.int32)
    end = jnp.int32(0)
    for n in range(length_ref.shape[1] - 1):
        end = end + length_ref[0, n]
        first = jnp.where(place >= end, end, first)
    return first


def mask_bias(length_ref, bias_ref):
    first = document_rows(length_ref)
    key, query = iota((512, 512), 0), iota((512, 512), 1)
    bias_ref[...] = jnp.where((key <= query) & (key >= first), 0.0, masked_fill)


def reading_row(length_ref, carried_ref):
    inside = iota((1, READ), 1) < length_ref[0, 0]
    return jnp.where(inside, carried_ref[0].astype(F32), 0.0)


def read_parameters(scaled, reads):
    lane_head = iota((1, PART), 1) // DH
    rows = [jnp.where(lane_head == h, reads[kind : kind + 1, :], 0.0) for kind in (0, 1) for h in (0, 1)]
    rows = jnp.concatenate(rows + [jnp.zeros((4, PART), F32)], axis=0)
    high, low = split(rows)
    lowest = (rows - high.astype(F32) - low.astype(F32)).astype(BF16)
    logits = nt(high, scaled) + (nt(low, scaled) + nt(lowest, scaled))
    found = []
    for h in (0, 1):
        centre = 1.0 / (1.0 + jnp.exp(-logits[h : h + 1, :]))
        raw = logits[2 + h : 3 + h, :]
        spread = spread_scale * (jnp.maximum(raw, 0.0) + jnp.log1p(jnp.exp(-jnp.abs(raw))))
        variance = 1.0 / (N * N) + spread * spread
        found.append((centre, spread, variance, raw))
    return rows, found


def basis_column():
    return (iota((N, 1), 0).astype(F32) + 0.5) / N


def density_of(centre, variance):
    distance = centre - basis_column()
    return lax.rsqrt(variance) / N * jnp.exp(distance * distance * (-0.5 / variance)), distance


def head_lanes(value, h):
    return jnp.where(iota((1, PART), 1) // DH == h, value, jnp.zeros_like(value))


def attend_kernel(length_ref, carried_ref, q_ref, k_ref, v_ref, mem_ref, reads_ref, out_ref, lse_ref, bias_ref):
    pl.when(pl.program_id(0) == 0)(lambda: mask_bias(length_ref, bias_ref))
    scaled = q_ref[...] * jnp.asarray(score_scale, BF16)
    outs, totals = [], []
    for h in (0, 1):
        halves, lse = [], []
        for first in (0, 256):
            keys = first + 256
            scores = nt(k_ref[:keys, :], head_lanes(scaled[first : first + 256, :], h))
            scores = scores + bias_ref[:keys, first : first + 256]
            top = jnp.max(scores, axis=0, keepdims=True)
            weights = jnp.exp(scores - top)
            total = jnp.sum(weights, axis=0, keepdims=True)
            probs = (weights * (1.0 / total)).astype(BF16)
            halves.append(tn(v_ref[:keys, :], probs)[h * DH : (h + 1) * DH, :])
            lse.append(top + jnp.log(total))
        outs.append(halves)
        totals.append(jnp.concatenate(lse, axis=1))
    lse_ref[...] = jnp.concatenate(totals + [jnp.zeros((6, 512), F32)], axis=0)
    _, found = read_parameters(scaled[:READ, :], reads_ref[...])
    reading = reading_row(length_ref, carried_ref)
    for h in (0, 1):
        centre, _, variance, _ = found[h]
        density, _ = density_of(centre, variance)
        recall = tn(mem_ref[...], density.astype(BF16))[h * DH : (h + 1) * DH, :]
        outs[h][0] = outs[h][0] + recall * reading
    for n in (0, 1):
        block = jnp.concatenate([outs[0][n], outs[1][n]], axis=0)
        out_ref[n * 256 : (n + 1) * 256, :] = jnp.transpose(block).astype(BF16)


def pair_block(shift=0):
    return pl.BlockSpec((512, PART), lambda i: (0, i + shift))


def attend_call(lengths, carried, projected, mem_values, reads, after=()):
    return call(
        attend_kernel,
        [shape_of((512, D)), shape_of((PAIRS * 8, 512), F32)],
        [SMEM, SMEM, pair_block(), pair_block(PAIRS), pair_block(2 * PAIRS), pair_block(), pl.BlockSpec((8, PART), lambda i: (0, i))],
        [pair_block(), pl.BlockSpec((8, 512), lambda i: (i, 0))],
        [pltpu.VMEM((512, 512), F32)],
        flops=FLOPS["attend"],
        after=after,
        grid=(PAIRS,),
    )(lengths, carried, projected, projected, projected, mem_values, reads)


def attend_back_kernel(length_ref, carried_ref, q_ref, k_ref, v_ref, lse_ref, heads_ref, more_ref, gq_ref, gk_ref, gv_ref, bias_ref):
    pl.when(pl.program_id(0) == 0)(lambda: mask_bias(length_ref, bias_ref))
    scaled = q_ref[...] * jnp.asarray(score_scale, BF16)
    keys, values, grad = k_ref[...], v_ref[...], heads_ref[...]
    lane_head = iota((1, PART), 1) // DH
    grad_queries, grad_keys, grad_values = [], [], []
    for h in (0, 1):
        parts = []
        gk, gv = [], []
        for first in (0, 256):
            last = first + 256
            own, own_grad = head_lanes(scaled[first:last, :], h), head_lanes(grad[first:last, :], h)
            scores = nt(keys[:last, :], own) + bias_ref[:last, first:last]
            probs = jnp.exp(scores - lse_ref[h : h + 1, first:last])
            grad_probs = nt(values[:last, :], own_grad)
            row_terms = jnp.sum(probs * grad_probs, axis=0, keepdims=True)
            grad_scores = (probs * (grad_probs - row_terms)).astype(BF16)
            gv.append(nn(probs.astype(BF16), grad[first:last, :]))
            gk.append(nn(grad_scores, scaled[first:last, :]))
            parts.append(tn(keys[:last, :], grad_scores)[h * DH : (h + 1) * DH, :])
        grad_queries.append(parts)
        grad_keys.append((gk[0] + gk[1][:256, :], gk[1][256:, :]))
        grad_values.append((gv[0] + gv[1][:256, :], gv[1][256:, :]))
    for n in (0, 1):
        at = slice(n * 256, (n + 1) * 256)
        gk_ref[at, :] = jnp.where(lane_head == 0, grad_keys[0][n], grad_keys[1][n]).astype(BF16)
        gv_ref[at, :] = jnp.where(lane_head == 0, grad_values[0][n], grad_values[1][n]).astype(BF16)
        block = jnp.concatenate([grad_queries[0][n], grad_queries[1][n]], axis=0)
        if n == 0:
            block = block + more_ref[...]
        gq_ref[at, :] = (jnp.transpose(block) * score_scale).astype(BF16)


def memory_read_back_kernel(length_ref, carried_ref, q_ref, mem_ref, reads_ref, heads_ref, more_ref, gmem_ref, sums_ref):
    scaled = q_ref[...] * jnp.asarray(score_scale, BF16)
    grad = heads_ref[...]
    lane_head = iota((1, PART), 1) // DH
    rows, found = read_parameters(scaled, reads_ref[...])
    reading = reading_row(length_ref, carried_ref)
    centre_grads, spread_grads, grad_mems = [], [], []
    for h in (0, 1):
        centre, spread, variance, raw = found[h]
        density, distance = density_of(centre, variance)
        own_grad = head_lanes(grad, h)
        grad_density = nt(mem_ref[...], own_grad) * reading
        grad_mems.append(nn((density * reading).astype(BF16), own_grad))
        weight = grad_density * density
        moment0 = jnp.sum(weight, axis=0, keepdims=True)
        weight = weight * distance
        moment1 = jnp.sum(weight, axis=0, keepdims=True)
        moment2 = jnp.sum(weight * distance, axis=0, keepdims=True)
        inverse = 1.0 / variance
        grad_variance = 0.5 * inverse * (moment2 * inverse - moment0)
        centre_grads.append(-moment1 * inverse * centre * (1.0 - centre))
        spread_grads.append(grad_variance * 2.0 * spread * spread_scale / (1.0 + jnp.exp(-raw)))
    gmem_ref[...] = (grad_mems[0] + grad_mems[1]).astype(BF16)
    logit_grads = jnp.concatenate(centre_grads + spread_grads + [jnp.zeros((4, READ), F32)], axis=0)
    sums = one_split(nn, logit_grads, scaled)
    centre_sum = jnp.where(lane_head == 0, sums[0:1, :], sums[1:2, :])
    spread_sum = jnp.where(lane_head == 0, sums[2:3, :], sums[3:4, :])
    sums_ref[...] = jnp.concatenate([centre_sum, spread_sum, jnp.zeros((6, PART), F32)], axis=0)
    more_ref[...] = both_split(tn, rows, logit_grads)


FEW = pl.BlockSpec((8, PART), lambda i: (0, i))


def memory_read_back_call(lengths, carried, projected, mem_values, reads, grad_heads, after=()):
    near = pl.BlockSpec((READ, PART), lambda i: (0, i))
    return call(
        memory_read_back_kernel,
        [shape_of((D, READ), F32), shape_of((N, D)), shape_of((8, D), F32)],
        [SMEM, SMEM, near, pair_block(), FEW, near],
        [pl.BlockSpec((PART, READ), lambda i: (i, 0)), pair_block(), FEW],
        flops=FLOPS["memory_read_back"],
        grid=(PAIRS,),
        after=after,
    )(lengths, carried, projected, mem_values, reads, grad_heads)


def attend_back_call(lengths, carried, projected, lse, grad_heads, more, first, count, after=()):
    def pair(shift):
        return pl.BlockSpec((512, PART), lambda i: (0, i + shift))

    return call(
        attend_back_kernel,
        [shape_of((512, count * PART))] * 3,
        [SMEM, SMEM, pair(first), pair(first + PAIRS), pair(first + 2 * PAIRS),
         pl.BlockSpec((8, 512), lambda i: (i + first, 0)), pair(first), pl.BlockSpec((PART, READ), lambda i: (i + first, 0))],
        [pair(0)] * 3,
        [pltpu.VMEM((512, 512), F32)],
        flops=FLOPS["attend_back"],
        grid=(count,),
        after=after,
    )(lengths, carried, projected, projected, projected, lse, grad_heads, more)


GELU_SCALE = 0.7978845608028654
GELU_CUBE = 0.044715


def column_tiles(step_columns):
    return pl.BlockSpec((512, step_columns), lambda t: (0, t))


def fixed(shape):
    return pl.BlockSpec(shape, lambda t: (0,) * len(shape))


def weight_refs(weights, refs):
    found, at = [], 0
    for weight in weights:
        found.append(refs[at : at + len(weight.parts)])
        at += len(weight.parts)
    return found, refs[at:]


def mlp_call(place, tokens, heads, cotangent, vectors, up_bias, out, up, down, target, after=()):
    weights = (out, up, down)
    steps = FF // TILE

    def kernel(place_ref, tokens_ref, heads_ref, cot_ref, vec_ref, bias_ref, *refs):
        sources, refs = weight_refs(weights, refs)
        result_ref, middle_ref, normed_ref, slope_ref = refs[:4]
        grad_refs, (out_ref, up_ref, down_ref, total_ref, staged_ref, sems) = refs[4 : 4 + len(target.shapes)], refs[4 + len(target.shapes) :]
        held = (out_ref, up_ref, down_ref)
        step = pl.program_id(0)

        @pl.when(step == 0)
        def _():
            copies = [w.fetch(s, place_ref, h, sems.at[n]) for n, (w, s, h) in enumerate(zip(weights, sources, held))]
            wait_all(copies[0])
            middle = tokens_ref[0].astype(F32) + nn(heads_ref[...], out_ref[...]) + vec_ref[4:5, :]
            middle_ref[...] = middle
            normed_ref[...] = normalise(middle, vec_ref[5:6, :], vec_ref[6:7, :]).astype(BF16)
            total_ref[...] = middle + vec_ref[7:8, :]
            wait_all(copies[1])
            wait_all(copies[2])

        at = aligned(step, TILE)
        hidden = nn(normed_ref[...], up_ref[:, at]) + bias_ref[0:1, :]
        square = hidden * hidden
        bent = jnp.tanh(GELU_SCALE * hidden * (1.0 + GELU_CUBE * square))
        half = 0.5 + 0.5 * bent
        active = (hidden * half).astype(BF16)
        slope_ref[...] = half + 0.5 * hidden * (1.0 - bent * bent) * (GELU_SCALE + 3.0 * GELU_SCALE * GELU_CUBE * square)
        total_ref[...] += nn(active, down_ref[at, :])
        grad = tn(active, cot_ref[0]).astype(BF16)
        for n in range(steps):
            pl.when(step == n)(lambda n=n: target.tile_put(n, grad, staged_ref, grad_refs, place_ref, sems))

        @pl.when(step == steps - 1)
        def _():
            result_ref[0] = total_ref[...].astype(BF16)
            target.tile_wait(staged_ref, grad_refs, sems)

    found = call(
        kernel,
        [shape_of((1, 512, D)), shape_of((512, D), F32), shape_of((512, D)), shape_of((512, FF), F32)] + target.shapes,
        [SMEM, fixed((1, 512, D)), fixed((512, D)), fixed((1, 512, D)), fixed((16, D)), pl.BlockSpec((8, TILE), lambda t: (0, t))]
        + [HBM] * sum(len(w.parts) for w in weights),
        [fixed((1, 512, D)), fixed((512, D)), fixed((512, D)), column_tiles(TILE)] + [HBM] * len(target.shapes),
        [
            pltpu.VMEM((D, D), BF16),
            pltpu.VMEM((D, FF), BF16),
            pltpu.VMEM((FF, D), BF16),
            pltpu.VMEM((512, D), F32),
            pltpu.VMEM((FF, D), BF16),
            pltpu.SemaphoreType.DMA((4,)),
        ],
        flops=FLOPS["mlp"],
        after=after,
        grid=(steps,),
    )(place, tokens, heads, cotangent, vectors, up_bias, *out.parts, *up.parts, *down.parts)
    return found[:4], found[4:]


class DownTarget:
    def __init__(self, blocks):
        self.blocks = blocks
        self.shapes = blocks.shapes if blocks else [shape_of((FF, D))]

    def pieces(self):
        rows, half = self.blocks.rows, self.blocks.columns // 4
        return [((4 * rows, half), (q * rows, 0), q * half, half) for q in range(4)]

    def tile_put(self, n, grad, staged, refs, place_ref, sems):
        rows = pl.ds(n * TILE, TILE)
        staged[rows, :] = grad
        if self.blocks:
            self.blocks.put(staged.at[rows, :], refs, place_ref, sems.at[3], self.pieces(), dps=range(4 * n, 4 * n + 4))

    def tile_wait(self, staged, refs, sems):
        if self.blocks:
            self.blocks.wait(staged, refs, sems.at[3], self.pieces())
        else:
            start(staged, refs[0], sems.at[3]).wait()


class UpTarget:
    def __init__(self, blocks):
        self.blocks = blocks
        self.shapes = blocks.shapes if blocks else [shape_of((D, FF))]

    def pieces(self, n):
        return [((self.blocks.rows, 0), (0, 0), (n % 2) * TILE, TILE)]

    def tile_put(self, n, grad, staged, refs, place_ref, sems):
        staged[:, n * TILE : (n + 1) * TILE] = grad
        if self.blocks:
            tile = staged.at[:, pl.ds(n * TILE, TILE)]
            self.blocks.put(tile, refs, place_ref, sems.at[3], self.pieces(n), sides=(n // 2,))

    def tile_wait(self, staged, refs, sems):
        if self.blocks:
            for n in range(FF // TILE):
                self.blocks.wait(staged, refs, sems.at[3], self.pieces(n), sides=(n // 2,))
        else:
            start(staged, refs[0], sems.at[3]).wait()


def mlp_back_call(place, cotangent, slope, normed, up, down, target, after=()):
    weights = (up, down)
    steps = FF // TILE

    def kernel(place_ref, cot_ref, slope_ref, normed_ref, *refs):
        sources, refs = weight_refs(weights, refs)
        total_ref, bias_ref = refs[:2]
        grad_refs, (up_ref, down_ref, staged_ref, sems) = refs[2 : 2 + len(target.shapes)], refs[2 + len(target.shapes) :]
        step = pl.program_id(0)

        @pl.when(step == 0)
        def _():
            copies = [w.fetch(s, place_ref, h, sems.at[n]) for n, (w, s, h) in enumerate(zip(weights, sources, (up_ref, down_ref)))]
            wait_all(copies[1])
            wait_all(copies[0])
            total_ref[...] = jnp.zeros((512, D), F32)

        at = aligned(step, TILE)
        grad_hidden = (nt(cot_ref[0], down_ref[at, :]) * slope_ref[...]).astype(BF16)
        bias_ref[...] = jnp.broadcast_to(jnp.sum(grad_hidden.astype(F32), axis=0, keepdims=True), (8, TILE))
        total_ref[...] += nt(grad_hidden, up_ref[:, at])
        grad = tn(normed_ref[...], grad_hidden).astype(BF16)
        for n in range(steps):
            pl.when(step == n)(lambda n=n: target.tile_put(n, grad, staged_ref, grad_refs, place_ref, sems))
        pl.when(step == steps - 1)(lambda: target.tile_wait(staged_ref, grad_refs, sems))

    found = call(
        kernel,
        [shape_of((512, D), F32), shape_of((8, FF), F32)] + target.shapes,
        [SMEM, fixed((1, 512, D)), column_tiles(TILE), fixed((512, D))] + [HBM] * sum(len(w.parts) for w in weights),
        [fixed((512, D)), pl.BlockSpec((8, TILE), lambda t: (0, t))] + [HBM] * len(target.shapes),
        [
            pltpu.VMEM((D, FF), BF16),
            pltpu.VMEM((FF, D), BF16),
            pltpu.VMEM((D, FF), BF16),
            pltpu.SemaphoreType.DMA((4,)),
        ],
        flops=FLOPS["mlp_back"],
        after=after,
        grid=(steps,),
    )(place, cotangent, slope, normed, *up.parts, *down.parts)
    return found[:2], found[2:]


def middle_back_call(place, cotangent, middle, grad_normed, vectors, heads, out, after=()):
    def kernel(place_ref, cot_ref, middle_ref, grad_ref, vec_ref, heads_ref, *refs):
        sources, refs = weight_refs((out,), refs)
        grad_middle_ref, grad_heads_ref, out_grad_ref, sums_ref, out_ref, sem = refs
        copies = out.fetch(sources[0], place_ref, out_ref, sem)
        cot = cot_ref[0].astype(F32)
        back, gain, shift = normalise_back(middle_ref[...], vec_ref[5:6, :], grad_ref[...])
        grad_middle = cot + back
        grad_middle_ref[...] = grad_middle
        attended = grad_middle.astype(BF16)
        bias = jnp.sum(attended.astype(F32), axis=0, keepdims=True)
        last = jnp.sum(cot, axis=0, keepdims=True)
        nothing = jnp.zeros((4, D), F32)
        sums_ref[...] = jnp.concatenate([nothing, bias, gain, shift, last, nothing, nothing], axis=0)
        wait_all(copies)
        grad_heads_ref[...] = nt(attended, out_ref[...]).astype(BF16)
        out_grad_ref[...] = tn(heads_ref[...], attended).astype(BF16)

    return call(
        kernel,
        [shape_of((512, D), F32), shape_of((512, D)), shape_of((D, D)), shape_of((16, D), F32)],
        [SMEM] + [VMEM] * 5 + [HBM] * len(out.parts),
        [VMEM] * 4,
        [pltpu.VMEM((D, D), BF16), pltpu.SemaphoreType.DMA],
        flops=FLOPS["middle_back"],
        after=after,
    )(place, cotangent, middle, grad_normed, vectors, heads, *out.parts)


def memory_back_call(place, coeff, grad_mem_values, tables, sums, out_grad, keys, blocks, after=()):
    shapes = blocks.shapes if blocks else [shape_of((D, D))] * 3

    def kernel(place_ref, coeff_ref, grad_values_ref, table_ref, sums_ref, out_grad_ref, *refs):
        sources, refs = weight_refs((keys,), refs)
        tables_ref = refs[0]
        grad_refs, (keys_ref, key_grad_ref, value_grad_ref, sems) = refs[1 : 1 + len(shapes)], refs[1 + len(shapes) :]
        copies = keys.fetch(sources[0], place_ref, keys_ref, sems.at[0])
        staged = (out_grad_ref, key_grad_ref, value_grad_ref)

        def pieces(n):
            return [((blocks.rows, D // 2), (0, 0), n * (D // 2), D // 2)]

        def put(n):
            if blocks:
                blocks.put(staged[n], grad_refs, place_ref, sems.at[1 + n], pieces(n))
            else:
                start(staged[n], grad_refs[n], sems.at[1 + n])

        put(0)
        value_grad_ref[...] = tn(coeff_ref[...], grad_values_ref[...]).astype(BF16)
        put(2)
        head, kind = iota((32, D), 1) // DH, iota((32, D), 0)
        by_head = jnp.where(kind == head, sums_ref[0:1, :], jnp.where(kind == head + H, sums_ref[1:2, :], 0.0))
        summary = tn(coeff_ref[...], table_ref[...])[:, :32]
        key_grad_ref[...] = both_split(nn, summary, by_head).astype(BF16)
        put(1)
        wait_all(copies)
        high, low = split(by_head)
        wide = jnp.concatenate([high, low, jnp.zeros((PART - 64, D), BF16)], axis=0)
        reads = nt(keys_ref[...], wide)
        high, low = split(reads)
        found = nn(coeff_ref[...], high) + nn(coeff_ref[...], low)
        lane = iota((N, PART), 1)
        found = found + jnp.concatenate([found[:, 32:64], jnp.zeros((N, PART - 32), F32)], axis=1)
        tables_ref[...] = jnp.where(lane < 2 * H, found, 0.0)
        for n in range(3):
            if blocks:
                blocks.wait(staged[n], grad_refs, sems.at[1 + n], pieces(n))
            else:
                pltpu.make_async_copy(staged[n], grad_refs[n], sems.at[1 + n]).wait()

    found = call(
        kernel,
        [shape_of((N, PART), F32)] + shapes,
        [SMEM] + [VMEM] * 5 + [HBM] * len(keys.parts),
        [VMEM] + [HBM] * len(shapes),
        [pltpu.VMEM((D, D), BF16)] * 3 + [pltpu.SemaphoreType.DMA((4,))],
        flops=FLOPS["memory_back"],
        after=after,
    )(place, coeff, grad_mem_values, tables, sums, out_grad, *keys.parts)
    return found[0], found[1:]


def project_back_call(normed, grads, place, blocks, after=()):
    shapes = [shape for block in blocks for shape in block.shapes] if blocks else [shape_of((D, 3 * D))]

    def kernel(place_ref, normed_ref, *refs):
        parts, refs = refs[: len(grads)], refs[len(grads) :]
        grad_refs, (staged_ref, sem) = refs[: len(shapes)], refs[len(shapes) :]
        at = 0
        for part in parts:
            columns = part.shape[1]
            staged_ref[:, at : at + columns] = tn(normed_ref[...], part[...]).astype(BF16)
            at += columns
        if blocks:
            at = 0
            for n, block in enumerate(blocks):
                piece = [((block.rows, 3 * D // 2), (0, at), 0, block.columns)]
                block.put(staged_ref, grad_refs[2 * n : 2 * n + 2], place_ref, sem, piece)
                at += block.columns
            for n, block in enumerate(blocks):
                piece = [((block.rows, 3 * D // 2), (0, 0), 0, block.columns)]
                block.wait(staged_ref, grad_refs[2 * n : 2 * n + 2], sem, piece)
        else:
            start(staged_ref, grad_refs[0], sem).wait()

    return call(
        kernel,
        shapes,
        [SMEM] + [VMEM] * (1 + len(grads)),
        [HBM] * len(shapes),
        [pltpu.VMEM((D, 3 * D), BF16), pltpu.SemaphoreType.DMA],
        flops=FLOPS["project_back"],
        after=after,
    )(place, normed, *grads)


def input_back_call(place, tokens, vectors, grads, grad_middle, sums, up_bias_grad, tables, proj, blocks, after=()):
    shapes = blocks.shapes if blocks else [shape_of((16, D), F32)]

    def kernel(place_ref, tokens_ref, vec_ref, middle_ref, sums_ref, up_ref, table_ref, *refs):
        parts, refs = refs[: len(grads)], refs[len(grads) :]
        sources, refs = weight_refs((proj,), refs)
        result_ref = refs[0]
        grad_refs, (proj_ref, small_ref, sems) = refs[1 : 1 + len(shapes)], refs[1 + len(shapes) :]
        wait_all(proj.fetch(sources[0], place_ref, proj_ref, sems.at[0]))
        grad_normed, column_sums, at = jnp.zeros((512, D), F32), [], 0
        for part in parts:
            columns = part.shape[1]
            grad_normed = grad_normed + nt(part[...], proj_ref[:, at : at + columns])
            column_sums.append(jnp.sum(part[...].astype(F32), axis=0, keepdims=True))
            at += columns
        column_sums = jnp.concatenate(column_sums, axis=1)
        back, gain, shift = normalise_back(tokens_ref[0].astype(F32), vec_ref[0:1, :], grad_normed)
        result_ref[0] = middle_ref[...] + back
        vectors_grad = jnp.concatenate([gain, shift, column_sums[:, :D], column_sums[:, 2 * D :], sums_ref[4:16, :]], axis=0)
        if blocks:
            rows = blocks.rows
            small_ref[...] = pack_vectors(vectors_grad, up_ref[...], table_ref[...]).reshape(32 * rows, PART)
            piece = [((2 * rows, rows), (0, 0), 0, PART)]

            def send(core_here):
                for n, m, where in blocks._each(grad_refs, place_ref, core_here, range(16), (0, 1)):
                    start(small_ref.at[pl.ds((2 * n + m) * rows, rows), :], where, sems.at[1])

            pl.when(place_ref[2] == 0)(lambda: send(0))
            pl.when(place_ref[2] == 1)(lambda: send(1))
            blocks.wait(small_ref, grad_refs, sems.at[1], piece)
        else:
            small_ref[...] = jnp.zeros(small_ref.shape, BF16)
            grad_refs[0][...] = vectors_grad

    found = call(
        kernel,
        [shape_of((1, 512, D), F32)] + shapes,
        [SMEM] + [VMEM] * (6 + len(grads)) + [HBM] * len(proj.parts),
        [VMEM] + ([HBM] * 2 if blocks else [VMEM]),
        [pltpu.VMEM((D, 3 * D), BF16), pltpu.VMEM((32 * 48, PART), BF16), pltpu.SemaphoreType.DMA((2,))],
        flops=FLOPS["input_back"],
        after=after,
    )(place, tokens, vectors, grad_middle, sums, up_bias_grad, tables, *grads, *proj.parts)
    return found[0], found[1:]


def hop(value, z=0, x=0, core=0, f=0):
    pairs = []
    for dp in range(16):
        for side in range(2):
            other = (((dp // 4) ^ z) * 4) + ((((dp // 2) % 2) ^ x) * 2) + ((dp % 2) ^ core)
            pairs.append((dp * 2 + side, other * 2 + (side ^ f)))
    return lax.ppermute(value, BOTH, pairs)


def z_hops(block):
    return [block] + [hop(block, z=k) for k in (1, 2, 3)]


def quads(pieces, cut, after):
    rows, columns = pieces[0].shape

    def kernel(*refs):
        blocks, (left, right) = refs[:4], refs[4:]
        for k, block in enumerate(blocks):
            left[k] = block[:, :cut]
            right[k] = block[:, cut:]

    shapes = [shape_of((4, rows, cut)), shape_of((4, rows, columns - cut))]
    return list(call(kernel, shapes, [VMEM] * 4, [VMEM] * 2, flops=FLOPS["pack"], after=after)(*pieces))


BITS = (dict(x=1), dict(f=1))


def far_hops(quad, near, second):
    return [quad, near, hop(quad, **second), hop(near, **second)]


def core_hops(mine):
    return mine + [hop(part, core=1) for part in mine]


def plus(a, b):
    return (a.astype(F32) + b.astype(F32)).astype(BF16)


def halves(kept, got):
    return plus(kept[1], got[1]), plus(kept[0], got[0])


def last_hops(pairs):
    def side_by_side(k, dtype):
        parts = [(kept[k].astype(F32) + got[k].astype(F32)).astype(dtype) for kept, got in pairs]
        return parts[0] if len(parts) == 1 else jnp.concatenate(parts, axis=1)

    sent = [side_by_side(k, BF16) for k in (1, 2, 3)]
    return side_by_side(0, F32), sent


def finish(own, sent):
    total = own
    for k, part in zip((1, 2, 3), sent):
        total = total + hop(part, z=k).astype(F32)
    return total


COLUMN_SPLIT = (2, 5, 7, 8, 13, 15)
VECTORS = (0, 1, 3, 4, 6, 11, 12, 16)


def gather_whole(shards):
    def whole(k, shard):
        near = lax.all_gather(shard, "fsdp", axis=1 if k in COLUMN_SPLIT else 0, tiled=True)
        return lax.all_gather(near, "dp", axis=0, tiled=True)

    found = [whole(k, shard) for k, shard in enumerate(shards)]
    vectors = jnp.stack([found[k].astype(F32) for k in VECTORS] + [jnp.zeros((D,), F32)] * 8)
    up_bias = jnp.broadcast_to(found[14].astype(F32)[None], (8, FF))
    tables = jnp.pad(jnp.concatenate([found[9], found[10]], axis=1), ((0, 0), (0, PART - 2 * H)))
    weights = {k: Whole(found[k]) for k in COLUMN_SPLIT}
    return weights, vectors, up_bias, tables


def scatter_whole(totals):
    def part(k, total):
        near = lax.psum_scatter(total.astype(BF16), "dp", scatter_dimension=0, tiled=True)
        return lax.psum_scatter(near, "fsdp", scatter_dimension=1 if k in COLUMN_SPLIT else 0, tiled=True).astype(F32)

    return [part(k, total) for k, total in enumerate(totals)]


def pack_call(shards):
    order = [2, 7, 8, 5, 13, 15, 9, 10, 14] + list(VECTORS)
    arrays = [shards[k] if shards[k].ndim == 2 else shards[k].reshape(1, -1) for k in order]
    rows, half = shards[5].shape
    early_columns = 5 * half + PART

    def kernel(proj, keys, values, out, up, down, centre, spread, up_bias, *refs):
        vectors, (early, late) = refs[:-2], refs[-2:]
        early[:, : 3 * half] = proj[...]
        early[:, 3 * half : 4 * half] = keys[...]
        early[:, 4 * half : 5 * half] = values[...]
        lines = []
        for ref in list(vectors) + [up_bias]:
            line = ref[...].astype(F32)
            lines.append(jnp.concatenate([line, jnp.zeros((1, PART - line.shape[1]), F32)], axis=1))
        lines.append(jnp.zeros((16 - len(lines), PART), F32))
        tables = jnp.concatenate(
            [centre[...].astype(F32), spread[...].astype(F32), jnp.zeros((16, PART - 2 * H), F32)], axis=1
        )
        small = jnp.concatenate(lines + [tables, jnp.zeros((rows - 32, PART), F32)], axis=0)
        early[:, 5 * half :] = small.astype(BF16)
        late[:, :half] = out[...]
        late[:, half : 5 * half] = up[...]
        for q in range(4):
            late[:, (5 + q) * half : (6 + q) * half] = down[q * rows : (q + 1) * rows, :]

    return call(
        kernel,
        [shape_of((rows, early_columns)), shape_of((rows, 9 * half))],
        [VMEM] * len(arrays),
        [VMEM] * 2,
        flops=FLOPS["pack"],
    )(*arrays)


def local(
    mesh_sizes, tokens, context, past_coeffs, doc_lengths, carried, histogram, cotangent, *shards
):
    hops = mesh_sizes == (16, 2)
    dp = lax.axis_index("dp")
    place = jnp.stack([dp // 4, (dp // 2) % 2, dp % 2, lax.axis_index("fsdp")]).astype(jnp.int32)
    rows, half = shards[5].shape
    x_hop, f_hop = BITS
    if hops:
        early, late = pack_call(shards)
        early, late = z_hops(early), z_hops(late)
        points, gram, right = memory_system(histogram, past_coeffs, context, after=[early[0]])
        early = quads(early, 3 * half, [gram])
        near = [hop(early[0], **x_hop), hop(early[1], **f_hop)]
        system = (gram, right)
        steps = [eliminate(system, early)]
        late = quads(late, 5 * half, [steps[0][0]])
        far = [far_hops(early[0], near[0], f_hop), far_hops(early[1], near[1], x_hop)]
        steps.append(eliminate(steps[0][2:], near + late))
        proj_parts, mem_parts = core_hops(far[0]), core_hops(far[1])
        late_near = [hop(late[0], **x_hop), hop(late[1], **f_hop)]
        steps.append(eliminate(steps[1][2:], far[0][2:] + far[1][2:]))
        late_far = [far_hops(late[0], late_near[0], f_hop), far_hops(late[1], late_near[1], x_hop)]
        steps.append(eliminate(steps[2][2:], late_near))
        out_up_parts, down_parts = core_hops(late_far[0]), core_hops(late_far[1])
        coeff = substitute(steps)
        vectors, up_bias, tables = gathered_vectors(place, mem_parts)
        weights = {
            2: Hops(proj_parts, True, 0, 3 * half),
            7: Hops(mem_parts, False, 0, half),
            8: Hops(mem_parts, False, half, half),
            5: Hops(out_up_parts, True, 0, half),
            13: Hops(out_up_parts, True, half, 4 * half),
            15: Hops(down_parts, False, 0, half, 4),
        }
        far_done = late_far[0][2:] + late_far[1][2:]
    else:
        weights, vectors, up_bias, tables = gather_whole(shards)
        far_done = []
        points, *system = memory_system(histogram, past_coeffs, context)
        steps = [eliminate(system)]
        while len(steps) < N // PART:
            steps.append(eliminate(steps[-1][2:]))
        coeff = substitute(steps)
    normed, projected, mem_values, reads = front_call(
        place, tokens, vectors, coeff, tables, weights[2], weights[7], weights[8]
    )
    heads, lse = attend_call(doc_lengths, carried, projected, mem_values, reads, after=far_done)
    down_blocks = Blocks(False, rows, 4 * half) if hops else None
    (result, middle, normed_mlp, slope), down_grad = mlp_call(
        place, tokens, heads, cotangent, vectors, up_bias, weights[5], weights[13], weights[15], DownTarget(down_blocks)
    )
    up_blocks = Blocks(True, rows, 4 * half) if hops else None
    (grad_normed_mlp, grad_up_bias), up_grad = mlp_back_call(
        place, cotangent, slope, normed_mlp, weights[13], weights[15], UpTarget(up_blocks)
    )
    waits = {"middle": [], "read": [], "memory": [], "attend": [], "again": [], "project": [], "input": []}
    if hops:
        sent, kept_down = halves(down_grad[0], hop(down_grad[1], core=1))
        waits["middle"] = [sent]
        got_down = hop(sent, **f_hop)
    grad_middle, grad_heads, grad_out, sums = middle_back_call(
        place, cotangent, middle, grad_normed_mlp, vectors, heads, weights[5], after=waits["middle"]
    )
    if hops:
        sent, kept_up = halves(up_grad[0], hop(up_grad[1], core=1))
        waits["read"] = [sent]
        got_up = hop(sent, **x_hop)
    more, grad_mem, read_sums = memory_read_back_call(
        doc_lengths, carried, projected, mem_values, reads, grad_heads, after=waits["read"]
    )
    mem_blocks = Blocks(False, rows, 3 * half) if hops else None
    grad_tables, mem_grad = memory_back_call(
        place, coeff, grad_mem, tables, read_sums, grad_out, weights[7], mem_blocks
    )
    if hops:
        sent, kept_down = halves(kept_down, got_down)
        waits["attend"] = [sent]
        got_down = hop(sent, **x_hop)
    first = attend_back_call(
        doc_lengths, carried, projected, lse, grad_heads, more, 0, PAIRS // 2, after=waits["attend"]
    )
    if hops:
        sent, kept_mem = halves(mem_grad[0], hop(mem_grad[1], core=1))
        waits["again"] = [sent]
        got_mem = hop(sent, **f_hop)
        sent, kept_up = halves(kept_up, got_up)
        waits["again"].append(sent)
        got_up = hop(sent, **f_hop)
    second = attend_back_call(
        doc_lengths, carried, projected, lse, grad_heads, more, PAIRS // 2, PAIRS // 2, after=waits["again"]
    )
    grads = [part for pair in zip(first, second) for part in pair]
    proj_blocks = [Blocks(True, rows, 5 * PART), Blocks(False, rows, 4 * PART)] if hops else None
    proj_grad = project_back_call(normed, grads, place, proj_blocks)
    if hops:
        own, sent = last_hops([(kept_down, got_down), (kept_up, got_up)])
        early_done = finish(own, sent)
        pairs = [
            halves(keep, hop(send, core=1)) for keep, send in (proj_grad[:2], proj_grad[2:])
        ]
        waits["input"] = sent + [pairs[0][0], pairs[1][0]]
        got = [hop(pairs[0][0], **x_hop), hop(pairs[1][0], **f_hop)]
    small_blocks = Blocks(True, rows, PART) if hops else None
    grad_tokens, small_grad = input_back_call(
        place, tokens, vectors, grads, grad_middle, sums, grad_up_bias, grad_tables, weights[2], small_blocks,
        after=waits["input"],
    )
    if hops:
        sent, kept_mem = halves(kept_mem, got_mem)
        got_mem = hop(sent, **x_hop)
        sent, kept_small = halves(small_grad[0], hop(small_grad[1], core=1))
        got_small = hop(sent, **x_hop)
        pairs = [halves(pair[1], g) for pair, g in zip(pairs, got)]
        got = [hop(pairs[0][0], **f_hop), hop(pairs[1][0], **x_hop)]
        sent, kept_small = halves(kept_small, got_small)
        got_small = hop(sent, **f_hop)
        own, sent = last_hops(
            [(kept_mem, got_mem), (pairs[0][1], got[0]), (pairs[1][1], got[1]), (kept_small, got_small)]
        )
        late_done = finish(own, sent)
        down = early_done[:, : 4 * half]
        down = jnp.concatenate([down[:, q * half : (q + 1) * half] for q in range(4)], axis=0)
        summed = {15: down, 13: early_done[:, 4 * half :]}
        for n, k in enumerate((5, 7, 8)):
            summed[k] = late_done[:, n * half : (n + 1) * half]
        summed[2] = late_done[:, 3 * half : 6 * half]
        small = late_done[:, 6 * half :]
        for n, k in enumerate(VECTORS):
            summed[k] = small[n, : shards[k].shape[0]]
        summed[14] = small[8, : shards[14].shape[0]]
        summed[9], summed[10] = small[16:32, :H], small[16:32, H : 2 * H]
    else:
        totals = {13: up_grad[0], 15: down_grad[0], 2: proj_grad[0], 14: grad_up_bias[0]}
        totals[5], totals[7], totals[8] = mem_grad
        totals[9], totals[10] = grad_tables[:, :H], grad_tables[:, H : 2 * H]
        for n, k in enumerate(VECTORS):
            totals[k] = small_grad[0][n]
        summed = scatter_whole([totals[k] for k in range(17)])
    return (result, grad_tokens, *(summed[k] for k in range(17)), points)


def solution(mesh):
    both, row, table = P(BOTH), P("dp", "fsdp"), P(BOTH, None)
    block = P(BOTH, None, None)
    weights = (
        both, both, row, both, both, row, both, row, row, table, table, both, both, row, both, row, both,
    )
    in_specs = (block, block, block, table, both, table, block) + weights
    out_specs = (block, block) + weights + (table,)
    sizes = (mesh.shape["dp"], mesh.shape["fsdp"])
    return jax.shard_map(
        functools.partial(local, sizes), mesh=mesh, in_specs=in_specs, out_specs=out_specs, check_vma=False
    )
```

```python
import functools

import jax
import jax.numpy as jnp
from jax import lax
from jax.experimental import pallas as pl
from jax.experimental.pallas import tpu as pltpu
from jax.sharding import PartitionSpec as P

H = 12
DH = 64
D = H * DH
N = 512
CTX = 1024
M = 512
NBINS = 64
FF = 4 * D
PAIRS = H // 2
PART = 128
TILE = 768

memory_tau = 0.75
ridge_weight = 1.0
norm_epsilon = 1e-05
spread_scale = 0.25
masked_fill = -1e30
score_scale = DH ** (-0.5)

F32, BF16 = jnp.float32, jnp.bfloat16
MIB = 1024 * 1024
BOTH = ("dp", "fsdp")
HBM = pl.BlockSpec(memory_space=pl.ANY)
SMEM = pl.BlockSpec(memory_space=pltpu.SMEM)
VMEM = pl.BlockSpec(memory_space=pltpu.VMEM)


FLOPS = {
    "pack": 1, "system": 8, "eliminate": 5, "substitute": 2, "vectors": 2, "front": 7, "attend": 14, "mlp": 19,
    "mlp_back": 9, "middle_back": 4, "memory_read_back": 7, "memory_back": 7, "attend_back": 7, "input_back": 11,
    "add": 10,
}
FLOPS = {name: work * 20000_000_000 for name, work in FLOPS.items()}


def shape_of(shape, dtype=BF16):
    return jax.ShapeDtypeStruct(shape, dtype)


def call(kernel, out_shape, in_specs, out_specs, scratch=(), flops=0, grid=None, after=(), vmem=20):
    extra = {} if grid is None else {"grid": grid}
    inputs, unread = len(in_specs), len(after)

    def body(*refs):
        kernel(*refs[:inputs], *refs[inputs + unread :])

    run = pl.pallas_call(
        body,
        out_shape=out_shape,
        in_specs=list(in_specs) + [HBM] * unread,
        out_specs=out_specs,
        scratch_shapes=list(scratch),
        compiler_params=pltpu.CompilerParams(vmem_limit_bytes=vmem * MIB),
        cost_estimate=pl.CostEstimate(flops=flops, bytes_accessed=0, transcendentals=0),
        **extra,
    )
    return lambda *operands: run(*operands, *after)


def nn(a, b):
    return lax.dot_general(a, b, (((1,), (0,)), ((), ())), preferred_element_type=F32)


def nt(a, b):
    return lax.dot_general(a, b, (((1,), (1,)), ((), ())), preferred_element_type=F32)


def tn(a, b):
    return lax.dot_general(a, b, (((0,), (0,)), ((), ())), preferred_element_type=F32)


def split(value):
    high = value.astype(BF16)
    return high, (value - high.astype(F32)).astype(BF16)


def both_split(product, a, b):
    a_high, a_low = split(a)
    b_high, b_low = split(b)
    return product(a_high, b_high) + (product(a_high, b_low) + product(a_low, b_high))


def one_split(product, a, b):
    a_high, a_low = split(a)
    return product(a_high, b) + product(a_low, b)


def iota(shape, axis):
    return lax.broadcasted_iota(jnp.int32, shape, axis)


def gaussian(points, centres):
    distance = points - centres
    return jnp.exp(-0.5 * distance * distance * (N * N))


def normalise(values, gain, shift):
    mean = jnp.mean(values, axis=-1, keepdims=True)
    centred = values - mean
    variance = jnp.mean(centred * centred, axis=-1, keepdims=True)
    inverse = lax.rsqrt(variance + norm_epsilon)
    return centred * inverse * gain + shift


def normalise_back(values, gain, grad):
    mean = jnp.mean(values, axis=-1, keepdims=True)
    centred = values - mean
    variance = jnp.mean(centred * centred, axis=-1, keepdims=True)
    inverse = lax.rsqrt(variance + norm_epsilon)
    standard = centred * inverse
    scaled = grad * gain
    first = jnp.mean(scaled, axis=-1, keepdims=True)
    second = jnp.mean(scaled * standard, axis=-1, keepdims=True)
    back = inverse * (scaled - first - standard * second)
    return back, jnp.sum(grad * standard, axis=0, keepdims=True), jnp.sum(grad, axis=0, keepdims=True)


def system_kernel(hist_ref, past_ref, context_ref, points_ref, gram_ref, right_ref):
    hist = hist_ref[...]
    counts = jnp.broadcast_to(hist, (NBINS, NBINS))
    row, column = iota((NBINS, NBINS), 0), iota((NBINS, NBINS), 1)

    def down(keep):
        return jnp.sum(jnp.where(keep, counts, 0), axis=1, keepdims=True)

    ends, starts, count = down(column <= row), down(column < row), down(column == row)
    slot = iota((NBINS, M), 1)
    inside = (slot >= starts) & (slot < ends)

    def across(values):
        return jnp.sum(jnp.where(inside, values, 0), axis=0, keepdims=True)

    first, amount, number = across(starts), across(count), across(iota((NBINS, M), 0))
    offset = (iota((1, M), 1) - first).astype(F32) + 0.5
    points = (number.astype(F32) + offset / amount.astype(F32)) / NBINS
    points_ref[...] = points
    upright = jnp.sum(
        jnp.where(iota((M, M), 0) == iota((M, M), 1), points, 0.0), axis=1, keepdims=True
    )
    centre_row = (iota((1, N), 1).astype(F32) + 0.5) / N
    centre_column = (iota((N, 1), 0).astype(F32) + 0.5) / N
    past_values = one_split(nn, gaussian(upright, centre_row), past_ref[0])
    recent = memory_tau + (1.0 - memory_tau) * (iota((1, CTX), 1).astype(F32) + 0.5) / CTX
    old = gaussian(memory_tau * points, centre_column)
    new = gaussian(recent, centre_column)
    right_ref[...] = both_split(nn, old, past_values) + one_split(nn, new, context_ref[0])
    eye = (iota((N, N), 0) == iota((N, N), 1)).astype(F32) * ridge_weight
    gram_ref[...] = both_split(nt, old, old) + both_split(nt, new, new) + eye


def memory_system(histogram, past, context, after=()):
    return call(
        system_kernel,
        [shape_of((1, M), F32), shape_of((N, N), F32), shape_of((N, D), F32)],
        [VMEM] * 3,
        [VMEM] * 3,
        flops=FLOPS["system"],
        vmem=24,
        after=after,
    )(histogram, past, context)


PANEL = 16


def three(value):
    high = value.astype(BF16)
    rest = value - high.astype(F32)
    middle = rest.astype(BF16)
    return high, middle, (rest - middle.astype(F32)).astype(BF16)


def small_inverse(m):
    def minor(r0, r1, c0, c1):
        return m[r0][c0] * m[r1][c1] - m[r0][c1] * m[r1][c0]

    places = ((0, 1), (0, 2), (0, 3), (1, 2), (1, 3), (2, 3))
    s = [minor(0, 1, *place) for place in places]
    c = [minor(2, 3, *place) for place in places]
    total = ((s[0] * c[5] - s[1] * c[4]) + (s[2] * c[3] + s[3] * c[2])) + (s[5] * c[0] - s[4] * c[1])
    r = 1.0 / total
    q = [[None] * 4 for _ in range(4)]
    q[0][0] = (m[1][1] * c[5] - m[1][2] * c[4] + m[1][3] * c[3]) * r
    q[0][1] = (m[0][2] * c[4] - m[0][1] * c[5] - m[0][3] * c[3]) * r
    q[0][2] = (m[3][1] * s[5] - m[3][2] * s[4] + m[3][3] * s[3]) * r
    q[0][3] = (m[2][2] * s[4] - m[2][1] * s[5] - m[2][3] * s[3]) * r
    q[1][1] = (m[0][0] * c[5] - m[0][2] * c[2] + m[0][3] * c[1]) * r
    q[1][2] = (m[3][2] * s[2] - m[3][0] * s[5] - m[3][3] * s[1]) * r
    q[1][3] = (m[2][0] * s[5] - m[2][2] * s[2] + m[2][3] * s[1]) * r
    q[2][2] = (m[3][0] * s[4] - m[3][1] * s[2] + m[3][3] * s[0]) * r
    q[2][3] = (m[2][1] * s[2] - m[2][0] * s[4] - m[2][3] * s[0]) * r
    q[3][3] = (m[2][0] * s[3] - m[2][1] * s[1] + m[2][2] * s[0]) * r
    for i in range(4):
        for j in range(i):
            q[i][j] = q[j][i]
    return q


def inverse_of(block):
    row, column = iota((PANEL, PART), 0), iota((PANEL, PART), 1)
    lane = iota((PART, PART), 1)
    work = block
    for k in range(0, PART, PANEL):
        panel = work[k : k + PANEL, :]
        left = jnp.where(column < k, -panel, jnp.where(column < k + PANEL, 0.0, panel))
        for s in range(0, PANEL, 4):
            at = k + s
            columns = [jnp.broadcast_to(panel[:, at + i : at + i + 1], (PANEL, PART)) for i in range(4)]
            lines = [
                jnp.where(
                    (column[:1] >= at) & (column[:1] < at + 4),
                    (column[:1] == at + i).astype(F32),
                    panel[s + i : s + i + 1, :],
                )
                for i in range(4)
            ]
            inverse = small_inverse([[columns[j][s + i : s + i + 1, :] for j in range(4)] for i in range(4)])
            inside = (row >= s) & (row < s + 4)
            panel = jnp.where(inside | ((column >= at) & (column < at + 4)), 0.0, panel)
            for i in range(4):
                line = (inverse[i][0] * lines[0] + inverse[i][1] * lines[1]) + (
                    inverse[i][2] * lines[2] + inverse[i][3] * lines[3]
                )
                panel = panel - jnp.where(inside, jnp.where(row == s + i, -1.0, 0.0), columns[i]) * line
        u, w = three(left), three(panel)
        update = tn(
            jnp.concatenate([u[0], u[0], u[1], u[0], u[2], u[1]], axis=0),
            jnp.concatenate([w[0], w[1], w[0], w[2], w[0], w[1]], axis=0),
        )
        others = jnp.where((lane >= k) & (lane < k + PANEL), 0.0, work) - update
        above = [others[:k, :]] if k else []
        below = [others[k + PANEL :, :]] if k + PANEL < PART else []
        work = jnp.concatenate(above + [panel] + below, axis=0)
    return work


def eliminate_kernel(gram_ref, right_ref, link_ref, known_ref, *rest):
    inverse = inverse_of(gram_ref[:PART, :PART])
    top = right_ref[:PART, :]
    known_ref[...] = both_split(nn, inverse, top)
    if rest:
        next_gram_ref, next_right_ref = rest
        beside = gram_ref[:PART, PART:]
        link = both_split(nn, inverse, beside)
        link_ref[...] = link
        next_gram_ref[...] = gram_ref[PART:, PART:] - both_split(tn, beside, link)
        next_right_ref[...] = right_ref[PART:, :] - both_split(tn, link, top)
    else:
        link_ref[...] = jnp.zeros(link_ref.shape, F32)


def substitute_kernel(*refs):
    links, known, out = refs[:3], refs[3:7], refs[7]
    found = known[3][...]
    out[pl.ds(3 * PART, PART), :] = found.astype(BF16)
    for k in (2, 1, 0):
        part = known[k][...] - both_split(nn, links[k][...], found)
        out[pl.ds(k * PART, PART), :] = part.astype(BF16)
        found = jnp.concatenate([part, found], axis=0)


def eliminate(system, after=()):
    gram, right = system
    left = gram.shape[0] - PART
    shapes = [shape_of((PART, max(left, PART)), F32), shape_of((PART, D), F32)]
    if left:
        shapes += [shape_of((left, left), F32), shape_of((left, D), F32)]
    return call(
        eliminate_kernel, shapes, [VMEM] * 2, [VMEM] * len(shapes), flops=FLOPS["eliminate"], after=after
    )(gram, right)


def substitute(steps, after=()):
    links, known = [step[0] for step in steps[:-1]], [step[1] for step in steps]
    return call(substitute_kernel, shape_of((N, D)), [VMEM] * 7, VMEM, flops=FLOPS["substitute"], after=after)(*links, *known)


def block_offsets(x_first):
    for array in range(4):
        core, second = array // 2, array % 2
        for index in range(8):
            first, z = index // 4, index % 4
            x, f = (first, second) if x_first else (second, first)
            yield array, index, z, x, core, f


def position(place_ref, z, x, core, f):
    dp = (place_ref[0] ^ z) * 4 + (place_ref[1] ^ x) * 2 + (place_ref[2] ^ core)
    return dp, place_ref[3] ^ f


def aligned(index, size):
    return pl.ds(pl.multiple_of(index * size, size), size)


def start(source, target, sem):
    copy = pltpu.make_async_copy(source, target, sem)
    copy.start()
    return copy


def wait_all(copies):
    for copy in copies:
        copy.wait()


class Hops:
    def __init__(self, parts, x_first, first, columns, groups=1):
        self.parts, self.x_first, self.columns, self.groups = parts, x_first, columns, groups
        self.first = first if isinstance(first, list) else [first] * len(parts)

    def fetch(self, refs, place_ref, whole, sem):
        copies, rows = [], self.parts[0].shape[1]
        for array, index, z, x, core, f in block_offsets(self.x_first):
            dp, side = position(place_ref, z, x, core, f)
            for q in range(self.groups):
                source = refs[array].at[index, :, pl.ds(self.first[array] + q * self.columns, self.columns)]
                target = whole.at[aligned(dp * self.groups + q, rows), aligned(side, self.columns)]
                copies.append(start(source, target, sem))
        return copies


class Whole:
    def __init__(self, array):
        self.parts = [array]

    def fetch(self, refs, place_ref, whole, sem):
        return [start(refs[0], whole, sem)]


class Blocks:
    def __init__(self, x_first, rows, columns):
        self.x_first, self.rows, self.columns = x_first, rows, columns
        self.shapes = [shape_of((2, 2, 4, rows, columns))] * 2

    def _each(self, refs, place_ref, core_here, dps, sides):
        z0, x0, f0 = place_ref[0], place_ref[1], place_ref[3]
        for n, dp in enumerate(dps):
            z, x, core = dp // 4, (dp // 2) % 2, dp % 2
            target = refs[0] if core == core_here else refs[1]
            for m, side in enumerate(sides):
                bits = (x ^ x0, side ^ f0) if self.x_first else (side ^ f0, x ^ x0)
                yield n, m, target.at[bits[0], bits[1], z ^ z0]

    def put(self, staged, refs, place_ref, sem, pieces, dps=range(16), sides=(0, 1)):
        def send(core_here):
            for n, m, where in self._each(refs, place_ref, core_here, dps, sides):
                for steps, offsets, first, columns in pieces:
                    rows = pl.ds(n * steps[0] + offsets[0], self.rows)
                    across = pl.ds(m * steps[1] + offsets[1], columns)
                    start(staged.at[rows, across], where.at[:, pl.ds(first, columns)], sem)

        pl.when(place_ref[2] == 0)(lambda: send(0))
        pl.when(place_ref[2] == 1)(lambda: send(1))

    def wait(self, staged, refs, sem, pieces, dps=range(16), sides=(0, 1)):
        for _ in range(len(dps) * len(sides)):
            for _, _, first, columns in pieces:
                source = staged.at[pl.ds(0, self.rows), pl.ds(0, columns)]
                pltpu.make_async_copy(source, refs[0].at[0, 0, 0, :, pl.ds(first, columns)], sem).wait()


def spread_table(width, lanes):
    return (iota((PART, lanes), 0) == iota((PART, lanes), 1) % width).astype(BF16)


def vectors_kernel(place_ref, *refs):
    parts, (vec_ref, up_ref, table_ref, held, sem) = refs[:4], refs[4:]
    copies = []
    for array, index, z, x, core, f in block_offsets(False):
        dp, side = position(place_ref, z, x, core, f)
        first = parts[array].shape[2] - PART
        copies.append(start(parts[array].at[index, :, pl.ds(first, PART)], held.at[dp * 2 + side], sem))
    wait_all(copies)
    table_ref[...] = held[:, 16:32, :].reshape(512, PART)
    rows = held[:, :16, :].reshape(512, PART)
    device = iota((512, D), 0) // 16
    spread = nn(rows, spread_table(24, D))
    spread = jnp.where(iota((512, D), 1) // 24 == device, spread, 0.0)
    vec_ref[...] = jnp.sum(spread.reshape(32, 16, D), axis=0)
    wide = nn(rows, spread_table(96, D))
    wide = jnp.where(iota((512, D), 1) // 96 == device % 8, wide, 0.0)
    for t in range(4):
        group = wide[t * 128 : (t + 1) * 128, :].reshape(8, 16, D)
        up_ref[:, t * D : (t + 1) * D] = jnp.sum(group, axis=0)[8:16, :]


def gathered_vectors(place, mem_parts, after=()):
    return call(
        vectors_kernel,
        [shape_of((16, D), F32), shape_of((8, FF), F32), shape_of((N, PART))],
        [SMEM] + [HBM] * 4,
        [VMEM] * 3,
        [pltpu.VMEM((32, 48, PART), BF16), pltpu.SemaphoreType.DMA],
        flops=FLOPS["vectors"],
        after=after,
    )(place, *mem_parts)


def pack_vectors(vectors, up_grad, tables):
    device, kind = iota((512, D), 0) // 16, iota((512, D), 0) % 16
    tiled = jnp.broadcast_to(vectors[None], (32, 16, D)).reshape(512, D)
    tiled = jnp.where((iota((512, D), 1) // 24 == device) & (kind < 8), tiled, 0.0).astype(BF16)
    ups = [jnp.broadcast_to(up_grad[0:1, t * D : (t + 1) * D], (128, D)) for t in range(4)]
    ups = jnp.concatenate(ups, axis=0)
    ups = jnp.where((iota((512, D), 1) // 96 == device % 8) & (kind == 8), ups, 0.0).astype(BF16)
    rows = nt(tiled, spread_table(24, D)) + nt(ups, spread_table(96, D))
    rows = rows.astype(BF16).reshape(32, 16, PART)
    table_rows = tables.astype(BF16).reshape(32, 16, PART)
    return jnp.concatenate([rows, table_rows, jnp.zeros((32, 16, PART), BF16)], axis=1)


def head_mask(rows, lanes, heads):
    return iota((rows, lanes), 1) // DH == heads


def front_call(place, tokens, vectors, coeff, tables, proj, keys, values, after=()):
    weights = (proj, keys, values)
    counts = [len(w.parts) for w in weights]

    def kernel(place_ref, tokens_ref, vec_ref, coeff_ref, table_ref, *refs):
        sources, at = [], 0
        for count in counts:
            sources.append(refs[at : at + count])
            at += count
        normed_ref, projected_ref, mem_values_ref, reads_ref, proj_ref, keys_ref, values_ref, sems = refs[at:]
        held = (proj_ref, keys_ref, values_ref)
        copies = [w.fetch(s, place_ref, h, sems.at[n]) for n, (w, s, h) in enumerate(zip(weights, sources, held))]
        normed = normalise(tokens_ref[0].astype(F32), vec_ref[0:1, :], vec_ref[1:2, :]).astype(BF16)
        normed_ref[...] = normed
        summary = tn(table_ref[...], coeff_ref[...])[:32, :]
        wait_all(copies[1])
        reads = one_split(nn, summary, keys_ref[...])
        head = iota((32, D), 1) // DH
        kind = iota((32, D), 0)
        centre = jnp.sum(jnp.where(kind == head, reads, 0.0), axis=0, keepdims=True)
        spread = jnp.sum(jnp.where(kind == head + H, reads, 0.0), axis=0, keepdims=True)
        row = iota((8, D), 0)
        reads_ref[...] = jnp.where(row == 0, centre, jnp.where(row == 1, spread, 0.0))
        wait_all(copies[2])
        mem_values_ref[...] = nn(coeff_ref[...], values_ref[...]).astype(BF16)
        wait_all(copies[0])

        def block(n, bias):
            at = pl.ds(n * D, D)
            projected_ref[:, at] = (nn(normed_ref[...], proj_ref[:, at]) + bias).astype(BF16)

        block(0, vec_ref[2:3, :])
        block(1, 0.0)
        block(2, vec_ref[3:4, :])

    return call(
        kernel,
        [shape_of((512, D)), shape_of((512, 3 * D)), shape_of((N, D)), shape_of((8, D), F32)],
        [SMEM] + [VMEM] * 4 + [HBM] * sum(counts),
        [VMEM] * 4,
        [
            pltpu.VMEM((D, 3 * D), BF16),
            pltpu.VMEM((D, D), BF16),
            pltpu.VMEM((D, D), BF16),
            pltpu.SemaphoreType.DMA((3,)),
        ],
        flops=FLOPS["front"],
        vmem=28,
        after=after,
    )(place, tokens, vectors, coeff, tables, *proj.parts, *keys.parts, *values.parts)


READ = 256


def document_rows(length_ref):
    place = iota((1, 512), 1)
    first = jnp.zeros((1, 512), jnp.int32)
    end = jnp.int32(0)
    for n in range(length_ref.shape[1] - 1):
        end = end + length_ref[0, n]
        first = jnp.where(place >= end, end, first)
    return first


def mask_bias(length_ref, bias_ref):
    first = document_rows(length_ref)
    key, query = iota((512, 512), 0), iota((512, 512), 1)
    bias_ref[...] = jnp.where((key <= query) & (key >= first), 0.0, masked_fill)


def reading_row(length_ref, carried_ref):
    inside = iota((1, READ), 1) < length_ref[0, 0]
    return jnp.where(inside, carried_ref[0].astype(F32), 0.0)


def read_parameters(scaled, reads):
    lane_head = iota((1, PART), 1) // DH
    rows = [jnp.where(lane_head == h, reads[kind : kind + 1, :], 0.0) for kind in (0, 1) for h in (0, 1)]
    rows = jnp.concatenate(rows + [jnp.zeros((4, PART), F32)], axis=0)
    high, low = split(rows)
    lowest = (rows - high.astype(F32) - low.astype(F32)).astype(BF16)
    logits = nt(high, scaled) + (nt(low, scaled) + nt(lowest, scaled))
    found = []
    for h in (0, 1):
        centre = 1.0 / (1.0 + jnp.exp(-logits[h : h + 1, :]))
        raw = logits[2 + h : 3 + h, :]
        spread = spread_scale * (jnp.maximum(raw, 0.0) + jnp.log1p(jnp.exp(-jnp.abs(raw))))
        variance = 1.0 / (N * N) + spread * spread
        found.append((centre, spread, variance, raw))
    return rows, found


def basis_column():
    return (iota((N, 1), 0).astype(F32) + 0.5) / N


def density_of(centre, variance):
    distance = centre - basis_column()
    return lax.rsqrt(variance) / N * jnp.exp(distance * distance * (-0.5 / variance)), distance


def head_lanes(value, h):
    return jnp.where(iota((1, PART), 1) // DH == h, value, jnp.zeros_like(value))


def attend_kernel(length_ref, carried_ref, q_ref, k_ref, v_ref, mem_ref, reads_ref, out_ref, lse_ref, bias_ref):
    pl.when(pl.program_id(0) == 0)(lambda: mask_bias(length_ref, bias_ref))
    scaled = q_ref[...] * jnp.asarray(score_scale, BF16)
    outs, totals = [], []
    for h in (0, 1):
        halves, lse = [], []
        for first in (0, 256):
            keys = first + 256
            scores = nt(k_ref[:keys, :], head_lanes(scaled[first : first + 256, :], h))
            scores = scores + bias_ref[:keys, first : first + 256]
            top = jnp.max(scores, axis=0, keepdims=True)
            weights = jnp.exp(scores - top)
            total = jnp.sum(weights, axis=0, keepdims=True)
            probs = (weights * (1.0 / total)).astype(BF16)
            halves.append(tn(v_ref[:keys, :], probs)[h * DH : (h + 1) * DH, :])
            lse.append(top + jnp.log(total))
        outs.append(halves)
        totals.append(jnp.concatenate(lse, axis=1))
    lse_ref[...] = jnp.concatenate(totals + [jnp.zeros((6, 512), F32)], axis=0)
    _, found = read_parameters(scaled[:READ, :], reads_ref[...])
    reading = reading_row(length_ref, carried_ref)
    for h in (0, 1):
        centre, _, variance, _ = found[h]
        density, _ = density_of(centre, variance)
        recall = tn(mem_ref[...], density.astype(BF16))[h * DH : (h + 1) * DH, :]
        outs[h][0] = outs[h][0] + recall * reading
    for n in (0, 1):
        block = jnp.concatenate([outs[0][n], outs[1][n]], axis=0)
        out_ref[n * 256 : (n + 1) * 256, :] = jnp.transpose(block).astype(BF16)


def pair_block(shift=0):
    return pl.BlockSpec((512, PART), lambda i: (0, i + shift))


def attend_call(lengths, carried, projected, mem_values, reads, after=()):
    return call(
        attend_kernel,
        [shape_of((512, D)), shape_of((PAIRS * 8, 512), F32)],
        [SMEM, SMEM, pair_block(), pair_block(PAIRS), pair_block(2 * PAIRS), pair_block(), pl.BlockSpec((8, PART), lambda i: (0, i))],
        [pair_block(), pl.BlockSpec((8, 512), lambda i: (i, 0))],
        [pltpu.VMEM((512, 512), F32)],
        flops=FLOPS["attend"],
        after=after,
        grid=(PAIRS,),
    )(lengths, carried, projected, projected, projected, mem_values, reads)


def attend_back_kernel(length_ref, carried_ref, q_ref, k_ref, v_ref, lse_ref, heads_ref, more_ref, gq_ref, gk_ref, gv_ref, bias_ref):
    pl.when(pl.program_id(0) == 0)(lambda: mask_bias(length_ref, bias_ref))
    scaled = q_ref[...] * jnp.asarray(score_scale, BF16)
    keys, values, grad = k_ref[...], v_ref[...], heads_ref[...]
    lane_head = iota((1, PART), 1) // DH
    grad_queries, grad_keys, grad_values = [], [], []
    for h in (0, 1):
        parts = []
        gk, gv = [], []
        for first in (0, 256):
            last = first + 256
            own, own_grad = head_lanes(scaled[first:last, :], h), head_lanes(grad[first:last, :], h)
            scores = nt(keys[:last, :], own) + bias_ref[:last, first:last]
            probs = jnp.exp(scores - lse_ref[h : h + 1, first:last])
            grad_probs = nt(values[:last, :], own_grad)
            row_terms = jnp.sum(probs * grad_probs, axis=0, keepdims=True)
            grad_scores = (probs * (grad_probs - row_terms)).astype(BF16)
            gv.append(nn(probs.astype(BF16), grad[first:last, :]))
            gk.append(nn(grad_scores, scaled[first:last, :]))
            parts.append(tn(keys[:last, :], grad_scores)[h * DH : (h + 1) * DH, :])
        grad_queries.append(parts)
        grad_keys.append((gk[0] + gk[1][:256, :], gk[1][256:, :]))
        grad_values.append((gv[0] + gv[1][:256, :], gv[1][256:, :]))
    for n in (0, 1):
        at = slice(n * 256, (n + 1) * 256)
        gk_ref[at, :] = jnp.where(lane_head == 0, grad_keys[0][n], grad_keys[1][n]).astype(BF16)
        gv_ref[at, :] = jnp.where(lane_head == 0, grad_values[0][n], grad_values[1][n]).astype(BF16)
        block = jnp.concatenate([grad_queries[0][n], grad_queries[1][n]], axis=0)
        if n == 0:
            block = block + more_ref[...]
        gq_ref[at, :] = (jnp.transpose(block) * score_scale).astype(BF16)


def memory_read_back_kernel(length_ref, carried_ref, q_ref, mem_ref, reads_ref, heads_ref, more_ref, gmem_ref, sums_ref):
    scaled = q_ref[...] * jnp.asarray(score_scale, BF16)
    grad = heads_ref[...]
    lane_head = iota((1, PART), 1) // DH
    rows, found = read_parameters(scaled, reads_ref[...])
    reading = reading_row(length_ref, carried_ref)
    centre_grads, spread_grads, grad_mems = [], [], []
    for h in (0, 1):
        centre, spread, variance, raw = found[h]
        density, distance = density_of(centre, variance)
        own_grad = head_lanes(grad, h)
        grad_density = nt(mem_ref[...], own_grad) * reading
        grad_mems.append(nn((density * reading).astype(BF16), own_grad))
        weight = grad_density * density
        moment0 = jnp.sum(weight, axis=0, keepdims=True)
        weight = weight * distance
        moment1 = jnp.sum(weight, axis=0, keepdims=True)
        moment2 = jnp.sum(weight * distance, axis=0, keepdims=True)
        inverse = 1.0 / variance
        grad_variance = 0.5 * inverse * (moment2 * inverse - moment0)
        centre_grads.append(-moment1 * inverse * centre * (1.0 - centre))
        spread_grads.append(grad_variance * 2.0 * spread * spread_scale / (1.0 + jnp.exp(-raw)))
    gmem_ref[...] = (grad_mems[0] + grad_mems[1]).astype(BF16)
    logit_grads = jnp.concatenate(centre_grads + spread_grads + [jnp.zeros((4, READ), F32)], axis=0)
    sums = one_split(nn, logit_grads, scaled)
    centre_sum = jnp.where(lane_head == 0, sums[0:1, :], sums[1:2, :])
    spread_sum = jnp.where(lane_head == 0, sums[2:3, :], sums[3:4, :])
    sums_ref[...] = jnp.concatenate([centre_sum, spread_sum, jnp.zeros((6, PART), F32)], axis=0)
    more_ref[...] = both_split(tn, rows, logit_grads)


FEW = pl.BlockSpec((8, PART), lambda i: (0, i))


def memory_read_back_call(lengths, carried, projected, mem_values, reads, grad_heads, after=()):
    near = pl.BlockSpec((READ, PART), lambda i: (0, i))
    return call(
        memory_read_back_kernel,
        [shape_of((D, READ), F32), shape_of((N, D)), shape_of((8, D), F32)],
        [SMEM, SMEM, near, pair_block(), FEW, near],
        [pl.BlockSpec((PART, READ), lambda i: (i, 0)), pair_block(), FEW],
        flops=FLOPS["memory_read_back"],
        grid=(PAIRS,),
        after=after,
    )(lengths, carried, projected, mem_values, reads, grad_heads)


def attend_back_call(lengths, carried, projected, lse, grad_heads, more, first, count, after=()):
    def pair(shift):
        return pl.BlockSpec((512, PART), lambda i: (0, i + shift))

    return call(
        attend_back_kernel,
        [shape_of((512, count * PART))] * 3,
        [SMEM, SMEM, pair(first), pair(first + PAIRS), pair(first + 2 * PAIRS),
         pl.BlockSpec((8, 512), lambda i: (i + first, 0)), pair(first), pl.BlockSpec((PART, READ), lambda i: (i + first, 0))],
        [pair(0)] * 3,
        [pltpu.VMEM((512, 512), F32)],
        flops=FLOPS["attend_back"],
        grid=(count,),
        after=after,
    )(lengths, carried, projected, projected, projected, lse, grad_heads, more)


GELU_SCALE = 0.7978845608028654
GELU_CUBE = 0.044715


def column_tiles(step_columns):
    return pl.BlockSpec((512, step_columns), lambda t: (0, t))


def fixed(shape):
    return pl.BlockSpec(shape, lambda t: (0,) * len(shape))


def weight_refs(weights, refs):
    found, at = [], 0
    for weight in weights:
        found.append(refs[at : at + len(weight.parts)])
        at += len(weight.parts)
    return found, refs[at:]


def mlp_call(place, tokens, heads, cotangent, vectors, up_bias, out, up, down, target, after=()):
    weights = (out, up, down)
    steps = FF // TILE

    def kernel(place_ref, tokens_ref, heads_ref, cot_ref, vec_ref, bias_ref, *refs):
        sources, refs = weight_refs(weights, refs)
        result_ref, middle_ref, normed_ref, slope_ref = refs[:4]
        grad_refs, (out_ref, up_ref, down_ref, total_ref, staged_ref, sems) = refs[4 : 4 + len(target.shapes)], refs[4 + len(target.shapes) :]
        held = (out_ref, up_ref, down_ref)
        step = pl.program_id(0)

        @pl.when(step == 0)
        def _():
            copies = [w.fetch(s, place_ref, h, sems.at[n]) for n, (w, s, h) in enumerate(zip(weights, sources, held))]
            wait_all(copies[0])
            middle = tokens_ref[0].astype(F32) + nn(heads_ref[...], out_ref[...]) + vec_ref[4:5, :]
            middle_ref[...] = middle
            normed_ref[...] = normalise(middle, vec_ref[5:6, :], vec_ref[6:7, :]).astype(BF16)
            total_ref[...] = middle + vec_ref[7:8, :]
            wait_all(copies[1])
            wait_all(copies[2])

        at = aligned(step, TILE)
        hidden = nn(normed_ref[...], up_ref[:, at]) + bias_ref[0:1, :]
        square = hidden * hidden
        bent = jnp.tanh(GELU_SCALE * hidden * (1.0 + GELU_CUBE * square))
        half = 0.5 + 0.5 * bent
        active = (hidden * half).astype(BF16)
        slope_ref[...] = half + 0.5 * hidden * (1.0 - bent * bent) * (GELU_SCALE + 3.0 * GELU_SCALE * GELU_CUBE * square)
        total_ref[...] += nn(active, down_ref[at, :])
        grad = tn(active, cot_ref[0]).astype(BF16)
        for n in range(steps):
            pl.when(step == n)(lambda n=n: target.tile_put(n, grad, staged_ref, grad_refs, place_ref, sems))

        @pl.when(step == steps - 1)
        def _():
            result_ref[0] = total_ref[...].astype(BF16)
            target.tile_wait(staged_ref, grad_refs, sems)

    found = call(
        kernel,
        [shape_of((1, 512, D)), shape_of((512, D), F32), shape_of((512, D)), shape_of((512, FF), F32)] + target.shapes,
        [SMEM, fixed((1, 512, D)), fixed((512, D)), fixed((1, 512, D)), fixed((16, D)), pl.BlockSpec((8, TILE), lambda t: (0, t))]
        + [HBM] * sum(len(w.parts) for w in weights),
        [fixed((1, 512, D)), fixed((512, D)), fixed((512, D)), column_tiles(TILE)] + [HBM] * len(target.shapes),
        [
            pltpu.VMEM((D, D), BF16),
            pltpu.VMEM((D, FF), BF16),
            pltpu.VMEM((FF, D), BF16),
            pltpu.VMEM((512, D), F32),
            pltpu.VMEM((FF, D), BF16),
            pltpu.SemaphoreType.DMA((4,)),
        ],
        flops=FLOPS["mlp"],
        vmem=44,
        after=after,
        grid=(steps,),
    )(place, tokens, heads, cotangent, vectors, up_bias, *out.parts, *up.parts, *down.parts)
    return found[:4], found[4:]


class DownTarget:
    def __init__(self, blocks):
        self.blocks = blocks
        self.shapes = blocks.shapes if blocks else [shape_of((FF, D))]

    def pieces(self):
        rows, half = self.blocks.rows, self.blocks.columns // 4
        return [((4 * rows, half), (q * rows, 0), q * half, half) for q in range(4)]

    def tile_put(self, n, grad, staged, refs, place_ref, sems):
        rows = pl.ds(n * TILE, TILE)
        staged[rows, :] = grad
        if self.blocks:
            self.blocks.put(staged.at[rows, :], refs, place_ref, sems.at[3], self.pieces(), dps=range(4 * n, 4 * n + 4))

    def tile_wait(self, staged, refs, sems):
        if self.blocks:
            self.blocks.wait(staged, refs, sems.at[3], self.pieces())
        else:
            start(staged, refs[0], sems.at[3]).wait()


class UpTarget:
    def __init__(self, blocks):
        self.blocks = blocks
        self.shapes = blocks.shapes if blocks else [shape_of((D, 2 * TILE))]

    def pieces(self):
        return [((self.blocks.rows, 0), (0, 0), 0, TILE)]

    def tile_put(self, n, grad, staged, refs, place_ref, sems):
        staged[:, n * TILE : (n + 1) * TILE] = grad
        if self.blocks:
            tile = staged.at[:, pl.ds(n * TILE, TILE)]
            self.blocks.put(tile, refs, place_ref, sems.at[3], self.pieces(), sides=(n,))

    def tile_wait(self, staged, refs, sems):
        if self.blocks:
            self.blocks.wait(staged, refs, sems.at[3], self.pieces())
        else:
            start(staged, refs[0], sems.at[3]).wait()


def mlp_back_call(place, cotangent, slope, normed, up, down, target, part, before=None, after=()):
    weights = (up, down)
    earlier = [] if before is None else [before]
    steps = 2

    def tile(t):
        return part + 2 * t

    def kernel(place_ref, cot_ref, slope_ref, normed_ref, *refs):
        before_refs, refs = refs[: len(earlier)], refs[len(earlier) :]
        sources, refs = weight_refs(weights, refs)
        total_ref, bias_ref = refs[:2]
        grad_refs, (up_ref, down_ref, staged_ref, sems) = refs[2 : 2 + len(target.shapes)], refs[2 + len(target.shapes) :]
        step = pl.program_id(0)

        @pl.when(step == 0)
        def _():
            copies = [w.fetch(s, place_ref, h, sems.at[n]) for n, (w, s, h) in enumerate(zip(weights, sources, (up_ref, down_ref)))]
            total_ref[...] = before_refs[0][...] if before_refs else jnp.zeros((512, D), F32)
            wait_all(copies[1])
            wait_all(copies[0])

        at = aligned(tile(step), TILE)
        grad_hidden = (nt(cot_ref[0], down_ref[at, :]) * slope_ref[...]).astype(BF16)
        bias_ref[...] = jnp.broadcast_to(jnp.sum(grad_hidden.astype(F32), axis=0, keepdims=True), (8, TILE))
        total_ref[...] += nt(grad_hidden, up_ref[:, at])
        grad = tn(normed_ref[...], grad_hidden).astype(BF16)
        for n in range(steps):
            pl.when(step == n)(lambda n=n: target.tile_put(n, grad, staged_ref, grad_refs, place_ref, sems))
        pl.when(step == steps - 1)(lambda: target.tile_wait(staged_ref, grad_refs, sems))

    found = call(
        kernel,
        [shape_of((512, D), F32), shape_of((8, 2 * TILE), F32)] + target.shapes,
        [SMEM, fixed((1, 512, D)), pl.BlockSpec((512, TILE), lambda t: (0, tile(t))), fixed((512, D))]
        + [fixed((512, D))] * len(earlier)
        + [HBM] * sum(len(w.parts) for w in weights),
        [fixed((512, D)), pl.BlockSpec((8, TILE), lambda t: (0, t))] + [HBM] * len(target.shapes),
        [
            pltpu.VMEM((D, FF), BF16),
            pltpu.VMEM((FF, D), BF16),
            pltpu.VMEM((D, 2 * TILE), BF16),
            pltpu.SemaphoreType.DMA((4,)),
        ],
        flops=FLOPS["mlp_back"],
        vmem=32,
        grid=(steps,),
        after=after,
    )(place, cotangent, slope, normed, *earlier, *up.parts, *down.parts)
    return found[:2], found[2:]


def middle_back_call(place, cotangent, middle, grad_normed, vectors, heads, out, after=()):
    def kernel(place_ref, cot_ref, middle_ref, grad_ref, vec_ref, heads_ref, *refs):
        sources, refs = weight_refs((out,), refs)
        grad_middle_ref, grad_heads_ref, out_grad_ref, sums_ref, out_ref, sem = refs
        copies = out.fetch(sources[0], place_ref, out_ref, sem)
        cot = cot_ref[0].astype(F32)
        back, gain, shift = normalise_back(middle_ref[...], vec_ref[5:6, :], grad_ref[...])
        grad_middle = cot + back
        grad_middle_ref[...] = grad_middle
        attended = grad_middle.astype(BF16)
        bias = jnp.sum(attended.astype(F32), axis=0, keepdims=True)
        last = jnp.sum(cot, axis=0, keepdims=True)
        nothing = jnp.zeros((4, D), F32)
        sums_ref[...] = jnp.concatenate([nothing, bias, gain, shift, last, nothing, nothing], axis=0)
        wait_all(copies)
        grad_heads_ref[...] = nt(attended, out_ref[...]).astype(BF16)
        out_grad_ref[...] = tn(heads_ref[...], attended).astype(BF16)

    return call(
        kernel,
        [shape_of((512, D), F32), shape_of((512, D)), shape_of((D, D)), shape_of((16, D), F32)],
        [SMEM] + [VMEM] * 5 + [HBM] * len(out.parts),
        [VMEM] * 4,
        [pltpu.VMEM((D, D), BF16), pltpu.SemaphoreType.DMA],
        flops=FLOPS["middle_back"],
        vmem=20,
        after=after,
    )(place, cotangent, middle, grad_normed, vectors, heads, *out.parts)


def memory_back_call(place, coeff, grad_mem_values, tables, sums, out_grad, keys, blocks, after=()):
    shapes = blocks.shapes if blocks else [shape_of((D, D))] * 3

    def kernel(place_ref, coeff_ref, grad_values_ref, table_ref, sums_ref, out_grad_ref, *refs):
        sources, refs = weight_refs((keys,), refs)
        tables_ref = refs[0]
        grad_refs, (keys_ref, key_grad_ref, value_grad_ref, sems) = refs[1 : 1 + len(shapes)], refs[1 + len(shapes) :]
        copies = keys.fetch(sources[0], place_ref, keys_ref, sems.at[0])
        staged = (out_grad_ref, key_grad_ref, value_grad_ref)

        def pieces(n):
            return [((blocks.rows, D // 2), (0, 0), n * (D // 2), D // 2)]

        def put(n):
            if blocks:
                blocks.put(staged[n], grad_refs, place_ref, sems.at[1 + n], pieces(n))
            else:
                start(staged[n], grad_refs[n], sems.at[1 + n])

        put(0)
        value_grad_ref[...] = tn(coeff_ref[...], grad_values_ref[...]).astype(BF16)
        put(2)
        head, kind = iota((32, D), 1) // DH, iota((32, D), 0)
        by_head = jnp.where(kind == head, sums_ref[0:1, :], jnp.where(kind == head + H, sums_ref[1:2, :], 0.0))
        summary = tn(coeff_ref[...], table_ref[...])[:, :32]
        key_grad_ref[...] = both_split(nn, summary, by_head).astype(BF16)
        put(1)
        wait_all(copies)
        high, low = split(by_head)
        wide = jnp.concatenate([high, low, jnp.zeros((PART - 64, D), BF16)], axis=0)
        reads = nt(keys_ref[...], wide)
        high, low = split(reads)
        found = nn(coeff_ref[...], high) + nn(coeff_ref[...], low)
        lane = iota((N, PART), 1)
        found = found + jnp.concatenate([found[:, 32:64], jnp.zeros((N, PART - 32), F32)], axis=1)
        tables_ref[...] = jnp.where(lane < 2 * H, found, 0.0)
        for n in range(3):
            if blocks:
                blocks.wait(staged[n], grad_refs, sems.at[1 + n], pieces(n))
            else:
                pltpu.make_async_copy(staged[n], grad_refs[n], sems.at[1 + n]).wait()

    found = call(
        kernel,
        [shape_of((N, PART), F32)] + shapes,
        [SMEM] + [VMEM] * 5 + [HBM] * len(keys.parts),
        [VMEM] + [HBM] * len(shapes),
        [pltpu.VMEM((D, D), BF16)] * 3 + [pltpu.SemaphoreType.DMA((4,))],
        flops=FLOPS["memory_back"],
        vmem=20,
        after=after,
    )(place, coeff, grad_mem_values, tables, sums, out_grad, *keys.parts)
    return found[0], found[1:]


def input_back_call(place, tokens, vectors, normed, grads, grad_middle, sums, up_bias_grad, tables, proj, blocks, after=()):
    shapes = blocks[0].shapes if blocks else [shape_of((D, 3 * D)), shape_of((16, D), F32)]

    def kernel(place_ref, tokens_ref, vec_ref, normed_ref, middle_ref, sums_ref, up_ref, table_ref, *refs):
        parts, refs = refs[: len(grads)], refs[len(grads) :]
        sources, refs = weight_refs((proj,), refs)
        result_ref = refs[0]
        grad_refs, (proj_ref, staged_ref, small_ref, sems) = refs[1 : 1 + len(shapes)], refs[1 + len(shapes) :]
        copies = proj.fetch(sources[0], place_ref, proj_ref, sems.at[0])
        at = 0
        for part in parts:
            columns = part.shape[1]
            staged_ref[:, at : at + columns] = tn(normed_ref[...], part[...]).astype(BF16)
            at += columns
        if blocks:
            rows, side = blocks[0].rows, 3 * D // 2
            half = blocks[0].columns // 2
            pieces = [((rows, side), (0, 0), 0, half), ((rows, side), (0, half), half, side - half)]
            for block, piece in zip(blocks, pieces):
                block.put(staged_ref, grad_refs, place_ref, sems.at[1], [piece])
        else:
            start(staged_ref, grad_refs[0], sems.at[1])
        wait_all(copies)
        grad_normed, column_sums, at = jnp.zeros((512, D), F32), [], 0
        for part in parts:
            columns = part.shape[1]
            grad_normed = grad_normed + nt(part[...], proj_ref[:, at : at + columns])
            column_sums.append(jnp.sum(part[...].astype(F32), axis=0, keepdims=True))
            at += columns
        column_sums = jnp.concatenate(column_sums, axis=1)
        back, gain, shift = normalise_back(tokens_ref[0].astype(F32), vec_ref[0:1, :], grad_normed)
        result_ref[0] = middle_ref[...] + back
        vectors_grad = jnp.concatenate([gain, shift, column_sums[:, :D], column_sums[:, 2 * D :], sums_ref[4:16, :]], axis=0)
        if blocks:
            small_ref[...] = pack_vectors(vectors_grad, up_ref[...], table_ref[...]).reshape(32 * rows, PART)

            def send(core_here):
                for n, m, where in blocks[1]._each(grad_refs, place_ref, core_here, range(16), (0, 1)):
                    source = small_ref.at[pl.ds((2 * n + m) * rows, rows), :]
                    start(source, where.at[:, pl.ds(side, PART)], sems.at[2])

            pl.when(place_ref[2] == 0)(lambda: send(0))
            pl.when(place_ref[2] == 1)(lambda: send(1))
            for block, piece in zip(blocks, pieces):
                block.wait(staged_ref, grad_refs, sems.at[1], [piece])
            blocks[1].wait(small_ref, grad_refs, sems.at[2], [((rows, 0), (0, 0), side, PART)])
        else:
            small_ref[...] = jnp.zeros(small_ref.shape, BF16)
            grad_refs[1][...] = vectors_grad
            pltpu.make_async_copy(staged_ref, grad_refs[0], sems.at[1]).wait()

    found = call(
        kernel,
        [shape_of((1, 512, D), F32)] + shapes,
        [SMEM] + [VMEM] * (7 + len(grads)) + [HBM] * len(proj.parts),
        [VMEM] + ([HBM] * 2 if blocks else [HBM, VMEM]),
        [
            pltpu.VMEM((D, 3 * D), BF16),
            pltpu.VMEM((D, 3 * D), BF16),
            pltpu.VMEM((32 * 48, PART), BF16),
            pltpu.SemaphoreType.DMA((3,)),
        ],
        flops=FLOPS["input_back"],
        vmem=36,
        after=after,
    )(place, tokens, vectors, normed, grad_middle, sums, up_bias_grad, tables, *grads, *proj.parts)
    return found[0], found[1:]


def hop(value, z=0, x=0, core=0, f=0):
    pairs = []
    for dp in range(16):
        for side in range(2):
            other = (((dp // 4) ^ z) * 4) + ((((dp // 2) % 2) ^ x) * 2) + ((dp % 2) ^ core)
            pairs.append((dp * 2 + side, other * 2 + (side ^ f)))
    return lax.ppermute(value, BOTH, pairs)


def z_hops(block):
    return [block] + [hop(block, z=k) for k in (1, 2, 3)]


def quads(pieces, cut, after):
    rows, columns = pieces[0].shape

    def kernel(*refs):
        blocks, (left, right) = refs[:4], refs[4:]
        for k, block in enumerate(blocks):
            left[k] = block[:, :cut]
            right[k] = block[:, cut:]

    shapes = [shape_of((4, rows, cut)), shape_of((4, rows, columns - cut))]
    return list(call(kernel, shapes, [VMEM] * 4, [VMEM] * 2, flops=FLOPS["pack"], after=after)(*pieces))


BITS = (dict(x=1), dict(f=1))


def joined(quads_here, nears, after):
    def kernel(*refs):
        for n in (0, 1):
            for m in (0, 1):
                refs[4 + n][pl.ds(4 * m, 4)] = refs[2 * m + n][...]

    shapes = [shape_of((8,) + quad.shape[1:]) for quad in quads_here]
    return list(call(kernel, shapes, [VMEM] * 4, [VMEM] * 2, flops=FLOPS["pack"], after=after)(*quads_here, *nears))


def side_by_side(arrays, after):
    widths = [array.shape[2] for array in arrays]

    def kernel(*refs):
        at = 0
        for ref, width in zip(refs, widths):
            refs[-1][:, :, at : at + width] = ref[...]
            at += width

    shape = shape_of(arrays[0].shape[:2] + (sum(widths),))
    return call(kernel, shape, [VMEM] * len(arrays), VMEM, flops=FLOPS["pack"], after=after)(*arrays)


def core_hops(mine):
    return mine + [hop(part, core=1) for part in mine]


def plus(a, b):
    return (a.astype(F32) + b.astype(F32)).astype(BF16)


def halves(kept, got):
    return plus(kept[1], got[1]), plus(kept[0], got[0])


def halves_after(pairs, after):
    widths = [kept.shape[-1] for kept, _ in pairs]

    def kernel(*refs):
        for bit, target in ((1, refs[-2]), (0, refs[-1])):
            at = 0
            for n, width in enumerate(widths):
                total = refs[2 * n][bit].astype(F32) + refs[2 * n + 1][bit].astype(F32)
                target[..., at : at + width] = total.astype(BF16)
                at += width

    shapes = [shape_of(pairs[0][0].shape[1:-1] + (sum(widths),))] * 2
    flat = [array for pair in pairs for array in pair]
    return call(kernel, shapes, [VMEM] * len(flat), [VMEM] * 2, flops=FLOPS["add"], after=after)(*flat)


def added(pairs, after=()):
    rows, columns = pairs[0][0].shape[1], [kept.shape[2] for kept, _ in pairs]

    def kernel(*refs):
        sent, own = refs[-2:]
        at = 0
        for n, width in enumerate(columns):
            kept, got = refs[2 * n], refs[2 * n + 1]
            for k in range(4):
                total = kept[k].astype(F32) + got[k].astype(F32)
                if k < 2:
                    own[k, :, at : at + width] = total
                else:
                    sent[k - 2, :, at : at + width] = total.astype(BF16)
            at += width

    shapes = [shape_of((2, rows, sum(columns))), shape_of((2, rows, sum(columns)), F32)]
    flat = [array for pair in pairs for array in pair]
    return call(kernel, shapes, [VMEM] * len(flat), [VMEM] * 2, flops=FLOPS["add"], after=after)(*flat)


def between(own, got, after=()):
    def kernel(own_ref, got_ref, sent_ref, total_ref):
        total_ref[...] = own_ref[0] + got_ref[0].astype(F32)
        sent_ref[...] = (own_ref[1] + got_ref[1].astype(F32)).astype(BF16)

    shapes = [shape_of(own.shape[1:]), shape_of(own.shape[1:], F32)]
    return call(kernel, shapes, [VMEM] * 2, [VMEM] * 2, flops=FLOPS["add"], after=after)(own, got)


def cut_halves(kept, got, cut, after=()):
    def kernel(kept_ref, got_ref, *refs):
        for n, columns in enumerate((slice(0, cut), slice(cut, None))):
            for bit, target in ((1, refs[n]), (0, refs[2 + n])):
                total = kept_ref[bit, :, :, :, columns].astype(F32) + got_ref[bit, :, :, :, columns].astype(F32)
                target[...] = total.astype(BF16)

    shapes = [shape_of(kept.shape[1:4] + (width,)) for width in (cut, kept.shape[4] - cut)] * 2
    found = call(kernel, shapes, [VMEM] * 2, [VMEM] * 4, flops=FLOPS["add"], after=after)(kept, got)
    return found[:2], found[2:]


def three_ways(pairs, after=()):
    rows, columns = pairs[0][0].shape[1], [kept.shape[2] for kept, _ in pairs]

    def kernel(*refs):
        targets = refs[-4:]
        at = 0
        for n, width in enumerate(columns):
            for k in range(4):
                total = refs[2 * n][k].astype(F32) + refs[2 * n + 1][k].astype(F32)
                targets[k][:, at : at + width] = total.astype(targets[k].dtype)
            at += width

    shapes = [shape_of((rows, sum(columns)), F32)] + [shape_of((rows, sum(columns)))] * 3
    flat = [array for pair in pairs for array in pair]
    return call(kernel, shapes, [VMEM] * len(flat), [VMEM] * 4, flops=FLOPS["add"], after=after)(*flat)


COLUMN_SPLIT = (2, 5, 7, 8, 13, 15)
VECTORS = (0, 1, 3, 4, 6, 11, 12, 16)


def gather_whole(shards):
    def whole(k, shard):
        near = lax.all_gather(shard, "fsdp", axis=1 if k in COLUMN_SPLIT else 0, tiled=True)
        return lax.all_gather(near, "dp", axis=0, tiled=True)

    found = [whole(k, shard) for k, shard in enumerate(shards)]
    vectors = jnp.stack([found[k].astype(F32) for k in VECTORS] + [jnp.zeros((D,), F32)] * 8)
    up_bias = jnp.broadcast_to(found[14].astype(F32)[None], (8, FF))
    tables = jnp.pad(jnp.concatenate([found[9], found[10]], axis=1), ((0, 0), (0, PART - 2 * H)))
    weights = {k: Whole(found[k]) for k in COLUMN_SPLIT}
    return weights, vectors, up_bias, tables


def scatter_whole(totals):
    def part(k, total):
        near = lax.psum_scatter(total.astype(BF16), "dp", scatter_dimension=0, tiled=True)
        return lax.psum_scatter(near, "fsdp", scatter_dimension=1 if k in COLUMN_SPLIT else 0, tiled=True).astype(F32)

    return [part(k, total) for k, total in enumerate(totals)]


def pack_early(shards):
    order = [2, 7, 8, 9, 10, 14] + list(VECTORS)
    arrays = [shards[k] if shards[k].ndim == 2 else shards[k].reshape(1, -1) for k in order]
    rows, half = shards[5].shape

    def kernel(proj, keys, values, centre, spread, up_bias, *refs):
        vectors, early = refs[:-1], refs[-1]
        early[:, : 3 * half] = proj[...]
        early[:, 3 * half : 4 * half] = keys[...]
        early[:, 4 * half : 5 * half] = values[...]
        lines = []
        for ref in list(vectors) + [up_bias]:
            line = ref[...].astype(F32)
            lines.append(jnp.concatenate([line, jnp.zeros((1, PART - line.shape[1]), F32)], axis=1))
        lines.append(jnp.zeros((16 - len(lines), PART), F32))
        tables = jnp.concatenate(
            [centre[...].astype(F32), spread[...].astype(F32), jnp.zeros((16, PART - 2 * H), F32)], axis=1
        )
        small = jnp.concatenate(lines + [tables, jnp.zeros((rows - 32, PART), F32)], axis=0)
        early[:, 5 * half :] = small.astype(BF16)

    return call(kernel, shape_of((rows, 5 * half + PART)), [VMEM] * len(arrays), VMEM, flops=FLOPS["pack"], vmem=56)(*arrays)


def pack_late(shards, after):
    rows, half = shards[5].shape

    def kernel(out, up, down, late):
        late[:, : 4 * half] = up[...]
        for q in range(4):
            late[:, (4 + q) * half : (5 + q) * half] = down[q * rows : (q + 1) * rows, :]
        late[:, 8 * half :] = out[...]

    return call(kernel, shape_of((rows, 9 * half)), [VMEM] * 3, VMEM, flops=FLOPS["pack"], after=after)(
        shards[5], shards[13], shards[15]
    )


def local(
    mesh_sizes, tokens, context, past_coeffs, doc_lengths, carried, histogram, cotangent, *shards
):
    hops = mesh_sizes == (16, 2)
    dp = lax.axis_index("dp")
    place = jnp.stack([dp // 4, (dp // 2) % 2, dp % 2, lax.axis_index("fsdp")]).astype(jnp.int32)
    rows, half = shards[5].shape
    x_hop, f_hop = BITS
    if hops:
        early = z_hops(pack_early(shards))
        points, gram, right = memory_system(histogram, past_coeffs, context, after=[early[0]])
        early = quads(early, 3 * half, [gram])
        near = [hop(early[0], **x_hop), hop(early[1], **f_hop)]
        steps = [eliminate((gram, right), early)]
        late = z_hops(pack_late(shards, [steps[0][0]]))
        early = joined(early, near, [steps[0][0]])
        far = [hop(early[0], **f_hop), hop(early[1], **x_hop)]
        steps.append(eliminate(steps[0][2:], early))
        late = quads(late, 4 * half, [steps[1][0]])
        late_near = [hop(late[0], **x_hop), hop(late[1], **f_hop)]
        steps.append(eliminate(steps[1][2:], late + far))
        proj_parts, mem_parts = core_hops([early[0], far[0]]), core_hops([early[1], far[1]])
        late = joined(late, late_near, [steps[2][0]])
        late_far = [hop(late[0], **f_hop), hop(late[1], **x_hop)]
        steps.append(eliminate(steps[2][2:], proj_parts[2:] + mem_parts[2:] + late))
        late_core = [hop(part, core=1) for part in late]
        coeff = substitute(steps)
        vectors, up_bias, tables = gathered_vectors(place, mem_parts)
        weights = {
            2: Hops(proj_parts, True, 0, 3 * half),
            7: Hops(mem_parts, False, 0, half),
            8: Hops(mem_parts, False, half, half),
        }
    else:
        weights, vectors, up_bias, tables = gather_whole(shards)
        points, *system = memory_system(histogram, past_coeffs, context)
        steps = [eliminate(system)]
        while len(steps) < N // PART:
            steps.append(eliminate(steps[-1][2:]))
        coeff = substitute(steps)
    normed, projected, mem_values, reads = front_call(
        place, tokens, vectors, coeff, tables, weights[2], weights[7], weights[8]
    )
    heads, lse = attend_call(doc_lengths, carried, projected, mem_values, reads)
    if hops:
        far_core = hop(side_by_side(late_far, [heads]), core=1)
        up_parts = [late[0], late_far[0], late_core[0], far_core]
        others = [late[1], late_far[1], late_core[1], far_core]
        weights[13] = Hops(up_parts, True, 0, 4 * half)
        weights[15] = Hops(others, False, [0, 0, 0, 4 * half], half, 4)
        weights[5] = Hops(others, False, [4 * half] * 3 + [8 * half], half)
    down_blocks = Blocks(False, rows, 4 * half) if hops else None
    (result, middle, normed_mlp, slope), down_grad = mlp_call(
        place, tokens, heads, cotangent, vectors, up_bias, weights[5], weights[13], weights[15], DownTarget(down_blocks)
    )
    up_blocks = Blocks(True, rows, 2 * half) if hops else None
    waits = {"again": [], "read": [], "second": [], "input": []}
    (grad_normed_mlp, up_bias_first), up_first = mlp_back_call(
        place, cotangent, slope, normed_mlp, weights[13], weights[15], UpTarget(up_blocks), 0
    )
    if hops:
        sent_down, kept_down = halves(down_grad[0], hop(down_grad[1], core=1))
        waits["again"] = [sent_down]
        got_down = hop(sent_down, **f_hop)
    (grad_normed_mlp, up_bias_second), up_second = mlp_back_call(
        place, cotangent, slope, normed_mlp, weights[13], weights[15], UpTarget(up_blocks), 1, grad_normed_mlp,
        after=waits["again"],
    )
    grad_middle, grad_heads, grad_out, sums = middle_back_call(
        place, cotangent, middle, grad_normed_mlp, vectors, heads, weights[5]
    )
    if hops:
        got_first, got_second = hop(up_first[1], core=1), hop(up_second[1], core=1)
        sent_up, kept_up = halves_after([(up_first[0], got_first), (up_second[0], got_second)], [grad_middle])
        waits["read"] = [sent_up]
        got_up = hop(sent_up, **x_hop)
    more, grad_mem, read_sums = memory_read_back_call(
        doc_lengths, carried, projected, mem_values, reads, grad_heads, after=waits["read"]
    )
    mem_blocks = Blocks(True, rows, 3 * half) if hops else None
    grad_tables, mem_grad = memory_back_call(
        place, coeff, grad_mem, tables, read_sums, grad_out, weights[7], mem_blocks
    )
    first = attend_back_call(doc_lengths, carried, projected, lse, grad_heads, more, 0, PAIRS // 2, after=[grad_tables])
    if hops:
        got_mem = hop(mem_grad[1], core=1)
        sent_down, kept_down = halves_after([(kept_down, got_down)], list(first[:1]))
        got_down = hop(sent_down, **x_hop)
        sent_up, kept_up = halves_after([(kept_up, got_up)], [sent_down])
        got_up = hop(sent_up, **f_hop)
        sent_mem, kept_mem = halves_after([(mem_grad[0], got_mem)], [sent_up])
        waits["second"] = [sent_mem, sent_up]
        got_mem = hop(sent_mem, **x_hop)
    second = attend_back_call(
        doc_lengths, carried, projected, lse, grad_heads, more, PAIRS // 2, PAIRS // 2, after=waits["second"]
    )
    if hops:
        sent_down, own_down = added([(kept_down, got_down)], list(second[:1]))
        got_down = hop(sent_down, z=2)
        sent_up, own_up = added([(kept_up, got_up)], [sent_down])
        waits["input"] = [sent_up]
        got_up = hop(sent_up, z=2)
    grad_up_bias = [part[:, n * TILE : (n + 1) * TILE] for n in (0, 1) for part in (up_bias_first, up_bias_second)]
    grad_up_bias = jnp.concatenate(grad_up_bias, axis=1)
    grads = [part for pair in zip(first, second) for part in pair]
    width = 3 * half + PART
    proj_blocks = [Blocks(x_first, rows, width) for x_first in (True, False)] if hops else None
    grad_tokens, proj_grad = input_back_call(
        place, tokens, vectors, normed, grads, grad_middle, sums, grad_up_bias, grad_tables, weights[2], proj_blocks,
        after=waits["input"],
    )
    if hops:
        got = hop(proj_grad[1], core=1)
        sent_mem, kept_mem = halves_after([(kept_mem, got_mem)], [grad_tokens])
        got_mem = hop(sent_mem, **f_hop)
        cut = width // 2
        sent, kept = cut_halves(proj_grad[0], got, cut, [sent_mem])
        got = [hop(sent[0], **x_hop), hop(sent[1], **f_hop)]
        sent, own_down = between(own_down, got_down, list(sent))
        got_down = hop(sent, z=1)
        pairs = [halves_after([(k, g)], [sent]) for k, g in zip(kept, got)]
        got = [hop(pairs[0][0], **f_hop), hop(pairs[1][0], **x_hop)]
        sent, own_mem = added([(kept_mem, got_mem)], [pairs[0][0], pairs[1][0]])
        got_mem = hop(sent, z=2)
        sent, own_up = between(own_up, got_up, [sent])
        got_up = hop(sent, z=1)
        own, *sents = three_ways([(pairs[0][1], got[0]), (pairs[1][1], got[1])], [sent])
        more = [hop(sent, z=k) for k, sent in zip((1, 2, 3), sents)]
        sent, own_mem = between(own_mem, got_mem, sents)
        got_mem = hop(sent, z=1)
        down = own_down + got_down.astype(F32)
        mem_done = own_mem + got_mem.astype(F32)
        late_done = own + more[0].astype(F32) + more[1].astype(F32) + more[2].astype(F32)
        down = jnp.concatenate([down[:, q * half : (q + 1) * half] for q in range(4)], axis=0)
        summed = {15: down, 13: own_up + got_up.astype(F32)}
        for n, k in enumerate((5, 7, 8)):
            summed[k] = mem_done[:, n * half : (n + 1) * half]
        summed[2] = late_done[:, : 3 * half]
        small = late_done[:, 3 * half :]
        for n, k in enumerate(VECTORS):
            summed[k] = small[n, : shards[k].shape[0]]
        summed[14] = small[8, : shards[14].shape[0]]
        summed[9], summed[10] = small[16:32, :H], small[16:32, H : 2 * H]
    else:
        up_grad = [part[0][:, n * TILE : (n + 1) * TILE] for n in (0, 1) for part in (up_first, up_second)]
        totals = {13: jnp.concatenate(up_grad, axis=1), 15: down_grad[0], 2: proj_grad[0], 14: grad_up_bias[0]}
        totals[5], totals[7], totals[8] = mem_grad
        totals[9], totals[10] = grad_tables[:, :H], grad_tables[:, H : 2 * H]
        for n, k in enumerate(VECTORS):
            totals[k] = proj_grad[1][n]
        summed = scatter_whole([totals[k] for k in range(17)])
    return (result, grad_tokens, *(summed[k] for k in range(17)), points)


def solution(mesh):
    both, row, table = P(BOTH), P("dp", "fsdp"), P(BOTH, None)
    block = P(BOTH, None, None)
    weights = (
        both, both, row, both, both, row, both, row, row, table, table, both, both, row, both, row, both,
    )
    in_specs = (block, block, block, table, both, table, block) + weights
    out_specs = (block, block) + weights + (table,)
    sizes = (mesh.shape["dp"], mesh.shape["fsdp"])
    return jax.shard_map(
        functools.partial(local, sizes), mesh=mesh, in_specs=in_specs, out_specs=out_specs, check_vma=False
    )
```

```python
import functools

import jax
import jax.numpy as jnp
from jax import lax
from jax.experimental import pallas as pl
from jax.experimental.pallas import tpu as pltpu
from jax.sharding import PartitionSpec as P

H = 12
DH = 64
D = H * DH
N = 512
CTX = 1024
M = 512
NBINS = 64
FF = 4 * D
PAIRS = H // 2
PART = 128
TILE = 768

memory_tau = 0.75
ridge_weight = 1.0
norm_epsilon = 1e-05
spread_scale = 0.25
masked_fill = -1e30
score_scale = DH ** (-0.5)

F32, BF16 = jnp.float32, jnp.bfloat16
MIB = 1024 * 1024
BOTH = ("dp", "fsdp")
HBM = pl.BlockSpec(memory_space=pl.ANY)
SMEM = pl.BlockSpec(memory_space=pltpu.SMEM)
VMEM = pl.BlockSpec(memory_space=pltpu.VMEM)


FLOPS = {
    "pack": 1, "system": 8, "eliminate": 5, "substitute": 2, "vectors": 2, "front": 7, "attend": 14, "mlp": 26,
    "middle_back": 4, "memory_read_back": 7, "memory_back": 7, "attend_back": 7, "input_back": 11,
    "add": 10,
}
FLOPS = {name: work * 20000_000_000 for name, work in FLOPS.items()}


def shape_of(shape, dtype=BF16):
    return jax.ShapeDtypeStruct(shape, dtype)


def call(kernel, out_shape, in_specs, out_specs, scratch=(), flops=0, grid=None, after=(), vmem=20):
    extra = {} if grid is None else {"grid": grid}
    inputs, unread = len(in_specs), len(after)

    def body(*refs):
        kernel(*refs[:inputs], *refs[inputs + unread :])

    run = pl.pallas_call(
        body,
        out_shape=out_shape,
        in_specs=list(in_specs) + [HBM] * unread,
        out_specs=out_specs,
        scratch_shapes=list(scratch),
        compiler_params=pltpu.CompilerParams(vmem_limit_bytes=vmem * MIB),
        cost_estimate=pl.CostEstimate(flops=flops, bytes_accessed=0, transcendentals=0),
        **extra,
    )
    return lambda *operands: run(*operands, *after)


def nn(a, b):
    return lax.dot_general(a, b, (((1,), (0,)), ((), ())), preferred_element_type=F32)


def nt(a, b):
    return lax.dot_general(a, b, (((1,), (1,)), ((), ())), preferred_element_type=F32)


def tn(a, b):
    return lax.dot_general(a, b, (((0,), (0,)), ((), ())), preferred_element_type=F32)


def split(value):
    high = value.astype(BF16)
    return high, (value - high.astype(F32)).astype(BF16)


def both_split(product, a, b):
    a_high, a_low = split(a)
    b_high, b_low = split(b)
    return product(a_high, b_high) + (product(a_high, b_low) + product(a_low, b_high))


def one_split(product, a, b):
    a_high, a_low = split(a)
    return product(a_high, b) + product(a_low, b)


def iota(shape, axis):
    return lax.broadcasted_iota(jnp.int32, shape, axis)


def gaussian(points, centres):
    distance = points - centres
    return jnp.exp(-0.5 * distance * distance * (N * N))


def normalise(values, gain, shift):
    mean = jnp.mean(values, axis=-1, keepdims=True)
    centred = values - mean
    variance = jnp.mean(centred * centred, axis=-1, keepdims=True)
    inverse = lax.rsqrt(variance + norm_epsilon)
    return centred * inverse * gain + shift


def normalise_back(values, gain, grad):
    mean = jnp.mean(values, axis=-1, keepdims=True)
    centred = values - mean
    variance = jnp.mean(centred * centred, axis=-1, keepdims=True)
    inverse = lax.rsqrt(variance + norm_epsilon)
    standard = centred * inverse
    scaled = grad * gain
    first = jnp.mean(scaled, axis=-1, keepdims=True)
    second = jnp.mean(scaled * standard, axis=-1, keepdims=True)
    back = inverse * (scaled - first - standard * second)
    return back, jnp.sum(grad * standard, axis=0, keepdims=True), jnp.sum(grad, axis=0, keepdims=True)


def system_kernel(hist_ref, past_ref, context_ref, points_ref, gram_ref, right_ref):
    hist = hist_ref[...]
    counts = jnp.broadcast_to(hist, (NBINS, NBINS))
    row, column = iota((NBINS, NBINS), 0), iota((NBINS, NBINS), 1)

    def down(keep):
        return jnp.sum(jnp.where(keep, counts, 0), axis=1, keepdims=True)

    ends, starts, count = down(column <= row), down(column < row), down(column == row)
    slot = iota((NBINS, M), 1)
    inside = (slot >= starts) & (slot < ends)

    def across(values):
        return jnp.sum(jnp.where(inside, values, 0), axis=0, keepdims=True)

    first, amount, number = across(starts), across(count), across(iota((NBINS, M), 0))
    offset = (iota((1, M), 1) - first).astype(F32) + 0.5
    points = (number.astype(F32) + offset / amount.astype(F32)) / NBINS
    points_ref[...] = points
    upright = jnp.sum(
        jnp.where(iota((M, M), 0) == iota((M, M), 1), points, 0.0), axis=1, keepdims=True
    )
    centre_row = (iota((1, N), 1).astype(F32) + 0.5) / N
    centre_column = (iota((N, 1), 0).astype(F32) + 0.5) / N
    past_values = one_split(nn, gaussian(upright, centre_row), past_ref[0])
    recent = memory_tau + (1.0 - memory_tau) * (iota((1, CTX), 1).astype(F32) + 0.5) / CTX
    old = gaussian(memory_tau * points, centre_column)
    new = gaussian(recent, centre_column)
    right_ref[...] = both_split(nn, old, past_values) + one_split(nn, new, context_ref[0])
    eye = (iota((N, N), 0) == iota((N, N), 1)).astype(F32) * ridge_weight
    gram_ref[...] = both_split(nt, old, old) + both_split(nt, new, new) + eye


def memory_system(histogram, past, context, after=()):
    return call(
        system_kernel,
        [shape_of((1, M), F32), shape_of((N, N), F32), shape_of((N, D), F32)],
        [VMEM] * 3,
        [VMEM] * 3,
        flops=FLOPS["system"],
        vmem=24,
        after=after,
    )(histogram, past, context)


PANEL = 16


def three(value):
    high = value.astype(BF16)
    rest = value - high.astype(F32)
    middle = rest.astype(BF16)
    return high, middle, (rest - middle.astype(F32)).astype(BF16)


def small_inverse(m):
    def minor(r0, r1, c0, c1):
        return m[r0][c0] * m[r1][c1] - m[r0][c1] * m[r1][c0]

    places = ((0, 1), (0, 2), (0, 3), (1, 2), (1, 3), (2, 3))
    s = [minor(0, 1, *place) for place in places]
    c = [minor(2, 3, *place) for place in places]
    total = ((s[0] * c[5] - s[1] * c[4]) + (s[2] * c[3] + s[3] * c[2])) + (s[5] * c[0] - s[4] * c[1])
    r = 1.0 / total
    q = [[None] * 4 for _ in range(4)]
    q[0][0] = (m[1][1] * c[5] - m[1][2] * c[4] + m[1][3] * c[3]) * r
    q[0][1] = (m[0][2] * c[4] - m[0][1] * c[5] - m[0][3] * c[3]) * r
    q[0][2] = (m[3][1] * s[5] - m[3][2] * s[4] + m[3][3] * s[3]) * r
    q[0][3] = (m[2][2] * s[4] - m[2][1] * s[5] - m[2][3] * s[3]) * r
    q[1][1] = (m[0][0] * c[5] - m[0][2] * c[2] + m[0][3] * c[1]) * r
    q[1][2] = (m[3][2] * s[2] - m[3][0] * s[5] - m[3][3] * s[1]) * r
    q[1][3] = (m[2][0] * s[5] - m[2][2] * s[2] + m[2][3] * s[1]) * r
    q[2][2] = (m[3][0] * s[4] - m[3][1] * s[2] + m[3][3] * s[0]) * r
    q[2][3] = (m[2][1] * s[2] - m[2][0] * s[4] - m[2][3] * s[0]) * r
    q[3][3] = (m[2][0] * s[3] - m[2][1] * s[1] + m[2][2] * s[0]) * r
    for i in range(4):
        for j in range(i):
            q[i][j] = q[j][i]
    return q


def inverse_of(block):
    row, column = iota((PANEL, PART), 0), iota((PANEL, PART), 1)
    lane = iota((PART, PART), 1)
    work = block
    for k in range(0, PART, PANEL):
        panel = work[k : k + PANEL, :]
        left = jnp.where(column < k, -panel, jnp.where(column < k + PANEL, 0.0, panel))
        for s in range(0, PANEL, 4):
            at = k + s
            columns = [jnp.broadcast_to(panel[:, at + i : at + i + 1], (PANEL, PART)) for i in range(4)]
            lines = [
                jnp.where(
                    (column[:1] >= at) & (column[:1] < at + 4),
                    (column[:1] == at + i).astype(F32),
                    panel[s + i : s + i + 1, :],
                )
                for i in range(4)
            ]
            inverse = small_inverse([[columns[j][s + i : s + i + 1, :] for j in range(4)] for i in range(4)])
            inside = (row >= s) & (row < s + 4)
            panel = jnp.where(inside | ((column >= at) & (column < at + 4)), 0.0, panel)
            for i in range(4):
                line = (inverse[i][0] * lines[0] + inverse[i][1] * lines[1]) + (
                    inverse[i][2] * lines[2] + inverse[i][3] * lines[3]
                )
                panel = panel - jnp.where(inside, jnp.where(row == s + i, -1.0, 0.0), columns[i]) * line
        u, w = three(left), three(panel)
        update = tn(
            jnp.concatenate([u[0], u[0], u[1], u[0], u[2], u[1]], axis=0),
            jnp.concatenate([w[0], w[1], w[0], w[2], w[0], w[1]], axis=0),
        )
        others = jnp.where((lane >= k) & (lane < k + PANEL), 0.0, work) - update
        above = [others[:k, :]] if k else []
        below = [others[k + PANEL :, :]] if k + PANEL < PART else []
        work = jnp.concatenate(above + [panel] + below, axis=0)
    return work


def eliminate_kernel(gram_ref, right_ref, link_ref, known_ref, *rest):
    inverse = inverse_of(gram_ref[:PART, :PART])
    top = right_ref[:PART, :]
    known_ref[...] = both_split(nn, inverse, top)
    if rest:
        next_gram_ref, next_right_ref = rest
        beside = gram_ref[:PART, PART:]
        link = both_split(nn, inverse, beside)
        link_ref[...] = link
        next_gram_ref[...] = gram_ref[PART:, PART:] - both_split(tn, beside, link)
        next_right_ref[...] = right_ref[PART:, :] - both_split(tn, link, top)
    else:
        link_ref[...] = jnp.zeros(link_ref.shape, F32)


def substitute_kernel(*refs):
    links, known, out = refs[:3], refs[3:7], refs[7]
    found = known[3][...]
    out[pl.ds(3 * PART, PART), :] = found.astype(BF16)
    for k in (2, 1, 0):
        part = known[k][...] - both_split(nn, links[k][...], found)
        out[pl.ds(k * PART, PART), :] = part.astype(BF16)
        found = jnp.concatenate([part, found], axis=0)


def eliminate(system, after=()):
    gram, right = system
    left = gram.shape[0] - PART
    shapes = [shape_of((PART, max(left, PART)), F32), shape_of((PART, D), F32)]
    if left:
        shapes += [shape_of((left, left), F32), shape_of((left, D), F32)]
    return call(
        eliminate_kernel, shapes, [VMEM] * 2, [VMEM] * len(shapes), flops=FLOPS["eliminate"], after=after
    )(gram, right)


def substitute(steps, after=()):
    links, known = [step[0] for step in steps[:-1]], [step[1] for step in steps]
    return call(substitute_kernel, shape_of((N, D)), [VMEM] * 7, VMEM, flops=FLOPS["substitute"], after=after)(*links, *known)


def block_offsets(x_first):
    for array in range(4):
        core, second = array // 2, array % 2
        for index in range(8):
            first, z = index // 4, index % 4
            x, f = (first, second) if x_first else (second, first)
            yield array, index, z, x, core, f


def position(place_ref, z, x, core, f):
    dp = (place_ref[0] ^ z) * 4 + (place_ref[1] ^ x) * 2 + (place_ref[2] ^ core)
    return dp, place_ref[3] ^ f


def aligned(index, size):
    return pl.ds(pl.multiple_of(index * size, size), size)


def start(source, target, sem):
    copy = pltpu.make_async_copy(source, target, sem)
    copy.start()
    return copy


def wait_all(copies):
    for copy in copies:
        copy.wait()


class Hops:
    def __init__(self, parts, x_first, columns, first=0, rows=None):
        self.parts, self.x_first, self.columns, self.first = parts, x_first, columns, first
        self.row, self.rows = rows or (0, parts[0].shape[1])

    def block(self, refs, array, index, first, columns):
        return refs[array].at[index, pl.ds(self.row, self.rows), pl.ds(self.first + first, columns)]

    def fetch(self, refs, place_ref, whole, sem):
        copies = []
        for array, index, z, x, core, f in block_offsets(self.x_first):
            dp, side = position(place_ref, z, x, core, f)
            target = whole.at[aligned(dp, self.rows), aligned(side, self.columns)]
            copies.append(start(self.block(refs, array, index, 0, self.columns), target, sem))
        return copies

    def fetch_columns(self, refs, place_ref, f, half, tile, sem):
        for array, index, z, x, core, side in block_offsets(self.x_first):
            if side == f:
                dp, _ = position(place_ref, z, x, core, f)
                start(self.block(refs, array, index, half * TILE, TILE), tile.at[aligned(dp, self.rows), :], sem)

    def fetch_rows(self, refs, place_ref, f, half, tile, sem):
        z = tile_at(place_ref, f, half) ^ place_ref[0]
        for array in range(4):
            core, x = array // 2, array % 2
            place = (x ^ place_ref[1]) * 2 + (core ^ place_ref[2])
            for other in (0, 1):
                target = tile.at[aligned(place, self.rows), aligned(other ^ place_ref[3], self.columns)]
                start(self.block(refs, array, other * 4 + z, 0, self.columns), target, sem)


class Whole:
    def __init__(self, array):
        self.parts = [array]

    def fetch(self, refs, place_ref, whole, sem):
        return [start(refs[0], whole, sem)]

    def fetch_columns(self, refs, place_ref, f, half, tile, sem):
        start(refs[0].at[:, pl.ds((2 * f + half) * TILE, TILE)], tile, sem)

    def fetch_rows(self, refs, place_ref, f, half, tile, sem):
        start(refs[0].at[pl.ds((2 * f + half) * TILE, TILE), :], tile, sem)


def tile_at(place_ref, f, half):
    return (f ^ place_ref[3]) * 2 + half


def await_tile(tile, sem):
    pltpu.make_async_copy(tile, tile, sem).wait()


EVERY_PLACE = tuple((dp // 4, (dp // 2) % 2, dp % 2) for dp in range(16))


class Blocks:
    def __init__(self, x_first, rows, columns, cut=0):
        self.x_first, self.rows, self.columns, self.cut = x_first, rows, columns, cut
        self.shapes = [shape_of((2, 2, 4, rows, columns))] * 2

    def each(self, refs, place_ref, core_here, places, sides):
        z0, x0, f0 = place_ref[0], place_ref[1], place_ref[3]
        for n, (z, x, core) in enumerate(places):
            target = refs[0] if core == core_here else refs[1]
            for m, side in enumerate(sides):
                bits = (x ^ x0, side ^ f0) if self.x_first else (side ^ f0, x ^ x0)
                yield n, m, target.at[bits[0], bits[1], z ^ z0]

    def put(self, staged, refs, place_ref, sem, pieces, places=EVERY_PLACE, sides=(0, 1)):
        def send(core_here):
            for n, m, where in self.each(refs, place_ref, core_here, places, sides):
                for steps, offsets, first, columns in pieces:
                    rows = pl.ds(n * steps[0] + offsets[0], self.rows)
                    across = pl.ds(m * steps[1] + offsets[1], columns)
                    start(staged.at[rows, across], where.at[:, pl.ds(first, columns)], sem)

        pl.when(place_ref[2] == 0)(lambda: send(0))
        pl.when(place_ref[2] == 1)(lambda: send(1))


def spread_table(width, lanes):
    return (iota((PART, lanes), 0) == iota((PART, lanes), 1) % width).astype(BF16)


def vectors_kernel(place_ref, *refs):
    parts, (vec_ref, up_ref, table_ref, held, sem) = refs[:4], refs[4:]
    copies = []
    for array, index, z, x, core, f in block_offsets(False):
        dp, side = position(place_ref, z, x, core, f)
        first = parts[array].shape[2] - PART
        copies.append(start(parts[array].at[index, :, pl.ds(first, PART)], held.at[dp * 2 + side], sem))
    wait_all(copies)
    table_ref[...] = held[:, 16:32, :].reshape(512, PART)
    rows = held[:, :16, :].reshape(512, PART)
    device = iota((512, D), 0) // 16
    spread = nn(rows, spread_table(24, D))
    spread = jnp.where(iota((512, D), 1) // 24 == device, spread, 0.0)
    vec_ref[...] = jnp.sum(spread.reshape(32, 16, D), axis=0)
    wide = nn(rows, spread_table(96, D))
    wide = jnp.where(iota((512, D), 1) // 96 == device % 8, wide, 0.0)
    for t in range(4):
        group = wide[t * 128 : (t + 1) * 128, :].reshape(8, 16, D)
        up_ref[:, t * D : (t + 1) * D] = jnp.sum(group, axis=0)[8:16, :]


def gathered_vectors(place, mem_parts, after=()):
    return call(
        vectors_kernel,
        [shape_of((16, D), F32), shape_of((8, FF), F32), shape_of((N, PART))],
        [SMEM] + [HBM] * 4,
        [VMEM] * 3,
        [pltpu.VMEM((32, 48, PART), BF16), pltpu.SemaphoreType.DMA],
        flops=FLOPS["vectors"],
        after=after,
    )(place, *mem_parts)


def pack_vectors(vectors, up_grad, tables):
    device, kind = iota((512, D), 0) // 16, iota((512, D), 0) % 16
    tiled = jnp.broadcast_to(vectors[None], (32, 16, D)).reshape(512, D)
    tiled = jnp.where((iota((512, D), 1) // 24 == device) & (kind < 8), tiled, 0.0).astype(BF16)
    ups = [jnp.broadcast_to(up_grad[0:1, t * D : (t + 1) * D], (128, D)) for t in range(4)]
    ups = jnp.concatenate(ups, axis=0)
    ups = jnp.where((iota((512, D), 1) // 96 == device % 8) & (kind == 8), ups, 0.0).astype(BF16)
    rows = nt(tiled, spread_table(24, D)) + nt(ups, spread_table(96, D))
    rows = rows.astype(BF16).reshape(32, 16, PART)
    table_rows = tables.astype(BF16).reshape(32, 16, PART)
    return jnp.concatenate([rows, table_rows, jnp.zeros((32, 16, PART), BF16)], axis=1)


def head_mask(rows, lanes, heads):
    return iota((rows, lanes), 1) // DH == heads


def front_call(place, tokens, vectors, coeff, tables, proj, keys, values, after=()):
    weights = (proj, keys, values)
    counts = [len(w.parts) for w in weights]

    def kernel(place_ref, tokens_ref, vec_ref, coeff_ref, table_ref, *refs):
        sources, at = [], 0
        for count in counts:
            sources.append(refs[at : at + count])
            at += count
        normed_ref, projected_ref, mem_values_ref, reads_ref, proj_ref, keys_ref, values_ref, sems = refs[at:]
        held = (proj_ref, keys_ref, values_ref)
        copies = [w.fetch(s, place_ref, h, sems.at[n]) for n, (w, s, h) in enumerate(zip(weights, sources, held))]
        normed = normalise(tokens_ref[0].astype(F32), vec_ref[0:1, :], vec_ref[1:2, :]).astype(BF16)
        normed_ref[...] = normed
        summary = tn(table_ref[...], coeff_ref[...])[:32, :]
        wait_all(copies[1])
        reads = one_split(nn, summary, keys_ref[...])
        head = iota((32, D), 1) // DH
        kind = iota((32, D), 0)
        centre = jnp.sum(jnp.where(kind == head, reads, 0.0), axis=0, keepdims=True)
        spread = jnp.sum(jnp.where(kind == head + H, reads, 0.0), axis=0, keepdims=True)
        row = iota((8, D), 0)
        reads_ref[...] = jnp.where(row == 0, centre, jnp.where(row == 1, spread, 0.0))
        wait_all(copies[2])
        mem_values_ref[...] = nn(coeff_ref[...], values_ref[...]).astype(BF16)
        wait_all(copies[0])

        def block(n, bias):
            at = pl.ds(n * D, D)
            projected_ref[:, at] = (nn(normed_ref[...], proj_ref[:, at]) + bias).astype(BF16)

        block(0, vec_ref[2:3, :])
        block(1, 0.0)
        block(2, vec_ref[3:4, :])

    return call(
        kernel,
        [shape_of((512, D)), shape_of((512, 3 * D)), shape_of((N, D)), shape_of((8, D), F32)],
        [SMEM] + [VMEM] * 4 + [HBM] * sum(counts),
        [VMEM] * 4,
        [
            pltpu.VMEM((D, 3 * D), BF16),
            pltpu.VMEM((D, D), BF16),
            pltpu.VMEM((D, D), BF16),
            pltpu.SemaphoreType.DMA((3,)),
        ],
        flops=FLOPS["front"],
        vmem=28,
        after=after,
    )(place, tokens, vectors, coeff, tables, *proj.parts, *keys.parts, *values.parts)


READ = 256


def document_rows(length_ref):
    place = iota((1, 512), 1)
    first = jnp.zeros((1, 512), jnp.int32)
    end = jnp.int32(0)
    for n in range(length_ref.shape[1] - 1):
        end = end + length_ref[0, n]
        first = jnp.where(place >= end, end, first)
    return first


def mask_bias(length_ref, bias_ref):
    first = document_rows(length_ref)
    key, query = iota((512, 512), 0), iota((512, 512), 1)
    bias_ref[...] = jnp.where((key <= query) & (key >= first), 0.0, masked_fill)


def reading_row(length_ref, carried_ref):
    inside = iota((1, READ), 1) < length_ref[0, 0]
    return jnp.where(inside, carried_ref[0].astype(F32), 0.0)


def read_parameters(scaled, reads):
    lane_head = iota((1, PART), 1) // DH
    rows = [jnp.where(lane_head == h, reads[kind : kind + 1, :], 0.0) for kind in (0, 1) for h in (0, 1)]
    rows = jnp.concatenate(rows + [jnp.zeros((4, PART), F32)], axis=0)
    high, low = split(rows)
    lowest = (rows - high.astype(F32) - low.astype(F32)).astype(BF16)
    logits = nt(high, scaled) + (nt(low, scaled) + nt(lowest, scaled))
    found = []
    for h in (0, 1):
        centre = 1.0 / (1.0 + jnp.exp(-logits[h : h + 1, :]))
        raw = logits[2 + h : 3 + h, :]
        spread = spread_scale * (jnp.maximum(raw, 0.0) + jnp.log1p(jnp.exp(-jnp.abs(raw))))
        variance = 1.0 / (N * N) + spread * spread
        found.append((centre, spread, variance, raw))
    return rows, found


def basis_column():
    return (iota((N, 1), 0).astype(F32) + 0.5) / N


def density_of(centre, variance):
    distance = centre - basis_column()
    return lax.rsqrt(variance) / N * jnp.exp(distance * distance * (-0.5 / variance)), distance


def head_lanes(value, h):
    return jnp.where(iota((1, PART), 1) // DH == h, value, jnp.zeros_like(value))


def attend_kernel(length_ref, carried_ref, q_ref, k_ref, v_ref, mem_ref, reads_ref, out_ref, lse_ref, bias_ref):
    pl.when(pl.program_id(0) == 0)(lambda: mask_bias(length_ref, bias_ref))
    scaled = q_ref[...] * jnp.asarray(score_scale, BF16)
    outs, totals = [], []
    for h in (0, 1):
        halves, lse = [], []
        for first in (0, 256):
            keys = first + 256
            scores = nt(k_ref[:keys, :], head_lanes(scaled[first : first + 256, :], h))
            scores = scores + bias_ref[:keys, first : first + 256]
            top = jnp.max(scores, axis=0, keepdims=True)
            weights = jnp.exp(scores - top)
            total = jnp.sum(weights, axis=0, keepdims=True)
            probs = (weights * (1.0 / total)).astype(BF16)
            halves.append(tn(v_ref[:keys, :], probs)[h * DH : (h + 1) * DH, :])
            lse.append(top + jnp.log(total))
        outs.append(halves)
        totals.append(jnp.concatenate(lse, axis=1))
    lse_ref[...] = jnp.concatenate(totals + [jnp.zeros((6, 512), F32)], axis=0)
    _, found = read_parameters(scaled[:READ, :], reads_ref[...])
    reading = reading_row(length_ref, carried_ref)
    for h in (0, 1):
        centre, _, variance, _ = found[h]
        density, _ = density_of(centre, variance)
        recall = tn(mem_ref[...], density.astype(BF16))[h * DH : (h + 1) * DH, :]
        outs[h][0] = outs[h][0] + recall * reading
    for n in (0, 1):
        block = jnp.concatenate([outs[0][n], outs[1][n]], axis=0)
        out_ref[n * 256 : (n + 1) * 256, :] = jnp.transpose(block).astype(BF16)


def pair_block(shift=0):
    return pl.BlockSpec((512, PART), lambda i: (0, i + shift))


def attend_call(lengths, carried, projected, mem_values, reads, after=()):
    return call(
        attend_kernel,
        [shape_of((512, D)), shape_of((PAIRS * 8, 512), F32)],
        [SMEM, SMEM, pair_block(), pair_block(PAIRS), pair_block(2 * PAIRS), pair_block(), pl.BlockSpec((8, PART), lambda i: (0, i))],
        [pair_block(), pl.BlockSpec((8, 512), lambda i: (i, 0))],
        [pltpu.VMEM((512, 512), F32)],
        flops=FLOPS["attend"],
        after=after,
        grid=(PAIRS,),
    )(lengths, carried, projected, projected, projected, mem_values, reads)


def attend_back_kernel(length_ref, carried_ref, q_ref, k_ref, v_ref, lse_ref, heads_ref, more_ref, gq_ref, gk_ref, gv_ref, bias_ref):
    pl.when(pl.program_id(0) == 0)(lambda: mask_bias(length_ref, bias_ref))
    scaled = q_ref[...] * jnp.asarray(score_scale, BF16)
    keys, values, grad = k_ref[...], v_ref[...], heads_ref[...]
    lane_head = iota((1, PART), 1) // DH
    grad_queries, grad_keys, grad_values = [], [], []
    for h in (0, 1):
        parts = []
        gk, gv = [], []
        for first in (0, 256):
            last = first + 256
            own, own_grad = head_lanes(scaled[first:last, :], h), head_lanes(grad[first:last, :], h)
            scores = nt(keys[:last, :], own) + bias_ref[:last, first:last]
            probs = jnp.exp(scores - lse_ref[h : h + 1, first:last])
            grad_probs = nt(values[:last, :], own_grad)
            row_terms = jnp.sum(probs * grad_probs, axis=0, keepdims=True)
            grad_scores = (probs * (grad_probs - row_terms)).astype(BF16)
            gv.append(nn(probs.astype(BF16), grad[first:last, :]))
            gk.append(nn(grad_scores, scaled[first:last, :]))
            parts.append(tn(keys[:last, :], grad_scores)[h * DH : (h + 1) * DH, :])
        grad_queries.append(parts)
        grad_keys.append((gk[0] + gk[1][:256, :], gk[1][256:, :]))
        grad_values.append((gv[0] + gv[1][:256, :], gv[1][256:, :]))
    for n in (0, 1):
        at = slice(n * 256, (n + 1) * 256)
        gk_ref[at, :] = jnp.where(lane_head == 0, grad_keys[0][n], grad_keys[1][n]).astype(BF16)
        gv_ref[at, :] = jnp.where(lane_head == 0, grad_values[0][n], grad_values[1][n]).astype(BF16)
        block = jnp.concatenate([grad_queries[0][n], grad_queries[1][n]], axis=0)
        if n == 0:
            block = block + more_ref[...]
        gq_ref[at, :] = (jnp.transpose(block) * score_scale).astype(BF16)


def memory_read_back_kernel(length_ref, carried_ref, q_ref, mem_ref, reads_ref, heads_ref, more_ref, gmem_ref, sums_ref):
    scaled = q_ref[...] * jnp.asarray(score_scale, BF16)
    grad = heads_ref[...]
    lane_head = iota((1, PART), 1) // DH
    rows, found = read_parameters(scaled, reads_ref[...])
    reading = reading_row(length_ref, carried_ref)
    centre_grads, spread_grads, grad_mems = [], [], []
    for h in (0, 1):
        centre, spread, variance, raw = found[h]
        density, distance = density_of(centre, variance)
        own_grad = head_lanes(grad, h)
        grad_density = nt(mem_ref[...], own_grad) * reading
        grad_mems.append(nn((density * reading).astype(BF16), own_grad))
        weight = grad_density * density
        moment0 = jnp.sum(weight, axis=0, keepdims=True)
        weight = weight * distance
        moment1 = jnp.sum(weight, axis=0, keepdims=True)
        moment2 = jnp.sum(weight * distance, axis=0, keepdims=True)
        inverse = 1.0 / variance
        grad_variance = 0.5 * inverse * (moment2 * inverse - moment0)
        centre_grads.append(-moment1 * inverse * centre * (1.0 - centre))
        spread_grads.append(grad_variance * 2.0 * spread * spread_scale / (1.0 + jnp.exp(-raw)))
    gmem_ref[...] = (grad_mems[0] + grad_mems[1]).astype(BF16)
    logit_grads = jnp.concatenate(centre_grads + spread_grads + [jnp.zeros((4, READ), F32)], axis=0)
    sums = one_split(nn, logit_grads, scaled)
    centre_sum = jnp.where(lane_head == 0, sums[0:1, :], sums[1:2, :])
    spread_sum = jnp.where(lane_head == 0, sums[2:3, :], sums[3:4, :])
    sums_ref[...] = jnp.concatenate([centre_sum, spread_sum, jnp.zeros((6, PART), F32)], axis=0)
    more_ref[...] = both_split(tn, rows, logit_grads)


FEW = pl.BlockSpec((8, PART), lambda i: (0, i))


def memory_read_back_call(lengths, carried, projected, mem_values, reads, grad_heads, after=()):
    near = pl.BlockSpec((READ, PART), lambda i: (0, i))
    return call(
        memory_read_back_kernel,
        [shape_of((D, READ), F32), shape_of((N, D)), shape_of((8, D), F32)],
        [SMEM, SMEM, near, pair_block(), FEW, near],
        [pl.BlockSpec((PART, READ), lambda i: (i, 0)), pair_block(), FEW],
        flops=FLOPS["memory_read_back"],
        grid=(PAIRS,),
        after=after,
    )(lengths, carried, projected, mem_values, reads, grad_heads)


def attend_back_call(lengths, carried, projected, lse, grad_heads, more, first, count, after=()):
    def pair(shift):
        return pl.BlockSpec((512, PART), lambda i: (0, i + shift))

    return call(
        attend_back_kernel,
        [shape_of((512, count * PART))] * 3,
        [SMEM, SMEM, pair(first), pair(first + PAIRS), pair(first + 2 * PAIRS),
         pl.BlockSpec((8, 512), lambda i: (i + first, 0)), pair(first), pl.BlockSpec((PART, READ), lambda i: (i + first, 0))],
        [pair(0)] * 3,
        [pltpu.VMEM((512, 512), F32)],
        flops=FLOPS["attend_back"],
        grid=(count,),
        after=after,
    )(lengths, carried, projected, projected, projected, lse, grad_heads, more)


GELU_SCALE = 0.7978845608028654
GELU_CUBE = 0.044715


def column_tiles(step_columns):
    return pl.BlockSpec((512, step_columns), lambda t: (0, t))


def fixed(shape):
    return pl.BlockSpec(shape, lambda t: (0,) * len(shape), pipeline_mode=pl.Buffered(1))


def weight_refs(weights, refs):
    found, at = [], 0
    for weight in weights:
        found.append(refs[at : at + len(weight.parts)])
        at += len(weight.parts)
    return found, refs[at:]


def mlp_call(place, tokens, heads, cotangent, vectors, up_bias, out, up, down, down_blocks, up_blocks):
    weights = (out, up, down)
    steps = FF // TILE
    down_shapes = down_blocks.shapes if down_blocks else [shape_of((FF, D))]
    up_shapes = up_blocks.shapes if up_blocks else [shape_of((D, FF))]
    count = len(down_shapes)

    def kernel(place_ref, tokens_ref, heads_ref, cot_ref, vec_ref, bias_ref, *refs):
        sources, refs = weight_refs(weights, refs)
        result_ref, middle_ref, back_ref, line_ref = refs[:4]
        down_grads, up_grads, refs = refs[4 : 4 + count], refs[4 + count : 4 + 2 * count], refs[4 + 2 * count :]
        out_ref, up_ref, down_ref, normed_ref, total_ref, down_staged, up_staged, sem, up_sems, down_sems, grad_sems = refs
        step = pl.program_id(0)
        tile = tile_at(place_ref, step // 2, step % 2)
        side = (step // 2) ^ place_ref[3]

        @pl.when(step == 0)
        def _():
            copies = out.fetch(sources[0], place_ref, out_ref, sem)
            for n in range(steps):
                up.fetch_columns(sources[1], place_ref, n // 2, n % 2, up_ref.at[n], up_sems.at[n])
                down.fetch_rows(sources[2], place_ref, n // 2, n % 2, down_ref.at[n], down_sems.at[n])
            wait_all(copies)
            middle = tokens_ref[0].astype(F32) + nn(heads_ref[...], out_ref[...]) + vec_ref[4:5, :]
            middle_ref[...] = middle
            normed_ref[...] = normalise(middle, vec_ref[5:6, :], vec_ref[6:7, :]).astype(BF16)
            total_ref[...] = middle + vec_ref[7:8, :]
            back_ref[...] = jnp.zeros((512, D), F32)

        await_tile(up_ref.at[step], up_sems.at[step])
        await_tile(down_ref.at[step], down_sems.at[step])
        hidden = nn(normed_ref[...], up_ref[step]) + bias_ref[0:1, aligned(tile, TILE)]
        grad_active = nt(cot_ref[0], down_ref[step])
        square = hidden * hidden
        bent = jnp.tanh(GELU_SCALE * hidden * (1.0 + GELU_CUBE * square))
        half = 0.5 + 0.5 * bent
        active = (hidden * half).astype(BF16)
        slope = half + 0.5 * hidden * (1.0 - bent * bent) * (GELU_SCALE + 3.0 * GELU_SCALE * GELU_CUBE * square)
        grad_hidden = (grad_active * slope).astype(BF16)
        line = jnp.sum(grad_hidden.astype(F32), axis=0, keepdims=True)
        line_ref[:, aligned(tile, TILE)] = jnp.broadcast_to(line, (8, TILE))
        down_staged[step] = tn(active, cot_ref[0]).astype(BF16)
        total_ref[...] += nn(active, down_ref[step])
        up_staged[step] = tn(normed_ref[...], grad_hidden).astype(BF16)
        back_ref[...] += nt(grad_hidden, up_ref[step])
        if down_blocks:
            rows, columns = down_blocks.rows, down_blocks.columns
            down_pieces = [((rows, columns), (0, 0), 0, columns)]
            places = [(tile, x, core) for x in (0, 1) for core in (0, 1)]
            down_blocks.put(down_staged.at[step], down_grads, place_ref, grad_sems.at[0], down_pieces, places)
            up_pieces = [((up_blocks.rows, 0), (0, 0), (step % 2) * TILE, TILE)]
            up_blocks.put(up_staged.at[step], up_grads, place_ref, grad_sems.at[1], up_pieces, sides=(side,))
        else:
            start(down_staged.at[step], down_grads[0].at[aligned(tile, TILE), :], grad_sems.at[0])
            start(up_staged.at[step], up_grads[0].at[:, aligned(tile, TILE)], grad_sems.at[1])

        @pl.when(step == steps - 1)
        def _():
            result_ref[0] = total_ref[...].astype(BF16)
            for n in range(steps):
                await_tile(down_staged.at[n], grad_sems.at[0])
                await_tile(up_staged.at[n], grad_sems.at[1])

    found = call(
        kernel,
        [shape_of((1, 512, D)), shape_of((512, D), F32), shape_of((512, D), F32), shape_of((8, FF), F32)]
        + down_shapes
        + up_shapes,
        [SMEM, fixed((1, 512, D)), fixed((512, D)), fixed((1, 512, D)), fixed((16, D)), fixed((8, FF))]
        + [HBM] * sum(len(w.parts) for w in weights),
        [fixed((1, 512, D)), fixed((512, D)), fixed((512, D)), fixed((8, FF))] + [HBM] * (2 * count),
        [
            pltpu.VMEM((D, D), BF16),
            pltpu.VMEM((steps, D, TILE), BF16),
            pltpu.VMEM((steps, TILE, D), BF16),
            pltpu.VMEM((512, D), BF16),
            pltpu.VMEM((512, D), F32),
            pltpu.VMEM((steps, TILE, D), BF16),
            pltpu.VMEM((steps, D, TILE), BF16),
            pltpu.SemaphoreType.DMA,
            pltpu.SemaphoreType.DMA((steps,)),
            pltpu.SemaphoreType.DMA((steps,)),
            pltpu.SemaphoreType.DMA((2,)),
        ],
        flops=FLOPS["mlp"],
        vmem=44,
        grid=(steps,),
    )(place, tokens, heads, cotangent, vectors, up_bias, *out.parts, *up.parts, *down.parts)
    return found[:4], found[4 : 4 + count], found[4 + count :]


def middle_back_call(place, cotangent, middle, grad_normed, vectors, heads, out, after=()):
    def kernel(place_ref, cot_ref, middle_ref, grad_ref, vec_ref, heads_ref, *refs):
        sources, refs = weight_refs((out,), refs)
        grad_middle_ref, grad_heads_ref, out_grad_ref, sums_ref, out_ref, sem = refs
        copies = out.fetch(sources[0], place_ref, out_ref, sem)
        cot = cot_ref[0].astype(F32)
        back, gain, shift = normalise_back(middle_ref[...], vec_ref[5:6, :], grad_ref[...])
        grad_middle = cot + back
        grad_middle_ref[...] = grad_middle
        attended = grad_middle.astype(BF16)
        bias = jnp.sum(attended.astype(F32), axis=0, keepdims=True)
        last = jnp.sum(cot, axis=0, keepdims=True)
        nothing = jnp.zeros((4, D), F32)
        sums_ref[...] = jnp.concatenate([nothing, bias, gain, shift, last, nothing, nothing], axis=0)
        wait_all(copies)
        grad_heads_ref[...] = nt(attended, out_ref[...]).astype(BF16)
        out_grad_ref[...] = tn(heads_ref[...], attended).astype(BF16)

    return call(
        kernel,
        [shape_of((512, D), F32), shape_of((512, D)), shape_of((D, D)), shape_of((16, D), F32)],
        [SMEM] + [VMEM] * 5 + [HBM] * len(out.parts),
        [VMEM] * 4,
        [pltpu.VMEM((D, D), BF16), pltpu.SemaphoreType.DMA],
        flops=FLOPS["middle_back"],
        vmem=56,
        after=after,
    )(place, cotangent, middle, grad_normed, vectors, heads, *out.parts)


def memory_back_call(place, coeff, grad_mem_values, tables, sums, out_grad, keys, blocks, after=()):
    shapes = blocks[0].shapes if blocks else [shape_of((D, D))] * 3

    def kernel(place_ref, coeff_ref, grad_values_ref, table_ref, sums_ref, out_grad_ref, *refs):
        sources, refs = weight_refs((keys,), refs)
        tables_ref = refs[0]
        grad_refs, (keys_ref, key_grad_ref, value_grad_ref, sems) = refs[1 : 1 + len(shapes)], refs[1 + len(shapes) :]
        copies = keys.fetch(sources[0], place_ref, keys_ref, sems.at[0])
        staged = (out_grad_ref, key_grad_ref, value_grad_ref)

        def put(n):
            if not blocks:
                start(staged[n], grad_refs[n], sems.at[1 + n])
                return
            half = D // 2
            first, last, cut = n * half, (n + 1) * half, blocks[0].cut
            for block, low, high in ((blocks[0], first, min(last, cut)), (blocks[1], max(first, cut), last)):
                if low < high:
                    piece = ((block.rows, half), (0, low - first), low, high - low)
                    block.put(staged[n], grad_refs, place_ref, sems.at[1 + n], [piece])

        put(0)
        value_grad_ref[...] = tn(coeff_ref[...], grad_values_ref[...]).astype(BF16)
        put(2)
        head, kind = iota((32, D), 1) // DH, iota((32, D), 0)
        by_head = jnp.where(kind == head, sums_ref[0:1, :], jnp.where(kind == head + H, sums_ref[1:2, :], 0.0))
        summary = tn(coeff_ref[...], table_ref[...])[:, :32]
        key_grad_ref[...] = both_split(nn, summary, by_head).astype(BF16)
        put(1)
        wait_all(copies)
        high, low = split(by_head)
        wide = jnp.concatenate([high, low, jnp.zeros((PART - 64, D), BF16)], axis=0)
        reads = nt(keys_ref[...], wide)
        high, low = split(reads)
        found = nn(coeff_ref[...], high) + nn(coeff_ref[...], low)
        lane = iota((N, PART), 1)
        found = found + jnp.concatenate([found[:, 32:64], jnp.zeros((N, PART - 32), F32)], axis=1)
        tables_ref[...] = jnp.where(lane < 2 * H, found, 0.0)
        for n in range(3):
            await_tile(staged[n], sems.at[1 + n])

    found = call(
        kernel,
        [shape_of((N, PART), F32)] + shapes,
        [SMEM] + [VMEM] * 5 + [HBM] * len(keys.parts),
        [VMEM] + [HBM] * len(shapes),
        [pltpu.VMEM((D, D), BF16)] * 3 + [pltpu.SemaphoreType.DMA((4,))],
        flops=FLOPS["memory_back"],
        vmem=20,
        after=after,
    )(place, coeff, grad_mem_values, tables, sums, out_grad, *keys.parts)
    return found[0], found[1:]


def input_back_call(place, tokens, vectors, normed, grads, grad_middle, sums, up_bias_grad, tables, proj, blocks, after=()):
    shapes = blocks[0].shapes if blocks else [shape_of((D, 3 * D)), shape_of((16, D), F32)]

    def kernel(place_ref, tokens_ref, vec_ref, normed_ref, middle_ref, sums_ref, up_ref, table_ref, *refs):
        parts, refs = refs[: len(grads)], refs[len(grads) :]
        sources, refs = weight_refs((proj,), refs)
        result_ref = refs[0]
        grad_refs, (proj_ref, staged_ref, small_ref, sems) = refs[1 : 1 + len(shapes)], refs[1 + len(shapes) :]
        copies = proj.fetch(sources[0], place_ref, proj_ref, sems.at[0])
        at = 0
        for part in parts:
            columns = part.shape[1]
            staged_ref[:, at : at + columns] = tn(normed_ref[...], part[...]).astype(BF16)
            at += columns
        if blocks:
            rows, side = blocks[0].rows, 3 * D // 2
            half = blocks[0].columns // 2
            pieces = [((rows, side), (0, 0), 0, half), ((rows, side), (0, half), half, side - half)]
            for block, piece in zip(blocks, pieces):
                block.put(staged_ref, grad_refs, place_ref, sems.at[1], [piece])
        else:
            start(staged_ref, grad_refs[0], sems.at[1])
        wait_all(copies)
        grad_normed, column_sums, at = jnp.zeros((512, D), F32), [], 0
        for part in parts:
            columns = part.shape[1]
            grad_normed = grad_normed + nt(part[...], proj_ref[:, at : at + columns])
            column_sums.append(jnp.sum(part[...].astype(F32), axis=0, keepdims=True))
            at += columns
        column_sums = jnp.concatenate(column_sums, axis=1)
        back, gain, shift = normalise_back(tokens_ref[0].astype(F32), vec_ref[0:1, :], grad_normed)
        result_ref[0] = middle_ref[...] + back
        vectors_grad = jnp.concatenate([gain, shift, column_sums[:, :D], column_sums[:, 2 * D :], sums_ref[4:16, :]], axis=0)
        if blocks:
            small_ref[...] = pack_vectors(vectors_grad, up_ref[...], table_ref[...]).reshape(32 * rows, PART)

            def send(core_here):
                for n, m, where in blocks[1].each(grad_refs, place_ref, core_here, EVERY_PLACE, (0, 1)):
                    source = small_ref.at[pl.ds((2 * n + m) * rows, rows), :]
                    start(source, where.at[:, pl.ds(side, PART)], sems.at[2])

            pl.when(place_ref[2] == 0)(lambda: send(0))
            pl.when(place_ref[2] == 1)(lambda: send(1))
            await_tile(staged_ref, sems.at[1])
            await_tile(small_ref, sems.at[2])
        else:
            small_ref[...] = jnp.zeros(small_ref.shape, BF16)
            grad_refs[1][...] = vectors_grad
            pltpu.make_async_copy(staged_ref, grad_refs[0], sems.at[1]).wait()

    found = call(
        kernel,
        [shape_of((1, 512, D), F32)] + shapes,
        [SMEM] + [VMEM] * (7 + len(grads)) + [HBM] * len(proj.parts),
        [VMEM] + ([HBM] * 2 if blocks else [HBM, VMEM]),
        [
            pltpu.VMEM((D, 3 * D), BF16),
            pltpu.VMEM((D, 3 * D), BF16),
            pltpu.VMEM((32 * 48, PART), BF16),
            pltpu.SemaphoreType.DMA((3,)),
        ],
        flops=FLOPS["input_back"],
        vmem=36,
        after=after,
    )(place, tokens, vectors, normed, grad_middle, sums, up_bias_grad, tables, *grads, *proj.parts)
    return found[0], found[1:]


def hop(value, z=0, x=0, core=0, f=0):
    pairs = []
    for dp in range(16):
        for side in range(2):
            other = (((dp // 4) ^ z) * 4) + ((((dp // 2) % 2) ^ x) * 2) + ((dp % 2) ^ core)
            pairs.append((dp * 2 + side, other * 2 + (side ^ f)))
    return lax.ppermute(value, BOTH, pairs)


def z_hops(block):
    return [block] + [hop(block, z=k) for k in (1, 2, 3)]


def quads(pieces, cut, after, stacked=1):
    rows, columns = pieces[0].shape
    width = (columns - cut) // stacked

    def kernel(*refs):
        blocks, (left, right) = refs[:4], refs[4:]
        for k, block in enumerate(blocks):
            left[k] = block[:, :cut]
            for n in range(stacked):
                right[k, n * rows : (n + 1) * rows, :] = block[:, cut + n * width : cut + (n + 1) * width]

    shapes = [shape_of((4, rows, cut)), shape_of((4, stacked * rows, width))]
    return list(call(kernel, shapes, [VMEM] * 4, [VMEM] * 2, flops=FLOPS["pack"], after=after)(*pieces))


BITS = (dict(x=1), dict(f=1))


def joined(quads_here, nears, after):
    def kernel(*refs):
        for n in (0, 1):
            for m in (0, 1):
                refs[4 + n][pl.ds(4 * m, 4)] = refs[2 * m + n][...]

    shapes = [shape_of((8,) + quad.shape[1:]) for quad in quads_here]
    return list(call(kernel, shapes, [VMEM] * 4, [VMEM] * 2, flops=FLOPS["pack"], after=after)(*quads_here, *nears))


def once_there(arrays, after):
    count = len(arrays)

    def kernel(*refs):
        for n in range(count):
            refs[count + n][...] = refs[n][...]

    shapes = [shape_of(array.shape) for array in arrays]
    return call(kernel, shapes, [VMEM] * count, [VMEM] * count, flops=FLOPS["pack"], after=after)(*arrays)


def plus(a, b):
    return (a.astype(F32) + b.astype(F32)).astype(BF16)


def halves(kept, got):
    return plus(kept[1], got[1]), plus(kept[0], got[0])


def halves_after(pairs, after):
    widths = [kept.shape[-1] for kept, _ in pairs]

    def kernel(*refs):
        for bit, target in ((1, refs[-2]), (0, refs[-1])):
            at = 0
            for n, width in enumerate(widths):
                total = refs[2 * n][bit].astype(F32) + refs[2 * n + 1][bit].astype(F32)
                target[..., at : at + width] = total.astype(BF16)
                at += width

    shapes = [shape_of(pairs[0][0].shape[1:-1] + (sum(widths),))] * 2
    flat = [array for pair in pairs for array in pair]
    return call(kernel, shapes, [VMEM] * len(flat), [VMEM] * 2, flops=FLOPS["add"], after=after)(*flat)


def added(pairs, after=()):
    rows, columns = pairs[0][0].shape[1], [kept.shape[2] for kept, _ in pairs]

    def kernel(*refs):
        sent, own = refs[-2:]
        at = 0
        for n, width in enumerate(columns):
            kept, got = refs[2 * n], refs[2 * n + 1]
            for k in range(4):
                total = kept[k].astype(F32) + got[k].astype(F32)
                if k < 2:
                    own[k, :, at : at + width] = total
                else:
                    sent[k - 2, :, at : at + width] = total.astype(BF16)
            at += width

    shapes = [shape_of((2, rows, sum(columns))), shape_of((2, rows, sum(columns)), F32)]
    flat = [array for pair in pairs for array in pair]
    return call(kernel, shapes, [VMEM] * len(flat), [VMEM] * 2, flops=FLOPS["add"], after=after)(*flat)


def between(own, got, after=()):
    def kernel(own_ref, got_ref, sent_ref, total_ref):
        total_ref[...] = own_ref[0] + got_ref[0].astype(F32)
        sent_ref[...] = (own_ref[1] + got_ref[1].astype(F32)).astype(BF16)

    shapes = [shape_of(own.shape[1:]), shape_of(own.shape[1:], F32)]
    return call(kernel, shapes, [VMEM] * 2, [VMEM] * 2, flops=FLOPS["add"], after=after)(own, got)


def cut_halves(kept, got, cut, after=()):
    def kernel(kept_ref, got_ref, *refs):
        for n, columns in enumerate((slice(0, cut), slice(cut, None))):
            for bit, target in ((1, refs[n]), (0, refs[2 + n])):
                total = kept_ref[bit, :, :, :, columns].astype(F32) + got_ref[bit, :, :, :, columns].astype(F32)
                target[...] = total.astype(BF16)

    shapes = [shape_of(kept.shape[1:4] + (width,)) for width in (cut, kept.shape[4] - cut)] * 2
    found = call(kernel, shapes, [VMEM] * 2, [VMEM] * 4, flops=FLOPS["add"], after=after)(kept, got)
    return found[:2], found[2:]


def both_halves(kept, got, after=()):
    def kernel(*refs):
        for n in (0, 1):
            for bit, target in ((1, refs[4 + n]), (0, refs[6 + n])):
                target[...] = (refs[n][bit].astype(F32) + refs[2 + n][bit].astype(F32)).astype(BF16)

    shapes = [shape_of(array.shape[1:]) for array in kept] * 2
    found = call(kernel, shapes, [VMEM] * 4, [VMEM] * 4, flops=FLOPS["add"], after=after)(*kept, *got)
    return found[:2], found[2:]


def finish(own, got, cuts, after=()):
    spans = [(rows.stop - rows.start, columns.stop - columns.start) for rows, columns in cuts]

    def kernel(own_ref, *refs):
        total = own_ref[...]
        for ref in refs[: len(got)]:
            total = total + ref[...].astype(F32)
        for target, (rows, columns) in zip(refs[len(got) :], cuts):
            target[...] = total[rows, columns]

    shapes = [shape_of(span, F32) for span in spans]
    return call(
        kernel, shapes, [VMEM] * (1 + len(got)), [VMEM] * len(cuts), flops=FLOPS["add"], after=after
    )(own, *got)


def three_ways(pairs, after=()):
    rows, columns = pairs[0][0].shape[1], [kept.shape[2] for kept, _ in pairs]

    def kernel(*refs):
        targets = refs[-4:]
        at = 0
        for n, width in enumerate(columns):
            for k in range(4):
                total = refs[2 * n][k].astype(F32) + refs[2 * n + 1][k].astype(F32)
                targets[k][:, at : at + width] = total.astype(targets[k].dtype)
            at += width

    shapes = [shape_of((rows, sum(columns)), F32)] + [shape_of((rows, sum(columns)))] * 3
    flat = [array for pair in pairs for array in pair]
    return call(kernel, shapes, [VMEM] * len(flat), [VMEM] * 4, flops=FLOPS["add"], after=after)(*flat)


COLUMN_SPLIT = (2, 5, 7, 8, 13, 15)
VECTORS = (0, 1, 3, 4, 6, 11, 12, 16)


def gather_whole(shards):
    def whole(k, shard):
        near = lax.all_gather(shard, "fsdp", axis=1 if k in COLUMN_SPLIT else 0, tiled=True)
        return lax.all_gather(near, "dp", axis=0, tiled=True)

    found = [whole(k, shard) for k, shard in enumerate(shards)]
    vectors = jnp.stack([found[k].astype(F32) for k in VECTORS] + [jnp.zeros((D,), F32)] * 8)
    up_bias = jnp.broadcast_to(found[14].astype(F32)[None], (8, FF))
    tables = jnp.pad(jnp.concatenate([found[9], found[10]], axis=1), ((0, 0), (0, PART - 2 * H)))
    weights = {k: Whole(found[k]) for k in COLUMN_SPLIT}
    return weights, vectors, up_bias, tables


def scatter_whole(totals):
    def part(k, total):
        near = lax.psum_scatter(total.astype(BF16), "dp", scatter_dimension=0, tiled=True)
        return lax.psum_scatter(near, "fsdp", scatter_dimension=1 if k in COLUMN_SPLIT else 0, tiled=True).astype(F32)

    return [part(k, total) for k, total in enumerate(totals)]


def pack_early(shards):
    order = [2, 7, 8, 9, 10, 14] + list(VECTORS)
    arrays = [shards[k] if shards[k].ndim == 2 else shards[k].reshape(1, -1) for k in order]
    rows, half = shards[5].shape

    def kernel(proj, keys, values, centre, spread, up_bias, *refs):
        vectors, early = refs[:-1], refs[-1]
        early[:, : 3 * half] = proj[...]
        early[:, 3 * half : 4 * half] = keys[...]
        early[:, 4 * half : 5 * half] = values[...]
        lines = []
        for ref in list(vectors) + [up_bias]:
            line = ref[...].astype(F32)
            lines.append(jnp.concatenate([line, jnp.zeros((1, PART - line.shape[1]), F32)], axis=1))
        lines.append(jnp.zeros((16 - len(lines), PART), F32))
        tables = jnp.concatenate(
            [centre[...].astype(F32), spread[...].astype(F32), jnp.zeros((16, PART - 2 * H), F32)], axis=1
        )
        small = jnp.concatenate(lines + [tables, jnp.zeros((rows - 32, PART), F32)], axis=0)
        early[:, 5 * half :] = small.astype(BF16)

    return call(kernel, shape_of((rows, 5 * half + PART)), [VMEM] * len(arrays), VMEM, flops=FLOPS["pack"], vmem=56)(*arrays)


def pack_late(shards, after):
    rows, half = shards[5].shape

    def kernel(out, up, down, late):
        late[:, : 4 * half] = up[...]
        for q in range(4):
            late[:, (4 + q) * half : (5 + q) * half] = down[q * rows : (q + 1) * rows, :]
        late[:, 8 * half :] = out[...]

    return call(kernel, shape_of((rows, 9 * half)), [VMEM] * 3, VMEM, flops=FLOPS["pack"], after=after)(
        shards[5], shards[13], shards[15]
    )


def local(
    mesh_sizes, tokens, context, past_coeffs, doc_lengths, carried, histogram, cotangent, *shards
):
    hops = mesh_sizes == (16, 2)
    dp = lax.axis_index("dp")
    place = jnp.stack([dp // 4, (dp // 2) % 2, dp % 2, lax.axis_index("fsdp")]).astype(jnp.int32)
    rows, half = shards[5].shape
    x_hop, f_hop = BITS
    if hops:
        early = z_hops(pack_early(shards))
        points, gram, right = memory_system(histogram, past_coeffs, context, after=[early[0]])
        early = quads(early, 3 * half, [gram])
        near = [hop(early[0], **x_hop), hop(early[1], **f_hop)]
        steps = [eliminate((gram, right), early)]
        late = z_hops(pack_late(shards, [steps[0][0]]))
        early = joined(early, near, [steps[0][0]])
        far = [hop(early[0], **f_hop), hop(early[1], **x_hop)]
        steps.append(eliminate(steps[0][2:], early))
        late = quads(late, 4 * half, [steps[1][0]], 5)
        late_near = [hop(late[0], **x_hop), hop(late[1], **f_hop)]
        steps.append(eliminate(steps[1][2:], late + far))
        pairs = once_there(early, [steps[2][0]])
        proj_parts, mem_parts = (
            [early[n], far[n], hop(pairs[n], core=1), hop(far[n], core=1)] for n in (0, 1)
        )
        late = joined(late, late_near, [steps[2][0]])
        late_far = [hop(late[0], **f_hop), hop(late[1], **x_hop)]
        steps.append(eliminate(steps[2][2:], proj_parts[2:] + mem_parts[2:] + late))
        late_core = [hop(part, core=1) for part in late]
        coeff = substitute(steps)
        vectors, up_bias, tables = gathered_vectors(place, mem_parts)
        weights = {
            2: Hops(proj_parts, True, 3 * half),
            7: Hops(mem_parts, False, half),
            8: Hops(mem_parts, False, half, half),
        }
    else:
        late_core = []
        weights, vectors, up_bias, tables = gather_whole(shards)
        points, *system = memory_system(histogram, past_coeffs, context)
        steps = [eliminate(system)]
        while len(steps) < N // PART:
            steps.append(eliminate(steps[-1][2:]))
        coeff = substitute(steps)
    normed, projected, mem_values, reads = front_call(
        place, tokens, vectors, coeff, tables, weights[2], weights[7], weights[8], after=late_core
    )
    heads, lse = attend_call(doc_lengths, carried, projected, mem_values, reads)
    if hops:
        far_core = [hop(part, core=1) for part in once_there(late_far, [heads])]
        parts = [[late[n], late_far[n], late_core[n], far_core[n]] for n in (0, 1)]
        weights[13] = Hops(parts[0], True, 4 * half)
        weights[15] = Hops(parts[1], False, half, rows=(0, 4 * rows))
        weights[5] = Hops(parts[1], False, half, rows=(4 * rows, rows))
    down_blocks = Blocks(False, 4 * rows, half) if hops else None
    up_blocks = Blocks(True, rows, 4 * half) if hops else None
    (result, middle, grad_normed_mlp, grad_up_bias), down_grad, up_grad = mlp_call(
        place, tokens, heads, cotangent, vectors, up_bias, weights[5], weights[13], weights[15], down_blocks, up_blocks
    )
    waits = {"read": [], "memory": [], "second": [], "input": []}
    grad_middle, grad_heads, grad_out, sums = middle_back_call(
        place, cotangent, middle, grad_normed_mlp, vectors, heads, weights[5]
    )
    if hops:
        got_down, got_up = hop(down_grad[1], core=1), hop(up_grad[1], core=1)
        sent_down, kept_down = halves_after([(down_grad[0], got_down)], [grad_middle])
        waits["read"] = [sent_down]
        got_down = hop(sent_down, **f_hop)
    more, grad_mem, read_sums = memory_read_back_call(
        doc_lengths, carried, projected, mem_values, reads, grad_heads, after=waits["read"]
    )
    if hops:
        sent_up, kept_up = halves_after([(up_grad[0], got_up)], [grad_mem])
        waits["memory"] = [sent_up]
        got_up = hop(sent_up, **x_hop)
    mem_width, mem_cut = 3 * half, 5 * PART
    mem_blocks = [Blocks(x_first, rows, mem_width, mem_cut) for x_first in (True, False)] if hops else None
    grad_tables, mem_grad = memory_back_call(
        place, coeff, grad_mem, tables, read_sums, grad_out, weights[7], mem_blocks, after=waits["memory"]
    )
    first = attend_back_call(doc_lengths, carried, projected, lse, grad_heads, more, 0, PAIRS // 2, after=[grad_tables])
    if hops:
        got_mem = hop(mem_grad[1], core=1)
        sent_down, kept_down = halves_after([(kept_down, got_down)], list(first[:1]))
        got_down = hop(sent_down, **x_hop)
        sent_mem, kept_mem = cut_halves(mem_grad[0], got_mem, mem_cut, [sent_down])
        waits["second"] = list(sent_mem)
        got_mem = [hop(sent_mem[0], **x_hop), hop(sent_mem[1], **f_hop)]
    second = attend_back_call(
        doc_lengths, carried, projected, lse, grad_heads, more, PAIRS // 2, PAIRS // 2, after=waits["second"]
    )
    if hops:
        sent_up, kept_up = halves_after([(kept_up, got_up)], list(second[:1]))
        got_up = hop(sent_up, **f_hop)
        sent_down, own_down = added([(kept_down, got_down)], [sent_up])
        waits["input"] = [sent_down]
        got_down = hop(sent_down, z=2)
    grads = [part for pair in zip(first, second) for part in pair]
    width = 3 * half + PART
    proj_blocks = [Blocks(x_first, rows, width) for x_first in (True, False)] if hops else None
    grad_tokens, proj_grad = input_back_call(
        place, tokens, vectors, normed, grads, grad_middle, sums, grad_up_bias, grad_tables, weights[2], proj_blocks,
        after=waits["input"],
    )
    if hops:
        got = hop(proj_grad[1], core=1)
        sent_mem, kept_mem = both_halves(kept_mem, got_mem, [grad_tokens])
        got_mem = [hop(sent_mem[0], **f_hop), hop(sent_mem[1], **x_hop)]
        sent, kept = cut_halves(proj_grad[0], got, width // 2, list(sent_mem))
        got = [hop(sent[0], **x_hop), hop(sent[1], **f_hop)]
        sent_up, own_up = added([(kept_up, got_up)], list(sent))
        got_up = hop(sent_up, z=2)
        sent_down, own_down = between(own_down, got_down, [sent_up])
        got_down = hop(sent_down, z=1)
        sent, kept = both_halves(kept, got, [sent_down])
        got = [hop(sent[0], **f_hop), hop(sent[1], **x_hop)]
        sent_mem, own_mem = added(list(zip(kept_mem, got_mem)), list(sent))
        got_mem = hop(sent_mem, z=2)
        every = slice(0, rows)
        summed = {}
        summed[15] = finish(own_down, [got_down], [(slice(0, 4 * rows), slice(0, half))], [sent_mem])[0]
        own, *sent = three_ways(list(zip(kept, got)), [summed[15]])
        got = [hop(part, z=k) for k, part in zip((1, 2, 3), sent)]
        sent_up, own_up = between(own_up, got_up, sent)
        got_up = hop(sent_up, z=1)
        sent_mem, own_mem = between(own_mem, got_mem, [sent_up])
        got_mem = hop(sent_mem, z=1)
        summed[13] = finish(own_up, [got_up], [(every, slice(0, 4 * half))], [sent_mem])[0]
        summed[5], summed[7], summed[8] = finish(
            own_mem, [got_mem], [(every, slice(n * half, (n + 1) * half)) for n in range(3)], [summed[13]]
        )
        side = 3 * half
        tables_rows = slice(16, 32)
        ends = [shards[k].shape[0] for k in VECTORS] + [shards[14].shape[0]]
        cuts = [(every, slice(0, side))]
        cuts += [(tables_rows, slice(side + n * H, side + (n + 1) * H)) for n in (0, 1)]
        cuts += [(slice(n, n + 1), slice(side, side + end)) for n, end in enumerate(ends)]
        summed[2], summed[9], summed[10], *lines = finish(own, got, cuts)
        for k, line in zip(VECTORS + (14,), lines):
            summed[k] = line.reshape(-1)
    else:
        totals = {13: up_grad[0], 15: down_grad[0], 2: proj_grad[0], 14: grad_up_bias[0]}
        totals[5], totals[7], totals[8] = mem_grad
        totals[9], totals[10] = grad_tables[:, :H], grad_tables[:, H : 2 * H]
        for n, k in enumerate(VECTORS):
            totals[k] = proj_grad[1][n]
        summed = scatter_whole([totals[k] for k in range(17)])
    return (result, grad_tokens, *(summed[k] for k in range(17)), points)


def solution(mesh):
    both, row, table = P(BOTH), P("dp", "fsdp"), P(BOTH, None)
    block = P(BOTH, None, None)
    weights = (
        both, both, row, both, both, row, both, row, row, table, table, both, both, row, both, row, both,
    )
    in_specs = (block, block, block, table, both, table, block) + weights
    out_specs = (block, block) + weights + (table,)
    sizes = (mesh.shape["dp"], mesh.shape["fsdp"])
    return jax.shard_map(
        functools.partial(local, sizes), mesh=mesh, in_specs=in_specs, out_specs=out_specs, check_vma=False
    )
```

```python
import functools

import jax
import jax.numpy as jnp
from jax import lax
from jax.experimental import pallas as pl
from jax.experimental.pallas import tpu as pltpu
from jax.sharding import PartitionSpec as P

H = 12
DH = 64
D = H * DH
N = 512
CTX = 1024
M = 512
NBINS = 64
FF = 4 * D
PAIRS = H // 2
PART = 128
TILE = 768

memory_tau = 0.75
ridge_weight = 1.0
norm_epsilon = 1e-05
spread_scale = 0.25
masked_fill = -1e30
score_scale = DH ** (-0.5)

F32, BF16 = jnp.float32, jnp.bfloat16
MIB = 1024 * 1024
BOTH = ("dp", "fsdp")
HBM = pl.BlockSpec(memory_space=pl.ANY)
SMEM = pl.BlockSpec(memory_space=pltpu.SMEM)
VMEM = pl.BlockSpec(memory_space=pltpu.VMEM)


FLOPS = {
    "pack": 1, "system": 8, "eliminate": 5, "substitute": 2, "vectors": 2, "front": 7, "attend": 14, "mlp": 26,
    "middle_back": 4, "memory_read_back": 7, "memory_back": 7, "attend_back": 7, "input_back": 11,
    "add": 10,
}
FLOPS = {name: work * 20000_000_000 for name, work in FLOPS.items()}


def shape_of(shape, dtype=BF16):
    return jax.ShapeDtypeStruct(shape, dtype)


def call(kernel, out_shape, in_specs, out_specs, scratch=(), flops=0, grid=None, after=(), vmem=20):
    extra = {} if grid is None else {"grid": grid}
    inputs, unread = len(in_specs), len(after)

    def body(*refs):
        kernel(*refs[:inputs], *refs[inputs + unread :])

    run = pl.pallas_call(
        body,
        out_shape=out_shape,
        in_specs=list(in_specs) + [HBM] * unread,
        out_specs=out_specs,
        scratch_shapes=list(scratch),
        compiler_params=pltpu.CompilerParams(vmem_limit_bytes=vmem * MIB),
        cost_estimate=pl.CostEstimate(flops=flops, bytes_accessed=0, transcendentals=0),
        **extra,
    )
    return lambda *operands: run(*operands, *after)


def nn(a, b):
    return lax.dot_general(a, b, (((1,), (0,)), ((), ())), preferred_element_type=F32)


def nt(a, b):
    return lax.dot_general(a, b, (((1,), (1,)), ((), ())), preferred_element_type=F32)


def tn(a, b):
    return lax.dot_general(a, b, (((0,), (0,)), ((), ())), preferred_element_type=F32)


def split(value):
    high = value.astype(BF16)
    return high, (value - high.astype(F32)).astype(BF16)


def both_split(product, a, b):
    a_high, a_low = split(a)
    b_high, b_low = split(b)
    return product(a_high, b_high) + (product(a_high, b_low) + product(a_low, b_high))


def one_split(product, a, b):
    a_high, a_low = split(a)
    return product(a_high, b) + product(a_low, b)


def iota(shape, axis):
    return lax.broadcasted_iota(jnp.int32, shape, axis)


def gaussian(points, centres):
    distance = points - centres
    return jnp.exp(-0.5 * distance * distance * (N * N))


def normalise(values, gain, shift):
    mean = jnp.mean(values, axis=-1, keepdims=True)
    centred = values - mean
    variance = jnp.mean(centred * centred, axis=-1, keepdims=True)
    inverse = lax.rsqrt(variance + norm_epsilon)
    return centred * inverse * gain + shift


def normalise_back(values, gain, grad):
    mean = jnp.mean(values, axis=-1, keepdims=True)
    centred = values - mean
    variance = jnp.mean(centred * centred, axis=-1, keepdims=True)
    inverse = lax.rsqrt(variance + norm_epsilon)
    standard = centred * inverse
    scaled = grad * gain
    first = jnp.mean(scaled, axis=-1, keepdims=True)
    second = jnp.mean(scaled * standard, axis=-1, keepdims=True)
    back = inverse * (scaled - first - standard * second)
    return back, jnp.sum(grad * standard, axis=0, keepdims=True), jnp.sum(grad, axis=0, keepdims=True)


def system_kernel(hist_ref, past_ref, context_ref, points_ref, gram_ref, right_ref):
    hist = hist_ref[...]
    counts = jnp.broadcast_to(hist, (NBINS, NBINS))
    row, column = iota((NBINS, NBINS), 0), iota((NBINS, NBINS), 1)

    def down(keep):
        return jnp.sum(jnp.where(keep, counts, 0), axis=1, keepdims=True)

    ends, starts, count = down(column <= row), down(column < row), down(column == row)
    slot = iota((NBINS, M), 1)
    inside = (slot >= starts) & (slot < ends)

    def across(values):
        return jnp.sum(jnp.where(inside, values, 0), axis=0, keepdims=True)

    first, amount, number = across(starts), across(count), across(iota((NBINS, M), 0))
    offset = (iota((1, M), 1) - first).astype(F32) + 0.5
    points = (number.astype(F32) + offset / amount.astype(F32)) / NBINS
    points_ref[...] = points
    upright = jnp.sum(
        jnp.where(iota((M, M), 0) == iota((M, M), 1), points, 0.0), axis=1, keepdims=True
    )
    centre_row = (iota((1, N), 1).astype(F32) + 0.5) / N
    centre_column = (iota((N, 1), 0).astype(F32) + 0.5) / N
    past_values = one_split(nn, gaussian(upright, centre_row), past_ref[0])
    recent = memory_tau + (1.0 - memory_tau) * (iota((1, CTX), 1).astype(F32) + 0.5) / CTX
    old = gaussian(memory_tau * points, centre_column)
    new = gaussian(recent, centre_column)
    right_ref[...] = both_split(nn, old, past_values) + one_split(nn, new, context_ref[0])
    eye = (iota((N, N), 0) == iota((N, N), 1)).astype(F32) * ridge_weight
    gram_ref[...] = both_split(nt, old, old) + both_split(nt, new, new) + eye


def memory_system(histogram, past, context, after=()):
    return call(
        system_kernel,
        [shape_of((1, M), F32), shape_of((N, N), F32), shape_of((N, D), F32)],
        [VMEM] * 3,
        [VMEM] * 3,
        flops=FLOPS["system"],
        vmem=24,
        after=after,
    )(histogram, past, context)


PANEL = 16


def three(value):
    high = value.astype(BF16)
    rest = value - high.astype(F32)
    middle = rest.astype(BF16)
    return high, middle, (rest - middle.astype(F32)).astype(BF16)


def small_inverse(m):
    def minor(r0, r1, c0, c1):
        return m[r0][c0] * m[r1][c1] - m[r0][c1] * m[r1][c0]

    places = ((0, 1), (0, 2), (0, 3), (1, 2), (1, 3), (2, 3))
    s = [minor(0, 1, *place) for place in places]
    c = [minor(2, 3, *place) for place in places]
    total = ((s[0] * c[5] - s[1] * c[4]) + (s[2] * c[3] + s[3] * c[2])) + (s[5] * c[0] - s[4] * c[1])
    r = 1.0 / total
    q = [[None] * 4 for _ in range(4)]
    q[0][0] = (m[1][1] * c[5] - m[1][2] * c[4] + m[1][3] * c[3]) * r
    q[0][1] = (m[0][2] * c[4] - m[0][1] * c[5] - m[0][3] * c[3]) * r
    q[0][2] = (m[3][1] * s[5] - m[3][2] * s[4] + m[3][3] * s[3]) * r
    q[0][3] = (m[2][2] * s[4] - m[2][1] * s[5] - m[2][3] * s[3]) * r
    q[1][1] = (m[0][0] * c[5] - m[0][2] * c[2] + m[0][3] * c[1]) * r
    q[1][2] = (m[3][2] * s[2] - m[3][0] * s[5] - m[3][3] * s[1]) * r
    q[1][3] = (m[2][0] * s[5] - m[2][2] * s[2] + m[2][3] * s[1]) * r
    q[2][2] = (m[3][0] * s[4] - m[3][1] * s[2] + m[3][3] * s[0]) * r
    q[2][3] = (m[2][1] * s[2] - m[2][0] * s[4] - m[2][3] * s[0]) * r
    q[3][3] = (m[2][0] * s[3] - m[2][1] * s[1] + m[2][2] * s[0]) * r
    for i in range(4):
        for j in range(i):
            q[i][j] = q[j][i]
    return q


def inverse_of(block):
    row, column = iota((PANEL, PART), 0), iota((PANEL, PART), 1)
    lane = iota((PART, PART), 1)
    work = block
    for k in range(0, PART, PANEL):
        panel = work[k : k + PANEL, :]
        left = jnp.where(column < k, -panel, jnp.where(column < k + PANEL, 0.0, panel))
        for s in range(0, PANEL, 4):
            at = k + s
            columns = [jnp.broadcast_to(panel[:, at + i : at + i + 1], (PANEL, PART)) for i in range(4)]
            lines = [
                jnp.where(
                    (column[:1] >= at) & (column[:1] < at + 4),
                    (column[:1] == at + i).astype(F32),
                    panel[s + i : s + i + 1, :],
                )
                for i in range(4)
            ]
            inverse = small_inverse([[columns[j][s + i : s + i + 1, :] for j in range(4)] for i in range(4)])
            inside = (row >= s) & (row < s + 4)
            panel = jnp.where(inside | ((column >= at) & (column < at + 4)), 0.0, panel)
            for i in range(4):
                line = (inverse[i][0] * lines[0] + inverse[i][1] * lines[1]) + (
                    inverse[i][2] * lines[2] + inverse[i][3] * lines[3]
                )
                panel = panel - jnp.where(inside, jnp.where(row == s + i, -1.0, 0.0), columns[i]) * line
        u, w = three(left), three(panel)
        update = tn(
            jnp.concatenate([u[0], u[0], u[1], u[0], u[2], u[1]], axis=0),
            jnp.concatenate([w[0], w[1], w[0], w[2], w[0], w[1]], axis=0),
        )
        others = jnp.where((lane >= k) & (lane < k + PANEL), 0.0, work) - update
        above = [others[:k, :]] if k else []
        below = [others[k + PANEL :, :]] if k + PANEL < PART else []
        work = jnp.concatenate(above + [panel] + below, axis=0)
    return work


def eliminate_kernel(gram_ref, right_ref, link_ref, known_ref, *rest):
    inverse = inverse_of(gram_ref[:PART, :PART])
    top = right_ref[:PART, :]
    known_ref[...] = both_split(nn, inverse, top)
    if rest:
        next_gram_ref, next_right_ref = rest
        beside = gram_ref[:PART, PART:]
        link = both_split(nn, inverse, beside)
        link_ref[...] = link
        next_gram_ref[...] = gram_ref[PART:, PART:] - both_split(tn, beside, link)
        next_right_ref[...] = right_ref[PART:, :] - both_split(tn, link, top)
    else:
        link_ref[...] = jnp.zeros(link_ref.shape, F32)


def substitute_kernel(*refs):
    links, known, out = refs[:3], refs[3:7], refs[7]
    found = known[3][...]
    out[pl.ds(3 * PART, PART), :] = found.astype(BF16)
    for k in (2, 1, 0):
        part = known[k][...] - both_split(nn, links[k][...], found)
        out[pl.ds(k * PART, PART), :] = part.astype(BF16)
        found = jnp.concatenate([part, found], axis=0)


def eliminate(system, after=()):
    gram, right = system
    left = gram.shape[0] - PART
    shapes = [shape_of((PART, max(left, PART)), F32), shape_of((PART, D), F32)]
    if left:
        shapes += [shape_of((left, left), F32), shape_of((left, D), F32)]
    return call(
        eliminate_kernel, shapes, [VMEM] * 2, [VMEM] * len(shapes), flops=FLOPS["eliminate"], after=after
    )(gram, right)


def substitute(steps, after=()):
    links, known = [step[0] for step in steps[:-1]], [step[1] for step in steps]
    return call(substitute_kernel, shape_of((N, D)), [VMEM] * 7, VMEM, flops=FLOPS["substitute"], after=after)(*links, *known)


def block_offsets(x_first):
    for array in range(4):
        core, second = array // 2, array % 2
        for index in range(8):
            first, z = index // 4, index % 4
            x, f = (first, second) if x_first else (second, first)
            yield array, index, z, x, core, f


def position(place_ref, z, x, core, f):
    dp = (place_ref[0] ^ z) * 4 + (place_ref[1] ^ x) * 2 + (place_ref[2] ^ core)
    return dp, place_ref[3] ^ f


def aligned(index, size):
    return pl.ds(pl.multiple_of(index * size, size), size)


def start(source, target, sem):
    copy = pltpu.make_async_copy(source, target, sem)
    copy.start()
    return copy


def wait_all(copies):
    for copy in copies:
        copy.wait()


class Hops:
    def __init__(self, parts, x_first, columns, first=0):
        self.parts, self.x_first, self.columns, self.first = parts, x_first, columns, first
        self.rows = parts[0].shape[1]

    def block(self, refs, array, index, first, columns):
        return refs[array].at[index, :, pl.ds(self.first + first, columns)]

    def fetch(self, refs, place_ref, whole, sem):
        copies = []
        for array, index, z, x, core, f in block_offsets(self.x_first):
            dp, side = position(place_ref, z, x, core, f)
            target = whole.at[aligned(dp, self.rows), aligned(side, self.columns)]
            copies.append(start(self.block(refs, array, index, 0, self.columns), target, sem))
        return copies

    def fetch_columns(self, refs, place_ref, f, half, tile, sem):
        for array, index, z, x, core, side in block_offsets(self.x_first):
            if side == f:
                dp, _ = position(place_ref, z, x, core, f)
                start(self.block(refs, array, index, half * TILE, TILE), tile.at[aligned(dp, self.rows), :], sem)

    def fetch_rows(self, refs, place_ref, f, half, tile, sem):
        z = tile_at(place_ref, f, half) ^ place_ref[0]
        for array in range(4):
            core, x = array // 2, array % 2
            place = (x ^ place_ref[1]) * 2 + (core ^ place_ref[2])
            for other in (0, 1):
                target = tile.at[aligned(place, self.rows), aligned(other ^ place_ref[3], self.columns)]
                start(self.block(refs, array, other * 4 + z, 0, self.columns), target, sem)


class Whole:
    def __init__(self, array):
        self.parts = [array]

    def fetch(self, refs, place_ref, whole, sem):
        return [start(refs[0], whole, sem)]

    def fetch_columns(self, refs, place_ref, f, half, tile, sem):
        start(refs[0].at[:, pl.ds((2 * f + half) * TILE, TILE)], tile, sem)

    def fetch_rows(self, refs, place_ref, f, half, tile, sem):
        start(refs[0].at[pl.ds((2 * f + half) * TILE, TILE), :], tile, sem)


def tile_at(place_ref, f, half):
    return (f ^ place_ref[3]) * 2 + half


def await_tile(tile, sem):
    pltpu.make_async_copy(tile, tile, sem).wait()


EVERY_PLACE = tuple((dp // 4, (dp // 2) % 2, dp % 2) for dp in range(16))


class Blocks:
    def __init__(self, x_first, rows, columns):
        self.x_first, self.rows, self.columns = x_first, rows, columns
        self.shapes = [shape_of((2, 2, 4, rows, columns))] * 2

    def each(self, refs, place_ref, core_here, places, sides):
        z0, x0, f0 = place_ref[0], place_ref[1], place_ref[3]
        for n, (z, x, core) in enumerate(places):
            target = refs[0] if core == core_here else refs[1]
            for m, side in enumerate(sides):
                bits = (x ^ x0, side ^ f0) if self.x_first else (side ^ f0, x ^ x0)
                yield n, m, target.at[bits[0], bits[1], z ^ z0]

    def put(self, staged, refs, place_ref, sem, pieces, places=EVERY_PLACE, sides=(0, 1)):
        def send(core_here):
            for n, m, where in self.each(refs, place_ref, core_here, places, sides):
                for steps, offsets, first, columns in pieces:
                    rows = pl.ds(n * steps[0] + offsets[0], self.rows)
                    across = pl.ds(m * steps[1] + offsets[1], columns)
                    start(staged.at[rows, across], where.at[:, pl.ds(first, columns)], sem)

        pl.when(place_ref[2] == 0)(lambda: send(0))
        pl.when(place_ref[2] == 1)(lambda: send(1))

    def put_stacked(self, staged, refs, place_ref, sem, side, part):
        rows = self.rows // 4

        def send(core_here):
            for n, _, where in self.each(refs, place_ref, core_here, EVERY_PLACE, (side,)):
                for q in (0, 1):
                    source = staged.at[pl.ds(n * rows, rows), pl.ds(q * self.columns, self.columns)]
                    start(source, where.at[aligned(2 * part + q, rows), :], sem)

        pl.when(place_ref[2] == 0)(lambda: send(0))
        pl.when(place_ref[2] == 1)(lambda: send(1))

    def put_devices(self, staged, refs, place_ref, sem, first):
        def send(core_here):
            for n, m, where in self.each(refs, place_ref, core_here, EVERY_PLACE, (0, 1)):
                source = staged.at[pl.ds((2 * n + m) * self.rows, self.rows), :]
                start(source, where.at[:, pl.ds(first, staged.shape[1])], sem)

        pl.when(place_ref[2] == 0)(lambda: send(0))
        pl.when(place_ref[2] == 1)(lambda: send(1))


def spread_table(width, lanes):
    return (iota((PART, lanes), 0) == iota((PART, lanes), 1) % width).astype(BF16)


def vectors_kernel(place_ref, *refs):
    parts, (vec_ref, up_ref, table_ref, held, sem) = refs[:4], refs[4:]
    copies = []
    for array, index, z, x, core, f in block_offsets(False):
        dp, side = position(place_ref, z, x, core, f)
        first = parts[array].shape[2] - PART
        copies.append(start(parts[array].at[index, :, pl.ds(first, PART)], held.at[dp * 2 + side], sem))
    wait_all(copies)
    table_ref[...] = held[:, 16:32, :].reshape(512, PART)
    rows = held[:, :16, :].reshape(512, PART)
    device = iota((512, D), 0) // 16
    spread = nn(rows, spread_table(24, D))
    spread = jnp.where(iota((512, D), 1) // 24 == device, spread, 0.0)
    vec_ref[...] = jnp.sum(spread.reshape(32, 16, D), axis=0)
    wide = nn(rows, spread_table(96, D))
    wide = jnp.where(iota((512, D), 1) // 96 == device % 8, wide, 0.0)
    for t in range(4):
        group = wide[t * 128 : (t + 1) * 128, :].reshape(8, 16, D)
        up_ref[:, t * D : (t + 1) * D] = jnp.sum(group, axis=0)[8:16, :]


def gathered_vectors(place, mem_parts, after=()):
    return call(
        vectors_kernel,
        [shape_of((16, D), F32), shape_of((8, FF), F32), shape_of((N, PART))],
        [SMEM] + [HBM] * 4,
        [VMEM] * 3,
        [pltpu.VMEM((32, 48, PART), BF16), pltpu.SemaphoreType.DMA],
        flops=FLOPS["vectors"],
        after=after,
    )(place, *mem_parts)


def pack_vectors(vectors, up_grad):
    device, kind = iota((512, D), 0) // 16, iota((512, D), 0) % 16
    tiled = jnp.broadcast_to(vectors[None], (32, 16, D)).reshape(512, D)
    tiled = jnp.where((iota((512, D), 1) // 24 == device) & (kind < 8), tiled, 0.0).astype(BF16)
    ups = [jnp.broadcast_to(up_grad[0:1, t * D : (t + 1) * D], (128, D)) for t in range(4)]
    ups = jnp.concatenate(ups, axis=0)
    ups = jnp.where((iota((512, D), 1) // 96 == device % 8) & (kind == 8), ups, 0.0).astype(BF16)
    rows = nt(tiled, spread_table(24, D)) + nt(ups, spread_table(96, D))
    return padded_blocks(rows)


def padded_blocks(rows):
    rows = rows.astype(BF16).reshape(32, 16, PART)
    return jnp.concatenate([rows, jnp.zeros((32, 32, PART), BF16)], axis=1)


def head_mask(rows, lanes, heads):
    return iota((rows, lanes), 1) // DH == heads


def front_call(place, tokens, vectors, coeff, tables, proj, keys, values, after=()):
    weights = (proj, keys, values)
    counts = [len(w.parts) for w in weights]

    def kernel(place_ref, tokens_ref, vec_ref, coeff_ref, table_ref, *refs):
        sources, at = [], 0
        for count in counts:
            sources.append(refs[at : at + count])
            at += count
        normed_ref, projected_ref, mem_values_ref, reads_ref, proj_ref, keys_ref, values_ref, sems = refs[at:]
        held = (proj_ref, keys_ref, values_ref)
        copies = [w.fetch(s, place_ref, h, sems.at[n]) for n, (w, s, h) in enumerate(zip(weights, sources, held))]
        normed = normalise(tokens_ref[0].astype(F32), vec_ref[0:1, :], vec_ref[1:2, :]).astype(BF16)
        normed_ref[...] = normed
        summary = tn(table_ref[...], coeff_ref[...])[:32, :]
        wait_all(copies[1])
        reads = one_split(nn, summary, keys_ref[...])
        head = iota((32, D), 1) // DH
        kind = iota((32, D), 0)
        centre = jnp.sum(jnp.where(kind == head, reads, 0.0), axis=0, keepdims=True)
        spread = jnp.sum(jnp.where(kind == head + H, reads, 0.0), axis=0, keepdims=True)
        row = iota((8, D), 0)
        reads_ref[...] = jnp.where(row == 0, centre, jnp.where(row == 1, spread, 0.0))
        wait_all(copies[2])
        mem_values_ref[...] = nn(coeff_ref[...], values_ref[...]).astype(BF16)
        wait_all(copies[0])

        def block(n, bias):
            at = pl.ds(n * D, D)
            projected_ref[:, at] = (nn(normed_ref[...], proj_ref[:, at]) + bias).astype(BF16)

        block(0, vec_ref[2:3, :])
        block(1, 0.0)
        block(2, vec_ref[3:4, :])

    return call(
        kernel,
        [shape_of((512, D)), shape_of((512, 3 * D)), shape_of((N, D)), shape_of((8, D), F32)],
        [SMEM] + [VMEM] * 4 + [HBM] * sum(counts),
        [VMEM] * 4,
        [
            pltpu.VMEM((D, 3 * D), BF16),
            pltpu.VMEM((D, D), BF16),
            pltpu.VMEM((D, D), BF16),
            pltpu.SemaphoreType.DMA((3,)),
        ],
        flops=FLOPS["front"],
        vmem=28,
        after=after,
    )(place, tokens, vectors, coeff, tables, *proj.parts, *keys.parts, *values.parts)


READ = 256


def document_rows(length_ref):
    place = iota((1, 512), 1)
    first = jnp.zeros((1, 512), jnp.int32)
    end = jnp.int32(0)
    for n in range(length_ref.shape[1] - 1):
        end = end + length_ref[0, n]
        first = jnp.where(place >= end, end, first)
    return first


def mask_bias(length_ref, bias_ref):
    first = document_rows(length_ref)
    key, query = iota((512, 512), 0), iota((512, 512), 1)
    bias_ref[...] = jnp.where((key <= query) & (key >= first), 0.0, masked_fill)


def reading_row(length_ref, carried_ref):
    inside = iota((1, READ), 1) < length_ref[0, 0]
    return jnp.where(inside, carried_ref[0].astype(F32), 0.0)


def read_parameters(scaled, reads):
    lane_head = iota((1, PART), 1) // DH
    rows = [jnp.where(lane_head == h, reads[kind : kind + 1, :], 0.0) for kind in (0, 1) for h in (0, 1)]
    rows = jnp.concatenate(rows + [jnp.zeros((4, PART), F32)], axis=0)
    high, low = split(rows)
    lowest = (rows - high.astype(F32) - low.astype(F32)).astype(BF16)
    logits = nt(high, scaled) + (nt(low, scaled) + nt(lowest, scaled))
    found = []
    for h in (0, 1):
        centre = 1.0 / (1.0 + jnp.exp(-logits[h : h + 1, :]))
        raw = logits[2 + h : 3 + h, :]
        spread = spread_scale * (jnp.maximum(raw, 0.0) + jnp.log1p(jnp.exp(-jnp.abs(raw))))
        variance = 1.0 / (N * N) + spread * spread
        found.append((centre, spread, variance, raw))
    return rows, found


def basis_column():
    return (iota((N, 1), 0).astype(F32) + 0.5) / N


def density_of(centre, variance):
    distance = centre - basis_column()
    return lax.rsqrt(variance) / N * jnp.exp(distance * distance * (-0.5 / variance)), distance


def head_lanes(value, h):
    return jnp.where(iota((1, PART), 1) // DH == h, value, jnp.zeros_like(value))


def attend_kernel(length_ref, carried_ref, q_ref, k_ref, v_ref, mem_ref, reads_ref, out_ref, lse_ref, bias_ref):
    pl.when(pl.program_id(0) == 0)(lambda: mask_bias(length_ref, bias_ref))
    scaled = q_ref[...] * jnp.asarray(score_scale, BF16)
    outs, totals = [], []
    for h in (0, 1):
        halves, lse = [], []
        for first in (0, 256):
            keys = first + 256
            scores = nt(k_ref[:keys, :], head_lanes(scaled[first : first + 256, :], h))
            scores = scores + bias_ref[:keys, first : first + 256]
            top = jnp.max(scores, axis=0, keepdims=True)
            weights = jnp.exp(scores - top)
            total = jnp.sum(weights, axis=0, keepdims=True)
            probs = (weights * (1.0 / total)).astype(BF16)
            halves.append(tn(v_ref[:keys, :], probs)[h * DH : (h + 1) * DH, :])
            lse.append(top + jnp.log(total))
        outs.append(halves)
        totals.append(jnp.concatenate(lse, axis=1))
    lse_ref[...] = jnp.concatenate(totals + [jnp.zeros((6, 512), F32)], axis=0)
    _, found = read_parameters(scaled[:READ, :], reads_ref[...])
    reading = reading_row(length_ref, carried_ref)
    for h in (0, 1):
        centre, _, variance, _ = found[h]
        density, _ = density_of(centre, variance)
        recall = tn(mem_ref[...], density.astype(BF16))[h * DH : (h + 1) * DH, :]
        outs[h][0] = outs[h][0] + recall * reading
    for n in (0, 1):
        block = jnp.concatenate([outs[0][n], outs[1][n]], axis=0)
        out_ref[n * 256 : (n + 1) * 256, :] = jnp.transpose(block).astype(BF16)


def pair_block(shift=0):
    return pl.BlockSpec((512, PART), lambda i: (0, i + shift))


def attend_call(lengths, carried, projected, mem_values, reads, after=()):
    return call(
        attend_kernel,
        [shape_of((512, D)), shape_of((PAIRS * 8, 512), F32)],
        [SMEM, SMEM, pair_block(), pair_block(PAIRS), pair_block(2 * PAIRS), pair_block(), pl.BlockSpec((8, PART), lambda i: (0, i))],
        [pair_block(), pl.BlockSpec((8, 512), lambda i: (i, 0))],
        [pltpu.VMEM((512, 512), F32)],
        flops=FLOPS["attend"],
        after=after,
        grid=(PAIRS,),
    )(lengths, carried, projected, projected, projected, mem_values, reads)


def attend_back_kernel(length_ref, carried_ref, q_ref, k_ref, v_ref, lse_ref, heads_ref, more_ref, gq_ref, gk_ref, gv_ref, bias_ref):
    pl.when(pl.program_id(0) == 0)(lambda: mask_bias(length_ref, bias_ref))
    scaled = q_ref[...] * jnp.asarray(score_scale, BF16)
    keys, values, grad = k_ref[...], v_ref[...], heads_ref[...]
    lane_head = iota((1, PART), 1) // DH
    grad_queries, grad_keys, grad_values = [], [], []
    for h in (0, 1):
        parts = []
        gk, gv = [], []
        for first in (0, 256):
            last = first + 256
            own, own_grad = head_lanes(scaled[first:last, :], h), head_lanes(grad[first:last, :], h)
            scores = nt(keys[:last, :], own) + bias_ref[:last, first:last]
            probs = jnp.exp(scores - lse_ref[h : h + 1, first:last])
            grad_probs = nt(values[:last, :], own_grad)
            row_terms = jnp.sum(probs * grad_probs, axis=0, keepdims=True)
            grad_scores = (probs * (grad_probs - row_terms)).astype(BF16)
            gv.append(nn(probs.astype(BF16), grad[first:last, :]))
            gk.append(nn(grad_scores, scaled[first:last, :]))
            parts.append(tn(keys[:last, :], grad_scores)[h * DH : (h + 1) * DH, :])
        grad_queries.append(parts)
        grad_keys.append((gk[0] + gk[1][:256, :], gk[1][256:, :]))
        grad_values.append((gv[0] + gv[1][:256, :], gv[1][256:, :]))
    for n in (0, 1):
        at = slice(n * 256, (n + 1) * 256)
        gk_ref[at, :] = jnp.where(lane_head == 0, grad_keys[0][n], grad_keys[1][n]).astype(BF16)
        gv_ref[at, :] = jnp.where(lane_head == 0, grad_values[0][n], grad_values[1][n]).astype(BF16)
        block = jnp.concatenate([grad_queries[0][n], grad_queries[1][n]], axis=0)
        if n == 0:
            block = block + more_ref[...]
        gq_ref[at, :] = (jnp.transpose(block) * score_scale).astype(BF16)


def memory_read_back_kernel(length_ref, carried_ref, q_ref, mem_ref, reads_ref, heads_ref, more_ref, gmem_ref, sums_ref):
    scaled = q_ref[...] * jnp.asarray(score_scale, BF16)
    grad = heads_ref[...]
    lane_head = iota((1, PART), 1) // DH
    rows, found = read_parameters(scaled, reads_ref[...])
    reading = reading_row(length_ref, carried_ref)
    centre_grads, spread_grads, grad_mems = [], [], []
    for h in (0, 1):
        centre, spread, variance, raw = found[h]
        density, distance = density_of(centre, variance)
        own_grad = head_lanes(grad, h)
        grad_density = nt(mem_ref[...], own_grad) * reading
        grad_mems.append(nn((density * reading).astype(BF16), own_grad))
        weight = grad_density * density
        moment0 = jnp.sum(weight, axis=0, keepdims=True)
        weight = weight * distance
        moment1 = jnp.sum(weight, axis=0, keepdims=True)
        moment2 = jnp.sum(weight * distance, axis=0, keepdims=True)
        inverse = 1.0 / variance
        grad_variance = 0.5 * inverse * (moment2 * inverse - moment0)
        centre_grads.append(-moment1 * inverse * centre * (1.0 - centre))
        spread_grads.append(grad_variance * 2.0 * spread * spread_scale / (1.0 + jnp.exp(-raw)))
    gmem_ref[...] = (grad_mems[0] + grad_mems[1]).astype(BF16)
    logit_grads = jnp.concatenate(centre_grads + spread_grads + [jnp.zeros((4, READ), F32)], axis=0)
    sums = one_split(nn, logit_grads, scaled)
    centre_sum = jnp.where(lane_head == 0, sums[0:1, :], sums[1:2, :])
    spread_sum = jnp.where(lane_head == 0, sums[2:3, :], sums[3:4, :])
    sums_ref[...] = jnp.concatenate([centre_sum, spread_sum, jnp.zeros((6, PART), F32)], axis=0)
    more_ref[...] = both_split(tn, rows, logit_grads)


FEW = pl.BlockSpec((8, PART), lambda i: (0, i))


def memory_read_back_call(lengths, carried, projected, mem_values, reads, grad_heads, after=()):
    near = pl.BlockSpec((READ, PART), lambda i: (0, i))
    return call(
        memory_read_back_kernel,
        [shape_of((D, READ), F32), shape_of((N, D)), shape_of((8, D), F32)],
        [SMEM, SMEM, near, pair_block(), FEW, near],
        [pl.BlockSpec((PART, READ), lambda i: (i, 0)), pair_block(), FEW],
        flops=FLOPS["memory_read_back"],
        grid=(PAIRS,),
        after=after,
    )(lengths, carried, projected, mem_values, reads, grad_heads)


def attend_back_call(lengths, carried, projected, lse, grad_heads, more, first, count, after=()):
    def pair(shift):
        return pl.BlockSpec((512, PART), lambda i: (0, i + shift))

    return call(
        attend_back_kernel,
        [shape_of((512, count * PART))] * 3,
        [SMEM, SMEM, pair(first), pair(first + PAIRS), pair(first + 2 * PAIRS),
         pl.BlockSpec((8, 512), lambda i: (i + first, 0)), pair(first), pl.BlockSpec((PART, READ), lambda i: (i + first, 0))],
        [pair(0)] * 3,
        [pltpu.VMEM((512, 512), F32)],
        flops=FLOPS["attend_back"],
        grid=(count,),
        after=after,
    )(lengths, carried, projected, projected, projected, lse, grad_heads, more)


GELU_SCALE = 0.7978845608028654
GELU_CUBE = 0.044715


def column_tiles(step_columns):
    return pl.BlockSpec((512, step_columns), lambda t: (0, t))


def fixed(shape):
    return pl.BlockSpec(shape, lambda t: (0,) * len(shape), pipeline_mode=pl.Buffered(1))


def weight_refs(weights, refs):
    found, at = [], 0
    for weight in weights:
        found.append(refs[at : at + len(weight.parts)])
        at += len(weight.parts)
    return found, refs[at:]


def mlp_call(place, tokens, heads, cotangent, vectors, up_bias, out, up, down, down_blocks, up_blocks):
    weights = (out, up, down)
    steps = FF // TILE
    down_shapes = down_blocks.shapes if down_blocks else [shape_of((FF, D))]
    up_shapes = up_blocks.shapes if up_blocks else [shape_of((D, FF))]
    count = len(down_shapes)

    def kernel(place_ref, tokens_ref, heads_ref, cot_ref, vec_ref, bias_ref, *refs):
        sources, refs = weight_refs(weights, refs)
        result_ref, middle_ref, back_ref, line_ref = refs[:4]
        down_grads, up_grads, refs = refs[4 : 4 + count], refs[4 + count : 4 + 2 * count], refs[4 + 2 * count :]
        out_ref, up_ref, down_ref, normed_ref, total_ref, down_staged, up_staged, sem, up_sems, down_sems, grad_sems = refs
        step = pl.program_id(0)
        tile = tile_at(place_ref, step // 2, step % 2)
        side = (step // 2) ^ place_ref[3]

        @pl.when(step == 0)
        def _():
            copies = out.fetch(sources[0], place_ref, out_ref, sem)
            for n in range(steps):
                up.fetch_columns(sources[1], place_ref, n // 2, n % 2, up_ref.at[n], up_sems.at[n])
                down.fetch_rows(sources[2], place_ref, n // 2, n % 2, down_ref.at[n], down_sems.at[n])
            wait_all(copies)
            middle = tokens_ref[0].astype(F32) + nn(heads_ref[...], out_ref[...]) + vec_ref[4:5, :]
            middle_ref[...] = middle
            normed_ref[...] = normalise(middle, vec_ref[5:6, :], vec_ref[6:7, :]).astype(BF16)
            total_ref[...] = middle + vec_ref[7:8, :]
            back_ref[...] = jnp.zeros((512, D), F32)

        await_tile(up_ref.at[step], up_sems.at[step])
        await_tile(down_ref.at[step], down_sems.at[step])
        hidden = nn(normed_ref[...], up_ref[step]) + bias_ref[0:1, aligned(tile, TILE)]
        grad_active = nt(cot_ref[0], down_ref[step])
        square = hidden * hidden
        bent = jnp.tanh(GELU_SCALE * hidden * (1.0 + GELU_CUBE * square))
        half = 0.5 + 0.5 * bent
        active = (hidden * half).astype(BF16)
        slope = half + 0.5 * hidden * (1.0 - bent * bent) * (GELU_SCALE + 3.0 * GELU_SCALE * GELU_CUBE * square)
        grad_hidden = (grad_active * slope).astype(BF16)
        line = jnp.sum(grad_hidden.astype(F32), axis=0, keepdims=True)
        line_ref[:, aligned(tile, TILE)] = jnp.broadcast_to(line, (8, TILE))
        down_staged[step] = tn(active, cot_ref[0]).astype(BF16)
        total_ref[...] += nn(active, down_ref[step])
        up_staged[step] = tn(normed_ref[...], grad_hidden).astype(BF16)
        back_ref[...] += nt(grad_hidden, up_ref[step])
        if down_blocks:
            rows, columns = down_blocks.rows, down_blocks.columns
            down_pieces = [((rows, columns), (0, 0), 0, columns)]
            places = [(tile, x, core) for x in (0, 1) for core in (0, 1)]
            down_blocks.put(down_staged.at[step], down_grads, place_ref, grad_sems.at[0], down_pieces, places)
            part = step % 2
            up_blocks.put_stacked(up_staged.at[step], up_grads, place_ref, grad_sems.at[1], side, part)
        else:
            start(down_staged.at[step], down_grads[0].at[aligned(tile, TILE), :], grad_sems.at[0])
            start(up_staged.at[step], up_grads[0].at[:, aligned(tile, TILE)], grad_sems.at[1])

        @pl.when(step == steps - 1)
        def _():
            result_ref[0] = total_ref[...].astype(BF16)
            for n in range(steps):
                await_tile(down_staged.at[n], grad_sems.at[0])
                await_tile(up_staged.at[n], grad_sems.at[1])

    found = call(
        kernel,
        [shape_of((1, 512, D)), shape_of((512, D), F32), shape_of((512, D), F32), shape_of((8, FF), F32)]
        + down_shapes
        + up_shapes,
        [SMEM, fixed((1, 512, D)), fixed((512, D)), fixed((1, 512, D)), fixed((16, D)), fixed((8, FF))]
        + [HBM] * sum(len(w.parts) for w in weights),
        [fixed((1, 512, D)), fixed((512, D)), fixed((512, D)), fixed((8, FF))] + [HBM] * (2 * count),
        [
            pltpu.VMEM((D, D), BF16),
            pltpu.VMEM((steps, D, TILE), BF16),
            pltpu.VMEM((steps, TILE, D), BF16),
            pltpu.VMEM((512, D), BF16),
            pltpu.VMEM((512, D), F32),
            pltpu.VMEM((steps, TILE, D), BF16),
            pltpu.VMEM((steps, D, TILE), BF16),
            pltpu.SemaphoreType.DMA,
            pltpu.SemaphoreType.DMA((steps,)),
            pltpu.SemaphoreType.DMA((steps,)),
            pltpu.SemaphoreType.DMA((2,)),
        ],
        flops=FLOPS["mlp"],
        vmem=44,
        grid=(steps,),
    )(place, tokens, heads, cotangent, vectors, up_bias, *out.parts, *up.parts, *down.parts)
    return found[:4], found[4 : 4 + count], found[4 + count :]


def middle_back_call(place, cotangent, middle, grad_normed, vectors, heads, out, after=()):
    def kernel(place_ref, cot_ref, middle_ref, grad_ref, vec_ref, heads_ref, *refs):
        sources, refs = weight_refs((out,), refs)
        grad_middle_ref, grad_heads_ref, out_grad_ref, sums_ref, out_ref, sem = refs
        copies = out.fetch(sources[0], place_ref, out_ref, sem)
        cot = cot_ref[0].astype(F32)
        back, gain, shift = normalise_back(middle_ref[...], vec_ref[5:6, :], grad_ref[...])
        grad_middle = cot + back
        grad_middle_ref[...] = grad_middle
        attended = grad_middle.astype(BF16)
        bias = jnp.sum(attended.astype(F32), axis=0, keepdims=True)
        last = jnp.sum(cot, axis=0, keepdims=True)
        nothing = jnp.zeros((4, D), F32)
        sums_ref[...] = jnp.concatenate([nothing, bias, gain, shift, last, nothing, nothing], axis=0)
        wait_all(copies)
        grad_heads_ref[...] = nt(attended, out_ref[...]).astype(BF16)
        out_grad_ref[...] = tn(heads_ref[...], attended).astype(BF16)

    return call(
        kernel,
        [shape_of((512, D), F32), shape_of((512, D)), shape_of((D, D)), shape_of((16, D), F32)],
        [SMEM] + [VMEM] * 5 + [HBM] * len(out.parts),
        [VMEM] * 4,
        [pltpu.VMEM((D, D), BF16), pltpu.SemaphoreType.DMA],
        flops=FLOPS["middle_back"],
        vmem=56,
        after=after,
    )(place, cotangent, middle, grad_normed, vectors, heads, *out.parts)


def memory_back_call(place, coeff, grad_mem_values, tables, sums, out_grad, keys, blocks, after=()):
    shapes = blocks.shapes if blocks else [shape_of((D, D))] * 3

    def kernel(place_ref, coeff_ref, grad_values_ref, table_ref, sums_ref, out_grad_ref, *refs):
        sources, refs = weight_refs((keys,), refs)
        tables_ref = refs[0]
        grad_refs, (keys_ref, key_grad_ref, value_grad_ref, small_ref, sems) = refs[1 : 1 + len(shapes)], refs[1 + len(shapes) :]
        copies = keys.fetch(sources[0], place_ref, keys_ref, sems.at[0])
        staged = (out_grad_ref, key_grad_ref, value_grad_ref)

        def put(n):
            if not blocks:
                start(staged[n], grad_refs[n], sems.at[1 + n])
                return
            piece = ((blocks.rows, D // 2), (0, 0), n * (D // 2), D // 2)
            blocks.put(staged[n], grad_refs, place_ref, sems.at[1 + n], [piece])

        put(0)
        value_grad_ref[...] = tn(coeff_ref[...], grad_values_ref[...]).astype(BF16)
        put(2)
        head, kind = iota((32, D), 1) // DH, iota((32, D), 0)
        by_head = jnp.where(kind == head, sums_ref[0:1, :], jnp.where(kind == head + H, sums_ref[1:2, :], 0.0))
        summary = tn(coeff_ref[...], table_ref[...])[:, :32]
        key_grad_ref[...] = both_split(nn, summary, by_head).astype(BF16)
        put(1)
        wait_all(copies)
        high, low = split(by_head)
        wide = jnp.concatenate([high, low, jnp.zeros((PART - 64, D), BF16)], axis=0)
        reads = nt(keys_ref[...], wide)
        high, low = split(reads)
        found = nn(coeff_ref[...], high) + nn(coeff_ref[...], low)
        lane = iota((N, PART), 1)
        found = found + jnp.concatenate([found[:, 32:64], jnp.zeros((N, PART - 32), F32)], axis=1)
        found = jnp.where(lane < 2 * H, found, 0.0)
        tables_ref[...] = found
        if blocks:
            small_ref[...] = padded_blocks(found).reshape(small_ref.shape)
            blocks.put_devices(small_ref, grad_refs, place_ref, sems.at[4], 3 * D // 2)
            await_tile(small_ref, sems.at[4])
        else:
            small_ref[...] = jnp.zeros(small_ref.shape, BF16)
        for n in range(3):
            await_tile(staged[n], sems.at[1 + n])

    found = call(
        kernel,
        [shape_of((N, PART), F32)] + shapes,
        [SMEM] + [VMEM] * 5 + [HBM] * len(keys.parts),
        [VMEM] + [HBM] * len(shapes),
        [pltpu.VMEM((D, D), BF16)] * 3 + [pltpu.VMEM((32 * 48, PART), BF16), pltpu.SemaphoreType.DMA((5,))],
        flops=FLOPS["memory_back"],
        vmem=20,
        after=after,
    )(place, coeff, grad_mem_values, tables, sums, out_grad, *keys.parts)
    return found[0], found[1:]


def input_back_call(place, tokens, vectors, normed, grads, grad_middle, sums, up_bias_grad, proj, blocks, after=()):
    shapes = blocks.shapes if blocks else [shape_of((D, 3 * D)), shape_of((16, D), F32)]

    def kernel(place_ref, tokens_ref, vec_ref, normed_ref, middle_ref, sums_ref, up_ref, *refs):
        parts, refs = refs[: len(grads)], refs[len(grads) :]
        sources, refs = weight_refs((proj,), refs)
        result_ref, done_ref = refs[:2]
        done_ref[...] = jnp.zeros(done_ref.shape, F32)
        grad_refs, (proj_ref, staged_ref, small_ref, sems) = refs[2 : 2 + len(shapes)], refs[2 + len(shapes) :]
        copies = proj.fetch(sources[0], place_ref, proj_ref, sems.at[0])
        at = 0
        for part in parts:
            columns = part.shape[1]
            staged_ref[:, at : at + columns] = tn(normed_ref[...], part[...]).astype(BF16)
            at += columns
        if blocks:
            rows, side = blocks.rows, 3 * D // 2
            blocks.put(staged_ref, grad_refs, place_ref, sems.at[1], [((rows, side), (0, 0), 0, side)])
        else:
            start(staged_ref, grad_refs[0], sems.at[1])
        wait_all(copies)
        grad_normed, column_sums, at = jnp.zeros((512, D), F32), [], 0
        for part in parts:
            columns = part.shape[1]
            grad_normed = grad_normed + nt(part[...], proj_ref[:, at : at + columns])
            column_sums.append(jnp.sum(part[...].astype(F32), axis=0, keepdims=True))
            at += columns
        column_sums = jnp.concatenate(column_sums, axis=1)
        back, gain, shift = normalise_back(tokens_ref[0].astype(F32), vec_ref[0:1, :], grad_normed)
        result_ref[0] = middle_ref[...] + back
        vectors_grad = jnp.concatenate([gain, shift, column_sums[:, :D], column_sums[:, 2 * D :], sums_ref[4:16, :]], axis=0)
        if blocks:
            small_ref[...] = pack_vectors(vectors_grad, up_ref[...]).reshape(32 * rows, PART)

            blocks.put_devices(small_ref, grad_refs, place_ref, sems.at[2], side)
            await_tile(staged_ref, sems.at[1])
            await_tile(small_ref, sems.at[2])
        else:
            small_ref[...] = jnp.zeros(small_ref.shape, BF16)
            grad_refs[1][...] = vectors_grad
            pltpu.make_async_copy(staged_ref, grad_refs[0], sems.at[1]).wait()

    found = call(
        kernel,
        [shape_of((1, 512, D), F32), shape_of((8, PART), F32)] + shapes,
        [SMEM] + [VMEM] * (6 + len(grads)) + [HBM] * len(proj.parts),
        [VMEM] * 2 + ([HBM] * 2 if blocks else [HBM, VMEM]),
        [
            pltpu.VMEM((D, 3 * D), BF16),
            pltpu.VMEM((D, 3 * D), BF16),
            pltpu.VMEM((32 * 48, PART), BF16),
            pltpu.SemaphoreType.DMA((3,)),
        ],
        flops=FLOPS["input_back"],
        vmem=36,
        after=after,
    )(place, tokens, vectors, normed, grad_middle, sums, up_bias_grad, *grads, *proj.parts)
    return found[0], found[1], found[2:]


def hop(value, z=0, x=0, core=0, f=0):
    pairs = []
    for dp in range(16):
        for side in range(2):
            other = (((dp // 4) ^ z) * 4) + ((((dp // 2) % 2) ^ x) * 2) + ((dp % 2) ^ core)
            pairs.append((dp * 2 + side, other * 2 + (side ^ f)))
    return lax.ppermute(value, BOTH, pairs)


def z_hops(block):
    return [block] + [hop(block, z=k) for k in (1, 2, 3)]


def quads(pieces, cut, after, stacked=1):
    rows, columns = pieces[0].shape
    width = (columns - cut) // stacked

    def kernel(*refs):
        blocks, (left, right) = refs[:4], refs[4:]
        for k, block in enumerate(blocks):
            left[k] = block[:, :cut]
            for n in range(stacked):
                right[k, n * rows : (n + 1) * rows, :] = block[:, cut + n * width : cut + (n + 1) * width]

    shapes = [shape_of((4, rows, cut)), shape_of((4, stacked * rows, width))]
    return list(call(kernel, shapes, [VMEM] * 4, [VMEM] * 2, flops=FLOPS["pack"], after=after)(*pieces))


BITS = (dict(x=1), dict(f=1))


def joined(quads_here, nears, after):
    def kernel(*refs):
        for n in (0, 1):
            for m in (0, 1):
                refs[4 + n][pl.ds(4 * m, 4)] = refs[2 * m + n][...]

    shapes = [shape_of((8,) + quad.shape[1:]) for quad in quads_here]
    return list(call(kernel, shapes, [VMEM] * 4, [VMEM] * 2, flops=FLOPS["pack"], after=after)(*quads_here, *nears))


def once_there(arrays, after):
    count = len(arrays)

    def kernel(*refs):
        for n in range(count):
            refs[count + n][...] = refs[n][...]

    shapes = [shape_of(array.shape) for array in arrays]
    return call(kernel, shapes, [VMEM] * count, [VMEM] * count, flops=FLOPS["pack"], after=after)(*arrays)


def plus(a, b):
    return (a.astype(F32) + b.astype(F32)).astype(BF16)


def halves(kept, got):
    return plus(kept[1], got[1]), plus(kept[0], got[0])


def halves_after(pairs, after):
    widths = [kept.shape[-1] for kept, _ in pairs]

    def kernel(*refs):
        for bit, target in ((1, refs[-2]), (0, refs[-1])):
            at = 0
            for n, width in enumerate(widths):
                total = refs[2 * n][bit].astype(F32) + refs[2 * n + 1][bit].astype(F32)
                target[..., at : at + width] = total.astype(BF16)
                at += width

    shapes = [shape_of(pairs[0][0].shape[1:-1] + (sum(widths),))] * 2
    flat = [array for pair in pairs for array in pair]
    return call(kernel, shapes, [VMEM] * len(flat), [VMEM] * 2, flops=FLOPS["add"], after=after)(*flat)


def added(pairs, after=()):
    _, rows, columns = pairs[0][0].shape

    def kernel(*refs):
        targets = refs[-1], refs[-2]
        for n in range(len(pairs)):
            for k in range(4):
                total = refs[2 * n][k].astype(F32) + refs[2 * n + 1][k].astype(F32)
                target = targets[k % 2]
                target[k // 2, n * rows : (n + 1) * rows, :] = total.astype(target.dtype)

    shape = (2, len(pairs) * rows, columns)
    flat = [array for pair in pairs for array in pair]
    return call(kernel, [shape_of(shape), shape_of(shape, F32)], [VMEM] * len(flat), [VMEM] * 2, flops=FLOPS["add"], after=after)(*flat)


def between(own, got, after=()):
    def kernel(own_ref, got_ref, sent_ref, total_ref):
        total_ref[...] = own_ref[0] + got_ref[0].astype(F32)
        sent_ref[...] = (own_ref[1] + got_ref[1].astype(F32)).astype(BF16)

    shapes = [shape_of(own.shape[1:]), shape_of(own.shape[1:], F32)]
    return call(kernel, shapes, [VMEM] * 2, [VMEM] * 2, flops=FLOPS["add"], after=after)(own, got)


def cut_halves(kept, got, cut, after=()):
    def kernel(kept_ref, got_ref, *refs):
        for bit, targets in ((1, refs[:2]), (0, refs[2:])):
            left, right = (bit, slice(None)), (slice(None), bit)
            for target, bits, columns in zip(targets, (left, right), (slice(0, cut), slice(cut, None))):
                at = (*bits, slice(None), slice(None), columns)
                target[...] = (kept_ref[at].astype(F32) + got_ref[at].astype(F32)).astype(BF16)

    shapes = [shape_of(kept.shape[1:4] + (width,)) for width in (cut, kept.shape[4] - cut)] * 2
    found = call(kernel, shapes, [VMEM] * 2, [VMEM] * 4, flops=FLOPS["add"], after=after)(kept, got)
    return found[:2], found[2:]


def both_halves(kept, got, after=()):
    def kernel(*refs):
        for n in (0, 1):
            for bit, target in ((1, refs[4 + n]), (0, refs[6 + n])):
                target[...] = (refs[n][bit].astype(F32) + refs[2 + n][bit].astype(F32)).astype(BF16)

    shapes = [shape_of(array.shape[1:]) for array in kept] * 2
    found = call(kernel, shapes, [VMEM] * 4, [VMEM] * 4, flops=FLOPS["add"], after=after)(*kept, *got)
    return found[:2], found[2:]


def finish(own, got, outputs, after=()):
    def width(columns):
        return columns.stop - columns.start

    def kernel(own_ref, *refs):
        total = own_ref[...]
        for ref in refs[: len(got)]:
            total = total + ref[...].astype(F32)
        for target, pieces in zip(refs[len(got) :], outputs):
            at = 0
            for rows, columns in pieces:
                target[:, at : at + width(columns)] = total[rows, columns]
                at += width(columns)

    shapes = [
        shape_of((pieces[0][0].stop - pieces[0][0].start, sum(width(piece[1]) for piece in pieces)), F32)
        for pieces in outputs
    ]
    return call(
        kernel, shapes, [VMEM] * (1 + len(got)), [VMEM] * len(outputs), flops=FLOPS["add"], after=after
    )(own, *got)


def three_ways(pairs, after=()):
    rows, columns = pairs[0][0].shape[1], [kept.shape[2] for kept, _ in pairs]

    def kernel(*refs):
        targets = refs[-4:]
        at = 0
        for n, width in enumerate(columns):
            for k in range(4):
                total = refs[2 * n][k].astype(F32) + refs[2 * n + 1][k].astype(F32)
                targets[k][:, at : at + width] = total.astype(targets[k].dtype)
            at += width

    shapes = [shape_of((rows, sum(columns)), F32)] + [shape_of((rows, sum(columns)))] * 3
    flat = [array for pair in pairs for array in pair]
    return call(kernel, shapes, [VMEM] * len(flat), [VMEM] * 4, flops=FLOPS["add"], after=after)(*flat)


COLUMN_SPLIT = (2, 5, 7, 8, 13, 15)
VECTORS = (0, 1, 3, 4, 6, 11, 12, 16)


def gather_whole(shards):
    def whole(k, shard):
        near = lax.all_gather(shard, "fsdp", axis=1 if k in COLUMN_SPLIT else 0, tiled=True)
        return lax.all_gather(near, "dp", axis=0, tiled=True)

    found = [whole(k, shard) for k, shard in enumerate(shards)]
    vectors = jnp.stack([found[k].astype(F32) for k in VECTORS] + [jnp.zeros((D,), F32)] * 8)
    up_bias = jnp.broadcast_to(found[14].astype(F32)[None], (8, FF))
    tables = jnp.pad(jnp.concatenate([found[9], found[10]], axis=1), ((0, 0), (0, PART - 2 * H)))
    weights = {k: Whole(found[k]) for k in COLUMN_SPLIT}
    return weights, vectors, up_bias, tables


def scatter_whole(totals):
    def part(k, total):
        near = lax.psum_scatter(total.astype(BF16), "dp", scatter_dimension=0, tiled=True)
        return lax.psum_scatter(near, "fsdp", scatter_dimension=1 if k in COLUMN_SPLIT else 0, tiled=True).astype(F32)

    return [part(k, total) for k, total in enumerate(totals)]


def pack_early(shards):
    order = [2, 7, 8, 5, 9, 10, 14] + list(VECTORS)
    arrays = [shards[k] if shards[k].ndim == 2 else shards[k].reshape(1, -1) for k in order]
    rows, half = shards[5].shape

    def kernel(proj, keys, values, out, centre, spread, up_bias, *refs):
        vectors, early = refs[:-1], refs[-1]
        early[:, : 3 * half] = proj[...]
        early[:, 3 * half : 4 * half] = keys[...]
        early[:, 4 * half : 5 * half] = values[...]
        early[:, 5 * half : 6 * half] = out[...]
        lines = []
        for ref in list(vectors) + [up_bias]:
            line = ref[...].astype(F32)
            lines.append(jnp.concatenate([line, jnp.zeros((1, PART - line.shape[1]), F32)], axis=1))
        lines.append(jnp.zeros((16 - len(lines), PART), F32))
        tables = jnp.concatenate(
            [centre[...].astype(F32), spread[...].astype(F32), jnp.zeros((16, PART - 2 * H), F32)], axis=1
        )
        small = jnp.concatenate(lines + [tables, jnp.zeros((rows - 32, PART), F32)], axis=0)
        early[:, 6 * half :] = small.astype(BF16)

    return call(kernel, shape_of((rows, 6 * half + PART)), [VMEM] * len(arrays), VMEM, flops=FLOPS["pack"], vmem=56)(*arrays)


def pack_late(shards, after):
    rows, half = shards[5].shape

    def kernel(up, down, late):
        late[:, : 4 * half] = up[...]
        for q in range(4):
            late[:, (4 + q) * half : (5 + q) * half] = down[q * rows : (q + 1) * rows, :]

    return call(kernel, shape_of((rows, 8 * half)), [VMEM] * 2, VMEM, flops=FLOPS["pack"], after=after)(
        shards[13], shards[15]
    )


def local(
    mesh_sizes, tokens, context, past_coeffs, doc_lengths, carried, histogram, cotangent, *shards
):
    hops = mesh_sizes == (16, 2)
    dp = lax.axis_index("dp")
    place = jnp.stack([dp // 4, (dp // 2) % 2, dp % 2, lax.axis_index("fsdp")]).astype(jnp.int32)
    rows, half = shards[5].shape
    x_hop, f_hop = BITS
    if hops:
        early = z_hops(pack_early(shards))
        points, gram, right = memory_system(histogram, past_coeffs, context, after=[early[0]])
        early = quads(early, 3 * half, [gram])
        near = [hop(early[0], **x_hop), hop(early[1], **f_hop)]
        steps = [eliminate((gram, right), early)]
        late = z_hops(pack_late(shards, [steps[0][0]]))
        early = joined(early, near, [steps[0][0]])
        far = [hop(early[0], **f_hop), hop(early[1], **x_hop)]
        steps.append(eliminate(steps[0][2:], early))
        late = quads(late, 4 * half, [steps[1][0]], 4)
        late_near = [hop(late[0], **x_hop), hop(late[1], **f_hop)]
        steps.append(eliminate(steps[1][2:], late + far))
        pairs = once_there(early, [steps[2][0]])
        proj_parts, mem_parts = (
            [early[n], far[n], hop(pairs[n], core=1), hop(far[n], core=1)] for n in (0, 1)
        )
        steps.append(eliminate(steps[2][2:]))
        coeff = substitute(steps)
        late = joined(late, late_near, [coeff])
        late_far = [hop(late[0], **f_hop), hop(late[1], **x_hop)]
        late_core = [hop(part, core=1) for part in late]
        vectors, up_bias, tables = gathered_vectors(place, mem_parts)
        weights = {
            2: Hops(proj_parts, True, 3 * half),
            7: Hops(mem_parts, False, half),
            8: Hops(mem_parts, False, half, half),
            5: Hops(mem_parts, False, half, 2 * half),
        }
    else:
        late_core = []
        weights, vectors, up_bias, tables = gather_whole(shards)
        points, *system = memory_system(histogram, past_coeffs, context)
        steps = [eliminate(system)]
        while len(steps) < N // PART:
            steps.append(eliminate(steps[-1][2:]))
        coeff = substitute(steps)
    normed, projected, mem_values, reads = front_call(
        place, tokens, vectors, coeff, tables, weights[2], weights[7], weights[8], after=late_core
    )
    heads, lse = attend_call(doc_lengths, carried, projected, mem_values, reads)
    if hops:
        far_core = [hop(part, core=1) for part in once_there(late_far, [heads])]
        parts = [[late[n], late_far[n], late_core[n], far_core[n]] for n in (0, 1)]
        weights[13] = Hops(parts[0], True, 4 * half)
        weights[15] = Hops(parts[1], False, half)
    down_blocks = Blocks(False, 4 * rows, half) if hops else None
    up_blocks = Blocks(True, 4 * rows, half) if hops else None
    (result, middle, grad_normed_mlp, grad_up_bias), down_grad, up_grad = mlp_call(
        place, tokens, heads, cotangent, vectors, up_bias, weights[5], weights[13], weights[15], down_blocks, up_blocks
    )
    waits = {"read": [], "second": [], "input": []}
    grad_middle, grad_heads, grad_out, sums = middle_back_call(
        place, cotangent, middle, grad_normed_mlp, vectors, heads, weights[5]
    )
    if hops:
        got_down, got_up = hop(down_grad[1], core=1), hop(up_grad[1], core=1)
        sent_down, kept_down = halves_after([(down_grad[0], got_down)], [sums])
        got_down = hop(sent_down, **f_hop)
        sent_up, kept_up = halves_after([(up_grad[0], got_up)], [sent_down])
        waits["read"] = [sent_up]
        got_up = hop(sent_up, **x_hop)
    more, grad_mem, read_sums = memory_read_back_call(
        doc_lengths, carried, projected, mem_values, reads, grad_heads, after=waits["read"]
    )
    width = 3 * half + PART
    cut = width // 2
    mem_blocks = Blocks(True, rows, width) if hops else None
    grad_tables, mem_grad = memory_back_call(
        place, coeff, grad_mem, tables, read_sums, grad_out, weights[7], mem_blocks
    )
    first = attend_back_call(doc_lengths, carried, projected, lse, grad_heads, more, 0, PAIRS // 2, after=[grad_tables])
    if hops:
        got_mem = hop(mem_grad[1], core=1)
        sent_mem, kept_mem = cut_halves(mem_grad[0], got_mem, cut, list(first[:1]))
        waits["second"] = list(sent_mem)
        got_mem = [hop(sent_mem[0], **x_hop), hop(sent_mem[1], **f_hop)]
    second = attend_back_call(
        doc_lengths, carried, projected, lse, grad_heads, more, PAIRS // 2, PAIRS // 2, after=waits["second"]
    )
    if hops:
        (sent_down, sent_up), kept_early = both_halves([kept_down, kept_up], [got_down, got_up], list(second[:1]))
        waits["input"] = [sent_down, sent_up]
        got_early = [hop(sent_down, **x_hop), hop(sent_up, **f_hop)]
    grads = [part for pair in zip(first, second) for part in pair]
    proj_blocks = Blocks(True, rows, width) if hops else None
    grad_tokens, done, proj_grad = input_back_call(
        place, tokens, vectors, normed, grads, grad_middle, sums, grad_up_bias, weights[2], proj_blocks,
        after=waits["input"],
    )
    if hops:
        got = hop(proj_grad[1], core=1)
        sent_mem, kept_mem = both_halves(kept_mem, got_mem, [done])
        got_mem = [hop(sent_mem[0], **f_hop), hop(sent_mem[1], **x_hop)]
        sent_early, own_early = added(list(zip(kept_early, got_early)), list(sent_mem))
        got_early = hop(sent_early, z=1)
        sent, kept = cut_halves(proj_grad[0], got, cut, [sent_early])
        got = [hop(sent[0], **x_hop), hop(sent[1], **f_hop)]
        sent_early, own_early = between(own_early, got_early, list(sent))
        got_early = hop(sent_early, z=2)
        sent, kept = both_halves(kept, got, [sent_early])
        got = [hop(sent[0], **f_hop), hop(sent[1], **x_hop)]
        sent_mem, own_mem = added(list(zip(kept_mem, got_mem)), list(sent))
        got_mem = hop(sent_mem, z=1)
        own, *sent = three_ways(list(zip(kept, got)), [sent_mem])
        got = [hop(part, z=k) for k, part in zip((1, 2, 3), sent)]
        sent_mem, own_mem = between(own_mem, got_mem, sent)
        got_mem = hop(sent_mem, z=2)
        every, below, quarter = slice(0, rows), slice(rows, 2 * rows), slice(0, half)
        outputs = [[(slice(0, 4 * rows), quarter)], [(slice((4 + q) * rows, (5 + q) * rows), quarter) for q in range(4)]]
        summed = {}
        summed[15], summed[13] = finish(own_early, [got_early], outputs, [sent_mem])
        outputs = [[(every, slice(0, half))], [(every, slice(half, cut)), (below, slice(0, 2 * half - cut))]]
        outputs += [[(below, slice(2 * half - cut, 3 * half - cut))]]
        first_table = 3 * half - cut
        outputs += [
            [(slice(rows, rows + 16), slice(first_table + n * H, first_table + (n + 1) * H))] for n in (0, 1)
        ]
        mem_outputs = outputs
        ends = [shards[k].shape[0] for k in VECTORS] + [shards[14].shape[0]]
        outputs = [[(every, slice(0, 3 * half))]]
        outputs += [[(slice(n, n + 1), slice(3 * half, 3 * half + end))] for n, end in enumerate(ends)]
        summed[2], *lines = finish(own, got, outputs, [summed[15]])
        summed[5], summed[7], summed[8], summed[9], summed[10] = finish(own_mem, [got_mem], mem_outputs, lines[:1])
        for k, line in zip(VECTORS + (14,), lines):
            summed[k] = line.reshape(-1)
    else:
        totals = {13: up_grad[0], 15: down_grad[0], 2: proj_grad[0], 14: grad_up_bias[0]}
        totals[5], totals[7], totals[8] = mem_grad
        totals[9], totals[10] = grad_tables[:, :H], grad_tables[:, H : 2 * H]
        for n, k in enumerate(VECTORS):
            totals[k] = proj_grad[1][n]
        summed = scatter_whole([totals[k] for k in range(17)])
    return (result, grad_tokens, *(summed[k] for k in range(17)), points)


def solution(mesh):
    both, row, table = P(BOTH), P("dp", "fsdp"), P(BOTH, None)
    block = P(BOTH, None, None)
    weights = (
        both, both, row, both, both, row, both, row, row, table, table, both, both, row, both, row, both,
    )
    in_specs = (block, block, block, table, both, table, block) + weights
    out_specs = (block, block) + weights + (table,)
    sizes = (mesh.shape["dp"], mesh.shape["fsdp"])
    return jax.shard_map(
        functools.partial(local, sizes), mesh=mesh, in_specs=in_specs, out_specs=out_specs, check_vma=False
    )
```

```python
import functools

import jax
import jax.numpy as jnp
from jax import lax
from jax.experimental import pallas as pl
from jax.experimental.pallas import tpu as pltpu
from jax.sharding import PartitionSpec as P

H = 12
DH = 64
D = H * DH
N = 512
CTX = 1024
M = 512
NBINS = 64
FF = 4 * D
PAIRS = H // 2
PART = 128
TILE = 768

memory_tau = 0.75
ridge_weight = 1.0
norm_epsilon = 1e-05
spread_scale = 0.25
masked_fill = -1e30
score_scale = DH ** (-0.5)

F32, BF16 = jnp.float32, jnp.bfloat16
MIB = 1024 * 1024
BOTH = ("dp", "fsdp")
HBM = pl.BlockSpec(memory_space=pl.ANY)
SMEM = pl.BlockSpec(memory_space=pltpu.SMEM)
VMEM = pl.BlockSpec(memory_space=pltpu.VMEM)


FLOPS = {
    "pack": 1, "system": 8, "eliminate": 5, "substitute": 2, "vectors": 2, "front": 7, "attend": 14, "mlp": 26,
    "middle_back": 4, "memory_read_back": 7, "memory_back": 7, "attend_back": 7, "attend_rest": 1, "input_back": 11,
    "add": 10,
}
FLOPS = {name: work * 20000_000_000 for name, work in FLOPS.items()}


def shape_of(shape, dtype=BF16):
    return jax.ShapeDtypeStruct(shape, dtype)


def call(kernel, out_shape, in_specs, out_specs, scratch=(), flops=0, grid=None, after=(), vmem=20):
    extra = {} if grid is None else {"grid": grid}
    inputs, unread = len(in_specs), len(after)

    def body(*refs):
        kernel(*refs[:inputs], *refs[inputs + unread :])

    run = pl.pallas_call(
        body,
        out_shape=out_shape,
        in_specs=list(in_specs) + [HBM] * unread,
        out_specs=out_specs,
        scratch_shapes=list(scratch),
        compiler_params=pltpu.CompilerParams(vmem_limit_bytes=vmem * MIB),
        cost_estimate=pl.CostEstimate(flops=flops, bytes_accessed=0, transcendentals=0),
        **extra,
    )
    return lambda *operands: run(*operands, *after)


def nn(a, b):
    return lax.dot_general(a, b, (((1,), (0,)), ((), ())), preferred_element_type=F32)


def nt(a, b):
    return lax.dot_general(a, b, (((1,), (1,)), ((), ())), preferred_element_type=F32)


def tn(a, b):
    return lax.dot_general(a, b, (((0,), (0,)), ((), ())), preferred_element_type=F32)


def split(value):
    high = value.astype(BF16)
    return high, (value - high.astype(F32)).astype(BF16)


def both_split(product, a, b):
    a_high, a_low = split(a)
    b_high, b_low = split(b)
    return product(a_high, b_high) + (product(a_high, b_low) + product(a_low, b_high))


def one_split(product, a, b):
    a_high, a_low = split(a)
    return product(a_high, b) + product(a_low, b)


def iota(shape, axis):
    return lax.broadcasted_iota(jnp.int32, shape, axis)


def gaussian(points, centres):
    distance = points - centres
    return jnp.exp(-0.5 * distance * distance * (N * N))


def normalise(values, gain, shift):
    mean = jnp.mean(values, axis=-1, keepdims=True)
    centred = values - mean
    variance = jnp.mean(centred * centred, axis=-1, keepdims=True)
    inverse = lax.rsqrt(variance + norm_epsilon)
    return centred * inverse * gain + shift


def normalise_back(values, gain, grad):
    mean = jnp.mean(values, axis=-1, keepdims=True)
    centred = values - mean
    variance = jnp.mean(centred * centred, axis=-1, keepdims=True)
    inverse = lax.rsqrt(variance + norm_epsilon)
    standard = centred * inverse
    scaled = grad * gain
    first = jnp.mean(scaled, axis=-1, keepdims=True)
    second = jnp.mean(scaled * standard, axis=-1, keepdims=True)
    back = inverse * (scaled - first - standard * second)
    return back, jnp.sum(grad * standard, axis=0, keepdims=True), jnp.sum(grad, axis=0, keepdims=True)


def system_kernel(hist_ref, past_ref, context_ref, points_ref, gram_ref, right_ref):
    hist = hist_ref[...]
    counts = jnp.broadcast_to(hist, (NBINS, NBINS))
    row, column = iota((NBINS, NBINS), 0), iota((NBINS, NBINS), 1)

    def down(keep):
        return jnp.sum(jnp.where(keep, counts, 0), axis=1, keepdims=True)

    ends, starts, count = down(column <= row), down(column < row), down(column == row)
    slot = iota((NBINS, M), 1)
    inside = (slot >= starts) & (slot < ends)

    def across(values):
        return jnp.sum(jnp.where(inside, values, 0), axis=0, keepdims=True)

    first, amount, number = across(starts), across(count), across(iota((NBINS, M), 0))
    offset = (iota((1, M), 1) - first).astype(F32) + 0.5
    points = (number.astype(F32) + offset / amount.astype(F32)) / NBINS
    points_ref[...] = points
    upright = jnp.sum(
        jnp.where(iota((M, M), 0) == iota((M, M), 1), points, 0.0), axis=1, keepdims=True
    )
    centre_row = (iota((1, N), 1).astype(F32) + 0.5) / N
    centre_column = (iota((N, 1), 0).astype(F32) + 0.5) / N
    past_values = one_split(nn, gaussian(upright, centre_row), past_ref[0])
    recent = memory_tau + (1.0 - memory_tau) * (iota((1, CTX), 1).astype(F32) + 0.5) / CTX
    old = gaussian(memory_tau * points, centre_column)
    new = gaussian(recent, centre_column)
    right_ref[...] = both_split(nn, old, past_values) + one_split(nn, new, context_ref[0])
    eye = (iota((N, N), 0) == iota((N, N), 1)).astype(F32) * ridge_weight
    gram_ref[...] = both_split(nt, old, old) + both_split(nt, new, new) + eye


def memory_system(histogram, past, context, after=()):
    return call(
        system_kernel,
        [shape_of((1, M), F32), shape_of((N, N), F32), shape_of((N, D), F32)],
        [VMEM] * 3,
        [VMEM] * 3,
        flops=FLOPS["system"],
        vmem=24,
        after=after,
    )(histogram, past, context)


PANEL = 16


def three(value):
    high = value.astype(BF16)
    rest = value - high.astype(F32)
    middle = rest.astype(BF16)
    return high, middle, (rest - middle.astype(F32)).astype(BF16)


def small_inverse(m):
    def minor(r0, r1, c0, c1):
        return m[r0][c0] * m[r1][c1] - m[r0][c1] * m[r1][c0]

    places = ((0, 1), (0, 2), (0, 3), (1, 2), (1, 3), (2, 3))
    s = [minor(0, 1, *place) for place in places]
    c = [minor(2, 3, *place) for place in places]
    total = ((s[0] * c[5] - s[1] * c[4]) + (s[2] * c[3] + s[3] * c[2])) + (s[5] * c[0] - s[4] * c[1])
    r = 1.0 / total
    q = [[None] * 4 for _ in range(4)]
    q[0][0] = (m[1][1] * c[5] - m[1][2] * c[4] + m[1][3] * c[3]) * r
    q[0][1] = (m[0][2] * c[4] - m[0][1] * c[5] - m[0][3] * c[3]) * r
    q[0][2] = (m[3][1] * s[5] - m[3][2] * s[4] + m[3][3] * s[3]) * r
    q[0][3] = (m[2][2] * s[4] - m[2][1] * s[5] - m[2][3] * s[3]) * r
    q[1][1] = (m[0][0] * c[5] - m[0][2] * c[2] + m[0][3] * c[1]) * r
    q[1][2] = (m[3][2] * s[2] - m[3][0] * s[5] - m[3][3] * s[1]) * r
    q[1][3] = (m[2][0] * s[5] - m[2][2] * s[2] + m[2][3] * s[1]) * r
    q[2][2] = (m[3][0] * s[4] - m[3][1] * s[2] + m[3][3] * s[0]) * r
    q[2][3] = (m[2][1] * s[2] - m[2][0] * s[4] - m[2][3] * s[0]) * r
    q[3][3] = (m[2][0] * s[3] - m[2][1] * s[1] + m[2][2] * s[0]) * r
    for i in range(4):
        for j in range(i):
            q[i][j] = q[j][i]
    return q


def inverse_of(block):
    row, column = iota((PANEL, PART), 0), iota((PANEL, PART), 1)
    lane = iota((PART, PART), 1)
    work = block
    for k in range(0, PART, PANEL):
        panel = work[k : k + PANEL, :]
        left = jnp.where(column < k, -panel, jnp.where(column < k + PANEL, 0.0, panel))
        for s in range(0, PANEL, 4):
            at = k + s
            columns = [jnp.broadcast_to(panel[:, at + i : at + i + 1], (PANEL, PART)) for i in range(4)]
            lines = [
                jnp.where(
                    (column[:1] >= at) & (column[:1] < at + 4),
                    (column[:1] == at + i).astype(F32),
                    panel[s + i : s + i + 1, :],
                )
                for i in range(4)
            ]
            inverse = small_inverse([[columns[j][s + i : s + i + 1, :] for j in range(4)] for i in range(4)])
            inside = (row >= s) & (row < s + 4)
            panel = jnp.where(inside | ((column >= at) & (column < at + 4)), 0.0, panel)
            for i in range(4):
                line = (inverse[i][0] * lines[0] + inverse[i][1] * lines[1]) + (
                    inverse[i][2] * lines[2] + inverse[i][3] * lines[3]
                )
                panel = panel - jnp.where(inside, jnp.where(row == s + i, -1.0, 0.0), columns[i]) * line
        u, w = three(left), three(panel)
        update = tn(
            jnp.concatenate([u[0], u[0], u[1], u[0], u[2], u[1]], axis=0),
            jnp.concatenate([w[0], w[1], w[0], w[2], w[0], w[1]], axis=0),
        )
        others = jnp.where((lane >= k) & (lane < k + PANEL), 0.0, work) - update
        above = [others[:k, :]] if k else []
        below = [others[k + PANEL :, :]] if k + PANEL < PART else []
        work = jnp.concatenate(above + [panel] + below, axis=0)
    return work


def eliminate_kernel(gram_ref, right_ref, link_ref, known_ref, *rest):
    inverse = inverse_of(gram_ref[:PART, :PART])
    top = right_ref[:PART, :]
    known_ref[...] = both_split(nn, inverse, top)
    if rest:
        next_gram_ref, next_right_ref = rest
        beside = gram_ref[:PART, PART:]
        link = both_split(nn, inverse, beside)
        link_ref[...] = link
        next_gram_ref[...] = gram_ref[PART:, PART:] - both_split(tn, beside, link)
        next_right_ref[...] = right_ref[PART:, :] - both_split(tn, link, top)
    else:
        link_ref[...] = jnp.zeros(link_ref.shape, F32)


def substitute_kernel(*refs):
    links, known, out = refs[:3], refs[3:7], refs[7]
    found = known[3][...]
    out[pl.ds(3 * PART, PART), :] = found.astype(BF16)
    for k in (2, 1, 0):
        part = known[k][...] - both_split(nn, links[k][...], found)
        out[pl.ds(k * PART, PART), :] = part.astype(BF16)
        found = jnp.concatenate([part, found], axis=0)


def eliminate(system, after=()):
    gram, right = system
    left = gram.shape[0] - PART
    shapes = [shape_of((PART, max(left, PART)), F32), shape_of((PART, D), F32)]
    if left:
        shapes += [shape_of((left, left), F32), shape_of((left, D), F32)]
    return call(
        eliminate_kernel, shapes, [VMEM] * 2, [VMEM] * len(shapes), flops=FLOPS["eliminate"], after=after
    )(gram, right)


def substitute(steps, after=()):
    links, known = [step[0] for step in steps[:-1]], [step[1] for step in steps]
    return call(substitute_kernel, shape_of((N, D)), [VMEM] * 7, VMEM, flops=FLOPS["substitute"], after=after)(*links, *known)


def block_offsets(x_first):
    for array in range(4):
        core, second = array // 2, array % 2
        for index in range(8):
            first, z = index // 4, index % 4
            x, f = (first, second) if x_first else (second, first)
            yield array, index, z, x, core, f


def position(place_ref, z, x, core, f):
    dp = (place_ref[0] ^ z) * 4 + (place_ref[1] ^ x) * 2 + (place_ref[2] ^ core)
    return dp, place_ref[3] ^ f


def aligned(index, size):
    return pl.ds(pl.multiple_of(index * size, size), size)


def start(source, target, sem):
    copy = pltpu.make_async_copy(source, target, sem)
    copy.start()
    return copy


def wait_all(copies):
    for copy in copies:
        copy.wait()


class Hops:
    def __init__(self, parts, x_first, columns, first=0):
        self.parts, self.x_first, self.columns, self.first = parts, x_first, columns, first
        self.rows = parts[0].shape[1]

    def block(self, refs, array, index, first, columns):
        return refs[array].at[index, :, pl.ds(self.first + first, columns)]

    def fetch(self, refs, place_ref, whole, sem):
        copies = []
        for array, index, z, x, core, f in block_offsets(self.x_first):
            dp, side = position(place_ref, z, x, core, f)
            target = whole.at[aligned(dp, self.rows), aligned(side, self.columns)]
            copies.append(start(self.block(refs, array, index, 0, self.columns), target, sem))
        return copies

    def fetch_columns(self, refs, place_ref, f, half, tile, sem):
        for array, index, z, x, core, side in block_offsets(self.x_first):
            if side == f:
                dp, _ = position(place_ref, z, x, core, f)
                start(self.block(refs, array, index, half * TILE, TILE), tile.at[aligned(dp, self.rows), :], sem)

    def fetch_rows(self, refs, place_ref, f, half, tile, sem):
        z = tile_at(place_ref, f, half) ^ place_ref[0]
        for array in range(4):
            core, x = array // 2, array % 2
            place = (x ^ place_ref[1]) * 2 + (core ^ place_ref[2])
            for other in (0, 1):
                target = tile.at[aligned(place, self.rows), aligned(other ^ place_ref[3], self.columns)]
                start(self.block(refs, array, other * 4 + z, 0, self.columns), target, sem)


class Whole:
    def __init__(self, array):
        self.parts = [array]

    def fetch(self, refs, place_ref, whole, sem):
        return [start(refs[0], whole, sem)]

    def fetch_columns(self, refs, place_ref, f, half, tile, sem):
        start(refs[0].at[:, pl.ds((2 * f + half) * TILE, TILE)], tile, sem)

    def fetch_rows(self, refs, place_ref, f, half, tile, sem):
        start(refs[0].at[pl.ds((2 * f + half) * TILE, TILE), :], tile, sem)


def tile_at(place_ref, f, half):
    return (f ^ place_ref[3]) * 2 + half


def await_tile(tile, sem):
    pltpu.make_async_copy(tile, tile, sem).wait()


EVERY_PLACE = tuple((dp // 4, (dp // 2) % 2, dp % 2) for dp in range(16))


class Blocks:
    def __init__(self, x_first, rows, columns):
        self.x_first, self.rows, self.columns = x_first, rows, columns
        self.shapes = [shape_of((2, 2, 4, rows, columns))] * 2

    def each(self, refs, place_ref, core_here, places, sides):
        z0, x0, f0 = place_ref[0], place_ref[1], place_ref[3]
        for n, (z, x, core) in enumerate(places):
            target = refs[0] if core == core_here else refs[1]
            for m, side in enumerate(sides):
                bits = (x ^ x0, side ^ f0) if self.x_first else (side ^ f0, x ^ x0)
                yield n, m, target.at[bits[0], bits[1], z ^ z0]

    def put(self, staged, refs, place_ref, sem, pieces, places=EVERY_PLACE, sides=(0, 1)):
        def send(core_here):
            for n, m, where in self.each(refs, place_ref, core_here, places, sides):
                for steps, offsets, first, columns in pieces:
                    rows = pl.ds(n * steps[0] + offsets[0], self.rows)
                    across = pl.ds(m * steps[1] + offsets[1], columns)
                    start(staged.at[rows, across], where.at[:, pl.ds(first, columns)], sem)

        pl.when(place_ref[2] == 0)(lambda: send(0))
        pl.when(place_ref[2] == 1)(lambda: send(1))

    def put_stacked(self, staged, refs, place_ref, sem, side, part):
        rows = self.rows // 4

        def send(core_here):
            for n, _, where in self.each(refs, place_ref, core_here, EVERY_PLACE, (side,)):
                for q in (0, 1):
                    source = staged.at[pl.ds(n * rows, rows), pl.ds(q * self.columns, self.columns)]
                    start(source, where.at[aligned(2 * part + q, rows), :], sem)

        pl.when(place_ref[2] == 0)(lambda: send(0))
        pl.when(place_ref[2] == 1)(lambda: send(1))

    def put_devices(self, staged, refs, place_ref, sem, first):
        def send(core_here):
            for n, m, where in self.each(refs, place_ref, core_here, EVERY_PLACE, (0, 1)):
                source = staged.at[pl.ds((2 * n + m) * self.rows, self.rows), :]
                start(source, where.at[:, pl.ds(first, staged.shape[1])], sem)

        pl.when(place_ref[2] == 0)(lambda: send(0))
        pl.when(place_ref[2] == 1)(lambda: send(1))


def spread_table(width, lanes):
    return (iota((PART, lanes), 0) == iota((PART, lanes), 1) % width).astype(BF16)


def vectors_kernel(place_ref, *refs):
    parts, (vec_ref, up_ref, table_ref, held, sem) = refs[:4], refs[4:]
    copies = []
    for array, index, z, x, core, f in block_offsets(False):
        dp, side = position(place_ref, z, x, core, f)
        first = parts[array].shape[2] - PART
        copies.append(start(parts[array].at[index, :, pl.ds(first, PART)], held.at[dp * 2 + side], sem))
    wait_all(copies)
    table_ref[...] = held[:, 16:32, :].reshape(512, PART)
    rows = held[:, :16, :].reshape(512, PART)
    device = iota((512, D), 0) // 16
    spread = nn(rows, spread_table(24, D))
    spread = jnp.where(iota((512, D), 1) // 24 == device, spread, 0.0)
    vec_ref[...] = jnp.sum(spread.reshape(32, 16, D), axis=0)
    wide = nn(rows, spread_table(96, D))
    wide = jnp.where(iota((512, D), 1) // 96 == device % 8, wide, 0.0)
    for t in range(4):
        group = wide[t * 128 : (t + 1) * 128, :].reshape(8, 16, D)
        up_ref[:, t * D : (t + 1) * D] = jnp.sum(group, axis=0)[8:16, :]


def gathered_vectors(place, mem_parts, after=()):
    return call(
        vectors_kernel,
        [shape_of((16, D), F32), shape_of((8, FF), F32), shape_of((N, PART))],
        [SMEM] + [HBM] * 4,
        [VMEM] * 3,
        [pltpu.VMEM((32, 48, PART), BF16), pltpu.SemaphoreType.DMA],
        flops=FLOPS["vectors"],
        after=after,
    )(place, *mem_parts)


def pack_vectors(vectors, up_grad):
    device, kind = iota((512, D), 0) // 16, iota((512, D), 0) % 16
    tiled = jnp.broadcast_to(vectors[None], (32, 16, D)).reshape(512, D)
    tiled = jnp.where((iota((512, D), 1) // 24 == device) & (kind < 8), tiled, 0.0).astype(BF16)
    ups = [jnp.broadcast_to(up_grad[0:1, t * D : (t + 1) * D], (128, D)) for t in range(4)]
    ups = jnp.concatenate(ups, axis=0)
    ups = jnp.where((iota((512, D), 1) // 96 == device % 8) & (kind == 8), ups, 0.0).astype(BF16)
    rows = nt(tiled, spread_table(24, D)) + nt(ups, spread_table(96, D))
    return padded_blocks(rows)


def padded_blocks(rows):
    rows = rows.astype(BF16).reshape(32, 16, PART)
    return jnp.concatenate([rows, jnp.zeros((32, 32, PART), BF16)], axis=1)


def head_mask(rows, lanes, heads):
    return iota((rows, lanes), 1) // DH == heads


def front_call(place, tokens, vectors, coeff, tables, proj, keys, values, after=()):
    weights = (proj, keys, values)
    counts = [len(w.parts) for w in weights]

    def kernel(place_ref, tokens_ref, vec_ref, coeff_ref, table_ref, *refs):
        sources, at = [], 0
        for count in counts:
            sources.append(refs[at : at + count])
            at += count
        normed_ref, projected_ref, mem_values_ref, reads_ref, proj_ref, keys_ref, values_ref, sems = refs[at:]
        held = (proj_ref, keys_ref, values_ref)
        copies = [w.fetch(s, place_ref, h, sems.at[n]) for n, (w, s, h) in enumerate(zip(weights, sources, held))]
        normed = normalise(tokens_ref[0].astype(F32), vec_ref[0:1, :], vec_ref[1:2, :]).astype(BF16)
        normed_ref[...] = normed
        summary = tn(table_ref[...], coeff_ref[...])[:32, :]
        wait_all(copies[1])
        reads = one_split(nn, summary, keys_ref[...])
        head = iota((32, D), 1) // DH
        kind = iota((32, D), 0)
        centre = jnp.sum(jnp.where(kind == head, reads, 0.0), axis=0, keepdims=True)
        spread = jnp.sum(jnp.where(kind == head + H, reads, 0.0), axis=0, keepdims=True)
        row = iota((8, D), 0)
        reads_ref[...] = jnp.where(row == 0, centre, jnp.where(row == 1, spread, 0.0))
        wait_all(copies[2])
        mem_values_ref[...] = nn(coeff_ref[...], values_ref[...]).astype(BF16)
        wait_all(copies[0])

        def block(n, bias):
            at = pl.ds(n * D, D)
            projected_ref[:, at] = (nn(normed_ref[...], proj_ref[:, at]) + bias).astype(BF16)

        block(0, vec_ref[2:3, :])
        block(1, 0.0)
        block(2, vec_ref[3:4, :])

    return call(
        kernel,
        [shape_of((512, D)), shape_of((512, 3 * D)), shape_of((N, D)), shape_of((8, D), F32)],
        [SMEM] + [VMEM] * 4 + [HBM] * sum(counts),
        [VMEM] * 4,
        [
            pltpu.VMEM((D, 3 * D), BF16),
            pltpu.VMEM((D, D), BF16),
            pltpu.VMEM((D, D), BF16),
            pltpu.SemaphoreType.DMA((3,)),
        ],
        flops=FLOPS["front"],
        vmem=28,
        after=after,
    )(place, tokens, vectors, coeff, tables, *proj.parts, *keys.parts, *values.parts)


READ = 256


def document_rows(length_ref):
    place = iota((1, 512), 1)
    first = jnp.zeros((1, 512), jnp.int32)
    end = jnp.int32(0)
    for n in range(length_ref.shape[1] - 1):
        end = end + length_ref[0, n]
        first = jnp.where(place >= end, end, first)
    return first


def mask_bias(length_ref, bias_ref):
    first = document_rows(length_ref)
    key, query = iota((512, 512), 0), iota((512, 512), 1)
    bias_ref[...] = jnp.where((key <= query) & (key >= first), 0.0, masked_fill)


def reading_row(length_ref, carried_ref):
    inside = iota((1, READ), 1) < length_ref[0, 0]
    return jnp.where(inside, carried_ref[0].astype(F32), 0.0)


def read_parameters(scaled, reads):
    lane_head = iota((1, PART), 1) // DH
    rows = [jnp.where(lane_head == h, reads[kind : kind + 1, :], 0.0) for kind in (0, 1) for h in (0, 1)]
    rows = jnp.concatenate(rows + [jnp.zeros((4, PART), F32)], axis=0)
    high, low = split(rows)
    lowest = (rows - high.astype(F32) - low.astype(F32)).astype(BF16)
    logits = nt(high, scaled) + (nt(low, scaled) + nt(lowest, scaled))
    found = []
    for h in (0, 1):
        centre = 1.0 / (1.0 + jnp.exp(-logits[h : h + 1, :]))
        raw = logits[2 + h : 3 + h, :]
        spread = spread_scale * (jnp.maximum(raw, 0.0) + jnp.log1p(jnp.exp(-jnp.abs(raw))))
        variance = 1.0 / (N * N) + spread * spread
        found.append((centre, spread, variance, raw))
    return rows, found


def basis_column():
    return (iota((N, 1), 0).astype(F32) + 0.5) / N


def density_of(centre, variance):
    distance = centre - basis_column()
    return lax.rsqrt(variance) / N * jnp.exp(distance * distance * (-0.5 / variance)), distance


def head_lanes(value, h):
    return jnp.where(iota((1, PART), 1) // DH == h, value, jnp.zeros_like(value))


def attend_kernel(length_ref, carried_ref, q_ref, k_ref, v_ref, mem_ref, reads_ref, out_ref, lse_ref, bias_ref):
    pl.when(pl.program_id(0) == 0)(lambda: mask_bias(length_ref, bias_ref))
    scaled = q_ref[...] * jnp.asarray(score_scale, BF16)
    outs, totals = [], []
    for h in (0, 1):
        halves, lse = [], []
        for first in (0, 256):
            keys = first + 256
            scores = nt(k_ref[:keys, :], head_lanes(scaled[first : first + 256, :], h))
            scores = scores + bias_ref[:keys, first : first + 256]
            top = jnp.max(scores, axis=0, keepdims=True)
            weights = jnp.exp(scores - top)
            total = jnp.sum(weights, axis=0, keepdims=True)
            probs = (weights * (1.0 / total)).astype(BF16)
            halves.append(tn(v_ref[:keys, :], probs)[h * DH : (h + 1) * DH, :])
            lse.append(top + jnp.log(total))
        outs.append(halves)
        totals.append(jnp.concatenate(lse, axis=1))
    lse_ref[...] = jnp.concatenate(totals + [jnp.zeros((6, 512), F32)], axis=0)
    _, found = read_parameters(scaled[:READ, :], reads_ref[...])
    reading = reading_row(length_ref, carried_ref)
    for h in (0, 1):
        centre, _, variance, _ = found[h]
        density, _ = density_of(centre, variance)
        recall = tn(mem_ref[...], density.astype(BF16))[h * DH : (h + 1) * DH, :]
        outs[h][0] = outs[h][0] + recall * reading
    for n in (0, 1):
        block = jnp.concatenate([outs[0][n], outs[1][n]], axis=0)
        out_ref[n * 256 : (n + 1) * 256, :] = jnp.transpose(block).astype(BF16)


def pair_block(shift=0):
    return pl.BlockSpec((512, PART), lambda i: (0, i + shift))


def attend_call(lengths, carried, projected, mem_values, reads, after=()):
    return call(
        attend_kernel,
        [shape_of((512, D)), shape_of((PAIRS * 8, 512), F32)],
        [SMEM, SMEM, pair_block(), pair_block(PAIRS), pair_block(2 * PAIRS), pair_block(), pl.BlockSpec((8, PART), lambda i: (0, i))],
        [pair_block(), pl.BlockSpec((8, 512), lambda i: (i, 0))],
        [pltpu.VMEM((512, 512), F32)],
        flops=FLOPS["attend"],
        after=after,
        grid=(PAIRS,),
    )(lengths, carried, projected, projected, projected, mem_values, reads)


def attend_back_kernel(length_ref, carried_ref, q_ref, k_ref, v_ref, lse_ref, heads_ref, more_ref, gq_ref, gk_ref, gv_ref, bias_ref):
    pl.when(pl.program_id(0) == 0)(lambda: mask_bias(length_ref, bias_ref))
    scaled = q_ref[...] * jnp.asarray(score_scale, BF16)
    keys, values, grad = k_ref[...], v_ref[...], heads_ref[...]
    lane_head = iota((1, PART), 1) // DH
    grad_queries, grad_keys, grad_values = [], [], []
    for h in (0, 1):
        parts = []
        gk, gv = [], []
        for first in (0, 256):
            last = first + 256
            own, own_grad = head_lanes(scaled[first:last, :], h), head_lanes(grad[first:last, :], h)
            scores = nt(keys[:last, :], own) + bias_ref[:last, first:last]
            probs = jnp.exp(scores - lse_ref[h : h + 1, first:last])
            grad_probs = nt(values[:last, :], own_grad)
            row_terms = jnp.sum(probs * grad_probs, axis=0, keepdims=True)
            grad_scores = (probs * (grad_probs - row_terms)).astype(BF16)
            gv.append(nn(probs.astype(BF16), grad[first:last, :]))
            gk.append(nn(grad_scores, scaled[first:last, :]))
            parts.append(tn(keys[:last, :], grad_scores)[h * DH : (h + 1) * DH, :])
        grad_queries.append(parts)
        grad_keys.append((gk[0] + gk[1][:256, :], gk[1][256:, :]))
        grad_values.append((gv[0] + gv[1][:256, :], gv[1][256:, :]))
    for n in (0, 1):
        at = slice(n * 256, (n + 1) * 256)
        gk_ref[at, :] = jnp.where(lane_head == 0, grad_keys[0][n], grad_keys[1][n]).astype(BF16)
        gv_ref[at, :] = jnp.where(lane_head == 0, grad_values[0][n], grad_values[1][n]).astype(BF16)
        block = jnp.concatenate([grad_queries[0][n], grad_queries[1][n]], axis=0)
        if n == 0:
            block = block + more_ref[...]
        gq_ref[at, :] = (jnp.transpose(block) * score_scale).astype(BF16)


def memory_read_back_kernel(length_ref, carried_ref, q_ref, mem_ref, reads_ref, heads_ref, more_ref, gmem_ref, sums_ref):
    scaled = q_ref[...] * jnp.asarray(score_scale, BF16)
    grad = heads_ref[...]
    lane_head = iota((1, PART), 1) // DH
    rows, found = read_parameters(scaled, reads_ref[...])
    reading = reading_row(length_ref, carried_ref)
    centre_grads, spread_grads, grad_mems = [], [], []
    for h in (0, 1):
        centre, spread, variance, raw = found[h]
        density, distance = density_of(centre, variance)
        own_grad = head_lanes(grad, h)
        grad_density = nt(mem_ref[...], own_grad) * reading
        grad_mems.append(nn((density * reading).astype(BF16), own_grad))
        weight = grad_density * density
        moment0 = jnp.sum(weight, axis=0, keepdims=True)
        weight = weight * distance
        moment1 = jnp.sum(weight, axis=0, keepdims=True)
        moment2 = jnp.sum(weight * distance, axis=0, keepdims=True)
        inverse = 1.0 / variance
        grad_variance = 0.5 * inverse * (moment2 * inverse - moment0)
        centre_grads.append(-moment1 * inverse * centre * (1.0 - centre))
        spread_grads.append(grad_variance * 2.0 * spread * spread_scale / (1.0 + jnp.exp(-raw)))
    gmem_ref[...] = (grad_mems[0] + grad_mems[1]).astype(BF16)
    logit_grads = jnp.concatenate(centre_grads + spread_grads + [jnp.zeros((4, READ), F32)], axis=0)
    sums = one_split(nn, logit_grads, scaled)
    centre_sum = jnp.where(lane_head == 0, sums[0:1, :], sums[1:2, :])
    spread_sum = jnp.where(lane_head == 0, sums[2:3, :], sums[3:4, :])
    sums_ref[...] = jnp.concatenate([centre_sum, spread_sum, jnp.zeros((6, PART), F32)], axis=0)
    more_ref[...] = both_split(tn, rows, logit_grads)


FEW = pl.BlockSpec((8, PART), lambda i: (0, i))


def memory_read_back_call(lengths, carried, projected, mem_values, reads, grad_heads, after=()):
    near = pl.BlockSpec((READ, PART), lambda i: (0, i))
    return call(
        memory_read_back_kernel,
        [shape_of((D, READ), F32), shape_of((N, D)), shape_of((8, D), F32)],
        [SMEM, SMEM, near, pair_block(), FEW, near],
        [pl.BlockSpec((PART, READ), lambda i: (i, 0)), pair_block(), FEW],
        flops=FLOPS["memory_read_back"],
        grid=(PAIRS,),
        after=after,
    )(lengths, carried, projected, mem_values, reads, grad_heads)


def attend_back_call(lengths, carried, projected, lse, grad_heads, more, first, count, after=(), work="attend_back"):
    def pair(shift):
        return pl.BlockSpec((512, PART), lambda i: (0, i + shift))

    return call(
        attend_back_kernel,
        [shape_of((512, count * PART))] * 3,
        [SMEM, SMEM, pair(first), pair(first + PAIRS), pair(first + 2 * PAIRS),
         pl.BlockSpec((8, 512), lambda i: (i + first, 0)), pair(first), pl.BlockSpec((PART, READ), lambda i: (i + first, 0))],
        [pair(0)] * 3,
        [pltpu.VMEM((512, 512), F32)],
        flops=FLOPS[work],
        grid=(count,),
        after=after,
    )(lengths, carried, projected, projected, projected, lse, grad_heads, more)


GELU_SCALE = 0.7978845608028654
GELU_CUBE = 0.044715


def column_tiles(step_columns):
    return pl.BlockSpec((512, step_columns), lambda t: (0, t))


def fixed(shape):
    return pl.BlockSpec(shape, lambda t: (0,) * len(shape), pipeline_mode=pl.Buffered(1))


def weight_refs(weights, refs):
    found, at = [], 0
    for weight in weights:
        found.append(refs[at : at + len(weight.parts)])
        at += len(weight.parts)
    return found, refs[at:]


def mlp_call(place, tokens, heads, cotangent, vectors, up_bias, out, up, down, down_blocks, up_blocks):
    weights = (out, up, down)
    steps = FF // TILE
    down_shapes = down_blocks.shapes if down_blocks else [shape_of((FF, D))]
    up_shapes = up_blocks.shapes if up_blocks else [shape_of((D, FF))]
    count = len(down_shapes)

    def kernel(place_ref, tokens_ref, heads_ref, cot_ref, vec_ref, bias_ref, *refs):
        sources, refs = weight_refs(weights, refs)
        result_ref, middle_ref, back_ref, line_ref = refs[:4]
        down_grads, up_grads, refs = refs[4 : 4 + count], refs[4 + count : 4 + 2 * count], refs[4 + 2 * count :]
        out_ref, up_ref, down_ref, normed_ref, total_ref, down_staged, up_staged, sem, up_sems, down_sems, grad_sems = refs
        step = pl.program_id(0)
        tile = tile_at(place_ref, step // 2, step % 2)
        side = (step // 2) ^ place_ref[3]

        @pl.when(step == 0)
        def _():
            copies = out.fetch(sources[0], place_ref, out_ref, sem)
            for n in range(steps):
                up.fetch_columns(sources[1], place_ref, n // 2, n % 2, up_ref.at[n], up_sems.at[n])
                down.fetch_rows(sources[2], place_ref, n // 2, n % 2, down_ref.at[n], down_sems.at[n])
            wait_all(copies)
            middle = tokens_ref[0].astype(F32) + nn(heads_ref[...], out_ref[...]) + vec_ref[4:5, :]
            middle_ref[...] = middle
            normed_ref[...] = normalise(middle, vec_ref[5:6, :], vec_ref[6:7, :]).astype(BF16)
            total_ref[...] = middle + vec_ref[7:8, :]
            back_ref[...] = jnp.zeros((512, D), F32)

        await_tile(up_ref.at[step], up_sems.at[step])
        await_tile(down_ref.at[step], down_sems.at[step])
        hidden = nn(normed_ref[...], up_ref[step]) + bias_ref[0:1, aligned(tile, TILE)]
        grad_active = nt(cot_ref[0], down_ref[step])
        square = hidden * hidden
        bent = jnp.tanh(GELU_SCALE * hidden * (1.0 + GELU_CUBE * square))
        half = 0.5 + 0.5 * bent
        active = (hidden * half).astype(BF16)
        slope = half + 0.5 * hidden * (1.0 - bent * bent) * (GELU_SCALE + 3.0 * GELU_SCALE * GELU_CUBE * square)
        grad_hidden = (grad_active * slope).astype(BF16)
        line = jnp.sum(grad_hidden.astype(F32), axis=0, keepdims=True)
        line_ref[:, aligned(tile, TILE)] = jnp.broadcast_to(line, (8, TILE))
        down_staged[step] = tn(active, cot_ref[0]).astype(BF16)
        total_ref[...] += nn(active, down_ref[step])
        up_staged[step] = tn(normed_ref[...], grad_hidden).astype(BF16)
        back_ref[...] += nt(grad_hidden, up_ref[step])
        if down_blocks:
            rows, columns = down_blocks.rows, down_blocks.columns
            down_pieces = [((rows, columns), (0, 0), 0, columns)]
            places = [(tile, x, core) for x in (0, 1) for core in (0, 1)]
            down_blocks.put(down_staged.at[step], down_grads, place_ref, grad_sems.at[0], down_pieces, places)
            part = step % 2
            up_blocks.put_stacked(up_staged.at[step], up_grads, place_ref, grad_sems.at[1], side, part)
        else:
            start(down_staged.at[step], down_grads[0].at[aligned(tile, TILE), :], grad_sems.at[0])
            start(up_staged.at[step], up_grads[0].at[:, aligned(tile, TILE)], grad_sems.at[1])

        @pl.when(step == steps - 1)
        def _():
            result_ref[0] = total_ref[...].astype(BF16)
            for n in range(steps):
                await_tile(down_staged.at[n], grad_sems.at[0])
                await_tile(up_staged.at[n], grad_sems.at[1])

    found = call(
        kernel,
        [shape_of((1, 512, D)), shape_of((512, D), F32), shape_of((512, D), F32), shape_of((8, FF), F32)]
        + down_shapes
        + up_shapes,
        [SMEM, fixed((1, 512, D)), fixed((512, D)), fixed((1, 512, D)), fixed((16, D)), fixed((8, FF))]
        + [HBM] * sum(len(w.parts) for w in weights),
        [fixed((1, 512, D)), fixed((512, D)), fixed((512, D)), fixed((8, FF))] + [HBM] * (2 * count),
        [
            pltpu.VMEM((D, D), BF16),
            pltpu.VMEM((steps, D, TILE), BF16),
            pltpu.VMEM((steps, TILE, D), BF16),
            pltpu.VMEM((512, D), BF16),
            pltpu.VMEM((512, D), F32),
            pltpu.VMEM((steps, TILE, D), BF16),
            pltpu.VMEM((steps, D, TILE), BF16),
            pltpu.SemaphoreType.DMA,
            pltpu.SemaphoreType.DMA((steps,)),
            pltpu.SemaphoreType.DMA((steps,)),
            pltpu.SemaphoreType.DMA((2,)),
        ],
        flops=FLOPS["mlp"],
        vmem=44,
        grid=(steps,),
    )(place, tokens, heads, cotangent, vectors, up_bias, *out.parts, *up.parts, *down.parts)
    return found[:4], found[4 : 4 + count], found[4 + count :]


def middle_back_call(place, cotangent, middle, grad_normed, vectors, heads, out, after=()):
    def kernel(place_ref, cot_ref, middle_ref, grad_ref, vec_ref, heads_ref, *refs):
        sources, refs = weight_refs((out,), refs)
        grad_middle_ref, grad_heads_ref, out_grad_ref, sums_ref, out_ref, sem = refs
        copies = out.fetch(sources[0], place_ref, out_ref, sem)
        cot = cot_ref[0].astype(F32)
        back, gain, shift = normalise_back(middle_ref[...], vec_ref[5:6, :], grad_ref[...])
        grad_middle = cot + back
        grad_middle_ref[...] = grad_middle
        attended = grad_middle.astype(BF16)
        bias = jnp.sum(attended.astype(F32), axis=0, keepdims=True)
        last = jnp.sum(cot, axis=0, keepdims=True)
        nothing = jnp.zeros((4, D), F32)
        sums_ref[...] = jnp.concatenate([nothing, bias, gain, shift, last, nothing, nothing], axis=0)
        wait_all(copies)
        grad_heads_ref[...] = nt(attended, out_ref[...]).astype(BF16)
        out_grad_ref[...] = tn(heads_ref[...], attended).astype(BF16)

    return call(
        kernel,
        [shape_of((512, D), F32), shape_of((512, D)), shape_of((D, D)), shape_of((16, D), F32)],
        [SMEM] + [VMEM] * 5 + [HBM] * len(out.parts),
        [VMEM] * 4,
        [pltpu.VMEM((D, D), BF16), pltpu.SemaphoreType.DMA],
        flops=FLOPS["middle_back"],
        vmem=56,
        after=after,
    )(place, cotangent, middle, grad_normed, vectors, heads, *out.parts)


def memory_back_call(place, coeff, grad_mem_values, tables, sums, out_grad, keys, blocks, after=()):
    shapes = blocks.shapes if blocks else [shape_of((D, D))] * 3

    def kernel(place_ref, coeff_ref, grad_values_ref, table_ref, sums_ref, out_grad_ref, *refs):
        sources, refs = weight_refs((keys,), refs)
        tables_ref = refs[0]
        grad_refs, (keys_ref, key_grad_ref, value_grad_ref, small_ref, sems) = refs[1 : 1 + len(shapes)], refs[1 + len(shapes) :]
        copies = keys.fetch(sources[0], place_ref, keys_ref, sems.at[0])
        staged = (out_grad_ref, key_grad_ref, value_grad_ref)

        def put(n):
            if not blocks:
                start(staged[n], grad_refs[n], sems.at[1 + n])
                return
            piece = ((blocks.rows, D // 2), (0, 0), n * (D // 2), D // 2)
            blocks.put(staged[n], grad_refs, place_ref, sems.at[1 + n], [piece])

        put(0)
        value_grad_ref[...] = tn(coeff_ref[...], grad_values_ref[...]).astype(BF16)
        put(2)
        head, kind = iota((32, D), 1) // DH, iota((32, D), 0)
        by_head = jnp.where(kind == head, sums_ref[0:1, :], jnp.where(kind == head + H, sums_ref[1:2, :], 0.0))
        summary = tn(coeff_ref[...], table_ref[...])[:, :32]
        key_grad_ref[...] = both_split(nn, summary, by_head).astype(BF16)
        put(1)
        wait_all(copies)
        high, low = split(by_head)
        wide = jnp.concatenate([high, low, jnp.zeros((PART - 64, D), BF16)], axis=0)
        reads = nt(keys_ref[...], wide)
        high, low = split(reads)
        found = nn(coeff_ref[...], high) + nn(coeff_ref[...], low)
        lane = iota((N, PART), 1)
        found = found + jnp.concatenate([found[:, 32:64], jnp.zeros((N, PART - 32), F32)], axis=1)
        found = jnp.where(lane < 2 * H, found, 0.0)
        tables_ref[...] = found
        if blocks:
            small_ref[...] = padded_blocks(found).reshape(small_ref.shape)
            blocks.put_devices(small_ref, grad_refs, place_ref, sems.at[4], 3 * D // 2)
            await_tile(small_ref, sems.at[4])
        else:
            small_ref[...] = jnp.zeros(small_ref.shape, BF16)
        for n in range(3):
            await_tile(staged[n], sems.at[1 + n])

    found = call(
        kernel,
        [shape_of((N, PART), F32)] + shapes,
        [SMEM] + [VMEM] * 5 + [HBM] * len(keys.parts),
        [VMEM] + [HBM] * len(shapes),
        [pltpu.VMEM((D, D), BF16)] * 3 + [pltpu.VMEM((32 * 48, PART), BF16), pltpu.SemaphoreType.DMA((5,))],
        flops=FLOPS["memory_back"],
        vmem=20,
        after=after,
    )(place, coeff, grad_mem_values, tables, sums, out_grad, *keys.parts)
    return found[0], found[1:]


def input_back_call(place, tokens, vectors, normed, grads, grad_middle, sums, up_bias_grad, proj, blocks, after=()):
    shapes = blocks.shapes if blocks else [shape_of((D, 3 * D)), shape_of((16, D), F32)]

    def kernel(place_ref, tokens_ref, vec_ref, normed_ref, middle_ref, sums_ref, up_ref, *refs):
        parts, refs = refs[: len(grads)], refs[len(grads) :]
        sources, refs = weight_refs((proj,), refs)
        result_ref, done_ref = refs[:2]
        done_ref[...] = jnp.zeros(done_ref.shape, F32)
        grad_refs, (proj_ref, staged_ref, small_ref, sems) = refs[2 : 2 + len(shapes)], refs[2 + len(shapes) :]
        copies = proj.fetch(sources[0], place_ref, proj_ref, sems.at[0])
        at = 0
        for part in parts:
            columns = part.shape[1]
            staged_ref[:, at : at + columns] = tn(normed_ref[...], part[...]).astype(BF16)
            at += columns
        if blocks:
            rows, side = blocks.rows, 3 * D // 2
            blocks.put(staged_ref, grad_refs, place_ref, sems.at[1], [((rows, side), (0, 0), 0, side)])
        else:
            start(staged_ref, grad_refs[0], sems.at[1])
        wait_all(copies)
        grad_normed, column_sums, at = jnp.zeros((512, D), F32), [], 0
        for part in parts:
            columns = part.shape[1]
            grad_normed = grad_normed + nt(part[...], proj_ref[:, at : at + columns])
            column_sums.append(jnp.sum(part[...].astype(F32), axis=0, keepdims=True))
            at += columns
        column_sums = jnp.concatenate(column_sums, axis=1)
        back, gain, shift = normalise_back(tokens_ref[0].astype(F32), vec_ref[0:1, :], grad_normed)
        result_ref[0] = middle_ref[...] + back
        vectors_grad = jnp.concatenate([gain, shift, column_sums[:, :D], column_sums[:, 2 * D :], sums_ref[4:16, :]], axis=0)
        if blocks:
            small_ref[...] = pack_vectors(vectors_grad, up_ref[...]).reshape(32 * rows, PART)

            blocks.put_devices(small_ref, grad_refs, place_ref, sems.at[2], side)
            await_tile(staged_ref, sems.at[1])
            await_tile(small_ref, sems.at[2])
        else:
            small_ref[...] = jnp.zeros(small_ref.shape, BF16)
            grad_refs[1][...] = vectors_grad
            pltpu.make_async_copy(staged_ref, grad_refs[0], sems.at[1]).wait()

    found = call(
        kernel,
        [shape_of((1, 512, D), F32), shape_of((8, PART), F32)] + shapes,
        [SMEM] + [VMEM] * (6 + len(grads)) + [HBM] * len(proj.parts),
        [VMEM] * 2 + ([HBM] * 2 if blocks else [HBM, VMEM]),
        [
            pltpu.VMEM((D, 3 * D), BF16),
            pltpu.VMEM((D, 3 * D), BF16),
            pltpu.VMEM((32 * 48, PART), BF16),
            pltpu.SemaphoreType.DMA((3,)),
        ],
        flops=FLOPS["input_back"],
        vmem=36,
        after=after,
    )(place, tokens, vectors, normed, grad_middle, sums, up_bias_grad, *grads, *proj.parts)
    return found[0], found[1], found[2:]


def hop(value, z=0, x=0, core=0, f=0):
    pairs = []
    for dp in range(16):
        for side in range(2):
            other = (((dp // 4) ^ z) * 4) + ((((dp // 2) % 2) ^ x) * 2) + ((dp % 2) ^ core)
            pairs.append((dp * 2 + side, other * 2 + (side ^ f)))
    return lax.ppermute(value, BOTH, pairs)


def z_hops(block):
    return [block] + [hop(block, z=k) for k in (1, 2, 3)]


def quads(pieces, cut, after, stacked=1):
    rows, columns = pieces[0].shape
    width = (columns - cut) // stacked

    def kernel(*refs):
        blocks, (left, right) = refs[:4], refs[4:]
        for k, block in enumerate(blocks):
            left[k] = block[:, :cut]
            for n in range(stacked):
                right[k, n * rows : (n + 1) * rows, :] = block[:, cut + n * width : cut + (n + 1) * width]

    shapes = [shape_of((4, rows, cut)), shape_of((4, stacked * rows, width))]
    return list(call(kernel, shapes, [VMEM] * 4, [VMEM] * 2, flops=FLOPS["pack"], after=after)(*pieces))


BITS = (dict(x=1), dict(f=1))


def joined(quads_here, nears, after):
    def kernel(*refs):
        for n in (0, 1):
            for m in (0, 1):
                refs[4 + n][pl.ds(4 * m, 4)] = refs[2 * m + n][...]

    shapes = [shape_of((8,) + quad.shape[1:]) for quad in quads_here]
    return list(call(kernel, shapes, [VMEM] * 4, [VMEM] * 2, flops=FLOPS["pack"], after=after)(*quads_here, *nears))


def once_there(arrays, after):
    count = len(arrays)

    def kernel(*refs):
        for n in range(count):
            refs[count + n][...] = refs[n][...]

    shapes = [shape_of(array.shape) for array in arrays]
    return call(kernel, shapes, [VMEM] * count, [VMEM] * count, flops=FLOPS["pack"], after=after)(*arrays)


def plus(a, b):
    return (a.astype(F32) + b.astype(F32)).astype(BF16)


def halves(kept, got):
    return plus(kept[1], got[1]), plus(kept[0], got[0])


def halves_after(pairs, after):
    widths = [kept.shape[-1] for kept, _ in pairs]

    def kernel(*refs):
        for bit, target in ((1, refs[-2]), (0, refs[-1])):
            at = 0
            for n, width in enumerate(widths):
                total = refs[2 * n][bit].astype(F32) + refs[2 * n + 1][bit].astype(F32)
                target[..., at : at + width] = total.astype(BF16)
                at += width

    shapes = [shape_of(pairs[0][0].shape[1:-1] + (sum(widths),))] * 2
    flat = [array for pair in pairs for array in pair]
    return call(kernel, shapes, [VMEM] * len(flat), [VMEM] * 2, flops=FLOPS["add"], after=after)(*flat)


def added(pairs, after=()):
    _, rows, columns = pairs[0][0].shape

    def kernel(*refs):
        targets = refs[-1], refs[-2]
        for n in range(len(pairs)):
            for k in range(4):
                total = refs[2 * n][k].astype(F32) + refs[2 * n + 1][k].astype(F32)
                target = targets[k % 2]
                target[k // 2, n * rows : (n + 1) * rows, :] = total.astype(target.dtype)

    shape = (2, len(pairs) * rows, columns)
    flat = [array for pair in pairs for array in pair]
    return call(kernel, [shape_of(shape), shape_of(shape, F32)], [VMEM] * len(flat), [VMEM] * 2, flops=FLOPS["add"], after=after)(*flat)


def between(own, got, after=()):
    def kernel(own_ref, got_ref, sent_ref, total_ref):
        total_ref[...] = own_ref[0] + got_ref[0].astype(F32)
        sent_ref[...] = (own_ref[1] + got_ref[1].astype(F32)).astype(BF16)

    shapes = [shape_of(own.shape[1:]), shape_of(own.shape[1:], F32)]
    return call(kernel, shapes, [VMEM] * 2, [VMEM] * 2, flops=FLOPS["add"], after=after)(own, got)


def cut_halves(kept, got, cut, after=()):
    def kernel(kept_ref, got_ref, *refs):
        for bit, targets in ((1, refs[:2]), (0, refs[2:])):
            left, right = (bit, slice(None)), (slice(None), bit)
            for target, bits, columns in zip(targets, (left, right), (slice(0, cut), slice(cut, None))):
                at = (*bits, slice(None), slice(None), columns)
                target[...] = (kept_ref[at].astype(F32) + got_ref[at].astype(F32)).astype(BF16)

    shapes = [shape_of(kept.shape[1:4] + (width,)) for width in (cut, kept.shape[4] - cut)] * 2
    found = call(kernel, shapes, [VMEM] * 2, [VMEM] * 4, flops=FLOPS["add"], after=after)(kept, got)
    return found[:2], found[2:]


def both_halves(kept, got, after=()):
    def kernel(*refs):
        for n in (0, 1):
            for bit, target in ((1, refs[4 + n]), (0, refs[6 + n])):
                target[...] = (refs[n][bit].astype(F32) + refs[2 + n][bit].astype(F32)).astype(BF16)

    shapes = [shape_of(array.shape[1:]) for array in kept] * 2
    found = call(kernel, shapes, [VMEM] * 4, [VMEM] * 4, flops=FLOPS["add"], after=after)(*kept, *got)
    return found[:2], found[2:]


def finish(own, got, outputs, after=()):
    def width(columns):
        return columns.stop - columns.start

    def kernel(own_ref, *refs):
        total = own_ref[...]
        for ref in refs[: len(got)]:
            total = total + ref[...].astype(F32)
        for target, pieces in zip(refs[len(got) :], outputs):
            at = 0
            for rows, columns in pieces:
                target[:, at : at + width(columns)] = total[rows, columns]
                at += width(columns)

    shapes = [
        shape_of((pieces[0][0].stop - pieces[0][0].start, sum(width(piece[1]) for piece in pieces)), F32)
        for pieces in outputs
    ]
    return call(
        kernel, shapes, [VMEM] * (1 + len(got)), [VMEM] * len(outputs), flops=FLOPS["add"], after=after
    )(own, *got)


def three_ways(pairs, after=()):
    rows, columns = pairs[0][0].shape[1], [kept.shape[2] for kept, _ in pairs]

    def kernel(*refs):
        targets = refs[-4:]
        at = 0
        for n, width in enumerate(columns):
            for k in range(4):
                total = refs[2 * n][k].astype(F32) + refs[2 * n + 1][k].astype(F32)
                targets[k][:, at : at + width] = total.astype(targets[k].dtype)
            at += width

    shapes = [shape_of((rows, sum(columns)), F32)] + [shape_of((rows, sum(columns)))] * 3
    flat = [array for pair in pairs for array in pair]
    return call(kernel, shapes, [VMEM] * len(flat), [VMEM] * 4, flops=FLOPS["add"], after=after)(*flat)


COLUMN_SPLIT = (2, 5, 7, 8, 13, 15)
VECTORS = (0, 1, 3, 4, 6, 11, 12, 16)


def gather_whole(shards):
    def whole(k, shard):
        near = lax.all_gather(shard, "fsdp", axis=1 if k in COLUMN_SPLIT else 0, tiled=True)
        return lax.all_gather(near, "dp", axis=0, tiled=True)

    found = [whole(k, shard) for k, shard in enumerate(shards)]
    vectors = jnp.stack([found[k].astype(F32) for k in VECTORS] + [jnp.zeros((D,), F32)] * 8)
    up_bias = jnp.broadcast_to(found[14].astype(F32)[None], (8, FF))
    tables = jnp.pad(jnp.concatenate([found[9], found[10]], axis=1), ((0, 0), (0, PART - 2 * H)))
    weights = {k: Whole(found[k]) for k in COLUMN_SPLIT}
    return weights, vectors, up_bias, tables


def scatter_whole(totals):
    def part(k, total):
        near = lax.psum_scatter(total.astype(BF16), "dp", scatter_dimension=0, tiled=True)
        return lax.psum_scatter(near, "fsdp", scatter_dimension=1 if k in COLUMN_SPLIT else 0, tiled=True).astype(F32)

    return [part(k, total) for k, total in enumerate(totals)]


def pack_early(shards):
    order = [2, 7, 8, 5, 9, 10, 14] + list(VECTORS)
    arrays = [shards[k] if shards[k].ndim == 2 else shards[k].reshape(1, -1) for k in order]
    rows, half = shards[5].shape

    def kernel(proj, keys, values, out, centre, spread, up_bias, *refs):
        vectors, early = refs[:-1], refs[-1]
        early[:, : 3 * half] = proj[...]
        early[:, 3 * half : 4 * half] = keys[...]
        early[:, 4 * half : 5 * half] = values[...]
        early[:, 5 * half : 6 * half] = out[...]
        lines = []
        for ref in list(vectors) + [up_bias]:
            line = ref[...].astype(F32)
            lines.append(jnp.concatenate([line, jnp.zeros((1, PART - line.shape[1]), F32)], axis=1))
        lines.append(jnp.zeros((16 - len(lines), PART), F32))
        tables = jnp.concatenate(
            [centre[...].astype(F32), spread[...].astype(F32), jnp.zeros((16, PART - 2 * H), F32)], axis=1
        )
        small = jnp.concatenate(lines + [tables, jnp.zeros((rows - 32, PART), F32)], axis=0)
        early[:, 6 * half :] = small.astype(BF16)

    return call(kernel, shape_of((rows, 6 * half + PART)), [VMEM] * len(arrays), VMEM, flops=FLOPS["pack"], vmem=56)(*arrays)


def pack_late(shards, after):
    rows, half = shards[5].shape

    def kernel(up, down, late):
        late[:, : 4 * half] = up[...]
        for q in range(4):
            late[:, (4 + q) * half : (5 + q) * half] = down[q * rows : (q + 1) * rows, :]

    return call(kernel, shape_of((rows, 8 * half)), [VMEM] * 2, VMEM, flops=FLOPS["pack"], after=after)(
        shards[13], shards[15]
    )


def local(
    mesh_sizes, tokens, context, past_coeffs, doc_lengths, carried, histogram, cotangent, *shards
):
    hops = mesh_sizes == (16, 2)
    dp = lax.axis_index("dp")
    place = jnp.stack([dp // 4, (dp // 2) % 2, dp % 2, lax.axis_index("fsdp")]).astype(jnp.int32)
    rows, half = shards[5].shape
    x_hop, f_hop = BITS
    if hops:
        early = z_hops(pack_early(shards))
        points, gram, right = memory_system(histogram, past_coeffs, context, after=[early[0]])
        early = quads(early, 3 * half, [gram])
        near = [hop(early[0], **x_hop), hop(early[1], **f_hop)]
        steps = [eliminate((gram, right), early)]
        late = z_hops(pack_late(shards, [steps[0][0]]))
        early = joined(early, near, [steps[0][0]])
        far = [hop(early[0], **f_hop), hop(early[1], **x_hop)]
        steps.append(eliminate(steps[0][2:], early))
        late = quads(late, 4 * half, [steps[1][0]], 4)
        late_near = [hop(late[0], **x_hop), hop(late[1], **f_hop)]
        steps.append(eliminate(steps[1][2:], late + far))
        pairs = once_there(early, [steps[2][0]])
        proj_parts, mem_parts = (
            [early[n], far[n], hop(pairs[n], core=1), hop(far[n], core=1)] for n in (0, 1)
        )
        steps.append(eliminate(steps[2][2:]))
        coeff = substitute(steps)
        late = joined(late, late_near, [coeff])
        late_far = [hop(late[0], **f_hop), hop(late[1], **x_hop)]
        late_core = [hop(part, core=1) for part in late]
        vectors, up_bias, tables = gathered_vectors(place, mem_parts)
        weights = {
            2: Hops(proj_parts, True, 3 * half),
            7: Hops(mem_parts, False, half),
            8: Hops(mem_parts, False, half, half),
            5: Hops(mem_parts, False, half, 2 * half),
        }
    else:
        late_core = []
        weights, vectors, up_bias, tables = gather_whole(shards)
        points, *system = memory_system(histogram, past_coeffs, context)
        steps = [eliminate(system)]
        while len(steps) < N // PART:
            steps.append(eliminate(steps[-1][2:]))
        coeff = substitute(steps)
    normed, projected, mem_values, reads = front_call(
        place, tokens, vectors, coeff, tables, weights[2], weights[7], weights[8], after=late_core
    )
    heads, lse = attend_call(doc_lengths, carried, projected, mem_values, reads)
    if hops:
        far_core = [hop(part, core=1) for part in once_there(late_far, [heads])]
        parts = [[late[n], late_far[n], late_core[n], far_core[n]] for n in (0, 1)]
        weights[13] = Hops(parts[0], True, 4 * half)
        weights[15] = Hops(parts[1], False, half)
    down_blocks = Blocks(False, 4 * rows, half) if hops else None
    up_blocks = Blocks(True, 4 * rows, half) if hops else None
    (result, middle, grad_normed_mlp, grad_up_bias), down_grad, up_grad = mlp_call(
        place, tokens, heads, cotangent, vectors, up_bias, weights[5], weights[13], weights[15], down_blocks, up_blocks
    )
    waits = {"read": [], "second": [], "input": []}
    grad_middle, grad_heads, grad_out, sums = middle_back_call(
        place, cotangent, middle, grad_normed_mlp, vectors, heads, weights[5]
    )
    if hops:
        got_down, got_up = hop(down_grad[1], core=1), hop(up_grad[1], core=1)
        sent_down, kept_down = halves_after([(down_grad[0], got_down)], [sums])
        got_down = hop(sent_down, **f_hop)
        sent_up, kept_up = halves_after([(up_grad[0], got_up)], [sent_down])
        waits["read"] = [sent_up]
        got_up = hop(sent_up, **x_hop)
    more, grad_mem, read_sums = memory_read_back_call(
        doc_lengths, carried, projected, mem_values, reads, grad_heads, after=waits["read"]
    )
    width = 3 * half + PART
    cut = width // 2
    mem_blocks = Blocks(True, rows, width) if hops else None
    grad_tables, mem_grad = memory_back_call(
        place, coeff, grad_mem, tables, read_sums, grad_out, weights[7], mem_blocks
    )
    first = attend_back_call(doc_lengths, carried, projected, lse, grad_heads, more, 0, PAIRS // 2, after=[grad_tables])
    if hops:
        got_mem = hop(mem_grad[1], core=1)
        sent_mem, kept_mem = cut_halves(mem_grad[0], got_mem, cut, list(first[:1]))
        waits["second"] = list(sent_mem)
        got_mem = [hop(sent_mem[0], **x_hop), hop(sent_mem[1], **f_hop)]
    second = attend_back_call(
        doc_lengths, carried, projected, lse, grad_heads, more, PAIRS // 2, PAIRS // 2, after=waits["second"],
        work="attend_rest",
    )
    if hops:
        (sent_down, sent_up), kept_early = both_halves([kept_down, kept_up], [got_down, got_up], list(second[:1]))
        waits["input"] = [sent_down, sent_up]
        got_early = [hop(sent_down, **x_hop), hop(sent_up, **f_hop)]
    grads = [part for pair in zip(first, second) for part in pair]
    proj_blocks = Blocks(True, rows, width) if hops else None
    grad_tokens, done, proj_grad = input_back_call(
        place, tokens, vectors, normed, grads, grad_middle, sums, grad_up_bias, weights[2], proj_blocks,
        after=waits["input"],
    )
    if hops:
        got = hop(proj_grad[1], core=1)
        sent_early, own_early = added(list(zip(kept_early, got_early)), [done])
        got_early = hop(sent_early, z=1)
        sent_mem, kept_mem = both_halves(kept_mem, got_mem, [sent_early])
        got_mem = [hop(sent_mem[0], **f_hop), hop(sent_mem[1], **x_hop)]
        sent, kept = cut_halves(proj_grad[0], got, cut, list(sent_mem))
        got = [hop(sent[0], **x_hop), hop(sent[1], **f_hop)]
        sent_early, own_early = between(own_early, got_early, list(sent))
        got_early = hop(sent_early, z=2)
        sent_mem, own_mem = added(list(zip(kept_mem, got_mem)), [sent_early])
        got_mem = hop(sent_mem, z=1)
        sent, kept = both_halves(kept, got, [sent_mem])
        got = [hop(sent[0], **f_hop), hop(sent[1], **x_hop)]
        sent_mem, own_mem = between(own_mem, got_mem, list(sent))
        got_mem = hop(sent_mem, z=2)
        own, *sent = three_ways(list(zip(kept, got)), [sent_mem])
        got = [hop(part, z=k) for k, part in zip((1, 2, 3), sent)]
        every, below, quarter = slice(0, rows), slice(rows, 2 * rows), slice(0, half)
        outputs = [[(slice(0, 4 * rows), quarter)], [(slice((4 + q) * rows, (5 + q) * rows), quarter) for q in range(4)]]
        summed = {}
        summed[15], summed[13] = finish(own_early, [got_early], outputs, sent)
        outputs = [[(every, slice(0, half))], [(every, slice(half, cut)), (below, slice(0, 2 * half - cut))]]
        outputs += [[(below, slice(2 * half - cut, 3 * half - cut))]]
        first_table = 3 * half - cut
        outputs += [
            [(slice(rows, rows + 16), slice(first_table + n * H, first_table + (n + 1) * H))] for n in (0, 1)
        ]
        summed[5], summed[7], summed[8], summed[9], summed[10] = finish(own_mem, [got_mem], outputs, [summed[15]])
        ends = [shards[k].shape[0] for k in VECTORS] + [shards[14].shape[0]]
        outputs = [[(every, slice(0, 3 * half))]]
        outputs += [[(slice(n, n + 1), slice(3 * half, 3 * half + end))] for n, end in enumerate(ends)]
        summed[2], *lines = finish(own, got, outputs, [summed[9]])
        for k, line in zip(VECTORS + (14,), lines):
            summed[k] = line.reshape(-1)
    else:
        totals = {13: up_grad[0], 15: down_grad[0], 2: proj_grad[0], 14: grad_up_bias[0]}
        totals[5], totals[7], totals[8] = mem_grad
        totals[9], totals[10] = grad_tables[:, :H], grad_tables[:, H : 2 * H]
        for n, k in enumerate(VECTORS):
            totals[k] = proj_grad[1][n]
        summed = scatter_whole([totals[k] for k in range(17)])
    return (result, grad_tokens, *(summed[k] for k in range(17)), points)


def solution(mesh):
    both, row, table = P(BOTH), P("dp", "fsdp"), P(BOTH, None)
    block = P(BOTH, None, None)
    weights = (
        both, both, row, both, both, row, both, row, row, table, table, both, both, row, both, row, both,
    )
    in_specs = (block, block, block, table, both, table, block) + weights
    out_specs = (block, block) + weights + (table,)
    sizes = (mesh.shape["dp"], mesh.shape["fsdp"])
    return jax.shard_map(
        functools.partial(local, sizes), mesh=mesh, in_specs=in_specs, out_specs=out_specs, check_vma=False
    )
```
